32 devices in a mesh: samp: 8 (over z, y), layer: 4 (over x, core).
Axes of the slice: x: 2, y: 2, z: 4, core: 2. Of those that a mesh axis runs over, the one named last changes fastest.
Arguments:
- spins: int32 [64, 256], P('samp'), may hold values 0 or 1
- activations: bfloat16 [64, 8, 256, 256], P('samp', 'layer'), may hold values from -6 to 6
- cotangents: bfloat16 [64, 8, 256, 256], P('samp', 'layer'), may hold values from -0.023925781 to 0.023925781
- offdiag: float32 [64], P('samp'), may hold values from -24 to 24
Outputs:
- weights: float32 [64], P('samp')
- update: float32 [8, 256, 256], P('layer', 'samp')
The draws below stay inside these ranges and needn't reach their ends.
All inputs are finite; a program needn't handle non-finite values. No bound on the sum of `spins` on one device may be relied on, other than what follows from the above.
Results may differ from the reference program's by a relative error of at most 0.0029.
Values may be sent and summed in bfloat16 or wider, within the bound.
No kernel may reach another device: no remote copies, remote signals or barrier semaphores. Data moves between devices by JAX's collectives and lax.ppermute only.
A program may use at most 64 MiB of HBM per device.

```python
import jax
import jax.numpy as jnp
from jax import lax

SIDE = 16
SITES = 256
D = 256
MATS = 8
SAMPLES = 64


def plant(values, rng, smallest, top_value):
    longest = values.shape.index(max(values.shape))
    spots = []
    for shift in (0, 1):
        where = [jax.random.randint(jax.random.fold_in(rng, axis), (), 0, length) for axis, length in enumerate(values.shape)]
        where[longest] = (where[longest] + shift) % values.shape[longest]
        spots.append(tuple(where))
    return values.at[spots[0]].set(smallest).at[spots[1]].set(top_value)


def block_scale(stream_key, shape, split, smallest, top_value):
    level = 1.0
    for position, shards_of in split:
        heights = jax.random.uniform(jax.random.fold_in(jax.random.fold_in(stream_key, 6), position), (shards_of,), jnp.float32, smallest / len(split), top_value / len(split))
        level = level * jnp.repeat(jnp.exp(heights), shape[position] // shards_of).reshape((-1,) + (1,) * (len(shape) - 1 - position))
    return level


def bell_draw(own_key, shape, spread, most, cuts=(), kind=jnp.bfloat16):
    array = jax.random.normal(own_key, shape, jnp.float32) * spread
    if len(cuts) > 0:
        array = block_scale(own_key, shape, cuts, -0.22, 0.18) * array
    return jnp.clip(array, min=-most, max=most).astype(kind)


def setup_inputs(seed: int = 0) -> dict:
    seeds = jax.random.split(jax.random.key(seed), 5)
    spins = plant((jax.random.randint(seeds[0], (SAMPLES, SITES), 0, 2) < 1).astype(jnp.int32), jax.random.fold_in(seeds[0], 1), 0, 1)
    activations = bell_draw(seeds[1], (SAMPLES, MATS, SITES, D), 1.0, 6.0, ((0, 8), (1, 4)))
    cotangents = bell_draw(seeds[2], (SAMPLES, MATS, SITES, D), 0.004, 0.023925781, ((0, 8), (1, 4)))
    offdiag = bell_draw(seeds[3], (SAMPLES,), 4.0, 24.0, ((0, 8),), jnp.float32)
    return {"spins": spins, "activations": activations, "cotangents": cotangents, "offdiag": offdiag}


shift_ratio = 0.1

def local_energy(spins, offdiag):
    zvals = (2 * spins - 1).astype(jnp.float32).reshape(spins.shape[0], SIDE, SIDE)
    bonds = zvals * jnp.roll(zvals, -1, 2) + zvals * jnp.roll(zvals, -1, 1)
    return offdiag + lax.optimization_barrier(jnp.sum(bonds, axis=(1, 2)))

def jacobian_rows(act_mat, cot_mat):
    jac = jnp.einsum('sad,sae->sde', act_mat.astype(jnp.float32), cot_mat.astype(jnp.float32)).astype(jnp.bfloat16)
    flat = jac.reshape(jac.shape[0], -1).astype(jnp.float32)
    return flat - lax.optimization_barrier(jnp.mean(flat, axis=0, keepdims=True))

def reference(spins, activations, cotangents, offdiag):
    energy = local_energy(spins, offdiag)
    total = energy.shape[0]
    eps = (energy - jnp.mean(energy)) / jnp.sqrt(jnp.float32(total))
    act_t = jnp.swapaxes(activations, 0, 1)
    cot_t = jnp.swapaxes(cotangents, 0, 1)

    def add_gram(carry, pair):
        centered = jacobian_rows(pair[0], pair[1])
        return (carry + jnp.dot(centered, centered.T, precision=lax.Precision.HIGHEST), None)
    gram, _ = lax.scan(add_gram, jnp.zeros((total, total), jnp.float32), (act_t, cot_t))
    gram = gram / total
    shift = shift_ratio * jnp.trace(gram) / total
    chol = jnp.linalg.cholesky(gram + shift * jnp.eye(total, dtype=jnp.float32))
    half = jax.scipy.linalg.solve_triangular(chol, eps, lower=True)
    weights = jax.scipy.linalg.solve_triangular(chol.T, half, lower=False)

    def project(pair):
        centered = jacobian_rows(pair[0], pair[1])
        return jnp.dot(weights, centered, precision=lax.Precision.HIGHEST).reshape(D, D)
    update = lax.map(project, (act_t, cot_t))
    return (weights, update)
```

```python
import functools

import jax
import jax.numpy as jnp
from jax import lax
from jax.experimental import pallas as pl
from jax.experimental.pallas import tpu as pltpu
from jax.sharding import PartitionSpec as P

SIDE = 16
LANES = 128
CHUNK = 16
shift_ratio = 0.1
F32 = jnp.float32
BF16 = jnp.bfloat16


def iota(shape, dim):
    return lax.broadcasted_iota(jnp.int32, shape, dim)


def jac_kernel(act_ref, cot_ref, out_ref):
    mats = act_ref.shape[1]
    owners = out_ref.shape[0]
    share = out_ref.shape[2] // mats
    jacs = [
        lax.dot_general(
            act_ref[0, m], cot_ref[0, m], (((0,), (0,)), ((), ())), preferred_element_type=F32
        )
        for m in range(mats)
    ]
    for owner in range(owners):
        rows = [jac[owner * share : (owner + 1) * share] for jac in jacs]
        out_ref[owner, 0] = jnp.concatenate(rows, axis=0).astype(BF16)


def jac_rows(activations, cotangents, owners):
    samples, mats, sites, d = activations.shape
    rows = mats * d // owners
    block = pl.BlockSpec((1, mats, sites, d), lambda s: (s, 0, 0, 0))
    return pl.pallas_call(
        jac_kernel,
        grid=(samples,),
        in_specs=[block, block],
        out_specs=pl.BlockSpec((owners, 1, rows, d), lambda s: (0, s, 0, 0)),
        out_shape=jax.ShapeDtypeStruct((owners, samples, rows, d), BF16),
        cost_estimate=pl.CostEstimate(
            flops=2 * samples * mats * sites * d * d,
            bytes_accessed=6 * samples * mats * sites * d,
            transcendentals=0,
        ),
        name="jac_rows",
    )(activations, cotangents)


def energy_kernel(spins_ref, offdiag_ref, out_ref):
    total, width = out_ref.shape
    local = spins_ref.shape[0]
    sites = SIDE * SIDE
    z = (2 * spins_ref[...] - 1).astype(F32)
    column = iota((local, sites), 1) % SIDE
    right = jnp.where(
        column == SIDE - 1, pltpu.roll(z, SIDE - 1, 1), pltpu.roll(z, sites - 1, 1)
    )
    below = pltpu.roll(z, sites - SIDE, 1)
    energy = offdiag_ref[...] + jnp.sum(z * (right + below), axis=1, keepdims=True)
    first = lax.axis_index("samp") * local
    mine = lax.axis_index("layer") == 0
    spread = jnp.concatenate([energy] * (total // local), axis=0)
    row = iota((total, width), 0)
    here = (row >= first) & (row < first + local) & (iota((total, width), 1) == total) & mine
    out_ref[...] = jnp.where(here, spread, F32(0.0))


def energy_column(spins, offdiag, total, width):
    return pl.pallas_call(
        energy_kernel,
        out_shape=jax.ShapeDtypeStruct((total, width), F32),
        name="energy_column",
    )(spins, offdiag[:, None])


def gram_kernel(rows_ref, start_ref, out_ref):
    total, _, d = rows_ref.shape
    width = out_ref.shape[1]

    @pl.when(pl.program_id(0) == 0)
    def _():
        out_ref[...] = start_ref[...]

    block = CHUNK * CHUNK
    dest = iota((block, block), 0)
    source = (dest % CHUNK) * CHUNK + dest // CHUNK
    swap = (iota((block, block), 1) == source).astype(F32).astype(BF16)
    swapped = []
    for c in range(total // CHUNK):
        piece = rows_ref[c * CHUNK : (c + 1) * CHUNK].reshape(block, d)
        swapped.append(jnp.dot(swap, piece, preferred_element_type=F32).astype(BF16))
    acc = jnp.zeros((total, total), F32)
    for r in range(CHUNK):
        flat = jnp.concatenate([t[r * CHUNK : (r + 1) * CHUNK] for t in swapped], axis=0)
        acc = acc + lax.dot_general(
            flat, flat, (((1,), (1,)), ((), ())), preferred_element_type=F32
        )
    out_ref[:, :total] += acc


def gram_partial(rows, start):
    total, count, d = rows.shape
    width = start.shape[1]
    whole = pl.BlockSpec((total, width), lambda i: (0, 0))
    return pl.pallas_call(
        gram_kernel,
        grid=(count // CHUNK,),
        in_specs=[pl.BlockSpec((total, CHUNK, d), lambda i: (0, i, 0)), whole],
        out_specs=whole,
        out_shape=jax.ShapeDtypeStruct((total, width), F32),
        cost_estimate=pl.CostEstimate(
            flops=2 * total * total * count * d,
            bytes_accessed=2 * total * count * d,
            transcendentals=0,
        ),
        name="gram_partial",
    )(rows, start)


def eliminate(matrix, total):
    row = iota(matrix.shape, 0)
    lane = iota(matrix.shape, 1)
    if total <= 64:
        for k in range(total):
            column = matrix[:, k : k + 1]
            pivot_row = matrix[k : k + 1, :]
            scaled = pivot_row * (F32(1.0) / pivot_row[:, k : k + 1])
            matrix = matrix - jnp.where(row == k, F32(0.0), column) * scaled
    else:

        def one(k, held):
            column = jnp.sum(jnp.where(lane == k, held, F32(0.0)), axis=1, keepdims=True)
            pivot_row = jnp.sum(jnp.where(row == k, held, F32(0.0)), axis=0, keepdims=True)
            here = lane[:1] == k
            pivot = jnp.sum(jnp.where(here, pivot_row, F32(0.0)), axis=1, keepdims=True)
            scaled = pivot_row * (F32(1.0) / pivot)
            return held - jnp.where(row == k, F32(0.0), column) * scaled

        matrix = lax.fori_loop(0, total, one, matrix)
    diag = jnp.sum(jnp.where(row == lane, matrix, F32(0.0)), axis=1, keepdims=True)
    return matrix[:, total : total + 1] / diag


def solve_kernel(gram_ref, rows_ref, weights_ref, update_ref):
    total, width = gram_ref.shape
    mats, share, d = update_ref.shape
    local = weights_ref.shape[1]
    raw = gram_ref[...]
    row = iota((total, width), 0)
    lane = iota((total, width), 1)
    inside = lane < total
    scale = F32(1.0 / total)
    row_mean = jnp.sum(jnp.where(inside, raw, F32(0.0)), axis=1, keepdims=True) * scale
    col_mean = jnp.sum(raw, axis=0, keepdims=True) * scale
    mean = jnp.sum(row_mean, axis=0, keepdims=True) * scale
    gram = (raw - col_mean - row_mean + mean) * scale
    eps = (raw - col_mean) * F32(1.0 / total**0.5)
    on_diag = row == lane
    trace = jnp.sum(
        jnp.sum(jnp.where(on_diag, gram, F32(0.0)), axis=1, keepdims=True), axis=0, keepdims=True
    )
    shift = F32(shift_ratio) * trace * scale
    system = jnp.where(inside, gram + jnp.where(on_diag, shift, F32(0.0)), eps)
    weights = eliminate(system, total)
    first = lax.axis_index("samp") * local
    own = jnp.where(row - first == lane, weights, F32(0.0))
    weights_ref[...] = jnp.sum(own, axis=0, keepdims=True)[:, :local]
    coeffs = weights - jnp.sum(weights, axis=0, keepdims=True) * scale
    coeffs = jnp.broadcast_to(coeffs, (total, d))
    acc = jnp.zeros((mats * share, d), F32)
    for s in range(total):
        acc = acc + coeffs[s : s + 1] * rows_ref[s].astype(F32)
    for m in range(mats):
        update_ref[m] = acc[m * share : (m + 1) * share]


def solve_and_project(gram, rows, local, mats):
    total, count, d = rows.shape
    return pl.pallas_call(
        solve_kernel,
        out_shape=(
            jax.ShapeDtypeStruct((1, local), F32),
            jax.ShapeDtypeStruct((mats, count // mats, d), F32),
        ),
        name="solve_and_project",
    )(gram, rows)


def body(spins, activations, cotangents, offdiag):
    local, mats = activations.shape[:2]
    owners = lax.axis_size("samp")
    total = local * owners
    width = (total // LANES + 1) * LANES
    jac = jac_rows(activations, cotangents, owners)
    rows = lax.all_to_all(jac, "samp", split_axis=0, concat_axis=0, tiled=True)
    rows = rows.reshape(total, rows.shape[2], rows.shape[3])
    partial = gram_partial(rows, energy_column(spins, offdiag, total, width))
    gram = lax.psum(partial, ("samp", "layer"))
    weights, update = solve_and_project(gram, rows, local, mats)
    return weights.reshape(local), update


def solution(mesh):
    placed = (
        P("samp", None),
        P("samp", "layer", None, None),
        P("samp", "layer", None, None),
        P("samp"),
    )
    return jax.shard_map(
        body,
        mesh=mesh,
        in_specs=placed,
        out_specs=(P("samp"), P("layer", "samp", None)),
        check_vma=False,
    )
```

```python
import functools

import jax
import jax.numpy as jnp
from jax import lax
from jax.experimental import pallas as pl
from jax.experimental.pallas import tpu as pltpu
from jax.sharding import PartitionSpec as P

SIDE = 16
LANES = 128
CHUNK = 16
shift_ratio = 0.1
F32 = jnp.float32
BF16 = jnp.bfloat16


def iota(shape, dim):
    return lax.broadcasted_iota(jnp.int32, shape, dim)


def jac_kernel(act_ref, cot_ref, out_ref):
    mats = act_ref.shape[1]
    owners = out_ref.shape[0]
    share = out_ref.shape[2] // mats
    jacs = [
        lax.dot_general(
            act_ref[0, m], cot_ref[0, m], (((0,), (0,)), ((), ())), preferred_element_type=F32
        )
        for m in range(mats)
    ]
    for owner in range(owners):
        rows = [jac[owner * share : (owner + 1) * share] for jac in jacs]
        out_ref[owner, 0] = jnp.concatenate(rows, axis=0).astype(BF16)


def jac_rows(activations, cotangents, owners):
    samples, mats, sites, d = activations.shape
    rows = mats * d // owners
    block = pl.BlockSpec((1, mats, sites, d), lambda s: (s, 0, 0, 0))
    return pl.pallas_call(
        jac_kernel,
        grid=(samples,),
        in_specs=[block, block],
        out_specs=pl.BlockSpec((owners, 1, rows, d), lambda s: (0, s, 0, 0)),
        out_shape=jax.ShapeDtypeStruct((owners, samples, rows, d), BF16),
        cost_estimate=pl.CostEstimate(
            flops=2 * samples * mats * sites * d * d,
            bytes_accessed=6 * samples * mats * sites * d,
            transcendentals=0,
        ),
        name="jac_rows",
    )(activations, cotangents)


def energy_kernel(spins_ref, offdiag_ref, out_ref):
    total, width = out_ref.shape
    local = spins_ref.shape[0]
    sites = SIDE * SIDE
    z = (2 * spins_ref[...] - 1).astype(F32)
    column = iota((local, sites), 1) % SIDE
    right = jnp.where(
        column == SIDE - 1, pltpu.roll(z, SIDE - 1, 1), pltpu.roll(z, sites - 1, 1)
    )
    below = pltpu.roll(z, sites - SIDE, 1)
    energy = offdiag_ref[...] + jnp.sum(z * (right + below), axis=1, keepdims=True)
    first = lax.axis_index("samp") * local
    mine = lax.axis_index("layer") == 0
    spread = jnp.concatenate([energy] * (total // local), axis=0)
    row = iota((total, width), 0)
    here = (row >= first) & (row < first + local) & (iota((total, width), 1) == total) & mine
    out_ref[...] = jnp.where(here, spread, F32(0.0))


def energy_column(spins, offdiag, total, width):
    return pl.pallas_call(
        energy_kernel,
        out_shape=jax.ShapeDtypeStruct((total, width), F32),
        name="energy_column",
    )(spins, offdiag[:, None])


def gram_kernel(rows_ref, start_ref, out_ref):
    total, _, d = rows_ref.shape
    width = out_ref.shape[1]

    @pl.when(pl.program_id(0) == 0)
    def _():
        out_ref[...] = start_ref[...]

    block = CHUNK * CHUNK
    dest = iota((block, block), 0)
    source = (dest % CHUNK) * CHUNK + dest // CHUNK
    swap = (iota((block, block), 1) == source).astype(F32).astype(BF16)
    swapped = []
    for c in range(total // CHUNK):
        piece = rows_ref[c * CHUNK : (c + 1) * CHUNK].reshape(block, d)
        swapped.append(jnp.dot(swap, piece, preferred_element_type=F32).astype(BF16))
    acc = jnp.zeros((total, total), F32)
    for r in range(CHUNK):
        flat = jnp.concatenate([t[r * CHUNK : (r + 1) * CHUNK] for t in swapped], axis=0)
        acc = acc + lax.dot_general(
            flat, flat, (((1,), (1,)), ((), ())), preferred_element_type=F32
        )
    out_ref[:, :total] += acc


def gram_partial(rows, start):
    total, count, d = rows.shape
    width = start.shape[1]
    whole = pl.BlockSpec((total, width), lambda i: (0, 0))
    return pl.pallas_call(
        gram_kernel,
        grid=(count // CHUNK,),
        in_specs=[pl.BlockSpec((total, CHUNK, d), lambda i: (0, i, 0)), whole],
        out_specs=whole,
        out_shape=jax.ShapeDtypeStruct((total, width), F32),
        cost_estimate=pl.CostEstimate(
            flops=2 * total * total * count * d,
            bytes_accessed=2 * total * count * d,
            transcendentals=0,
        ),
        name="gram_partial",
    )(rows, start)


def eliminate(matrix, total):
    row = iota(matrix.shape, 0)
    lane = iota(matrix.shape, 1)
    if total <= 64:
        for k in range(total):
            column = matrix[:, k : k + 1]
            pivot_row = matrix[k : k + 1, :]
            scaled = pivot_row * (F32(1.0) / pivot_row[:, k : k + 1])
            matrix = matrix - jnp.where(row == k, F32(0.0), column) * scaled
    else:

        def one(k, held):
            column = jnp.sum(jnp.where(lane == k, held, F32(0.0)), axis=1, keepdims=True)
            pivot_row = jnp.sum(jnp.where(row == k, held, F32(0.0)), axis=0, keepdims=True)
            here = lane[:1] == k
            pivot = jnp.sum(jnp.where(here, pivot_row, F32(0.0)), axis=1, keepdims=True)
            scaled = pivot_row * (F32(1.0) / pivot)
            return held - jnp.where(row == k, F32(0.0), column) * scaled

        matrix = lax.fori_loop(0, total, one, matrix)
    diag = jnp.sum(jnp.where(row == lane, matrix, F32(0.0)), axis=1, keepdims=True)
    return matrix[:, total : total + 1] / diag


def tree_sum(parts):
    while len(parts) > 1:
        parts = [a + b for a, b in zip(parts[::2], parts[1::2])]
    return parts[0]


def partners(value, axis, first, count):
    size = lax.axis_size(axis)
    parts = [value]
    for k in range(1, count):
        perm = [(i, i ^ (k * first)) for i in range(size)]
        parts.append(lax.ppermute(value, axis, perm))
    return parts


def solve_kernel(*refs):
    *gram_refs, rows_ref, weights_ref, update_ref = refs
    total, width = gram_refs[0].shape
    mats, share, d = update_ref.shape
    local = weights_ref.shape[1]
    raw = tree_sum([ref[...] for ref in gram_refs])
    row = iota((total, width), 0)
    lane = iota((total, width), 1)
    inside = lane < total
    scale = F32(1.0 / total)
    row_mean = jnp.sum(jnp.where(inside, raw, F32(0.0)), axis=1, keepdims=True) * scale
    col_mean = jnp.sum(raw, axis=0, keepdims=True) * scale
    mean = jnp.sum(row_mean, axis=0, keepdims=True) * scale
    gram = (raw - col_mean - row_mean + mean) * scale
    eps = (raw - col_mean) * F32(1.0 / total**0.5)
    on_diag = row == lane
    trace = jnp.sum(
        jnp.sum(jnp.where(on_diag, gram, F32(0.0)), axis=1, keepdims=True), axis=0, keepdims=True
    )
    shift = F32(shift_ratio) * trace * scale
    system = jnp.where(inside, gram + jnp.where(on_diag, shift, F32(0.0)), eps)
    weights = eliminate(system, total)
    first = lax.axis_index("samp") * local
    own = jnp.where(row - first == lane, weights, F32(0.0))
    weights_ref[...] = jnp.sum(own, axis=0, keepdims=True)[:, :local]
    coeffs = weights - jnp.sum(weights, axis=0, keepdims=True) * scale
    coeffs = jnp.broadcast_to(coeffs, (total, d))
    acc = jnp.zeros((mats * share, d), F32)
    for s in range(total):
        acc = acc + coeffs[s : s + 1] * rows_ref[s].astype(F32)
    for m in range(mats):
        update_ref[m] = acc[m * share : (m + 1) * share]


def solve_and_project(grams, rows, local, mats):
    total, count, d = rows.shape
    return pl.pallas_call(
        solve_kernel,
        out_shape=(
            jax.ShapeDtypeStruct((1, local), F32),
            jax.ShapeDtypeStruct((mats, count // mats, d), F32),
        ),
        name="solve_and_project",
    )(*grams, rows)


def body(spins, activations, cotangents, offdiag):
    local, mats = activations.shape[:2]
    owners = lax.axis_size("samp")
    total = local * owners
    width = (total // LANES + 1) * LANES
    jac = jac_rows(activations, cotangents, owners)
    rows = lax.all_to_all(jac, "samp", split_axis=0, concat_axis=0, tiled=True)
    rows = rows.reshape(total, rows.shape[2], rows.shape[3])
    partial = gram_partial(rows, energy_column(spins, offdiag, total, width))
    gram = tree_sum(partners(partial, "layer", 1, lax.axis_size("layer")))
    reach = min(owners, 8)
    grams = partners(gram, "samp", 1, reach)
    if owners > reach:
        grams = partners(tree_sum(grams), "samp", reach, owners // reach)
    weights, update = solve_and_project(grams, rows, local, mats)
    return weights.reshape(local), update


def solution(mesh):
    placed = (
        P("samp", None),
        P("samp", "layer", None, None),
        P("samp", "layer", None, None),
        P("samp"),
    )
    return jax.shard_map(
        body,
        mesh=mesh,
        in_specs=placed,
        out_specs=(P("samp"), P("layer", "samp", None)),
        check_vma=False,
    )
```

```python
import functools

import jax
import jax.numpy as jnp
from jax import lax
from jax.experimental import pallas as pl
from jax.experimental.pallas import tpu as pltpu
from jax.sharding import PartitionSpec as P

SIDE = 16
LANES = 128
CHUNK = 16
shift_ratio = 0.1
F32 = jnp.float32
BF16 = jnp.bfloat16


def iota(shape, dim):
    return lax.broadcasted_iota(jnp.int32, shape, dim)


def jac_kernel(act_ref, cot_ref, out_ref):
    mats = act_ref.shape[1]
    owners = out_ref.shape[0]
    share = out_ref.shape[2] // mats
    jacs = [
        lax.dot_general(
            act_ref[0, m], cot_ref[0, m], (((0,), (0,)), ((), ())), preferred_element_type=F32
        )
        for m in range(mats)
    ]
    for owner in range(owners):
        rows = [jac[owner * share : (owner + 1) * share] for jac in jacs]
        out_ref[owner, 0] = jnp.concatenate(rows, axis=0).astype(BF16)


def jac_rows(activations, cotangents, owners):
    samples, mats, sites, d = activations.shape
    rows = mats * d // owners
    block = pl.BlockSpec((1, mats, sites, d), lambda s: (s, 0, 0, 0))
    return pl.pallas_call(
        jac_kernel,
        grid=(samples,),
        in_specs=[block, block],
        out_specs=pl.BlockSpec((owners, 1, rows, d), lambda s: (0, s, 0, 0)),
        out_shape=jax.ShapeDtypeStruct((owners, samples, rows, d), BF16),
        cost_estimate=pl.CostEstimate(
            flops=2 * samples * mats * sites * d * d,
            bytes_accessed=6 * samples * mats * sites * d,
            transcendentals=0,
        ),
        name="jac_rows",
    )(activations, cotangents)


def energy_kernel(spins_ref, offdiag_ref, out_ref):
    total, width = out_ref.shape
    local = spins_ref.shape[0]
    sites = SIDE * SIDE
    z = (2 * spins_ref[...] - 1).astype(F32)
    column = iota((local, sites), 1) % SIDE
    right = jnp.where(
        column == SIDE - 1, pltpu.roll(z, SIDE - 1, 1), pltpu.roll(z, sites - 1, 1)
    )
    below = pltpu.roll(z, sites - SIDE, 1)
    energy = offdiag_ref[...] + jnp.sum(z * (right + below), axis=1, keepdims=True)
    first = lax.axis_index("samp") * local
    mine = lax.axis_index("layer") == 0
    spread = jnp.concatenate([energy] * (total // local), axis=0)
    row = iota((total, width), 0)
    here = (row >= first) & (row < first + local) & (iota((total, width), 1) == total) & mine
    out_ref[...] = jnp.where(here, spread, F32(0.0))


def energy_column(spins, offdiag, total, width):
    return pl.pallas_call(
        energy_kernel,
        out_shape=jax.ShapeDtypeStruct((total, width), F32),
        name="energy_column",
    )(spins, offdiag[:, None])


def gram_kernel(rows_ref, start_ref, out_ref):
    total, _, d = rows_ref.shape
    width = out_ref.shape[1]

    @pl.when(pl.program_id(0) == 0)
    def _():
        out_ref[...] = start_ref[...]

    block = CHUNK * CHUNK
    dest = iota((block, block), 0)
    source = (dest % CHUNK) * CHUNK + dest // CHUNK
    swap = (iota((block, block), 1) == source).astype(F32).astype(BF16)
    swapped = []
    for c in range(total // CHUNK):
        piece = rows_ref[c * CHUNK : (c + 1) * CHUNK].reshape(block, d)
        swapped.append(jnp.dot(swap, piece, preferred_element_type=F32).astype(BF16))
    acc = jnp.zeros((total, total), F32)
    for r in range(CHUNK):
        flat = jnp.concatenate([t[r * CHUNK : (r + 1) * CHUNK] for t in swapped], axis=0)
        acc = acc + lax.dot_general(
            flat, flat, (((1,), (1,)), ((), ())), preferred_element_type=F32
        )
    out_ref[:, :total] += acc


def gram_partial(rows, start):
    total, count, d = rows.shape
    width = start.shape[1]
    whole = pl.BlockSpec((total, width), lambda i: (0, 0))
    return pl.pallas_call(
        gram_kernel,
        grid=(count // CHUNK,),
        in_specs=[pl.BlockSpec((total, CHUNK, d), lambda i: (0, i, 0)), whole],
        out_specs=whole,
        out_shape=jax.ShapeDtypeStruct((total, width), F32),
        cost_estimate=pl.CostEstimate(
            flops=2 * total * total * count * d,
            bytes_accessed=2 * total * count * d,
            transcendentals=0,
        ),
        name="gram_partial",
    )(rows, start)


def eliminate(matrix, total):
    row = iota(matrix.shape, 0)
    lane = iota(matrix.shape, 1)
    if total <= 64:
        for k in range(total):
            column = matrix[:, k : k + 1]
            pivot_row = matrix[k : k + 1, :]
            scaled = pivot_row * (F32(1.0) / pivot_row[:, k : k + 1])
            matrix = matrix - jnp.where(row == k, F32(0.0), column) * scaled
    else:

        def one(k, held):
            column = jnp.sum(jnp.where(lane == k, held, F32(0.0)), axis=1, keepdims=True)
            pivot_row = jnp.sum(jnp.where(row == k, held, F32(0.0)), axis=0, keepdims=True)
            here = lane[:1] == k
            pivot = jnp.sum(jnp.where(here, pivot_row, F32(0.0)), axis=1, keepdims=True)
            scaled = pivot_row * (F32(1.0) / pivot)
            return held - jnp.where(row == k, F32(0.0), column) * scaled

        matrix = lax.fori_loop(0, total, one, matrix)
    diag = jnp.sum(jnp.where(row == lane, matrix, F32(0.0)), axis=1, keepdims=True)
    return matrix[:, total : total + 1] / diag


def tree_sum(parts):
    while len(parts) > 1:
        parts = [a + b for a, b in zip(parts[::2], parts[1::2])]
    return parts[0]


def partners(value, axis, first, count):
    size = lax.axis_size(axis)
    parts = [value]
    for k in range(1, count):
        perm = [(i, i ^ (k * first)) for i in range(size)]
        parts.append(lax.ppermute(value, axis, perm))
    return parts


def solve_kernel(*refs):
    *gram_refs, rows_ref, weights_ref, update_ref = refs
    total, width = gram_refs[0].shape
    mats, share, d = update_ref.shape
    local = weights_ref.shape[1]
    raw = tree_sum([ref[...] for ref in gram_refs])
    row = iota((total, width), 0)
    lane = iota((total, width), 1)
    inside = lane < total
    scale = F32(1.0 / total)
    row_mean = jnp.sum(jnp.where(inside, raw, F32(0.0)), axis=1, keepdims=True) * scale
    col_mean = jnp.sum(raw, axis=0, keepdims=True) * scale
    mean = jnp.sum(row_mean, axis=0, keepdims=True) * scale
    gram = (raw - col_mean - row_mean + mean) * scale
    eps = (raw - col_mean) * F32(1.0 / total**0.5)
    on_diag = row == lane
    trace = jnp.sum(
        jnp.sum(jnp.where(on_diag, gram, F32(0.0)), axis=1, keepdims=True), axis=0, keepdims=True
    )
    shift = F32(shift_ratio) * trace * scale
    system = jnp.where(inside, gram + jnp.where(on_diag, shift, F32(0.0)), eps)
    weights = eliminate(system, total)
    first = lax.axis_index("samp") * local
    own = jnp.where(row - first == lane, weights, F32(0.0))
    weights_ref[...] = jnp.sum(own, axis=0, keepdims=True)[:, :local]
    coeffs = weights - jnp.sum(weights, axis=0, keepdims=True) * scale
    coeffs = jnp.broadcast_to(coeffs, (total, d))
    acc = jnp.zeros((mats * share, d), F32)
    for s in range(total):
        acc = acc + coeffs[s : s + 1] * rows_ref[s].astype(F32)
    for m in range(mats):
        update_ref[m] = acc[m * share : (m + 1) * share]


def solve_and_project(grams, rows, local, mats):
    total, count, d = rows.shape
    return pl.pallas_call(
        solve_kernel,
        out_shape=(
            jax.ShapeDtypeStruct((1, local), F32),
            jax.ShapeDtypeStruct((mats, count // mats, d), F32),
        ),
        name="solve_and_project",
    )(*grams, rows)


def body(spins, activations, cotangents, offdiag):
    local, mats = activations.shape[:2]
    owners = lax.axis_size("samp")
    total = local * owners
    width = (total // LANES + 1) * LANES
    jac = jac_rows(activations, cotangents, owners)
    rows = lax.all_to_all(jac, "samp", split_axis=0, concat_axis=0, tiled=True)
    rows = rows.reshape(total, rows.shape[2], rows.shape[3])
    partial = gram_partial(rows, energy_column(spins, offdiag, total, width))
    grams = partners(partial, "layer", 1, lax.axis_size("layer"))
    first = 1
    while first < owners:
        count = 2 if first == 1 else min(4, owners // first)
        grams = partners(tree_sum(grams), "samp", first, count)
        first *= count
    weights, update = solve_and_project(grams, rows, local, mats)
    return weights.reshape(local), update


def solution(mesh):
    placed = (
        P("samp", None),
        P("samp", "layer", None, None),
        P("samp", "layer", None, None),
        P("samp"),
    )
    return jax.shard_map(
        body,
        mesh=mesh,
        in_specs=placed,
        out_specs=(P("samp"), P("layer", "samp", None)),
        check_vma=False,
    )
```

```python
import functools

import jax
import jax.numpy as jnp
from jax import lax
from jax.experimental import pallas as pl
from jax.experimental.pallas import tpu as pltpu
from jax.sharding import PartitionSpec as P

SIDE = 16
LANES = 128
CHUNK = 16
shift_ratio = 0.1
F32 = jnp.float32
BF16 = jnp.bfloat16


def iota(shape, dim):
    return lax.broadcasted_iota(jnp.int32, shape, dim)


def jac_kernel(act_ref, cot_ref, out_ref):
    mats = act_ref.shape[1]
    owners = out_ref.shape[0]
    share = out_ref.shape[2] // mats
    jacs = [
        lax.dot_general(
            act_ref[0, m], cot_ref[0, m], (((0,), (0,)), ((), ())), preferred_element_type=F32
        )
        for m in range(mats)
    ]
    for owner in range(owners):
        rows = [jac[owner * share : (owner + 1) * share] for jac in jacs]
        out_ref[owner, 0] = jnp.concatenate(rows, axis=0).astype(BF16)


def jac_rows(activations, cotangents, owners, part, parts):
    samples, mats, sites, d = activations.shape
    mats //= parts
    rows = mats * d // owners
    block = pl.BlockSpec((1, mats, sites, d), lambda s: (s, part, 0, 0))
    return pl.pallas_call(
        jac_kernel,
        grid=(samples,),
        in_specs=[block, block],
        out_specs=pl.BlockSpec((owners, 1, rows, d), lambda s: (0, s, 0, 0)),
        out_shape=jax.ShapeDtypeStruct((owners, samples, rows, d), BF16),
        cost_estimate=pl.CostEstimate(
            flops=2 * samples * mats * sites * d * d,
            bytes_accessed=6 * samples * mats * sites * d,
            transcendentals=0,
        ),
        name="jac_rows",
    )(activations, cotangents)


def energy_kernel(spins_ref, offdiag_ref, out_ref):
    total, width = out_ref.shape
    local = spins_ref.shape[0]
    sites = SIDE * SIDE
    z = (2 * spins_ref[...] - 1).astype(F32)
    column = iota((local, sites), 1) % SIDE
    right = jnp.where(
        column == SIDE - 1, pltpu.roll(z, SIDE - 1, 1), pltpu.roll(z, sites - 1, 1)
    )
    below = pltpu.roll(z, sites - SIDE, 1)
    energy = offdiag_ref[...] + jnp.sum(z * (right + below), axis=1, keepdims=True)
    first = lax.axis_index("samp") * local
    mine = lax.axis_index("layer") == 0
    spread = jnp.concatenate([energy] * (total // local), axis=0)
    row = iota((total, width), 0)
    here = (row >= first) & (row < first + local) & (iota((total, width), 1) == total) & mine
    out_ref[...] = jnp.where(here, spread, F32(0.0))


def energy_column(spins, offdiag, total, width):
    return pl.pallas_call(
        energy_kernel,
        out_shape=jax.ShapeDtypeStruct((total, width), F32),
        name="energy_column",
    )(spins, offdiag[:, None])


def gram_kernel(rows_ref, start_ref, out_ref):
    total, _, d = rows_ref.shape
    width = out_ref.shape[1]

    @pl.when(pl.program_id(0) == 0)
    def _():
        out_ref[...] = start_ref[...]

    block = CHUNK * CHUNK
    dest = iota((block, block), 0)
    source = (dest % CHUNK) * CHUNK + dest // CHUNK
    swap = (iota((block, block), 1) == source).astype(F32).astype(BF16)
    swapped = []
    for c in range(total // CHUNK):
        piece = rows_ref[c * CHUNK : (c + 1) * CHUNK].reshape(block, d)
        swapped.append(jnp.dot(swap, piece, preferred_element_type=F32).astype(BF16))
    acc = jnp.zeros((total, total), F32)
    for r in range(CHUNK):
        flat = jnp.concatenate([t[r * CHUNK : (r + 1) * CHUNK] for t in swapped], axis=0)
        acc = acc + lax.dot_general(
            flat, flat, (((1,), (1,)), ((), ())), preferred_element_type=F32
        )
    out_ref[:, :total] += acc


def gram_partial(rows, start):
    total, count, d = rows.shape
    width = start.shape[1]
    whole = pl.BlockSpec((total, width), lambda i: (0, 0))
    return pl.pallas_call(
        gram_kernel,
        grid=(count // CHUNK,),
        in_specs=[pl.BlockSpec((total, CHUNK, d), lambda i: (0, i, 0)), whole],
        out_specs=whole,
        out_shape=jax.ShapeDtypeStruct((total, width), F32),
        cost_estimate=pl.CostEstimate(
            flops=2 * total * total * count * d,
            bytes_accessed=2 * total * count * d,
            transcendentals=0,
        ),
        name="gram_partial",
    )(rows, start)


def eliminate(matrix, total):
    row = iota(matrix.shape, 0)
    lane = iota(matrix.shape, 1)
    if total <= 64:
        for k in range(total):
            column = matrix[:, k : k + 1]
            pivot_row = matrix[k : k + 1, :]
            scaled = pivot_row * (F32(1.0) / pivot_row[:, k : k + 1])
            matrix = matrix - jnp.where(row == k, F32(0.0), column) * scaled
    else:

        def one(k, held):
            column = jnp.sum(jnp.where(lane == k, held, F32(0.0)), axis=1, keepdims=True)
            pivot_row = jnp.sum(jnp.where(row == k, held, F32(0.0)), axis=0, keepdims=True)
            here = lane[:1] == k
            pivot = jnp.sum(jnp.where(here, pivot_row, F32(0.0)), axis=1, keepdims=True)
            scaled = pivot_row * (F32(1.0) / pivot)
            return held - jnp.where(row == k, F32(0.0), column) * scaled

        matrix = lax.fori_loop(0, total, one, matrix)
    diag = jnp.sum(jnp.where(row == lane, matrix, F32(0.0)), axis=1, keepdims=True)
    return matrix[:, total : total + 1] / diag


def tree_sum(parts):
    while len(parts) > 1:
        parts = [a + b for a, b in zip(parts[::2], parts[1::2])]
    return parts[0]


def partners(value, axis, first, count):
    size = lax.axis_size(axis)
    parts = [value]
    for k in range(1, count):
        perm = [(i, i ^ (k * first)) for i in range(size)]
        parts.append(lax.ppermute(value, axis, perm))
    return parts


def solve_kernel(*refs):
    weights_ref, update_ref = refs[-2:]
    mats, share, d = update_ref.shape
    local = weights_ref.shape[1]
    gram_refs = [ref for ref in refs[:-2] if len(ref.shape) == 2]
    rows_refs = [ref for ref in refs[:-2] if len(ref.shape) == 3]
    total, width = gram_refs[0].shape
    raw = tree_sum([ref[...] for ref in gram_refs])
    row = iota((total, width), 0)
    lane = iota((total, width), 1)
    inside = lane < total
    scale = F32(1.0 / total)
    row_mean = jnp.sum(jnp.where(inside, raw, F32(0.0)), axis=1, keepdims=True) * scale
    col_mean = jnp.sum(raw, axis=0, keepdims=True) * scale
    mean = jnp.sum(row_mean, axis=0, keepdims=True) * scale
    gram = (raw - col_mean - row_mean + mean) * scale
    eps = (raw - col_mean) * F32(1.0 / total**0.5)
    on_diag = row == lane
    trace = jnp.sum(
        jnp.sum(jnp.where(on_diag, gram, F32(0.0)), axis=1, keepdims=True), axis=0, keepdims=True
    )
    shift = F32(shift_ratio) * trace * scale
    system = jnp.where(inside, gram + jnp.where(on_diag, shift, F32(0.0)), eps)
    weights = eliminate(system, total)
    first = lax.axis_index("samp") * local
    own = jnp.where(row - first == lane, weights, F32(0.0))
    weights_ref[...] = jnp.sum(own, axis=0, keepdims=True)[:, :local]
    coeffs = weights - jnp.sum(weights, axis=0, keepdims=True) * scale
    coeffs = jnp.broadcast_to(coeffs, (total, d))
    held = mats // len(rows_refs)
    for part, rows_ref in enumerate(rows_refs):
        acc = jnp.zeros((held * share, d), F32)
        for s in range(total):
            acc = acc + coeffs[s : s + 1] * rows_ref[s].astype(F32)
        for m in range(held):
            update_ref[part * held + m] = acc[m * share : (m + 1) * share]


def solve_and_project(grams, rows, local, mats):
    total, count, d = rows[0].shape
    return pl.pallas_call(
        solve_kernel,
        out_shape=(
            jax.ShapeDtypeStruct((1, local), F32),
            jax.ShapeDtypeStruct((mats, count * len(rows) // mats, d), F32),
        ),
        name="solve_and_project",
    )(*grams, *rows)


def body(spins, activations, cotangents, offdiag):
    local, mats = activations.shape[:2]
    owners = lax.axis_size("samp")
    total = local * owners
    width = (total // LANES + 1) * LANES
    share = activations.shape[3] // owners
    parts = mats if share % CHUNK == 0 else 1
    partial = energy_column(spins, offdiag, total, width)
    rows = []
    for part in range(parts):
        jac = jac_rows(activations, cotangents, owners, part, parts)
        held = lax.all_to_all(jac, "samp", split_axis=0, concat_axis=0, tiled=True)
        rows.append(held.reshape(total, held.shape[2], held.shape[3]))
    for held in rows:
        partial = gram_partial(held, partial)
    grams = partners(partial, "layer", 1, lax.axis_size("layer"))
    first = 1
    while first < owners:
        count = 2 if first == 1 else min(4, owners // first)
        grams = partners(tree_sum(grams), "samp", first, count)
        first *= count
    weights, update = solve_and_project(grams, rows, local, mats)
    return weights.reshape(local), update


def solution(mesh):
    placed = (
        P("samp", None),
        P("samp", "layer", None, None),
        P("samp", "layer", None, None),
        P("samp"),
    )
    return jax.shard_map(
        body,
        mesh=mesh,
        in_specs=placed,
        out_specs=(P("samp"), P("layer", "samp", None)),
        check_vma=False,
    )
```

```python
import functools

import jax
import jax.numpy as jnp
from jax import lax
from jax.experimental import pallas as pl
from jax.experimental.pallas import tpu as pltpu
from jax.sharding import PartitionSpec as P

SIDE = 16
LANES = 128
CHUNK = 16
VMEM_LIMIT = 24 * 2**20
shift_ratio = 0.1
F32 = jnp.float32
BF16 = jnp.bfloat16


def iota(shape, dim):
    return lax.broadcasted_iota(jnp.int32, shape, dim)


def jac_kernel(first, act_hbm, cot_hbm, *refs):
    *out_refs, act_buf, cot_buf, held, sems = refs
    samples, mats = act_buf.shape[:2]
    share = out_refs[0].shape[1] // mats
    me = lax.axis_index("samp")
    copies = []
    for s in range(samples):
        here = (s, pl.ds(first, mats))
        copies.append(pltpu.make_async_copy(act_hbm.at[here], act_buf.at[s], sems.at[0, s]))
        copies.append(pltpu.make_async_copy(cot_hbm.at[here], cot_buf.at[s], sems.at[1, s]))
    for copy in copies:
        copy.start()
    for s in range(samples):
        copies[2 * s].wait()
        copies[2 * s + 1].wait()
        for m in range(mats):
            held[s, m] = lax.dot_general(
                act_buf[s, m],
                cot_buf[s, m],
                (((0,), (0,)), ((), ())),
                preferred_element_type=F32,
            )
        for k, out_ref in enumerate(out_refs):
            owned = pl.ds(pl.multiple_of((me ^ k) * share, share), share)
            rows = [held[s, m, owned] for m in range(mats)]
            out_ref[s] = jnp.concatenate(rows, axis=0).astype(BF16)


def jac_rows(activations, cotangents, owners, part, parts):
    samples, mats, sites, d = activations.shape
    mats //= parts
    rows = mats * d // owners
    hbm = pl.BlockSpec(memory_space=pltpu.HBM)
    return pl.pallas_call(
        functools.partial(jac_kernel, part * mats),
        in_specs=[hbm, hbm],
        out_shape=[jax.ShapeDtypeStruct((samples, rows, d), BF16)] * owners,
        scratch_shapes=[
            pltpu.VMEM((samples, mats, sites, d), BF16),
            pltpu.VMEM((samples, mats, sites, d), BF16),
            pltpu.VMEM((samples, mats, d, d), F32),
            pltpu.SemaphoreType.DMA((2, samples)),
        ],
        compiler_params=pltpu.CompilerParams(vmem_limit_bytes=VMEM_LIMIT),
        cost_estimate=pl.CostEstimate(
            flops=2 * samples * mats * sites * d * d,
            bytes_accessed=6 * samples * mats * sites * d,
            transcendentals=0,
        ),
        name="jac_rows",
    )(activations, cotangents)


def energy_kernel(spins_ref, offdiag_ref, out_ref):
    total, width = out_ref.shape
    local = spins_ref.shape[0]
    sites = SIDE * SIDE
    z = (2 * spins_ref[...] - 1).astype(F32)
    column = iota((local, sites), 1) % SIDE
    right = jnp.where(
        column == SIDE - 1, pltpu.roll(z, SIDE - 1, 1), pltpu.roll(z, sites - 1, 1)
    )
    below = pltpu.roll(z, sites - SIDE, 1)
    energy = offdiag_ref[...] + jnp.sum(z * (right + below), axis=1, keepdims=True)
    first = lax.axis_index("samp") * local
    mine = lax.axis_index("layer") == 0
    spread = jnp.concatenate([energy] * (total // local), axis=0)
    row = iota((total, width), 0)
    here = (row >= first) & (row < first + local) & (iota((total, width), 1) == total) & mine
    out_ref[...] = jnp.where(here, spread, F32(0.0))


def energy_column(spins, offdiag, total, width):
    return pl.pallas_call(
        energy_kernel,
        out_shape=jax.ShapeDtypeStruct((total, width), F32),
        compiler_params=pltpu.CompilerParams(vmem_limit_bytes=VMEM_LIMIT),
        name="energy_column",
    )(spins, offdiag[:, None])


def gram_kernel(*refs):
    *block_refs, start_ref, out_ref, flat = refs
    local, count, d = block_refs[0].shape
    total = local * len(block_refs)
    joined = CHUNK // local
    me = lax.axis_index("samp")
    block = CHUNK * CHUNK
    dest = iota((block, block), 0)
    sample = dest % CHUNK
    sample = (sample // local ^ me % joined) * local + sample % local
    source = sample * CHUNK + dest // CHUNK
    swap = (iota((block, block), 1) == source).astype(F32).astype(BF16)
    for row in range(0, count, CHUNK):
        for j in range(len(block_refs) // joined):
            pieces = [ref[:, row : row + CHUNK] for ref in block_refs[j * joined : (j + 1) * joined]]
            piece = jnp.concatenate(pieces, axis=0).reshape(block, d)
            turned = jnp.dot(swap, piece, preferred_element_type=F32).astype(BF16)
            place = pl.ds(pl.multiple_of((me // joined ^ j) * CHUNK, CHUNK), CHUNK)
            for r in range(CHUNK):
                flat[row + r, place] = turned[r * CHUNK : (r + 1) * CHUNK]
    lined = jnp.concatenate([flat[r] for r in range(count)], axis=1)
    gram = lax.dot_general(lined, lined, (((1,), (1,)), ((), ())), preferred_element_type=F32)
    out_ref[...] = start_ref[...]
    out_ref[:, :total] += gram


def gram_partial(blocks, start):
    local, count, d = blocks[0].shape
    total, width = start.shape
    return pl.pallas_call(
        gram_kernel,
        out_shape=jax.ShapeDtypeStruct((total, width), F32),
        scratch_shapes=[pltpu.VMEM((count, total, d), BF16)],
        compiler_params=pltpu.CompilerParams(vmem_limit_bytes=VMEM_LIMIT),
        cost_estimate=pl.CostEstimate(
            flops=2 * total * total * count * d,
            bytes_accessed=2 * total * count * d,
            transcendentals=0,
        ),
        name="gram_partial",
    )(*blocks, start)


def eliminate(matrix, total):
    row = iota(matrix.shape, 0)
    lane = iota(matrix.shape, 1)
    if total <= 64:
        for k in range(total):
            column = matrix[:, k : k + 1]
            pivot_row = matrix[k : k + 1, :]
            scaled = pivot_row * (F32(1.0) / pivot_row[:, k : k + 1])
            matrix = matrix - jnp.where(row == k, F32(0.0), column) * scaled
    else:

        def one(k, held):
            column = jnp.sum(jnp.where(lane == k, held, F32(0.0)), axis=1, keepdims=True)
            pivot_row = jnp.sum(jnp.where(row == k, held, F32(0.0)), axis=0, keepdims=True)
            here = lane[:1] == k
            pivot = jnp.sum(jnp.where(here, pivot_row, F32(0.0)), axis=1, keepdims=True)
            scaled = pivot_row * (F32(1.0) / pivot)
            return held - jnp.where(row == k, F32(0.0), column) * scaled

        matrix = lax.fori_loop(0, total, one, matrix)
    diag = jnp.sum(jnp.where(row == lane, matrix, F32(0.0)), axis=1, keepdims=True)
    return matrix[:, total : total + 1] / diag


def tree_sum(parts):
    while len(parts) > 1:
        parts = [a + b for a, b in zip(parts[::2], parts[1::2])]
    return parts[0]


def partners(value, axis, first, count):
    size = lax.axis_size(axis)
    parts = [value]
    for k in range(1, count):
        perm = [(i, i ^ (k * first)) for i in range(size)]
        parts.append(lax.ppermute(value, axis, perm))
    return parts


def solve_kernel(owners, *refs):
    *in_refs, weights_ref, update_ref, held = refs
    mats, share, d = update_ref.shape
    local = weights_ref.shape[1]
    gram_refs = [ref for ref in in_refs if len(ref.shape) == 2]
    block_refs = [ref for ref in in_refs if len(ref.shape) == 3]
    total, width = gram_refs[0].shape
    raw = tree_sum([ref[...] for ref in gram_refs])
    row = iota((total, width), 0)
    lane = iota((total, width), 1)
    inside = lane < total
    scale = F32(1.0 / total)
    row_mean = jnp.sum(jnp.where(inside, raw, F32(0.0)), axis=1, keepdims=True) * scale
    col_mean = jnp.sum(raw, axis=0, keepdims=True) * scale
    mean = jnp.sum(row_mean, axis=0, keepdims=True) * scale
    gram = (raw - col_mean - row_mean + mean) * scale
    eps = (raw - col_mean) * F32(1.0 / total**0.5)
    on_diag = row == lane
    trace = jnp.sum(
        jnp.sum(jnp.where(on_diag, gram, F32(0.0)), axis=1, keepdims=True), axis=0, keepdims=True
    )
    shift = F32(shift_ratio) * trace * scale
    system = jnp.where(inside, gram + jnp.where(on_diag, shift, F32(0.0)), eps)
    weights = eliminate(system, total)
    me = lax.axis_index("samp")
    own = jnp.where(row - me * local == lane, weights, F32(0.0))
    weights_ref[...] = jnp.sum(own, axis=0, keepdims=True)[:, :local]
    coeffs = weights - jnp.sum(weights, axis=0, keepdims=True) * scale
    held[...] = jnp.broadcast_to(coeffs, (total, d))
    parts = len(block_refs) // owners
    each = mats // parts
    for part in range(parts):
        acc = jnp.zeros((each * share, d), F32)
        for k in range(owners):
            mine = held[pl.ds(pl.multiple_of((me ^ k) * local, local), local)]
            for s in range(local):
                acc = acc + mine[s : s + 1] * block_refs[part * owners + k][s].astype(F32)
        for m in range(each):
            update_ref[part * each + m] = acc[m * share : (m + 1) * share]


def solve_and_project(grams, parts, mats):
    total, width = grams[0].shape
    owners = len(parts[0])
    local, count, d = parts[0][0].shape
    share = count * len(parts) // mats
    return pl.pallas_call(
        functools.partial(solve_kernel, owners),
        out_shape=(
            jax.ShapeDtypeStruct((1, local), F32),
            jax.ShapeDtypeStruct((mats, share, d), F32),
        ),
        scratch_shapes=[pltpu.VMEM((total, d), F32)],
        compiler_params=pltpu.CompilerParams(vmem_limit_bytes=VMEM_LIMIT),
        name="solve_and_project",
    )(*grams, *[block for blocks in parts for block in blocks])


def body(spins, activations, cotangents, offdiag):
    local, mats = activations.shape[:2]
    owners = lax.axis_size("samp")
    total = local * owners
    width = (total // LANES + 1) * LANES
    share = activations.shape[3] // owners
    parts = mats if share % CHUNK == 0 else 1
    partial = energy_column(spins, offdiag, total, width)
    held = []
    for part in range(parts):
        blocks = list(jac_rows(activations, cotangents, owners, part, parts))
        for k in range(owners - 1, 0, -1):
            perm = [(i, i ^ k) for i in range(owners)]
            blocks[k] = lax.ppermute(blocks[k], "samp", perm)
        held.append(blocks)
    for blocks in held:
        partial = gram_partial(blocks, partial)
    grams = partners(partial, "layer", 1, lax.axis_size("layer"))
    first = 1
    while first < owners:
        count = 2 if first == 1 else min(4, owners // first)
        grams = partners(tree_sum(grams), "samp", first, count)
        first *= count
    weights, update = solve_and_project(grams, held, mats)
    return weights.reshape(local), update


def solution(mesh):
    placed = (
        P("samp", None),
        P("samp", "layer", None, None),
        P("samp", "layer", None, None),
        P("samp"),
    )
    return jax.shard_map(
        body,
        mesh=mesh,
        in_specs=placed,
        out_specs=(P("samp"), P("layer", "samp", None)),
        check_vma=False,
    )
```

```python
import functools

import jax
import jax.numpy as jnp
from jax import lax
from jax.experimental import pallas as pl
from jax.experimental.pallas import tpu as pltpu
from jax.sharding import PartitionSpec as P

SIDE = 16
LANES = 128
CHUNK = 16
VMEM_LIMIT = 24 * 2**20
JAC_VMEM_LIMIT = 60 * 2**20
shift_ratio = 0.1
F32 = jnp.float32
BF16 = jnp.bfloat16


def iota(shape, dim):
    return lax.broadcasted_iota(jnp.int32, shape, dim)


def jac_kernel(far, act_hbm, cot_hbm, *refs):
    *out_refs, act_buf, cot_buf, held, sems = refs
    samples, mats = act_buf.shape[:2]
    width = act_buf.shape[3]
    near = lax.axis_size("samp") // 2
    share = width // near
    me = lax.axis_index("samp")
    half = 1 - me // near if far else me // near
    columns = pl.ds(pl.multiple_of(half * width, width), width)
    copies = []
    for s in range(samples):
        copies.append(
            (
                pltpu.make_async_copy(act_hbm.at[s, :, :, columns], act_buf.at[s], sems.at[0, s]),
                pltpu.make_async_copy(cot_hbm.at[s], cot_buf.at[s], sems.at[1, s]),
            )
        )
    for pair in copies:
        for copy in pair:
            copy.start()
    group = 2
    for first in range(0, samples, group):
        for s in range(first, first + group):
            for copy in copies[s]:
                copy.wait()
        for s in range(first, first + group):
            for m in range(mats):
                held[s, m] = lax.dot_general(
                    act_buf[s, m],
                    cot_buf[s, m],
                    (((0,), (0,)), ((), ())),
                    preferred_element_type=F32,
                )
    for k in range(near):
        owner = (me ^ k) % near if far else k
        owned = pl.ds(owner * share, share)
        for s in range(samples):
            rows = jnp.concatenate([held[s, m, owned] for m in range(mats)], axis=0).astype(BF16)
            if far:
                out_refs[k][s] = rows
            else:
                out_refs[0][k, s] = rows


def jac_rows(activations, cotangents, owners, far):
    samples, mats, sites, d = activations.shape
    near = owners // 2
    rows = mats * d // owners
    hbm = pl.BlockSpec(memory_space=pltpu.HBM)
    if far:
        out_shape = [jax.ShapeDtypeStruct((samples, rows, d), BF16)] * near
    else:
        out_shape = [jax.ShapeDtypeStruct((near, samples, rows, d), BF16)]
    return pl.pallas_call(
        functools.partial(jac_kernel, far),
        in_specs=[hbm, hbm],
        out_shape=out_shape,
        scratch_shapes=[
            pltpu.VMEM((samples, mats, sites, d // 2), BF16),
            pltpu.VMEM((samples, mats, sites, d), BF16),
            pltpu.VMEM((samples, mats, d // 2, d), F32),
            pltpu.SemaphoreType.DMA((2, samples)),
        ],
        compiler_params=pltpu.CompilerParams(vmem_limit_bytes=JAC_VMEM_LIMIT),
        cost_estimate=pl.CostEstimate(
            flops=samples * mats * sites * d * d,
            bytes_accessed=4 * samples * mats * sites * d,
            transcendentals=0,
        ),
        name="jac_rows",
    )(activations, cotangents)


def energy_kernel(spins_ref, offdiag_ref, out_ref):
    total, width = out_ref.shape
    local = spins_ref.shape[0]
    sites = SIDE * SIDE
    z = (2 * spins_ref[...] - 1).astype(F32)
    column = iota((local, sites), 1) % SIDE
    right = jnp.where(
        column == SIDE - 1, pltpu.roll(z, SIDE - 1, 1), pltpu.roll(z, sites - 1, 1)
    )
    below = pltpu.roll(z, sites - SIDE, 1)
    energy = offdiag_ref[...] + jnp.sum(z * (right + below), axis=1, keepdims=True)
    first = lax.axis_index("samp") * local
    mine = lax.axis_index("layer") == 0
    spread = jnp.concatenate([energy] * (total // local), axis=0)
    row = iota((total, width), 0)
    here = (row >= first) & (row < first + local) & (iota((total, width), 1) == total) & mine
    out_ref[...] = jnp.where(here, spread, F32(0.0))


def energy_column(spins, offdiag, total, width):
    return pl.pallas_call(
        energy_kernel,
        out_shape=jax.ShapeDtypeStruct((total, width), F32),
        compiler_params=pltpu.CompilerParams(vmem_limit_bytes=VMEM_LIMIT),
        name="energy_column",
    )(spins, offdiag[:, None])


def gram_kernel(*refs):
    near_ref, *far_refs, start_ref, out_ref, flat = refs
    near, local, count, d = near_ref.shape
    total = 2 * near * local
    joined = CHUNK // local
    me = lax.axis_index("samp")
    block = CHUNK * CHUNK
    dest = iota((block, block), 0)
    place = dest % CHUNK
    column = iota((block, block), 1)

    def turn(order):
        sample = (place // local ^ order) * local + place % local
        return (column == sample * CHUNK + dest // CHUNK).astype(F32).astype(BF16)

    turns = (turn(0), turn(me % joined))
    for row in range(0, count, CHUNK):
        here = slice(row, row + CHUNK)
        for j in range(near // joined):
            ks = range(j * joined, (j + 1) * joined)
            spots = ((me // near) * (near // joined) + j, me // joined ^ (near // joined + j))
            pieces = ([near_ref[k, :, here] for k in ks], [far_refs[k][:, here] for k in ks])
            for spot, piece, swap in zip(spots, pieces, turns):
                piece = jnp.concatenate(piece, axis=0).reshape(block, d)
                turned = jnp.dot(swap, piece, preferred_element_type=F32).astype(BF16)
                rows = pl.ds(pl.multiple_of(spot * CHUNK, CHUNK), CHUNK)
                for r in range(CHUNK):
                    flat[row + r, rows] = turned[r * CHUNK : (r + 1) * CHUNK]
    lined = jnp.concatenate([flat[r] for r in range(count)], axis=1)
    gram = lax.dot_general(lined, lined, (((1,), (1,)), ((), ())), preferred_element_type=F32)
    out_ref[...] = start_ref[...]
    out_ref[:, :total] += gram


def gram_partial(near, far, start):
    _, local, count, d = near.shape
    total, width = start.shape
    return pl.pallas_call(
        gram_kernel,
        out_shape=jax.ShapeDtypeStruct((total, width), F32),
        scratch_shapes=[pltpu.VMEM((count, total, d), BF16)],
        compiler_params=pltpu.CompilerParams(vmem_limit_bytes=VMEM_LIMIT),
        cost_estimate=pl.CostEstimate(
            flops=2 * total * total * count * d,
            bytes_accessed=2 * total * count * d,
            transcendentals=0,
        ),
        name="gram_partial",
    )(near, *far, start)


def eliminate(matrix, total):
    row = iota(matrix.shape, 0)
    lane = iota(matrix.shape, 1)
    if total <= 64:
        for k in range(total):
            column = matrix[:, k : k + 1]
            pivot_row = matrix[k : k + 1, :]
            scaled = pivot_row * (F32(1.0) / pivot_row[:, k : k + 1])
            matrix = matrix - jnp.where(row == k, F32(0.0), column) * scaled
    else:

        def one(k, held):
            column = jnp.sum(jnp.where(lane == k, held, F32(0.0)), axis=1, keepdims=True)
            pivot_row = jnp.sum(jnp.where(row == k, held, F32(0.0)), axis=0, keepdims=True)
            here = lane[:1] == k
            pivot = jnp.sum(jnp.where(here, pivot_row, F32(0.0)), axis=1, keepdims=True)
            scaled = pivot_row * (F32(1.0) / pivot)
            return held - jnp.where(row == k, F32(0.0), column) * scaled

        matrix = lax.fori_loop(0, total, one, matrix)
    diag = jnp.sum(jnp.where(row == lane, matrix, F32(0.0)), axis=1, keepdims=True)
    return matrix[:, total : total + 1] / diag


def tree_sum(parts):
    while len(parts) > 1:
        parts = [a + b for a, b in zip(parts[::2], parts[1::2])]
    return parts[0]


def partners(value, axis, first, count):
    size = lax.axis_size(axis)
    parts = [value]
    for k in range(1, count):
        perm = [(i, i ^ (k * first)) for i in range(size)]
        parts.append(lax.ppermute(value, axis, perm))
    return parts


def spread(held, owner, local):
    return held[pl.ds(pl.multiple_of(owner * local, local), local)]


def solve_kernel(grams, *refs):
    gram_refs, refs = refs[:grams], refs[grams:]
    near_ref, *far_refs, weights_ref, update_ref, held = refs
    mats, share, d = update_ref.shape
    near, local = near_ref.shape[:2]
    total, width = gram_refs[0].shape
    raw = tree_sum([ref[...] for ref in gram_refs])
    row = iota((total, width), 0)
    lane = iota((total, width), 1)
    inside = lane < total
    scale = F32(1.0 / total)
    row_mean = jnp.sum(jnp.where(inside, raw, F32(0.0)), axis=1, keepdims=True) * scale
    col_mean = jnp.sum(raw, axis=0, keepdims=True) * scale
    mean = jnp.sum(row_mean, axis=0, keepdims=True) * scale
    gram = (raw - col_mean - row_mean + mean) * scale
    eps = (raw - col_mean) * F32(1.0 / total**0.5)
    on_diag = row == lane
    trace = jnp.sum(
        jnp.sum(jnp.where(on_diag, gram, F32(0.0)), axis=1, keepdims=True), axis=0, keepdims=True
    )
    shift = F32(shift_ratio) * trace * scale
    system = jnp.where(inside, gram + jnp.where(on_diag, shift, F32(0.0)), eps)
    weights = eliminate(system, total)
    me = lax.axis_index("samp")
    own = jnp.where(row - me * local == lane, weights, F32(0.0))
    weights_ref[...] = jnp.sum(own, axis=0, keepdims=True)[:, :local]
    coeffs = weights - jnp.sum(weights, axis=0, keepdims=True) * scale
    held[...] = jnp.broadcast_to(coeffs, (total, d))
    acc = jnp.zeros((mats * share, d), F32)
    for k in range(near):
        mine = spread(held, (me // near) * near + k, local)
        for s in range(local):
            acc = acc + mine[s : s + 1] * near_ref[k, s].astype(F32)
    for k, far_ref in enumerate(far_refs):
        mine = spread(held, me ^ (near + k), local)
        for s in range(local):
            acc = acc + mine[s : s + 1] * far_ref[s].astype(F32)
    for m in range(mats):
        update_ref[m] = acc[m * share : (m + 1) * share]


def solve_and_project(grams, near, far, mats):
    total, width = grams[0].shape
    _, local, count, d = near.shape
    return pl.pallas_call(
        functools.partial(solve_kernel, len(grams)),
        out_shape=(
            jax.ShapeDtypeStruct((1, local), F32),
            jax.ShapeDtypeStruct((mats, count // mats, d), F32),
        ),
        scratch_shapes=[pltpu.VMEM((total, d), F32)],
        compiler_params=pltpu.CompilerParams(vmem_limit_bytes=VMEM_LIMIT),
        name="solve_and_project",
    )(*grams, near, *far)


def body(spins, activations, cotangents, offdiag):
    local, mats = activations.shape[:2]
    owners = lax.axis_size("samp")
    near = owners // 2
    total = local * owners
    width = (total // LANES + 1) * LANES
    far_jac = jac_rows(activations, cotangents, owners, True)
    far = [
        lax.ppermute(block, "samp", [(i, i ^ (near + k)) for i in range(owners)])
        for k, block in enumerate(far_jac)
    ]
    near_jac = jac_rows(activations, cotangents, owners, False)[0]
    halves = [list(range(near)), list(range(near, owners))]
    near_rows = lax.all_to_all(
        near_jac, "samp", split_axis=0, concat_axis=0, tiled=True, axis_index_groups=halves
    )
    start = energy_column(spins, offdiag, total, width)
    partial = gram_partial(near_rows, far, start)
    grams = partners(partial, "layer", 1, lax.axis_size("layer"))
    first = 1
    while first < owners:
        count = 2 if first == 1 else min(4, owners // first)
        grams = partners(tree_sum(grams), "samp", first, count)
        first *= count
    weights, update = solve_and_project(grams, near_rows, far, mats)
    return weights.reshape(local), update


def solution(mesh):
    placed = (
        P("samp", None),
        P("samp", "layer", None, None),
        P("samp", "layer", None, None),
        P("samp"),
    )
    return jax.shard_map(
        body,
        mesh=mesh,
        in_specs=placed,
        out_specs=(P("samp"), P("layer", "samp", None)),
        check_vma=False,
    )
```

```python
import functools

import jax
import jax.numpy as jnp
from jax import lax
from jax.experimental import pallas as pl
from jax.experimental.pallas import tpu as pltpu
from jax.sharding import PartitionSpec as P

SIDE = 16
LANES = 128
CHUNK = 16
VMEM_LIMIT = 24 * 2**20
JAC_VMEM_LIMIT = 60 * 2**20
shift_ratio = 0.1
F32 = jnp.float32
BF16 = jnp.bfloat16


def iota(shape, dim):
    return lax.broadcasted_iota(jnp.int32, shape, dim)


def jac_kernel(far, after, act_hbm, cot_hbm, *refs):
    *out_refs, act_buf, cot_buf, held, sems = refs[after:]
    samples, mats = act_buf.shape[:2]
    width = act_buf.shape[3]
    near = lax.axis_size("samp") // 2
    share = width // near
    me = lax.axis_index("samp")
    half = 1 - me // near if far else me // near
    columns = pl.ds(pl.multiple_of(half * width, width), width)
    copies = []
    for s in range(samples):
        copies.append(
            (
                pltpu.make_async_copy(act_hbm.at[s, :, :, columns], act_buf.at[s], sems.at[0, s]),
                pltpu.make_async_copy(cot_hbm.at[s], cot_buf.at[s], sems.at[1, s]),
            )
        )
    for pair in copies:
        for copy in pair:
            copy.start()
    group = 2
    for first in range(0, samples, group):
        for s in range(first, first + group):
            for copy in copies[s]:
                copy.wait()
        for s in range(first, first + group):
            for m in range(mats):
                held[s, m] = lax.dot_general(
                    act_buf[s, m],
                    cot_buf[s, m],
                    (((0,), (0,)), ((), ())),
                    preferred_element_type=F32,
                )
    for k in range(near):
        owner = (me ^ k) % near if far else k
        owned = pl.ds(owner * share, share)
        for s in range(samples):
            rows = jnp.concatenate([held[s, m, owned] for m in range(mats)], axis=0).astype(BF16)
            if far:
                out_refs[k][s] = rows
            else:
                out_refs[0][k, s] = rows


def jac_rows(activations, cotangents, owners, far, after=()):
    samples, mats, sites, d = activations.shape
    near = owners // 2
    rows = mats * d // owners
    hbm = pl.BlockSpec(memory_space=pltpu.HBM)
    if far:
        out_shape = [jax.ShapeDtypeStruct((samples, rows, d), BF16)] * near
    else:
        out_shape = [jax.ShapeDtypeStruct((near, samples, rows, d), BF16)]
    return pl.pallas_call(
        functools.partial(jac_kernel, far, len(after)),
        in_specs=[hbm] * (2 + len(after)),
        out_shape=out_shape,
        scratch_shapes=[
            pltpu.VMEM((samples, mats, sites, d // 2), BF16),
            pltpu.VMEM((samples, mats, sites, d), BF16),
            pltpu.VMEM((samples, mats, d // 2, d), F32),
            pltpu.SemaphoreType.DMA((2, samples)),
        ],
        compiler_params=pltpu.CompilerParams(vmem_limit_bytes=JAC_VMEM_LIMIT),
        cost_estimate=pl.CostEstimate(
            flops=samples * mats * sites * d * d,
            bytes_accessed=4 * samples * mats * sites * d,
            transcendentals=0,
        ),
        name="jac_rows",
    )(activations, cotangents, *after)


def energy_kernel(spins_ref, offdiag_ref, out_ref):
    total, width = out_ref.shape
    local = spins_ref.shape[0]
    sites = SIDE * SIDE
    z = (2 * spins_ref[...] - 1).astype(F32)
    column = iota((local, sites), 1) % SIDE
    right = jnp.where(
        column == SIDE - 1, pltpu.roll(z, SIDE - 1, 1), pltpu.roll(z, sites - 1, 1)
    )
    below = pltpu.roll(z, sites - SIDE, 1)
    energy = offdiag_ref[...] + jnp.sum(z * (right + below), axis=1, keepdims=True)
    first = lax.axis_index("samp") * local
    mine = lax.axis_index("layer") == 0
    spread = jnp.concatenate([energy] * (total // local), axis=0)
    row = iota((total, width), 0)
    here = (row >= first) & (row < first + local) & (iota((total, width), 1) == total) & mine
    out_ref[...] = jnp.where(here, spread, F32(0.0))


def energy_column(spins, offdiag, total, width):
    return pl.pallas_call(
        energy_kernel,
        out_shape=jax.ShapeDtypeStruct((total, width), F32),
        compiler_params=pltpu.CompilerParams(vmem_limit_bytes=VMEM_LIMIT),
        name="energy_column",
    )(spins, offdiag[:, None])


def gram_kernel(*refs):
    near_ref, *far_refs, start_ref, out_ref, flat = refs
    near, local, count, d = near_ref.shape
    total = 2 * near * local
    joined = CHUNK // local
    me = lax.axis_index("samp")
    block = CHUNK * CHUNK
    dest = iota((block, block), 0)
    place = dest % CHUNK
    column = iota((block, block), 1)

    def turn(order):
        sample = (place // local ^ order) * local + place % local
        return (column == sample * CHUNK + dest // CHUNK).astype(F32).astype(BF16)

    turns = (turn(0), turn(me % joined))
    for row in range(0, count, CHUNK):
        here = slice(row, row + CHUNK)
        for j in range(near // joined):
            ks = range(j * joined, (j + 1) * joined)
            spots = ((me // near) * (near // joined) + j, me // joined ^ (near // joined + j))
            pieces = ([near_ref[k, :, here] for k in ks], [far_refs[k][:, here] for k in ks])
            for spot, piece, swap in zip(spots, pieces, turns):
                piece = jnp.concatenate(piece, axis=0).reshape(block, d)
                turned = jnp.dot(swap, piece, preferred_element_type=F32).astype(BF16)
                rows = pl.ds(pl.multiple_of(spot * CHUNK, CHUNK), CHUNK)
                for r in range(CHUNK):
                    flat[row + r, rows] = turned[r * CHUNK : (r + 1) * CHUNK]
    lined = jnp.concatenate([flat[r] for r in range(count)], axis=1)
    gram = lax.dot_general(lined, lined, (((1,), (1,)), ((), ())), preferred_element_type=F32)
    out_ref[...] = start_ref[...]
    out_ref[:, :total] += gram


def gram_partial(near, far, start):
    _, local, count, d = near.shape
    total, width = start.shape
    return pl.pallas_call(
        gram_kernel,
        out_shape=jax.ShapeDtypeStruct((total, width), F32),
        scratch_shapes=[pltpu.VMEM((count, total, d), BF16)],
        compiler_params=pltpu.CompilerParams(vmem_limit_bytes=VMEM_LIMIT),
        cost_estimate=pl.CostEstimate(
            flops=2 * total * total * count * d,
            bytes_accessed=2 * total * count * d,
            transcendentals=0,
        ),
        name="gram_partial",
    )(near, *far, start)


def eliminate(matrix, total):
    row = iota(matrix.shape, 0)
    lane = iota(matrix.shape, 1)
    if total <= 64:
        for k in range(total):
            column = matrix[:, k : k + 1]
            pivot_row = matrix[k : k + 1, :]
            scaled = pivot_row * (F32(1.0) / pivot_row[:, k : k + 1])
            matrix = matrix - jnp.where(row == k, F32(0.0), column) * scaled
    else:

        def one(k, held):
            column = jnp.sum(jnp.where(lane == k, held, F32(0.0)), axis=1, keepdims=True)
            pivot_row = jnp.sum(jnp.where(row == k, held, F32(0.0)), axis=0, keepdims=True)
            here = lane[:1] == k
            pivot = jnp.sum(jnp.where(here, pivot_row, F32(0.0)), axis=1, keepdims=True)
            scaled = pivot_row * (F32(1.0) / pivot)
            return held - jnp.where(row == k, F32(0.0), column) * scaled

        matrix = lax.fori_loop(0, total, one, matrix)
    diag = jnp.sum(jnp.where(row == lane, matrix, F32(0.0)), axis=1, keepdims=True)
    return matrix[:, total : total + 1] / diag


def tree_sum(parts):
    while len(parts) > 1:
        parts = [a + b for a, b in zip(parts[::2], parts[1::2])]
    return parts[0]


def partners(value, axis, first, count):
    size = lax.axis_size(axis)
    parts = [value]
    for k in range(1, count):
        perm = [(i, i ^ (k * first)) for i in range(size)]
        parts.append(lax.ppermute(value, axis, perm))
    return parts


def spread(held, owner, local):
    return held[pl.ds(pl.multiple_of(owner * local, local), local)]


def solve_kernel(grams, *refs):
    gram_refs, refs = refs[:grams], refs[grams:]
    near_ref, *far_refs, weights_ref, update_ref, held = refs
    mats, share, d = update_ref.shape
    near, local = near_ref.shape[:2]
    total, width = gram_refs[0].shape
    raw = tree_sum([ref[...] for ref in gram_refs])
    row = iota((total, width), 0)
    lane = iota((total, width), 1)
    inside = lane < total
    scale = F32(1.0 / total)
    row_mean = jnp.sum(jnp.where(inside, raw, F32(0.0)), axis=1, keepdims=True) * scale
    col_mean = jnp.sum(raw, axis=0, keepdims=True) * scale
    mean = jnp.sum(row_mean, axis=0, keepdims=True) * scale
    gram = (raw - col_mean - row_mean + mean) * scale
    eps = (raw - col_mean) * F32(1.0 / total**0.5)
    on_diag = row == lane
    trace = jnp.sum(
        jnp.sum(jnp.where(on_diag, gram, F32(0.0)), axis=1, keepdims=True), axis=0, keepdims=True
    )
    shift = F32(shift_ratio) * trace * scale
    system = jnp.where(inside, gram + jnp.where(on_diag, shift, F32(0.0)), eps)
    weights = eliminate(system, total)
    me = lax.axis_index("samp")
    own = jnp.where(row - me * local == lane, weights, F32(0.0))
    weights_ref[...] = jnp.sum(own, axis=0, keepdims=True)[:, :local]
    coeffs = weights - jnp.sum(weights, axis=0, keepdims=True) * scale
    held[...] = jnp.broadcast_to(coeffs, (total, d))
    acc = jnp.zeros((mats * share, d), F32)
    for k in range(near):
        mine = spread(held, (me // near) * near + k, local)
        for s in range(local):
            acc = acc + mine[s : s + 1] * near_ref[k, s].astype(F32)
    for k, far_ref in enumerate(far_refs):
        mine = spread(held, me ^ (near + k), local)
        for s in range(local):
            acc = acc + mine[s : s + 1] * far_ref[s].astype(F32)
    for m in range(mats):
        update_ref[m] = acc[m * share : (m + 1) * share]


def solve_and_project(grams, near, far, mats):
    total, width = grams[0].shape
    _, local, count, d = near.shape
    return pl.pallas_call(
        functools.partial(solve_kernel, len(grams)),
        out_shape=(
            jax.ShapeDtypeStruct((1, local), F32),
            jax.ShapeDtypeStruct((mats, count // mats, d), F32),
        ),
        scratch_shapes=[pltpu.VMEM((total, d), F32)],
        compiler_params=pltpu.CompilerParams(vmem_limit_bytes=VMEM_LIMIT),
        name="solve_and_project",
    )(*grams, near, *far)


def body(spins, activations, cotangents, offdiag):
    local, mats = activations.shape[:2]
    owners = lax.axis_size("samp")
    near = owners // 2
    total = local * owners
    width = (total // LANES + 1) * LANES
    far_jac = jac_rows(activations, cotangents, owners, True)
    far = [
        lax.ppermute(block, "samp", [(i, i ^ (near + k)) for i in range(owners)])
        for k, block in enumerate(far_jac)
    ]
    near_jac = jac_rows(activations, cotangents, owners, False, far_jac[:1])[0]
    halves = [list(range(near)), list(range(near, owners))]
    near_rows = lax.all_to_all(
        near_jac, "samp", split_axis=0, concat_axis=0, tiled=True, axis_index_groups=halves
    )
    start = energy_column(spins, offdiag, total, width)
    partial = gram_partial(near_rows, far, start)
    grams = partners(partial, "layer", 1, lax.axis_size("layer"))
    first = 1
    while first < owners:
        count = 2 if first == 1 else min(4, owners // first)
        grams = partners(tree_sum(grams), "samp", first, count)
        first *= count
    weights, update = solve_and_project(grams, near_rows, far, mats)
    return weights.reshape(local), update


def solution(mesh):
    placed = (
        P("samp", None),
        P("samp", "layer", None, None),
        P("samp", "layer", None, None),
        P("samp"),
    )
    return jax.shard_map(
        body,
        mesh=mesh,
        in_specs=placed,
        out_specs=(P("samp"), P("layer", "samp", None)),
        check_vma=False,
    )
```

```python
import functools

import jax
import jax.numpy as jnp
from jax import lax
from jax.experimental import pallas as pl
from jax.experimental.pallas import tpu as pltpu
from jax.sharding import PartitionSpec as P

SIDE = 16
LANES = 128
CHUNK = 16
VMEM_LIMIT = 24 * 2**20
JAC_VMEM_LIMIT = 60 * 2**20
shift_ratio = 0.1
F32 = jnp.float32
BF16 = jnp.bfloat16


def iota(shape, dim):
    return lax.broadcasted_iota(jnp.int32, shape, dim)


def jac_kernel(far, parts, act_hbm, cot_hbm, *refs):
    *out_refs, act_buf, cot_buf, held, sems = refs
    samples, mats = act_buf.shape[:2]
    width = act_buf.shape[3]
    near = lax.axis_size("samp") // 2
    share = width // near
    me = lax.axis_index("samp")
    half = 1 - me // near if far else me // near
    columns = pl.ds(pl.multiple_of(half * width, width), width)
    copies = []
    for s in range(samples):
        copies.append(
            (
                pltpu.make_async_copy(act_hbm.at[s, :, :, columns], act_buf.at[s], sems.at[0, s]),
                pltpu.make_async_copy(cot_hbm.at[s], cot_buf.at[s], sems.at[1, s]),
            )
        )
    for pair in copies:
        for copy in pair:
            copy.start()
    group = 2
    for first in range(0, samples, group):
        for s in range(first, first + group):
            for copy in copies[s]:
                copy.wait()
        for s in range(first, first + group):
            for m in range(mats):
                held[s, m] = lax.dot_general(
                    act_buf[s, m],
                    cot_buf[s, m],
                    (((0,), (0,)), ((), ())),
                    preferred_element_type=F32,
                )
    each = mats // parts
    for k in range(near):
        owned = pl.ds(pl.multiple_of((me ^ k) % near * share, share), share)
        for part in range(parts):
            for s in range(samples):
                rows = [held[s, part * each + m, owned] for m in range(each)]
                out_refs[part * near + k][s] = jnp.concatenate(rows, axis=0).astype(BF16)


def jac_rows(activations, cotangents, owners, parts, far):
    samples, mats, sites, d = activations.shape
    near = owners // 2
    rows = mats // parts * d // owners
    hbm = pl.BlockSpec(memory_space=pltpu.HBM)
    blocks = pl.pallas_call(
        functools.partial(jac_kernel, far, parts),
        in_specs=[hbm, hbm],
        out_shape=[jax.ShapeDtypeStruct((samples, rows, d), BF16)] * (parts * near),
        scratch_shapes=[
            pltpu.VMEM((samples, mats, sites, d // 2), BF16),
            pltpu.VMEM((samples, mats, sites, d), BF16),
            pltpu.VMEM((samples, mats, d // 2, d), F32),
            pltpu.SemaphoreType.DMA((2, samples)),
        ],
        compiler_params=pltpu.CompilerParams(vmem_limit_bytes=JAC_VMEM_LIMIT),
        cost_estimate=pl.CostEstimate(
            flops=samples * mats * sites * d * d,
            bytes_accessed=4 * samples * mats * sites * d,
            transcendentals=0,
        ),
        name="far_rows" if far else "near_rows",
    )(activations, cotangents)
    return [list(blocks[part * near : (part + 1) * near]) for part in range(parts)]


def energy_kernel(spins_ref, offdiag_ref, out_ref):
    total, width = out_ref.shape
    local = spins_ref.shape[0]
    sites = SIDE * SIDE
    z = (2 * spins_ref[...] - 1).astype(F32)
    column = iota((local, sites), 1) % SIDE
    right = jnp.where(
        column == SIDE - 1, pltpu.roll(z, SIDE - 1, 1), pltpu.roll(z, sites - 1, 1)
    )
    below = pltpu.roll(z, sites - SIDE, 1)
    energy = offdiag_ref[...] + jnp.sum(z * (right + below), axis=1, keepdims=True)
    first = lax.axis_index("samp") * local
    mine = lax.axis_index("layer") == 0
    spread = jnp.concatenate([energy] * (total // local), axis=0)
    row = iota((total, width), 0)
    here = (row >= first) & (row < first + local) & (iota((total, width), 1) == total) & mine
    out_ref[...] = jnp.where(here, spread, F32(0.0))


def energy_column(spins, offdiag, total, width):
    return pl.pallas_call(
        energy_kernel,
        out_shape=jax.ShapeDtypeStruct((total, width), F32),
        compiler_params=pltpu.CompilerParams(vmem_limit_bytes=VMEM_LIMIT),
        name="energy_column",
    )(spins, offdiag[:, None])


def gram_kernel(*refs):
    *block_refs, start_ref, out_ref, flat = refs
    local, count, d = block_refs[0].shape
    total = local * len(block_refs)
    joined = CHUNK // local
    me = lax.axis_index("samp")
    block = CHUNK * CHUNK
    dest = iota((block, block), 0)
    sample = dest % CHUNK
    sample = (sample // local ^ me % joined) * local + sample % local
    source = sample * CHUNK + dest // CHUNK
    swap = (iota((block, block), 1) == source).astype(F32).astype(BF16)
    for row in range(0, count, CHUNK):
        for j in range(len(block_refs) // joined):
            pieces = [ref[:, row : row + CHUNK] for ref in block_refs[j * joined : (j + 1) * joined]]
            piece = jnp.concatenate(pieces, axis=0).reshape(block, d)
            turned = jnp.dot(swap, piece, preferred_element_type=F32).astype(BF16)
            place = pl.ds(pl.multiple_of((me // joined ^ j) * CHUNK, CHUNK), CHUNK)
            for r in range(CHUNK):
                flat[row + r, place] = turned[r * CHUNK : (r + 1) * CHUNK]
    lined = jnp.concatenate([flat[r] for r in range(count)], axis=1)
    gram = lax.dot_general(lined, lined, (((1,), (1,)), ((), ())), preferred_element_type=F32)
    out_ref[...] = start_ref[...]
    out_ref[:, :total] += gram


def gram_partial(blocks, start):
    local, count, d = blocks[0].shape
    total, width = start.shape
    return pl.pallas_call(
        gram_kernel,
        out_shape=jax.ShapeDtypeStruct((total, width), F32),
        scratch_shapes=[pltpu.VMEM((count, total, d), BF16)],
        compiler_params=pltpu.CompilerParams(vmem_limit_bytes=VMEM_LIMIT),
        cost_estimate=pl.CostEstimate(
            flops=2 * total * total * count * d,
            bytes_accessed=2 * total * count * d,
            transcendentals=0,
        ),
        name="gram_partial",
    )(*blocks, start)


def eliminate(matrix, total):
    row = iota(matrix.shape, 0)
    lane = iota(matrix.shape, 1)
    if total <= 64:
        for k in range(total):
            column = matrix[:, k : k + 1]
            pivot_row = matrix[k : k + 1, :]
            scaled = pivot_row * (F32(1.0) / pivot_row[:, k : k + 1])
            matrix = matrix - jnp.where(row == k, F32(0.0), column) * scaled
    else:

        def one(k, held):
            column = jnp.sum(jnp.where(lane == k, held, F32(0.0)), axis=1, keepdims=True)
            pivot_row = jnp.sum(jnp.where(row == k, held, F32(0.0)), axis=0, keepdims=True)
            here = lane[:1] == k
            pivot = jnp.sum(jnp.where(here, pivot_row, F32(0.0)), axis=1, keepdims=True)
            scaled = pivot_row * (F32(1.0) / pivot)
            return held - jnp.where(row == k, F32(0.0), column) * scaled

        matrix = lax.fori_loop(0, total, one, matrix)
    diag = jnp.sum(jnp.where(row == lane, matrix, F32(0.0)), axis=1, keepdims=True)
    return matrix[:, total : total + 1] / diag


def tree_sum(parts):
    while len(parts) > 1:
        parts = [a + b for a, b in zip(parts[::2], parts[1::2])]
    return parts[0]


def partners(value, axis, first, count):
    size = lax.axis_size(axis)
    parts = [value]
    for k in range(1, count):
        perm = [(i, i ^ (k * first)) for i in range(size)]
        parts.append(lax.ppermute(value, axis, perm))
    return parts


def solve_kernel(owners, *refs):
    *in_refs, weights_ref, update_ref, held = refs
    mats, share, d = update_ref.shape
    local = weights_ref.shape[1]
    gram_refs = [ref for ref in in_refs if len(ref.shape) == 2]
    block_refs = [ref for ref in in_refs if len(ref.shape) == 3]
    total, width = gram_refs[0].shape
    raw = tree_sum([ref[...] for ref in gram_refs])
    row = iota((total, width), 0)
    lane = iota((total, width), 1)
    inside = lane < total
    scale = F32(1.0 / total)
    row_mean = jnp.sum(jnp.where(inside, raw, F32(0.0)), axis=1, keepdims=True) * scale
    col_mean = jnp.sum(raw, axis=0, keepdims=True) * scale
    mean = jnp.sum(row_mean, axis=0, keepdims=True) * scale
    gram = (raw - col_mean - row_mean + mean) * scale
    eps = (raw - col_mean) * F32(1.0 / total**0.5)
    on_diag = row == lane
    trace = jnp.sum(
        jnp.sum(jnp.where(on_diag, gram, F32(0.0)), axis=1, keepdims=True), axis=0, keepdims=True
    )
    shift = F32(shift_ratio) * trace * scale
    system = jnp.where(inside, gram + jnp.where(on_diag, shift, F32(0.0)), eps)
    weights = eliminate(system, total)
    me = lax.axis_index("samp")
    own = jnp.where(row - me * local == lane, weights, F32(0.0))
    weights_ref[...] = jnp.sum(own, axis=0, keepdims=True)[:, :local]
    coeffs = weights - jnp.sum(weights, axis=0, keepdims=True) * scale
    held[...] = jnp.broadcast_to(coeffs, (total, d))
    parts = len(block_refs) // owners
    each = mats // parts
    for part in range(parts):
        acc = jnp.zeros((each * share, d), F32)
        for k in range(owners):
            mine = held[pl.ds(pl.multiple_of((me ^ k) * local, local), local)]
            for s in range(local):
                acc = acc + mine[s : s + 1] * block_refs[part * owners + k][s].astype(F32)
        for m in range(each):
            update_ref[part * each + m] = acc[m * share : (m + 1) * share]


def solve_and_project(grams, parts, mats):
    total, width = grams[0].shape
    owners = len(parts[0])
    local, count, d = parts[0][0].shape
    share = count * len(parts) // mats
    return pl.pallas_call(
        functools.partial(solve_kernel, owners),
        out_shape=(
            jax.ShapeDtypeStruct((1, local), F32),
            jax.ShapeDtypeStruct((mats, share, d), F32),
        ),
        scratch_shapes=[pltpu.VMEM((total, d), F32)],
        compiler_params=pltpu.CompilerParams(vmem_limit_bytes=VMEM_LIMIT),
        name="solve_and_project",
    )(*grams, *[block for blocks in parts for block in blocks])


def exchange(far, near):
    parts, half = len(far), len(far[0])
    owners = 2 * half
    done = {(part, 0): near[part][0] for part in range(parts)}
    order = []
    far_left = [(part, k) for part in range(parts) for k in range(owners - 1, half - 1, -1)]
    near_left = [(part, k) for part in range(parts) for k in range(half - 1, 0, -1)]
    order += far_left[:half] + near_left[:1]
    far_left, near_left = far_left[half:], near_left[1:]
    while far_left or near_left:
        order += far_left[:2] + near_left[:1]
        far_left, near_left = far_left[2:], near_left[1:]
    for part, k in order:
        block = far[part][k - half] if k >= half else near[part][k]
        done[part, k] = lax.ppermute(block, "samp", [(i, i ^ k) for i in range(owners)])
    return [[done[part, k] for k in range(owners)] for part in range(parts)]


def body(spins, activations, cotangents, offdiag):
    local, mats = activations.shape[:2]
    owners = lax.axis_size("samp")
    total = local * owners
    width = (total // LANES + 1) * LANES
    share = activations.shape[3] // owners
    parts = mats if share % CHUNK == 0 else 1
    far = jac_rows(activations, cotangents, owners, parts, True)
    near = jac_rows(activations, cotangents, owners, parts, False)
    held = exchange(far, near)
    partial = energy_column(spins, offdiag, total, width)
    for blocks in held:
        partial = gram_partial(blocks, partial)
    grams = partners(partial, "layer", 1, lax.axis_size("layer"))
    first = 1
    while first < owners:
        count = 2 if first == 1 else min(4, owners // first)
        grams = partners(tree_sum(grams), "samp", first, count)
        first *= count
    weights, update = solve_and_project(grams, held, mats)
    return weights.reshape(local), update


def solution(mesh):
    placed = (
        P("samp", None),
        P("samp", "layer", None, None),
        P("samp", "layer", None, None),
        P("samp"),
    )
    return jax.shard_map(
        body,
        mesh=mesh,
        in_specs=placed,
        out_specs=(P("samp"), P("layer", "samp", None)),
        check_vma=False,
    )
```

```python
import functools

import jax
import jax.numpy as jnp
from jax import lax
from jax.experimental import pallas as pl
from jax.experimental.pallas import tpu as pltpu
from jax.sharding import PartitionSpec as P

SIDE = 16
LANES = 128
CHUNK = 16
VMEM_LIMIT = 24 * 2**20
FAR_VMEM_LIMIT = 60 * 2**20
shift_ratio = 0.1
F32 = jnp.float32
BF16 = jnp.bfloat16


def iota(shape, dim):
    return lax.broadcasted_iota(jnp.int32, shape, dim)


def jac_kernel(far, parts, act_hbm, cot_hbm, *refs):
    *out_refs, act_buf, cot_buf, held, sems = refs
    samples, mats = act_buf.shape[:2]
    width = act_buf.shape[3]
    near = lax.axis_size("samp") // 2
    share = width // near
    me = lax.axis_index("samp")
    half = 1 - me // near if far else me // near
    columns = pl.ds(pl.multiple_of(half * width, width), width)
    copies = []
    for s in range(samples):
        copies.append(
            (
                pltpu.make_async_copy(act_hbm.at[s, :, :, columns], act_buf.at[s], sems.at[0, s]),
                pltpu.make_async_copy(cot_hbm.at[s], cot_buf.at[s], sems.at[1, s]),
            )
        )
    for pair in copies:
        for copy in pair:
            copy.start()
    group = 2
    for first in range(0, samples, group):
        for s in range(first, first + group):
            for copy in copies[s]:
                copy.wait()
        for s in range(first, first + group):
            for m in range(mats):
                held[s, m] = lax.dot_general(
                    act_buf[s, m],
                    cot_buf[s, m],
                    (((0,), (0,)), ((), ())),
                    preferred_element_type=F32,
                )
    each = mats // parts
    for k in range(near):
        owned = pl.ds(pl.multiple_of((me ^ k) % near * share, share), share)
        for part in range(parts):
            for s in range(samples):
                rows = [held[s, part * each + m, owned] for m in range(each)]
                out_refs[part * near + k][s] = jnp.concatenate(rows, axis=0).astype(BF16)


def jac_rows(activations, cotangents, owners, parts, far):
    samples, mats, sites, d = activations.shape
    near = owners // 2
    rows = mats // parts * d // owners
    hbm = pl.BlockSpec(memory_space=pltpu.HBM)
    blocks = pl.pallas_call(
        functools.partial(jac_kernel, far, parts),
        in_specs=[hbm, hbm],
        out_shape=[jax.ShapeDtypeStruct((samples, rows, d), BF16)] * (parts * near),
        scratch_shapes=[
            pltpu.VMEM((samples, mats, sites, d // 2), BF16),
            pltpu.VMEM((samples, mats, sites, d), BF16),
            pltpu.VMEM((samples, mats, d // 2, d), F32),
            pltpu.SemaphoreType.DMA((2, samples)),
        ],
        compiler_params=pltpu.CompilerParams(
            vmem_limit_bytes=FAR_VMEM_LIMIT if far else VMEM_LIMIT
        ),
        cost_estimate=pl.CostEstimate(
            flops=samples * mats * sites * d * d,
            bytes_accessed=4 * samples * mats * sites * d,
            transcendentals=0,
        ),
        name="far_rows" if far else "near_rows",
    )(activations, cotangents)
    return [list(blocks[part * near : (part + 1) * near]) for part in range(parts)]


def energy_kernel(spins_ref, offdiag_ref, out_ref):
    total, width = out_ref.shape
    local = spins_ref.shape[0]
    sites = SIDE * SIDE
    z = (2 * spins_ref[...] - 1).astype(F32)
    column = iota((local, sites), 1) % SIDE
    right = jnp.where(
        column == SIDE - 1, pltpu.roll(z, SIDE - 1, 1), pltpu.roll(z, sites - 1, 1)
    )
    below = pltpu.roll(z, sites - SIDE, 1)
    energy = offdiag_ref[...] + jnp.sum(z * (right + below), axis=1, keepdims=True)
    first = lax.axis_index("samp") * local
    mine = lax.axis_index("layer") == 0
    spread = jnp.concatenate([energy] * (total // local), axis=0)
    row = iota((total, width), 0)
    here = (row >= first) & (row < first + local) & (iota((total, width), 1) == total) & mine
    out_ref[...] = jnp.where(here, spread, F32(0.0))


def energy_column(spins, offdiag, total, width):
    return pl.pallas_call(
        energy_kernel,
        out_shape=jax.ShapeDtypeStruct((total, width), F32),
        compiler_params=pltpu.CompilerParams(vmem_limit_bytes=VMEM_LIMIT),
        name="energy_column",
    )(spins, offdiag[:, None])


def gram_kernel(*refs):
    *block_refs, start_ref, out_ref, flat = refs
    local, count, d = block_refs[0].shape
    total = local * len(block_refs)
    joined = CHUNK // local
    me = lax.axis_index("samp")
    block = CHUNK * CHUNK
    dest = iota((block, block), 0)
    sample = dest % CHUNK
    sample = (sample // local ^ me % joined) * local + sample % local
    source = sample * CHUNK + dest // CHUNK
    swap = (iota((block, block), 1) == source).astype(F32).astype(BF16)
    for row in range(0, count, CHUNK):
        for j in range(len(block_refs) // joined):
            pieces = [ref[:, row : row + CHUNK] for ref in block_refs[j * joined : (j + 1) * joined]]
            piece = jnp.concatenate(pieces, axis=0).reshape(block, d)
            turned = jnp.dot(swap, piece, preferred_element_type=F32).astype(BF16)
            place = pl.ds(pl.multiple_of((me // joined ^ j) * CHUNK, CHUNK), CHUNK)
            for r in range(CHUNK):
                flat[row + r, place] = turned[r * CHUNK : (r + 1) * CHUNK]
    lined = jnp.concatenate([flat[r] for r in range(count)], axis=1)
    gram = lax.dot_general(lined, lined, (((1,), (1,)), ((), ())), preferred_element_type=F32)
    out_ref[...] = start_ref[...]
    out_ref[:, :total] += gram


def gram_partial(blocks, start):
    local, count, d = blocks[0].shape
    total, width = start.shape
    return pl.pallas_call(
        gram_kernel,
        out_shape=jax.ShapeDtypeStruct((total, width), F32),
        scratch_shapes=[pltpu.VMEM((count, total, d), BF16)],
        compiler_params=pltpu.CompilerParams(vmem_limit_bytes=VMEM_LIMIT),
        cost_estimate=pl.CostEstimate(
            flops=2 * total * total * count * d,
            bytes_accessed=2 * total * count * d,
            transcendentals=0,
        ),
        name="gram_partial",
    )(*blocks, start)


def eliminate(matrix, total):
    row = iota(matrix.shape, 0)
    lane = iota(matrix.shape, 1)
    if total <= 64:
        for k in range(total):
            column = matrix[:, k : k + 1]
            pivot_row = matrix[k : k + 1, :]
            scaled = pivot_row * (F32(1.0) / pivot_row[:, k : k + 1])
            matrix = matrix - jnp.where(row == k, F32(0.0), column) * scaled
    else:

        def one(k, held):
            column = jnp.sum(jnp.where(lane == k, held, F32(0.0)), axis=1, keepdims=True)
            pivot_row = jnp.sum(jnp.where(row == k, held, F32(0.0)), axis=0, keepdims=True)
            here = lane[:1] == k
            pivot = jnp.sum(jnp.where(here, pivot_row, F32(0.0)), axis=1, keepdims=True)
            scaled = pivot_row * (F32(1.0) / pivot)
            return held - jnp.where(row == k, F32(0.0), column) * scaled

        matrix = lax.fori_loop(0, total, one, matrix)
    diag = jnp.sum(jnp.where(row == lane, matrix, F32(0.0)), axis=1, keepdims=True)
    return matrix[:, total : total + 1] / diag


def tree_sum(parts):
    while len(parts) > 1:
        parts = [a + b for a, b in zip(parts[::2], parts[1::2])]
    return parts[0]


def partners(value, axis, first, count):
    size = lax.axis_size(axis)
    parts = [value]
    for k in range(1, count):
        perm = [(i, i ^ (k * first)) for i in range(size)]
        parts.append(lax.ppermute(value, axis, perm))
    return parts


def solve_kernel(owners, *refs):
    *in_refs, weights_ref, update_ref, held = refs
    mats, share, d = update_ref.shape
    local = weights_ref.shape[1]
    gram_refs = [ref for ref in in_refs if len(ref.shape) == 2]
    block_refs = [ref for ref in in_refs if len(ref.shape) == 3]
    total, width = gram_refs[0].shape
    raw = tree_sum([ref[...] for ref in gram_refs])
    row = iota((total, width), 0)
    lane = iota((total, width), 1)
    inside = lane < total
    scale = F32(1.0 / total)
    row_mean = jnp.sum(jnp.where(inside, raw, F32(0.0)), axis=1, keepdims=True) * scale
    col_mean = jnp.sum(raw, axis=0, keepdims=True) * scale
    mean = jnp.sum(row_mean, axis=0, keepdims=True) * scale
    gram = (raw - col_mean - row_mean + mean) * scale
    eps = (raw - col_mean) * F32(1.0 / total**0.5)
    on_diag = row == lane
    trace = jnp.sum(
        jnp.sum(jnp.where(on_diag, gram, F32(0.0)), axis=1, keepdims=True), axis=0, keepdims=True
    )
    shift = F32(shift_ratio) * trace * scale
    system = jnp.where(inside, gram + jnp.where(on_diag, shift, F32(0.0)), eps)
    weights = eliminate(system, total)
    me = lax.axis_index("samp")
    own = jnp.where(row - me * local == lane, weights, F32(0.0))
    weights_ref[...] = jnp.sum(own, axis=0, keepdims=True)[:, :local]
    coeffs = weights - jnp.sum(weights, axis=0, keepdims=True) * scale
    held[...] = jnp.broadcast_to(coeffs, (total, d))
    parts = len(block_refs) // owners
    each = mats // parts
    for part in range(parts):
        acc = jnp.zeros((each * share, d), F32)
        for k in range(owners):
            mine = held[pl.ds(pl.multiple_of((me ^ k) * local, local), local)]
            for s in range(local):
                acc = acc + mine[s : s + 1] * block_refs[part * owners + k][s].astype(F32)
        for m in range(each):
            update_ref[part * each + m] = acc[m * share : (m + 1) * share]


def solve_and_project(grams, parts, mats):
    total, width = grams[0].shape
    owners = len(parts[0])
    local, count, d = parts[0][0].shape
    share = count * len(parts) // mats
    return pl.pallas_call(
        functools.partial(solve_kernel, owners),
        out_shape=(
            jax.ShapeDtypeStruct((1, local), F32),
            jax.ShapeDtypeStruct((mats, share, d), F32),
        ),
        scratch_shapes=[pltpu.VMEM((total, d), F32)],
        compiler_params=pltpu.CompilerParams(vmem_limit_bytes=VMEM_LIMIT),
        name="solve_and_project",
    )(*grams, *[block for blocks in parts for block in blocks])


def exchange(far, near):
    parts, half = len(far), len(far[0])
    owners = 2 * half
    done = {(part, 0): near[part][0] for part in range(parts)}
    order = []
    far_left = [(part, k) for part in range(parts) for k in range(owners - 1, half - 1, -1)]
    near_left = [(part, k) for part in range(parts) for k in range(half - 1, 0, -1)]
    order += far_left[:half] + near_left[:1]
    far_left, near_left = far_left[half:], near_left[1:]
    while far_left or near_left:
        order += far_left[:2] + near_left[:1]
        far_left, near_left = far_left[2:], near_left[1:]
    for part, k in order:
        block = far[part][k - half] if k >= half else near[part][k]
        done[part, k] = lax.ppermute(block, "samp", [(i, i ^ k) for i in range(owners)])
    return [[done[part, k] for k in range(owners)] for part in range(parts)]


def body(spins, activations, cotangents, offdiag):
    local, mats = activations.shape[:2]
    owners = lax.axis_size("samp")
    total = local * owners
    width = (total // LANES + 1) * LANES
    parts = 1
    far = jac_rows(activations, cotangents, owners, parts, True)
    near = jac_rows(activations, cotangents, owners, parts, False)
    held = exchange(far, near)
    partial = energy_column(spins, offdiag, total, width)
    for blocks in held:
        partial = gram_partial(blocks, partial)
    grams = partners(partial, "layer", 1, lax.axis_size("layer"))
    first = 1
    while first < owners:
        count = 2 if first == 1 else min(4, owners // first)
        grams = partners(tree_sum(grams), "samp", first, count)
        first *= count
    weights, update = solve_and_project(grams, held, mats)
    return weights.reshape(local), update


def solution(mesh):
    placed = (
        P("samp", None),
        P("samp", "layer", None, None),
        P("samp", "layer", None, None),
        P("samp"),
    )
    return jax.shard_map(
        body,
        mesh=mesh,
        in_specs=placed,
        out_specs=(P("samp"), P("layer", "samp", None)),
        check_vma=False,
    )
```

```python
import functools

import jax
import jax.numpy as jnp
from jax import lax
from jax.experimental import pallas as pl
from jax.experimental.pallas import tpu as pltpu
from jax.sharding import PartitionSpec as P

SIDE = 16
LANES = 128
CHUNK = 16
VMEM_LIMIT = 24 * 2**20
JAC_VMEM_LIMIT = 52 * 2**20
shift_ratio = 0.1
F32 = jnp.float32
BF16 = jnp.bfloat16


def iota(shape, dim):
    return lax.broadcasted_iota(jnp.int32, shape, dim)


def jac_kernel(act_hbm, cot_hbm, *refs):
    *out_refs, act_buf, cot_buf, held, sems = refs
    samples, mats = act_buf.shape[:2]
    share = out_refs[0].shape[1] // mats
    me = lax.axis_index("samp")
    copies = []
    for s in range(samples):
        copies.append(
            (
                pltpu.make_async_copy(act_hbm.at[s], act_buf.at[s], sems.at[0, s]),
                pltpu.make_async_copy(cot_hbm.at[s], cot_buf.at[s], sems.at[1, s]),
            )
        )
    for pair in copies:
        for copy in pair:
            copy.start()
    group = 2
    for first in range(0, samples, group):
        for s in range(first, first + group):
            for copy in copies[s]:
                copy.wait()
        for s in range(first, first + group):
            for m in range(mats):
                held[s, m] = lax.dot_general(
                    act_buf[s, m],
                    cot_buf[s, m],
                    (((0,), (0,)), ((), ())),
                    preferred_element_type=F32,
                )
    for k, out_ref in enumerate(out_refs):
        owned = pl.ds(pl.multiple_of((me ^ k) * share, share), share)
        for s in range(samples):
            rows = [held[s, m, owned] for m in range(mats)]
            out_ref[s] = jnp.concatenate(rows, axis=0).astype(BF16)


def jac_rows(activations, cotangents, owners):
    samples, mats, sites, d = activations.shape
    rows = mats * d // owners
    hbm = pl.BlockSpec(memory_space=pltpu.HBM)
    return pl.pallas_call(
        jac_kernel,
        in_specs=[hbm, hbm],
        out_shape=[jax.ShapeDtypeStruct((samples, rows, d), BF16)] * owners,
        scratch_shapes=[
            pltpu.VMEM((samples, mats, sites, d), BF16),
            pltpu.VMEM((samples, mats, sites, d), BF16),
            pltpu.VMEM((samples, mats, d, d), F32),
            pltpu.SemaphoreType.DMA((2, samples)),
        ],
        compiler_params=pltpu.CompilerParams(vmem_limit_bytes=JAC_VMEM_LIMIT),
        cost_estimate=pl.CostEstimate(
            flops=2 * samples * mats * sites * d * d,
            bytes_accessed=6 * samples * mats * sites * d,
            transcendentals=0,
        ),
        name="jac_rows",
    )(activations, cotangents)


def energy_kernel(spins_ref, offdiag_ref, out_ref):
    total, width = out_ref.shape
    local = spins_ref.shape[0]
    sites = SIDE * SIDE
    z = (2 * spins_ref[...] - 1).astype(F32)
    column = iota((local, sites), 1) % SIDE
    right = jnp.where(
        column == SIDE - 1, pltpu.roll(z, SIDE - 1, 1), pltpu.roll(z, sites - 1, 1)
    )
    below = pltpu.roll(z, sites - SIDE, 1)
    energy = offdiag_ref[...] + jnp.sum(z * (right + below), axis=1, keepdims=True)
    first = lax.axis_index("samp") * local
    mine = lax.axis_index("layer") == 0
    spread = jnp.concatenate([energy] * (total // local), axis=0)
    row = iota((total, width), 0)
    here = (row >= first) & (row < first + local) & (iota((total, width), 1) == total) & mine
    out_ref[...] = jnp.where(here, spread, F32(0.0))


def energy_column(spins, offdiag, total, width):
    return pl.pallas_call(
        energy_kernel,
        out_shape=jax.ShapeDtypeStruct((total, width), F32),
        compiler_params=pltpu.CompilerParams(vmem_limit_bytes=VMEM_LIMIT),
        name="energy_column",
    )(spins, offdiag[:, None])


def gram_kernel(*refs):
    *block_refs, start_ref, out_ref, flat = refs
    block_refs = block_refs[::-1]
    local, count, d = block_refs[0].shape
    total = local * len(block_refs)
    joined = CHUNK // local
    me = lax.axis_index("samp")
    block = CHUNK * CHUNK
    dest = iota((block, block), 0)
    sample = dest % CHUNK
    sample = (sample // local ^ me % joined) * local + sample % local
    source = sample * CHUNK + dest // CHUNK
    swap = (iota((block, block), 1) == source).astype(F32).astype(BF16)
    for row in range(0, count, CHUNK):
        for j in range(len(block_refs) // joined):
            pieces = [ref[:, row : row + CHUNK] for ref in block_refs[j * joined : (j + 1) * joined]]
            piece = jnp.concatenate(pieces, axis=0).reshape(block, d)
            turned = jnp.dot(swap, piece, preferred_element_type=F32).astype(BF16)
            place = pl.ds(pl.multiple_of((me // joined ^ j) * CHUNK, CHUNK), CHUNK)
            for r in range(CHUNK):
                flat[row + r, place] = turned[r * CHUNK : (r + 1) * CHUNK]
    lined = jnp.concatenate([flat[r] for r in range(count)], axis=1)
    gram = lax.dot_general(lined, lined, (((1,), (1,)), ((), ())), preferred_element_type=F32)
    out_ref[...] = start_ref[...]
    out_ref[:, :total] += gram


def gram_partial(blocks, start):
    local, count, d = blocks[0].shape
    total, width = start.shape
    return pl.pallas_call(
        gram_kernel,
        out_shape=jax.ShapeDtypeStruct((total, width), F32),
        scratch_shapes=[pltpu.VMEM((count, total, d), BF16)],
        compiler_params=pltpu.CompilerParams(vmem_limit_bytes=VMEM_LIMIT),
        cost_estimate=pl.CostEstimate(
            flops=2 * total * total * count * d,
            bytes_accessed=2 * total * count * d,
            transcendentals=0,
        ),
        name="gram_partial",
    )(*blocks[::-1], start)


def eliminate(matrix, total):
    row = iota(matrix.shape, 0)
    lane = iota(matrix.shape, 1)
    if total <= 64:
        for k in range(total):
            column = matrix[:, k : k + 1]
            pivot_row = matrix[k : k + 1, :]
            scaled = pivot_row * (F32(1.0) / pivot_row[:, k : k + 1])
            matrix = matrix - jnp.where(row == k, F32(0.0), column) * scaled
    else:

        def one(k, held):
            column = jnp.sum(jnp.where(lane == k, held, F32(0.0)), axis=1, keepdims=True)
            pivot_row = jnp.sum(jnp.where(row == k, held, F32(0.0)), axis=0, keepdims=True)
            here = lane[:1] == k
            pivot = jnp.sum(jnp.where(here, pivot_row, F32(0.0)), axis=1, keepdims=True)
            scaled = pivot_row * (F32(1.0) / pivot)
            return held - jnp.where(row == k, F32(0.0), column) * scaled

        matrix = lax.fori_loop(0, total, one, matrix)
    diag = jnp.sum(jnp.where(row == lane, matrix, F32(0.0)), axis=1, keepdims=True)
    return matrix[:, total : total + 1] / diag


def tree_sum(parts):
    while len(parts) > 1:
        parts = [a + b for a, b in zip(parts[::2], parts[1::2])]
    return parts[0]


def partners(value, axis, first, count):
    size = lax.axis_size(axis)
    parts = [value]
    for k in range(1, count):
        perm = [(i, i ^ (k * first)) for i in range(size)]
        parts.append(lax.ppermute(value, axis, perm))
    return parts


def solve_kernel(grams, *refs):
    gram_refs, (*block_refs, weights_ref, update_ref, held) = refs[:grams], refs[grams:]
    block_refs = block_refs[::-1]
    mats, share, d = update_ref.shape
    local = weights_ref.shape[1]
    total, width = gram_refs[0].shape
    raw = tree_sum([ref[...] for ref in gram_refs])
    row = iota((total, width), 0)
    lane = iota((total, width), 1)
    inside = lane < total
    scale = F32(1.0 / total)
    row_mean = jnp.sum(jnp.where(inside, raw, F32(0.0)), axis=1, keepdims=True) * scale
    col_mean = jnp.sum(raw, axis=0, keepdims=True) * scale
    mean = jnp.sum(row_mean, axis=0, keepdims=True) * scale
    gram = (raw - col_mean - row_mean + mean) * scale
    eps = (raw - col_mean) * F32(1.0 / total**0.5)
    on_diag = row == lane
    trace = jnp.sum(
        jnp.sum(jnp.where(on_diag, gram, F32(0.0)), axis=1, keepdims=True), axis=0, keepdims=True
    )
    shift = F32(shift_ratio) * trace * scale
    system = jnp.where(inside, gram + jnp.where(on_diag, shift, F32(0.0)), eps)
    weights = eliminate(system, total)
    me = lax.axis_index("samp")
    own = jnp.where(row - me * local == lane, weights, F32(0.0))
    weights_ref[...] = jnp.sum(own, axis=0, keepdims=True)[:, :local]
    coeffs = weights - jnp.sum(weights, axis=0, keepdims=True) * scale
    held[...] = jnp.broadcast_to(coeffs, (total, d))
    acc = jnp.zeros((mats * share, d), F32)
    for k, block_ref in enumerate(block_refs):
        mine = held[pl.ds(pl.multiple_of((me ^ k) * local, local), local)]
        for s in range(local):
            acc = acc + mine[s : s + 1] * block_ref[s].astype(F32)
    for m in range(mats):
        update_ref[m] = acc[m * share : (m + 1) * share]


def solve_and_project(grams, blocks, mats):
    total, width = grams[0].shape
    local, count, d = blocks[0].shape
    return pl.pallas_call(
        functools.partial(solve_kernel, len(grams)),
        out_shape=(
            jax.ShapeDtypeStruct((1, local), F32),
            jax.ShapeDtypeStruct((mats, count // mats, d), F32),
        ),
        scratch_shapes=[pltpu.VMEM((total, d), F32)],
        compiler_params=pltpu.CompilerParams(vmem_limit_bytes=VMEM_LIMIT),
        name="solve_and_project",
    )(*grams, *blocks[::-1])


def body(spins, activations, cotangents, offdiag):
    local, mats = activations.shape[:2]
    owners = lax.axis_size("samp")
    total = local * owners
    width = (total // LANES + 1) * LANES
    blocks = list(jac_rows(activations, cotangents, owners))
    for k in range(owners - 1, 0, -1):
        blocks[k] = lax.ppermute(blocks[k], "samp", [(i, i ^ k) for i in range(owners)])
    partial = gram_partial(blocks, energy_column(spins, offdiag, total, width))
    grams = partners(partial, "layer", 1, lax.axis_size("layer"))
    first = 1
    while first < owners:
        count = 2 if first == 1 else min(4, owners // first)
        grams = partners(tree_sum(grams), "samp", first, count)
        first *= count
    weights, update = solve_and_project(grams, blocks, mats)
    return weights.reshape(local), update


def solution(mesh):
    placed = (
        P("samp", None),
        P("samp", "layer", None, None),
        P("samp", "layer", None, None),
        P("samp"),
    )
    return jax.shard_map(
        body,
        mesh=mesh,
        in_specs=placed,
        out_specs=(P("samp"), P("layer", "samp", None)),
        check_vma=False,
    )
```

```python
import functools

import jax
import jax.numpy as jnp
from jax import lax
from jax.experimental import pallas as pl
from jax.experimental.pallas import tpu as pltpu
from jax.sharding import PartitionSpec as P

SIDE = 16
LANES = 128
CHUNK = 16
VMEM_LIMIT = 24 * 2**20
JAC_VMEM_LIMIT = 52 * 2**20
shift_ratio = 0.1
F32 = jnp.float32
BF16 = jnp.bfloat16


def iota(shape, dim):
    return lax.broadcasted_iota(jnp.int32, shape, dim)


def turns(owners):
    far, near = list(range(owners // 2, owners)), list(range(owners // 2 - 1, 0, -1))
    order = [far.pop(0)]
    while far or near:
        order += far[:1] + near[:1]
        far, near = far[1:], near[1:]
    return order + [0]


def in_turn(blocks):
    return [blocks[k] for k in turns(len(blocks))]


def in_place(blocks):
    order = turns(len(blocks))
    return [blocks[order.index(k)] for k in range(len(blocks))]


def jac_kernel(act_hbm, cot_hbm, *refs):
    *out_refs, act_buf, cot_buf, held, sems = refs
    samples, mats = act_buf.shape[:2]
    share = out_refs[0].shape[1] // mats
    me = lax.axis_index("samp")
    copies = []
    for s in range(samples):
        copies.append(
            (
                pltpu.make_async_copy(act_hbm.at[s], act_buf.at[s], sems.at[0, s]),
                pltpu.make_async_copy(cot_hbm.at[s], cot_buf.at[s], sems.at[1, s]),
            )
        )
    for pair in copies:
        for copy in pair:
            copy.start()
    group = 2
    for first in range(0, samples, group):
        for s in range(first, first + group):
            for copy in copies[s]:
                copy.wait()
        for s in range(first, first + group):
            for m in range(mats):
                held[s, m] = lax.dot_general(
                    act_buf[s, m],
                    cot_buf[s, m],
                    (((0,), (0,)), ((), ())),
                    preferred_element_type=F32,
                )
    for k, out_ref in enumerate(out_refs):
        owned = pl.ds(pl.multiple_of((me ^ k) * share, share), share)
        for s in range(samples):
            rows = [held[s, m, owned] for m in range(mats)]
            out_ref[s] = jnp.concatenate(rows, axis=0).astype(BF16)


def jac_rows(activations, cotangents, owners):
    samples, mats, sites, d = activations.shape
    rows = mats * d // owners
    hbm = pl.BlockSpec(memory_space=pltpu.HBM)
    return pl.pallas_call(
        jac_kernel,
        in_specs=[hbm, hbm],
        out_shape=[jax.ShapeDtypeStruct((samples, rows, d), BF16)] * owners,
        scratch_shapes=[
            pltpu.VMEM((samples, mats, sites, d), BF16),
            pltpu.VMEM((samples, mats, sites, d), BF16),
            pltpu.VMEM((samples, mats, d, d), F32),
            pltpu.SemaphoreType.DMA((2, samples)),
        ],
        compiler_params=pltpu.CompilerParams(vmem_limit_bytes=JAC_VMEM_LIMIT),
        cost_estimate=pl.CostEstimate(
            flops=2 * samples * mats * sites * d * d,
            bytes_accessed=6 * samples * mats * sites * d,
            transcendentals=0,
        ),
        name="jac_rows",
    )(activations, cotangents)


def energy_kernel(spins_ref, offdiag_ref, out_ref):
    total, width = out_ref.shape
    local = spins_ref.shape[0]
    sites = SIDE * SIDE
    z = (2 * spins_ref[...] - 1).astype(F32)
    column = iota((local, sites), 1) % SIDE
    right = jnp.where(
        column == SIDE - 1, pltpu.roll(z, SIDE - 1, 1), pltpu.roll(z, sites - 1, 1)
    )
    below = pltpu.roll(z, sites - SIDE, 1)
    energy = offdiag_ref[...] + jnp.sum(z * (right + below), axis=1, keepdims=True)
    first = lax.axis_index("samp") * local
    mine = lax.axis_index("layer") == 0
    spread = jnp.concatenate([energy] * (total // local), axis=0)
    row = iota((total, width), 0)
    here = (row >= first) & (row < first + local) & (iota((total, width), 1) == total) & mine
    out_ref[...] = jnp.where(here, spread, F32(0.0))


def energy_column(spins, offdiag, total, width):
    return pl.pallas_call(
        energy_kernel,
        out_shape=jax.ShapeDtypeStruct((total, width), F32),
        compiler_params=pltpu.CompilerParams(vmem_limit_bytes=VMEM_LIMIT),
        name="energy_column",
    )(spins, offdiag[:, None])


def gram_kernel(*refs):
    *block_refs, start_ref, out_ref, flat = refs
    block_refs = in_place(block_refs)
    local, count, d = block_refs[0].shape
    total = local * len(block_refs)
    joined = CHUNK // local
    me = lax.axis_index("samp")
    block = CHUNK * CHUNK
    dest = iota((block, block), 0)
    sample = dest % CHUNK
    sample = (sample // local ^ me % joined) * local + sample % local
    source = sample * CHUNK + dest // CHUNK
    swap = (iota((block, block), 1) == source).astype(F32).astype(BF16)
    for row in range(0, count, CHUNK):
        for j in range(len(block_refs) // joined):
            pieces = [ref[:, row : row + CHUNK] for ref in block_refs[j * joined : (j + 1) * joined]]
            piece = jnp.concatenate(pieces, axis=0).reshape(block, d)
            turned = jnp.dot(swap, piece, preferred_element_type=F32).astype(BF16)
            place = pl.ds(pl.multiple_of((me // joined ^ j) * CHUNK, CHUNK), CHUNK)
            for r in range(CHUNK):
                flat[row + r, place] = turned[r * CHUNK : (r + 1) * CHUNK]
    lined = jnp.concatenate([flat[r] for r in range(count)], axis=1)
    gram = lax.dot_general(lined, lined, (((1,), (1,)), ((), ())), preferred_element_type=F32)
    out_ref[...] = start_ref[...]
    out_ref[:, :total] += gram


def gram_partial(blocks, start):
    local, count, d = blocks[0].shape
    total, width = start.shape
    return pl.pallas_call(
        gram_kernel,
        out_shape=jax.ShapeDtypeStruct((total, width), F32),
        scratch_shapes=[pltpu.VMEM((count, total, d), BF16)],
        compiler_params=pltpu.CompilerParams(vmem_limit_bytes=VMEM_LIMIT),
        cost_estimate=pl.CostEstimate(
            flops=2 * total * total * count * d,
            bytes_accessed=2 * total * count * d,
            transcendentals=0,
        ),
        name="gram_partial",
    )(*in_turn(blocks), start)


def eliminate(matrix, total):
    row = iota(matrix.shape, 0)
    lane = iota(matrix.shape, 1)
    if total <= 64:
        for k in range(total):
            column = matrix[:, k : k + 1]
            pivot_row = matrix[k : k + 1, :]
            scaled = pivot_row * (F32(1.0) / pivot_row[:, k : k + 1])
            matrix = matrix - jnp.where(row == k, F32(0.0), column) * scaled
    else:

        def one(k, held):
            column = jnp.sum(jnp.where(lane == k, held, F32(0.0)), axis=1, keepdims=True)
            pivot_row = jnp.sum(jnp.where(row == k, held, F32(0.0)), axis=0, keepdims=True)
            here = lane[:1] == k
            pivot = jnp.sum(jnp.where(here, pivot_row, F32(0.0)), axis=1, keepdims=True)
            scaled = pivot_row * (F32(1.0) / pivot)
            return held - jnp.where(row == k, F32(0.0), column) * scaled

        matrix = lax.fori_loop(0, total, one, matrix)
    diag = jnp.sum(jnp.where(row == lane, matrix, F32(0.0)), axis=1, keepdims=True)
    return matrix[:, total : total + 1] / diag


def tree_sum(parts):
    while len(parts) > 1:
        parts = [a + b for a, b in zip(parts[::2], parts[1::2])]
    return parts[0]


def partners(value, axis, first, count):
    size = lax.axis_size(axis)
    parts = [value]
    for k in range(1, count):
        perm = [(i, i ^ (k * first)) for i in range(size)]
        parts.append(lax.ppermute(value, axis, perm))
    return parts


def solve_kernel(grams, *refs):
    gram_refs, (*block_refs, weights_ref, update_ref, held) = refs[:grams], refs[grams:]
    block_refs = in_place(block_refs)
    mats, share, d = update_ref.shape
    local = weights_ref.shape[1]
    total, width = gram_refs[0].shape
    raw = tree_sum([ref[...] for ref in gram_refs])
    row = iota((total, width), 0)
    lane = iota((total, width), 1)
    inside = lane < total
    scale = F32(1.0 / total)
    row_mean = jnp.sum(jnp.where(inside, raw, F32(0.0)), axis=1, keepdims=True) * scale
    col_mean = jnp.sum(raw, axis=0, keepdims=True) * scale
    mean = jnp.sum(row_mean, axis=0, keepdims=True) * scale
    gram = (raw - col_mean - row_mean + mean) * scale
    eps = (raw - col_mean) * F32(1.0 / total**0.5)
    on_diag = row == lane
    trace = jnp.sum(
        jnp.sum(jnp.where(on_diag, gram, F32(0.0)), axis=1, keepdims=True), axis=0, keepdims=True
    )
    shift = F32(shift_ratio) * trace * scale
    system = jnp.where(inside, gram + jnp.where(on_diag, shift, F32(0.0)), eps)
    weights = eliminate(system, total)
    me = lax.axis_index("samp")
    own = jnp.where(row - me * local == lane, weights, F32(0.0))
    weights_ref[...] = jnp.sum(own, axis=0, keepdims=True)[:, :local]
    coeffs = weights - jnp.sum(weights, axis=0, keepdims=True) * scale
    held[...] = jnp.broadcast_to(coeffs, (total, d))
    acc = jnp.zeros((mats * share, d), F32)
    for k, block_ref in enumerate(block_refs):
        mine = held[pl.ds(pl.multiple_of((me ^ k) * local, local), local)]
        for s in range(local):
            acc = acc + mine[s : s + 1] * block_ref[s].astype(F32)
    for m in range(mats):
        update_ref[m] = acc[m * share : (m + 1) * share]


def solve_and_project(grams, blocks, mats):
    total, width = grams[0].shape
    local, count, d = blocks[0].shape
    return pl.pallas_call(
        functools.partial(solve_kernel, len(grams)),
        out_shape=(
            jax.ShapeDtypeStruct((1, local), F32),
            jax.ShapeDtypeStruct((mats, count // mats, d), F32),
        ),
        scratch_shapes=[pltpu.VMEM((total, d), F32)],
        compiler_params=pltpu.CompilerParams(vmem_limit_bytes=VMEM_LIMIT),
        name="solve_and_project",
    )(*grams, *in_turn(blocks))


def body(spins, activations, cotangents, offdiag):
    local, mats = activations.shape[:2]
    owners = lax.axis_size("samp")
    total = local * owners
    width = (total // LANES + 1) * LANES
    blocks = list(jac_rows(activations, cotangents, owners))
    for k in turns(owners)[:-1]:
        blocks[k] = lax.ppermute(blocks[k], "samp", [(i, i ^ k) for i in range(owners)])
    partial = gram_partial(blocks, energy_column(spins, offdiag, total, width))
    grams = partners(partial, "layer", 1, lax.axis_size("layer"))
    first = 1
    while first < owners:
        count = 2 if first == 1 else min(4, owners // first)
        grams = partners(tree_sum(grams), "samp", first, count)
        first *= count
    weights, update = solve_and_project(grams, blocks, mats)
    return weights.reshape(local), update


def solution(mesh):
    placed = (
        P("samp", None),
        P("samp", "layer", None, None),
        P("samp", "layer", None, None),
        P("samp"),
    )
    return jax.shard_map(
        body,
        mesh=mesh,
        in_specs=placed,
        out_specs=(P("samp"), P("layer", "samp", None)),
        check_vma=False,
    )
```

```python
import jax
import jax.numpy as jnp
from jax import lax
from jax.experimental import pallas as pl
from jax.experimental.pallas import tpu as pltpu
from jax.sharding import PartitionSpec as P

SIDE = 16
LANES = 128
CHUNK = 16
VMEM_LIMIT = 24 * 2**20
JAC_VMEM_LIMIT = 52 * 2**20
shift_ratio = 0.1
F32 = jnp.float32
BF16 = jnp.bfloat16


def iota(shape, dim):
    return lax.broadcasted_iota(jnp.int32, shape, dim)


def turns(owners):
    far, near = list(range(owners // 2, owners)), list(range(owners // 2 - 1, 0, -1))
    order = [far.pop(0)]
    while far or near:
        order += far[:1] + near[:1]
        far, near = far[1:], near[1:]
    return order + [0]


def in_turn(blocks):
    return [blocks[k] for k in turns(len(blocks))]


def in_place(blocks):
    order = turns(len(blocks))
    return [blocks[order.index(k)] for k in range(len(blocks))]


def jac_kernel(act_hbm, cot_hbm, *refs):
    *out_refs, act_buf, cot_buf, held, sems = refs
    samples, mats = act_buf.shape[:2]
    share = out_refs[0].shape[1] // mats
    me = lax.axis_index("samp")
    copies = []
    for s in range(samples):
        copies.append(
            (
                pltpu.make_async_copy(act_hbm.at[s], act_buf.at[s], sems.at[0, s]),
                pltpu.make_async_copy(cot_hbm.at[s], cot_buf.at[s], sems.at[1, s]),
            )
        )
    for pair in copies:
        for copy in pair:
            copy.start()
    group = 2
    for first in range(0, samples, group):
        for s in range(first, first + group):
            for copy in copies[s]:
                copy.wait()
        for s in range(first, first + group):
            for m in range(mats):
                held[s, m] = lax.dot_general(
                    act_buf[s, m],
                    cot_buf[s, m],
                    (((0,), (0,)), ((), ())),
                    preferred_element_type=F32,
                )
    for k, out_ref in enumerate(out_refs):
        owned = pl.ds(pl.multiple_of((me ^ k) * share, share), share)
        for s in range(samples):
            rows = [held[s, m, owned] for m in range(mats)]
            out_ref[s] = jnp.concatenate(rows, axis=0).astype(BF16)


def jac_rows(activations, cotangents, owners):
    samples, mats, sites, d = activations.shape
    rows = mats * d // owners
    hbm = pl.BlockSpec(memory_space=pltpu.HBM)
    return pl.pallas_call(
        jac_kernel,
        in_specs=[hbm, hbm],
        out_shape=[jax.ShapeDtypeStruct((samples, rows, d), BF16)] * owners,
        scratch_shapes=[
            pltpu.VMEM((samples, mats, sites, d), BF16),
            pltpu.VMEM((samples, mats, sites, d), BF16),
            pltpu.VMEM((samples, mats, d, d), F32),
            pltpu.SemaphoreType.DMA((2, samples)),
        ],
        compiler_params=pltpu.CompilerParams(vmem_limit_bytes=JAC_VMEM_LIMIT),
        cost_estimate=pl.CostEstimate(
            flops=2 * samples * mats * sites * d * d,
            bytes_accessed=6 * samples * mats * sites * d,
            transcendentals=0,
        ),
        name="jac_rows",
    )(activations, cotangents)


def energy_kernel(spins_ref, offdiag_ref, out_ref):
    local, width = out_ref.shape
    sites = SIDE * SIDE
    z = (2 * spins_ref[...] - 1).astype(F32)
    column = iota((local, sites), 1) % SIDE
    right = jnp.where(
        column == SIDE - 1, pltpu.roll(z, SIDE - 1, 1), pltpu.roll(z, sites - 1, 1)
    )
    below = pltpu.roll(z, sites - SIDE, 1)
    energy = offdiag_ref[...] + jnp.sum(z * (right + below), axis=1, keepdims=True)
    here = (iota((local, width), 1) == lax.axis_index("samp")) & (lax.axis_index("layer") == 0)
    out_ref[...] = jnp.where(here, energy, F32(0.0))


def energy_rows(spins, offdiag, width):
    return pl.pallas_call(
        energy_kernel,
        out_shape=jax.ShapeDtypeStruct((spins.shape[0], width), F32),
        compiler_params=pltpu.CompilerParams(vmem_limit_bytes=VMEM_LIMIT),
        name="energy_rows",
    )(spins, offdiag[:, None])


def gram_kernel(*refs):
    *block_refs, energy_ref, out_ref, flat = refs
    block_refs = in_place(block_refs)
    local, count, d = block_refs[0].shape
    total = local * len(block_refs)
    joined = CHUNK // local
    me = lax.axis_index("samp")
    block = CHUNK * CHUNK
    dest = iota((block, block), 0)
    sample = dest % CHUNK
    sample = (sample // local ^ me % joined) * local + sample % local
    source = sample * CHUNK + dest // CHUNK
    swap = (iota((block, block), 1) == source).astype(F32).astype(BF16)
    for row in range(0, count, CHUNK):
        for j in range(len(block_refs) // joined):
            pieces = [ref[:, row : row + CHUNK] for ref in block_refs[j * joined : (j + 1) * joined]]
            piece = jnp.concatenate(pieces, axis=0).reshape(block, d)
            turned = jnp.dot(swap, piece, preferred_element_type=F32).astype(BF16)
            place = pl.ds(pl.multiple_of((me // joined ^ j) * CHUNK, CHUNK), CHUNK)
            for r in range(CHUNK):
                flat[row + r, place] = turned[r * CHUNK : (r + 1) * CHUNK]
    lined = jnp.concatenate([flat[r] for r in range(count)], axis=1)
    gram = lax.dot_general(lined, lined, (((1,), (1,)), ((), ())), preferred_element_type=F32)
    top = total // 2
    out_ref[:top] = jnp.concatenate([gram[:top], gram[top:]], axis=1)
    out_ref[top:] = energy_ref[...]


def gram_partial(blocks, energies):
    local, count, d = blocks[0].shape
    total = local * len(blocks)
    return pl.pallas_call(
        gram_kernel,
        out_shape=jax.ShapeDtypeStruct((total // 2 + local, 2 * total), F32),
        scratch_shapes=[pltpu.VMEM((count, total, d), BF16)],
        compiler_params=pltpu.CompilerParams(vmem_limit_bytes=VMEM_LIMIT),
        cost_estimate=pl.CostEstimate(
            flops=2 * total * total * count * d,
            bytes_accessed=2 * total * count * d,
            transcendentals=0,
        ),
        name="gram_partial",
    )(*in_turn(blocks), energies)


def eliminate(matrix, total):
    row = iota(matrix.shape, 0)
    lane = iota(matrix.shape, 1)
    if total <= 64:
        for k in range(total):
            column = matrix[:, k : k + 1]
            pivot_row = matrix[k : k + 1, :]
            scaled = pivot_row * (F32(1.0) / pivot_row[:, k : k + 1])
            matrix = matrix - jnp.where(row == k, F32(0.0), column) * scaled
    else:

        def one(k, held):
            column = jnp.sum(jnp.where(lane == k, held, F32(0.0)), axis=1, keepdims=True)
            pivot_row = jnp.sum(jnp.where(row == k, held, F32(0.0)), axis=0, keepdims=True)
            here = lane[:1] == k
            pivot = jnp.sum(jnp.where(here, pivot_row, F32(0.0)), axis=1, keepdims=True)
            scaled = pivot_row * (F32(1.0) / pivot)
            return held - jnp.where(row == k, F32(0.0), column) * scaled

        matrix = lax.fori_loop(0, total, one, matrix)
    diag = jnp.sum(jnp.where(row == lane, matrix, F32(0.0)), axis=1, keepdims=True)
    return matrix[:, total : total + 1] / diag


def tree_sum(parts):
    while len(parts) > 1:
        parts = [a + b for a, b in zip(parts[::2], parts[1::2])]
    return parts[0]


def partners(value, axis, first, count):
    size = lax.axis_size(axis)
    parts = [value]
    for k in range(1, count):
        perm = [(i, i ^ (k * first)) for i in range(size)]
        parts.append(lax.ppermute(value, axis, perm))
    return parts


def copies_kernel(*refs):
    *part_refs, out_ref = refs
    total = tree_sum([ref[...] for ref in part_refs])
    for i in range(out_ref.shape[0]):
        out_ref[i] = total


def summed_copies(parts, count):
    return pl.pallas_call(
        copies_kernel,
        out_shape=jax.ShapeDtypeStruct((count, *parts[0].shape), F32),
        compiler_params=pltpu.CompilerParams(vmem_limit_bytes=VMEM_LIMIT),
        name="summed_copies",
    )(*parts)


def solve_kernel(*refs):
    gram_ref, *block_refs, weights_ref, update_ref, held = refs
    block_refs = in_place(block_refs)
    mats, share, d = update_ref.shape
    local = weights_ref.shape[1]
    total = gram_ref.shape[2] // 2
    top = total // 2
    width = (total // LANES + 1) * LANES
    packed = tree_sum([gram_ref[i] for i in range(gram_ref.shape[0])])
    raw = jnp.concatenate([packed[:top, :total], packed[:top, total:]], axis=0)
    energy = [packed[top:, i : i + 1] for i in range(total // local)]
    energy = jnp.concatenate(energy, axis=0)
    raw = jnp.concatenate([raw, jnp.broadcast_to(energy, (total, width - total))], axis=1)
    row = iota((total, width), 0)
    lane = iota((total, width), 1)
    inside = lane < total
    scale = F32(1.0 / total)
    row_mean = jnp.sum(jnp.where(inside, raw, F32(0.0)), axis=1, keepdims=True) * scale
    col_mean = jnp.sum(raw, axis=0, keepdims=True) * scale
    mean = jnp.sum(row_mean, axis=0, keepdims=True) * scale
    gram = (raw - col_mean - row_mean + mean) * scale
    eps = (raw - col_mean) * F32(1.0 / total**0.5)
    on_diag = row == lane
    trace = jnp.sum(
        jnp.sum(jnp.where(on_diag, gram, F32(0.0)), axis=1, keepdims=True), axis=0, keepdims=True
    )
    shift = F32(shift_ratio) * trace * scale
    system = jnp.where(inside, gram + jnp.where(on_diag, shift, F32(0.0)), eps)
    weights = eliminate(system, total)
    me = lax.axis_index("samp")
    own = jnp.where(row - me * local == lane, weights, F32(0.0))
    weights_ref[...] = jnp.sum(own, axis=0, keepdims=True)[:, :local]
    coeffs = weights - jnp.sum(weights, axis=0, keepdims=True) * scale
    held[...] = jnp.broadcast_to(coeffs, (total, d))
    acc = jnp.zeros((mats * share, d), F32)
    for k, block_ref in enumerate(block_refs):
        mine = held[pl.ds(pl.multiple_of((me ^ k) * local, local), local)]
        for s in range(local):
            acc = acc + mine[s : s + 1] * block_ref[s].astype(F32)
    for m in range(mats):
        update_ref[m] = acc[m * share : (m + 1) * share]


def solve_and_project(gram, blocks, mats):
    local, count, d = blocks[0].shape
    total = local * len(blocks)
    return pl.pallas_call(
        solve_kernel,
        out_shape=(
            jax.ShapeDtypeStruct((1, local), F32),
            jax.ShapeDtypeStruct((mats, count // mats, d), F32),
        ),
        scratch_shapes=[pltpu.VMEM((total, d), F32)],
        compiler_params=pltpu.CompilerParams(vmem_limit_bytes=VMEM_LIMIT),
        name="solve_and_project",
    )(gram, *in_turn(blocks))


def body(spins, activations, cotangents, offdiag):
    local, mats = activations.shape[:2]
    owners = lax.axis_size("samp")
    total = local * owners
    blocks = list(jac_rows(activations, cotangents, owners))
    for k in turns(owners)[:-1]:
        blocks[k] = lax.ppermute(blocks[k], "samp", [(i, i ^ k) for i in range(owners)])
    partial = gram_partial(blocks, energy_rows(spins, offdiag, 2 * total))
    parts = partners(partial, "layer", 1, lax.axis_size("layer"))
    gram = lax.all_to_all(
        summed_copies(parts, owners), "samp", split_axis=0, concat_axis=0, tiled=True
    )
    weights, update = solve_and_project(gram, blocks, mats)
    return weights.reshape(local), update


def solution(mesh):
    placed = (
        P("samp", None),
        P("samp", "layer", None, None),
        P("samp", "layer", None, None),
        P("samp"),
    )
    return jax.shard_map(
        body,
        mesh=mesh,
        in_specs=placed,
        out_specs=(P("samp"), P("layer", "samp", None)),
        check_vma=False,
    )
```

```python
import functools

import jax
import jax.numpy as jnp
from jax import lax
from jax.experimental import pallas as pl
from jax.experimental.pallas import tpu as pltpu
from jax.sharding import PartitionSpec as P

SIDE = 16
LANES = 128
CHUNK = 16
VMEM_LIMIT = 24 * 2**20
JAC_VMEM_LIMIT = 52 * 2**20
shift_ratio = 0.1
F32 = jnp.float32
BF16 = jnp.bfloat16


def iota(shape, dim):
    return lax.broadcasted_iota(jnp.int32, shape, dim)


def turns(owners):
    far, near = list(range(owners // 2, owners)), list(range(owners // 2 - 1, 0, -1))
    order = [far.pop(0)]
    while far or near:
        order += far[:1] + near[:1]
        far, near = far[1:], near[1:]
    return order + [0]


def in_turn(blocks):
    return [blocks[k] for k in turns(len(blocks))]


def in_place(blocks):
    order = turns(len(blocks))
    return [blocks[order.index(k)] for k in range(len(blocks))]


def jac_kernel(act_hbm, cot_hbm, *refs):
    *out_refs, act_buf, cot_buf, held, sems = refs
    samples, mats = act_buf.shape[:2]
    share = out_refs[0].shape[1] // mats
    me = lax.axis_index("samp")
    copies = []
    for s in range(samples):
        copies.append(
            (
                pltpu.make_async_copy(act_hbm.at[s], act_buf.at[s], sems.at[0, s]),
                pltpu.make_async_copy(cot_hbm.at[s], cot_buf.at[s], sems.at[1, s]),
            )
        )
    for pair in copies:
        for copy in pair:
            copy.start()
    group = 2
    for first in range(0, samples, group):
        for s in range(first, first + group):
            for copy in copies[s]:
                copy.wait()
        for s in range(first, first + group):
            for m in range(mats):
                held[s, m] = lax.dot_general(
                    act_buf[s, m],
                    cot_buf[s, m],
                    (((0,), (0,)), ((), ())),
                    preferred_element_type=F32,
                )
    for k, out_ref in enumerate(out_refs):
        owned = pl.ds(pl.multiple_of((me ^ k) * share, share), share)
        for s in range(samples):
            rows = [held[s, m, owned] for m in range(mats)]
            out_ref[s] = jnp.concatenate(rows, axis=0).astype(BF16)


def jac_rows(activations, cotangents, owners):
    samples, mats, sites, d = activations.shape
    rows = mats * d // owners
    hbm = pl.BlockSpec(memory_space=pltpu.HBM)
    return pl.pallas_call(
        jac_kernel,
        in_specs=[hbm, hbm],
        out_shape=[jax.ShapeDtypeStruct((samples, rows, d), BF16)] * owners,
        scratch_shapes=[
            pltpu.VMEM((samples, mats, sites, d), BF16),
            pltpu.VMEM((samples, mats, sites, d), BF16),
            pltpu.VMEM((samples, mats, d, d), F32),
            pltpu.SemaphoreType.DMA((2, samples)),
        ],
        compiler_params=pltpu.CompilerParams(vmem_limit_bytes=JAC_VMEM_LIMIT),
        cost_estimate=pl.CostEstimate(
            flops=2 * samples * mats * sites * d * d,
            bytes_accessed=6 * samples * mats * sites * d,
            transcendentals=0,
        ),
        name="jac_rows",
    )(activations, cotangents)


def energy_kernel(spins_ref, offdiag_ref, out_ref):
    total, width = out_ref.shape
    local = spins_ref.shape[0]
    sites = SIDE * SIDE
    z = (2 * spins_ref[...] - 1).astype(F32)
    column = iota((local, sites), 1) % SIDE
    right = jnp.where(
        column == SIDE - 1, pltpu.roll(z, SIDE - 1, 1), pltpu.roll(z, sites - 1, 1)
    )
    below = pltpu.roll(z, sites - SIDE, 1)
    energy = offdiag_ref[...] + jnp.sum(z * (right + below), axis=1, keepdims=True)
    first = lax.axis_index("samp") * local
    mine = lax.axis_index("layer") == 0
    spread = jnp.concatenate([energy] * (total // local), axis=0)
    row = iota((total, width), 0)
    here = (row >= first) & (row < first + local) & (iota((total, width), 1) == total) & mine
    out_ref[...] = jnp.where(here, spread, F32(0.0))


def energy_column(spins, offdiag, total, width):
    return pl.pallas_call(
        energy_kernel,
        out_shape=jax.ShapeDtypeStruct((total, width), F32),
        compiler_params=pltpu.CompilerParams(vmem_limit_bytes=VMEM_LIMIT),
        name="energy_column",
    )(spins, offdiag[:, None])


def gram_kernel(*refs):
    *block_refs, start_ref, out_ref, flat = refs
    block_refs = in_place(block_refs)
    local, count, d = block_refs[0].shape
    total = local * len(block_refs)
    joined = CHUNK // local
    me = lax.axis_index("samp")
    block = CHUNK * CHUNK
    dest = iota((block, block), 0)
    sample = dest % CHUNK
    sample = (sample // local ^ me % joined) * local + sample % local
    source = sample * CHUNK + dest // CHUNK
    swap = (iota((block, block), 1) == source).astype(F32).astype(BF16)
    for row in range(0, count, CHUNK):
        for j in range(len(block_refs) // joined):
            pieces = [ref[:, row : row + CHUNK] for ref in block_refs[j * joined : (j + 1) * joined]]
            piece = jnp.concatenate(pieces, axis=0).reshape(block, d)
            turned = jnp.dot(swap, piece, preferred_element_type=F32).astype(BF16)
            place = pl.ds(pl.multiple_of((me // joined ^ j) * CHUNK, CHUNK), CHUNK)
            for r in range(CHUNK):
                flat[row + r, place] = turned[r * CHUNK : (r + 1) * CHUNK]
    lined = jnp.concatenate([flat[r] for r in range(count)], axis=1)
    gram = lax.dot_general(lined, lined, (((1,), (1,)), ((), ())), preferred_element_type=F32)
    out_ref[...] = start_ref[...]
    out_ref[:, :total] += gram


def gram_partial(blocks, start):
    local, count, d = blocks[0].shape
    total, width = start.shape
    return pl.pallas_call(
        gram_kernel,
        out_shape=jax.ShapeDtypeStruct((total, width), F32),
        scratch_shapes=[pltpu.VMEM((count, total, d), BF16)],
        compiler_params=pltpu.CompilerParams(vmem_limit_bytes=VMEM_LIMIT),
        cost_estimate=pl.CostEstimate(
            flops=2 * total * total * count * d,
            bytes_accessed=2 * total * count * d,
            transcendentals=0,
        ),
        name="gram_partial",
    )(*in_turn(blocks), start)


def eliminate(matrix, total):
    row = iota(matrix.shape, 0)
    lane = iota(matrix.shape, 1)
    if total <= 64:
        for k in range(total):
            column = matrix[:, k : k + 1]
            pivot_row = matrix[k : k + 1, :]
            scaled = pivot_row * (F32(1.0) / pivot_row[:, k : k + 1])
            matrix = matrix - jnp.where(row == k, F32(0.0), column) * scaled
    else:

        def one(k, held):
            column = jnp.sum(jnp.where(lane == k, held, F32(0.0)), axis=1, keepdims=True)
            pivot_row = jnp.sum(jnp.where(row == k, held, F32(0.0)), axis=0, keepdims=True)
            here = lane[:1] == k
            pivot = jnp.sum(jnp.where(here, pivot_row, F32(0.0)), axis=1, keepdims=True)
            scaled = pivot_row * (F32(1.0) / pivot)
            return held - jnp.where(row == k, F32(0.0), column) * scaled

        matrix = lax.fori_loop(0, total, one, matrix)
    diag = jnp.sum(jnp.where(row == lane, matrix, F32(0.0)), axis=1, keepdims=True)
    return matrix[:, total : total + 1] / diag


def tree_sum(parts):
    while len(parts) > 1:
        parts = [a + b for a, b in zip(parts[::2], parts[1::2])]
    return parts[0]


def partners(value, axis, first, count):
    size = lax.axis_size(axis)
    parts = [value]
    for k in range(1, count):
        perm = [(i, i ^ (k * first)) for i in range(size)]
        parts.append(lax.ppermute(value, axis, perm))
    return parts


def solve_kernel(grams, *refs):
    gram_refs, (*block_refs, weights_ref, update_ref, held) = refs[:grams], refs[grams:]
    block_refs = in_place(block_refs)
    mats, share, d = update_ref.shape
    local = weights_ref.shape[1]
    total, width = gram_refs[0].shape
    raw = tree_sum([ref[...] for ref in gram_refs])
    row = iota((total, width), 0)
    lane = iota((total, width), 1)
    inside = lane < total
    scale = F32(1.0 / total)
    row_mean = jnp.sum(jnp.where(inside, raw, F32(0.0)), axis=1, keepdims=True) * scale
    col_mean = jnp.sum(raw, axis=0, keepdims=True) * scale
    mean = jnp.sum(row_mean, axis=0, keepdims=True) * scale
    gram = (raw - col_mean - row_mean + mean) * scale
    eps = (raw - col_mean) * F32(1.0 / total**0.5)
    on_diag = row == lane
    trace = jnp.sum(
        jnp.sum(jnp.where(on_diag, gram, F32(0.0)), axis=1, keepdims=True), axis=0, keepdims=True
    )
    shift = F32(shift_ratio) * trace * scale
    system = jnp.where(inside, gram + jnp.where(on_diag, shift, F32(0.0)), eps)
    weights = eliminate(system, total)
    me = lax.axis_index("samp")
    own = jnp.where(row - me * local == lane, weights, F32(0.0))
    weights_ref[...] = jnp.sum(own, axis=0, keepdims=True)[:, :local]
    coeffs = weights - jnp.sum(weights, axis=0, keepdims=True) * scale
    held[...] = jnp.broadcast_to(coeffs, (total, d))
    acc = jnp.zeros((mats * share, d), F32)
    for k, block_ref in enumerate(block_refs):
        mine = held[pl.ds(pl.multiple_of((me ^ k) * local, local), local)]
        for s in range(local):
            acc = acc + mine[s : s + 1] * block_ref[s].astype(F32)
    for m in range(mats):
        update_ref[m] = acc[m * share : (m + 1) * share]


def solve_and_project(grams, blocks, mats):
    total, width = grams[0].shape
    local, count, d = blocks[0].shape
    return pl.pallas_call(
        functools.partial(solve_kernel, len(grams)),
        out_shape=(
            jax.ShapeDtypeStruct((1, local), F32),
            jax.ShapeDtypeStruct((mats, count // mats, d), F32),
        ),
        scratch_shapes=[pltpu.VMEM((total, d), F32)],
        compiler_params=pltpu.CompilerParams(vmem_limit_bytes=VMEM_LIMIT),
        name="solve_and_project",
    )(*grams, *in_turn(blocks))


def body(spins, activations, cotangents, offdiag):
    local, mats = activations.shape[:2]
    owners = lax.axis_size("samp")
    total = local * owners
    width = (total // LANES + 1) * LANES
    blocks = list(jac_rows(activations, cotangents, owners))
    for k in turns(owners)[:-1]:
        blocks[k] = lax.ppermute(blocks[k], "samp", [(i, i ^ k) for i in range(owners)])
    partial = gram_partial(blocks, energy_column(spins, offdiag, total, width))
    grams = partners(partial, "layer", 1, lax.axis_size("layer"))
    first = 1
    while first < owners:
        count = min(4, owners // first)
        grams = partners(tree_sum(grams), "samp", first, count)
        first *= count
    weights, update = solve_and_project(grams, blocks, mats)
    return weights.reshape(local), update


def solution(mesh):
    placed = (
        P("samp", None),
        P("samp", "layer", None, None),
        P("samp", "layer", None, None),
        P("samp"),
    )
    return jax.shard_map(
        body,
        mesh=mesh,
        in_specs=placed,
        out_specs=(P("samp"), P("layer", "samp", None)),
        check_vma=False,
    )
```

```python
import functools

import jax
import jax.numpy as jnp
from jax import lax
from jax.experimental import pallas as pl
from jax.experimental.pallas import tpu as pltpu
from jax.sharding import PartitionSpec as P

SIDE = 16
LANES = 128
CHUNK = 16
PIVOTS = 8
VMEM_LIMIT = 24 * 2**20
JAC_VMEM_LIMIT = 52 * 2**20
shift_ratio = 0.1
F32 = jnp.float32
BF16 = jnp.bfloat16


def iota(shape, dim):
    return lax.broadcasted_iota(jnp.int32, shape, dim)


def turns(owners):
    far, near = list(range(owners // 2, owners)), list(range(owners // 2 - 1, 0, -1))
    order = [far.pop(0)]
    while far or near:
        order += far[:1] + near[:1]
        far, near = far[1:], near[1:]
    return order + [0]


def in_turn(blocks):
    return [blocks[k] for k in turns(len(blocks))]


def in_place(blocks):
    order = turns(len(blocks))
    return [blocks[order.index(k)] for k in range(len(blocks))]


def jac_kernel(act_hbm, cot_hbm, *refs):
    *out_refs, act_buf, cot_buf, held, sems = refs
    samples, mats = act_buf.shape[:2]
    share = out_refs[0].shape[1] // mats
    me = lax.axis_index("samp")
    copies = []
    for s in range(samples):
        copies.append(
            (
                pltpu.make_async_copy(act_hbm.at[s], act_buf.at[s], sems.at[0, s]),
                pltpu.make_async_copy(cot_hbm.at[s], cot_buf.at[s], sems.at[1, s]),
            )
        )
    for pair in copies:
        for copy in pair:
            copy.start()
    group = 2
    for first in range(0, samples, group):
        for s in range(first, first + group):
            for copy in copies[s]:
                copy.wait()
        for s in range(first, first + group):
            for m in range(mats):
                held[s, m] = lax.dot_general(
                    act_buf[s, m],
                    cot_buf[s, m],
                    (((0,), (0,)), ((), ())),
                    preferred_element_type=F32,
                )
    for k, out_ref in enumerate(out_refs):
        owned = pl.ds(pl.multiple_of((me ^ k) * share, share), share)
        for s in range(samples):
            rows = [held[s, m, owned] for m in range(mats)]
            out_ref[s] = jnp.concatenate(rows, axis=0).astype(BF16)


def jac_rows(activations, cotangents, owners):
    samples, mats, sites, d = activations.shape
    rows = mats * d // owners
    hbm = pl.BlockSpec(memory_space=pltpu.HBM)
    return pl.pallas_call(
        jac_kernel,
        in_specs=[hbm, hbm],
        out_shape=[jax.ShapeDtypeStruct((samples, rows, d), BF16)] * owners,
        scratch_shapes=[
            pltpu.VMEM((samples, mats, sites, d), BF16),
            pltpu.VMEM((samples, mats, sites, d), BF16),
            pltpu.VMEM((samples, mats, d, d), F32),
            pltpu.SemaphoreType.DMA((2, samples)),
        ],
        compiler_params=pltpu.CompilerParams(vmem_limit_bytes=JAC_VMEM_LIMIT),
        cost_estimate=pl.CostEstimate(
            flops=2 * samples * mats * sites * d * d,
            bytes_accessed=6 * samples * mats * sites * d,
            transcendentals=0,
        ),
        name="jac_rows",
    )(activations, cotangents)


def energy_kernel(spins_ref, offdiag_ref, out_ref):
    total, width = out_ref.shape
    local = spins_ref.shape[0]
    sites = SIDE * SIDE
    z = (2 * spins_ref[...] - 1).astype(F32)
    column = iota((local, sites), 1) % SIDE
    right = jnp.where(
        column == SIDE - 1, pltpu.roll(z, SIDE - 1, 1), pltpu.roll(z, sites - 1, 1)
    )
    below = pltpu.roll(z, sites - SIDE, 1)
    energy = offdiag_ref[...] + jnp.sum(z * (right + below), axis=1, keepdims=True)
    first = lax.axis_index("samp") * local
    mine = lax.axis_index("layer") == 0
    spread = jnp.concatenate([energy] * (total // local), axis=0)
    row = iota((total, width), 0)
    here = (row >= first) & (row < first + local) & (iota((total, width), 1) == total) & mine
    out_ref[...] = jnp.where(here, spread, F32(0.0))


def energy_column(spins, offdiag, total, width):
    return pl.pallas_call(
        energy_kernel,
        out_shape=jax.ShapeDtypeStruct((total, width), F32),
        compiler_params=pltpu.CompilerParams(vmem_limit_bytes=VMEM_LIMIT),
        name="energy_column",
    )(spins, offdiag[:, None])


def gram_kernel(*refs):
    *block_refs, start_ref, out_ref, flat = refs
    block_refs = in_place(block_refs)
    local, count, d = block_refs[0].shape
    total = local * len(block_refs)
    joined = CHUNK // local
    me = lax.axis_index("samp")
    block = CHUNK * CHUNK
    dest = iota((block, block), 0)
    sample = dest % CHUNK
    sample = (sample // local ^ me % joined) * local + sample % local
    source = sample * CHUNK + dest // CHUNK
    swap = (iota((block, block), 1) == source).astype(F32).astype(BF16)
    for row in range(0, count, CHUNK):
        for j in range(len(block_refs) // joined):
            pieces = [ref[:, row : row + CHUNK] for ref in block_refs[j * joined : (j + 1) * joined]]
            piece = jnp.concatenate(pieces, axis=0).reshape(block, d)
            turned = jnp.dot(swap, piece, preferred_element_type=F32).astype(BF16)
            place = pl.ds(pl.multiple_of((me // joined ^ j) * CHUNK, CHUNK), CHUNK)
            for r in range(CHUNK):
                flat[row + r, place] = turned[r * CHUNK : (r + 1) * CHUNK]
    lined = jnp.concatenate([flat[r] for r in range(count)], axis=1)
    gram = lax.dot_general(lined, lined, (((1,), (1,)), ((), ())), preferred_element_type=F32)
    out_ref[...] = start_ref[...]
    out_ref[:, :total] += gram


def gram_partial(blocks, start):
    local, count, d = blocks[0].shape
    total, width = start.shape
    return pl.pallas_call(
        gram_kernel,
        out_shape=jax.ShapeDtypeStruct((total, width), F32),
        scratch_shapes=[pltpu.VMEM((count, total, d), BF16)],
        compiler_params=pltpu.CompilerParams(vmem_limit_bytes=VMEM_LIMIT),
        cost_estimate=pl.CostEstimate(
            flops=2 * total * total * count * d,
            bytes_accessed=2 * total * count * d,
            transcendentals=0,
        ),
        name="gram_partial",
    )(*in_turn(blocks), start)


def tree_sum(parts):
    while len(parts) > 1:
        odd = parts[len(parts) // 2 * 2 :]
        parts = [a + b for a, b in zip(parts[::2], parts[1::2])] + odd
    return parts[0]


def pivot_rows(rows, entries):
    count = len(rows)
    rows = list(rows)
    p = [[entries[min(i, l)][max(i, l)] for l in range(count)] for i in range(count)]
    uppers = {}
    for j in range(0, count, 2):
        a, b, c = p[j][j], p[j][j + 1], p[j + 1][j + 1]
        inverse = F32(1.0) / (a * c - b * b)

        def scaled(x, y):
            return (c * x - b * y) * inverse, (a * y - b * x) * inverse

        first, second = rows[j], rows[j + 1]
        rows[j], rows[j + 1] = scaled(first, second)
        later = range(j + 2, count)
        for l in later:
            uppers[j, l], uppers[j + 1, l] = scaled(p[j][l], p[j + 1][l])
        for i in later:
            rows[i] = rows[i] - (p[j][i] * rows[j] + p[j + 1][i] * rows[j + 1])
            for l in range(i, count):
                change = p[j][i] * uppers[j, l] + p[j + 1][i] * uppers[j + 1, l]
                p[i][l] = p[l][i] = p[i][l] - change
    for j in range(count - 4, -1, -2):
        for i in (j, j + 1):
            rows[i] = rows[i] - tree_sum([uppers[i, l] * rows[l] for l in range(j + 2, count)])
    return rows


def eliminate(matrix, total):
    width = matrix.shape[1]
    if total <= 64:
        blocks = [matrix[i : i + PIVOTS] for i in range(0, total, PIVOTS)]
        sub = iota((PIVOTS, width), 0)
        for b in range(len(blocks)):
            spread = [
                [
                    jnp.broadcast_to(block[:, b * PIVOTS + j : b * PIVOTS + j + 1], (PIVOTS, width))
                    for block in blocks
                ]
                for j in range(PIVOTS)
            ]

            def line(value, i):
                return jnp.broadcast_to(value[i : i + 1], (PIVOTS, width))

            entries = [
                [line(spread[l][b], i) if l >= i else None for l in range(PIVOTS)]
                for i in range(PIVOTS)
            ]
            rows = pivot_rows([line(blocks[b], i) for i in range(PIVOTS)], entries)
            for i in range(len(blocks)):
                if i != b:
                    terms = [spread[j][i] * rows[j] for j in range(PIVOTS)]
                    blocks[i] = blocks[i] - tree_sum(terms)
            solved = rows[0]
            for j in range(1, PIVOTS):
                solved = jnp.where(sub == j, rows[j], solved)
            blocks[b] = solved
        return jnp.concatenate([block[:, total : total + 1] for block in blocks], axis=0)
    row = iota(matrix.shape, 0)
    lane = iota(matrix.shape, 1)

    def one(k, held):
        column = jnp.sum(jnp.where(lane == k, held, F32(0.0)), axis=1, keepdims=True)
        pivot_row = jnp.sum(jnp.where(row == k, held, F32(0.0)), axis=0, keepdims=True)
        here = lane[:1] == k
        pivot = jnp.sum(jnp.where(here, pivot_row, F32(0.0)), axis=1, keepdims=True)
        scaled = pivot_row * (F32(1.0) / pivot)
        return held - jnp.where(row == k, F32(0.0), column) * scaled

    matrix = lax.fori_loop(0, total, one, matrix)
    diag = jnp.sum(jnp.where(row == lane, matrix, F32(0.0)), axis=1, keepdims=True)
    return matrix[:, total : total + 1] / diag


def partners(value, axis, first, count):
    size = lax.axis_size(axis)
    parts = [value]
    for k in range(1, count):
        perm = [(i, i ^ (k * first)) for i in range(size)]
        parts.append(lax.ppermute(value, axis, perm))
    return parts


def solve_kernel(grams, *refs):
    gram_refs, (*block_refs, weights_ref, update_ref, held) = refs[:grams], refs[grams:]
    block_refs = in_place(block_refs)
    mats, share, d = update_ref.shape
    local = weights_ref.shape[1]
    total, width = gram_refs[0].shape
    raw = tree_sum([ref[...] for ref in gram_refs])
    row = iota((total, width), 0)
    lane = iota((total, width), 1)
    inside = lane < total
    scale = F32(1.0 / total)
    row_mean = jnp.sum(jnp.where(inside, raw, F32(0.0)), axis=1, keepdims=True) * scale
    col_mean = jnp.sum(raw, axis=0, keepdims=True) * scale
    mean = jnp.sum(row_mean, axis=0, keepdims=True) * scale
    gram = (raw - col_mean - row_mean + mean) * scale
    eps = (raw - col_mean) * F32(1.0 / total**0.5)
    on_diag = row == lane
    trace = jnp.sum(
        jnp.sum(jnp.where(on_diag, gram, F32(0.0)), axis=1, keepdims=True), axis=0, keepdims=True
    )
    shift = F32(shift_ratio) * trace * scale
    system = jnp.where(inside, gram + jnp.where(on_diag, shift, F32(0.0)), eps)
    weights = eliminate(system, total)
    me = lax.axis_index("samp")
    own = jnp.where(row - me * local == lane, weights, F32(0.0))
    weights_ref[...] = jnp.sum(own, axis=0, keepdims=True)[:, :local]
    coeffs = weights - jnp.sum(weights, axis=0, keepdims=True) * scale
    held[...] = jnp.broadcast_to(coeffs, (total, d))
    acc = jnp.zeros((mats * share, d), F32)
    for k, block_ref in enumerate(block_refs):
        mine = held[pl.ds(pl.multiple_of((me ^ k) * local, local), local)]
        for s in range(local):
            acc = acc + mine[s : s + 1] * block_ref[s].astype(F32)
    for m in range(mats):
        update_ref[m] = acc[m * share : (m + 1) * share]


def solve_and_project(grams, blocks, mats):
    total, width = grams[0].shape
    local, count, d = blocks[0].shape
    return pl.pallas_call(
        functools.partial(solve_kernel, len(grams)),
        out_shape=(
            jax.ShapeDtypeStruct((1, local), F32),
            jax.ShapeDtypeStruct((mats, count // mats, d), F32),
        ),
        scratch_shapes=[pltpu.VMEM((total, d), F32)],
        compiler_params=pltpu.CompilerParams(vmem_limit_bytes=VMEM_LIMIT),
        name="solve_and_project",
    )(*grams, *in_turn(blocks))


def body(spins, activations, cotangents, offdiag):
    local, mats = activations.shape[:2]
    owners = lax.axis_size("samp")
    total = local * owners
    width = (total // LANES + 1) * LANES
    blocks = list(jac_rows(activations, cotangents, owners))
    for k in turns(owners)[:-1]:
        blocks[k] = lax.ppermute(blocks[k], "samp", [(i, i ^ k) for i in range(owners)])
    partial = gram_partial(blocks, energy_column(spins, offdiag, total, width))
    grams = partners(partial, "layer", 1, lax.axis_size("layer"))
    first = 1
    while first < owners:
        count = min(4, owners // first)
        grams = partners(tree_sum(grams), "samp", first, count)
        first *= count
    weights, update = solve_and_project(grams, blocks, mats)
    return weights.reshape(local), update


def solution(mesh):
    placed = (
        P("samp", None),
        P("samp", "layer", None, None),
        P("samp", "layer", None, None),
        P("samp"),
    )
    return jax.shard_map(
        body,
        mesh=mesh,
        in_specs=placed,
        out_specs=(P("samp"), P("layer", "samp", None)),
        check_vma=False,
    )
```

```python
import functools

import jax
import jax.numpy as jnp
from jax import lax
from jax.experimental import pallas as pl
from jax.experimental.pallas import tpu as pltpu
from jax.sharding import PartitionSpec as P

SIDE = 16
LANES = 128
CHUNK = 16
PIVOTS = 8
VMEM_LIMIT = 24 * 2**20
JAC_VMEM_LIMIT = 52 * 2**20
shift_ratio = 0.1
F32 = jnp.float32
BF16 = jnp.bfloat16


def iota(shape, dim):
    return lax.broadcasted_iota(jnp.int32, shape, dim)


def turns(owners):
    far, near = list(range(owners // 2, owners)), list(range(owners // 2 - 1, 0, -1))
    order = [far.pop(0)]
    while far or near:
        order += far[:1] + near[:1]
        far, near = far[1:], near[1:]
    return order + [0]


def in_turn(blocks):
    return [blocks[k] for k in turns(len(blocks))]


def in_place(blocks):
    order = turns(len(blocks))
    return [blocks[order.index(k)] for k in range(len(blocks))]


def jac_kernel(act_hbm, cot_hbm, *refs):
    *out_refs, act_buf, cot_buf, held, sems = refs
    samples, mats = act_buf.shape[:2]
    share = out_refs[0].shape[1] // mats
    me = lax.axis_index("samp")
    copies = []
    for s in range(samples):
        copies.append(
            (
                pltpu.make_async_copy(act_hbm.at[s], act_buf.at[s], sems.at[0, s]),
                pltpu.make_async_copy(cot_hbm.at[s], cot_buf.at[s], sems.at[1, s]),
            )
        )
    for pair in copies:
        for copy in pair:
            copy.start()
    group = 2
    for first in range(0, samples, group):
        for s in range(first, first + group):
            for copy in copies[s]:
                copy.wait()
        for s in range(first, first + group):
            for m in range(mats):
                held[s, m] = lax.dot_general(
                    act_buf[s, m],
                    cot_buf[s, m],
                    (((0,), (0,)), ((), ())),
                    preferred_element_type=F32,
                )
    for k, out_ref in enumerate(out_refs):
        owned = pl.ds(pl.multiple_of((me ^ k) * share, share), share)
        for s in range(samples):
            rows = [held[s, m, owned] for m in range(mats)]
            out_ref[s] = jnp.concatenate(rows, axis=0).astype(BF16)


def jac_rows(activations, cotangents, owners):
    samples, mats, sites, d = activations.shape
    rows = mats * d // owners
    hbm = pl.BlockSpec(memory_space=pltpu.HBM)
    return pl.pallas_call(
        jac_kernel,
        in_specs=[hbm, hbm],
        out_shape=[jax.ShapeDtypeStruct((samples, rows, d), BF16)] * owners,
        scratch_shapes=[
            pltpu.VMEM((samples, mats, sites, d), BF16),
            pltpu.VMEM((samples, mats, sites, d), BF16),
            pltpu.VMEM((samples, mats, d, d), F32),
            pltpu.SemaphoreType.DMA((2, samples)),
        ],
        compiler_params=pltpu.CompilerParams(vmem_limit_bytes=JAC_VMEM_LIMIT),
        cost_estimate=pl.CostEstimate(
            flops=2 * samples * mats * sites * d * d,
            bytes_accessed=6 * samples * mats * sites * d,
            transcendentals=0,
        ),
        name="jac_rows",
    )(activations, cotangents)


def packed_shape(total):
    half = total // 2
    return half, -(-(3 * half + 2) // LANES) * LANES


def energy_kernel(total, spins_ref, offdiag_ref, out_ref):
    shape = out_ref.shape
    local = spins_ref.shape[0]
    sites = SIDE * SIDE
    z = (2 * spins_ref[...] - 1).astype(F32)
    column = iota((local, sites), 1) % SIDE
    right = jnp.where(
        column == SIDE - 1, pltpu.roll(z, SIDE - 1, 1), pltpu.roll(z, sites - 1, 1)
    )
    below = pltpu.roll(z, sites - SIDE, 1)
    energy = offdiag_ref[...] + jnp.sum(z * (right + below), axis=1, keepdims=True)
    half = total // 2
    first = lax.axis_index("samp") * local
    lower = first // half
    first = first - lower * half
    spread = jnp.concatenate([energy] * (half // local), axis=0)
    row = iota(shape, 0)
    here = (row >= first) & (row < first + local) & (iota(shape, 1) == 3 * half + lower)
    here = here & (lax.axis_index("layer") == 0)
    out_ref[...] = jnp.where(here, spread, F32(0.0))


def packed_energy(spins, offdiag, total):
    return pl.pallas_call(
        functools.partial(energy_kernel, total),
        out_shape=jax.ShapeDtypeStruct(packed_shape(total), F32),
        compiler_params=pltpu.CompilerParams(vmem_limit_bytes=VMEM_LIMIT),
        name="packed_energy",
    )(spins, offdiag[:, None])


def gram_kernel(*refs):
    *block_refs, energy_ref, out_ref, flat = refs
    block_refs = in_place(block_refs)
    local, count, d = block_refs[0].shape
    total = local * len(block_refs)
    joined = CHUNK // local
    me = lax.axis_index("samp")
    block = CHUNK * CHUNK
    dest = iota((block, block), 0)
    sample = dest % CHUNK
    sample = (sample // local ^ me % joined) * local + sample % local
    source = sample * CHUNK + dest // CHUNK
    swap = (iota((block, block), 1) == source).astype(F32).astype(BF16)
    for row in range(0, count, CHUNK):
        for j in range(len(block_refs) // joined):
            pieces = [ref[:, row : row + CHUNK] for ref in block_refs[j * joined : (j + 1) * joined]]
            piece = jnp.concatenate(pieces, axis=0).reshape(block, d)
            turned = jnp.dot(swap, piece, preferred_element_type=F32).astype(BF16)
            place = pl.ds(pl.multiple_of((me // joined ^ j) * CHUNK, CHUNK), CHUNK)
            for r in range(CHUNK):
                flat[row + r, place] = turned[r * CHUNK : (r + 1) * CHUNK]
    lined = jnp.concatenate([flat[r] for r in range(count)], axis=1)
    gram = lax.dot_general(lined, lined, (((1,), (1,)), ((), ())), preferred_element_type=F32)
    half, width = out_ref.shape
    gram = jnp.concatenate([gram, jnp.zeros((total, width - total), F32)], axis=1)
    lane = iota((half, width), 1)
    lower = pltpu.roll(gram[half:], half, 1)
    packed = jnp.where(lane < 3 * half, lower, energy_ref[...])
    out_ref[...] = jnp.where(lane < half, gram[:half], packed)


def gram_partial(blocks, energies):
    local, count, d = blocks[0].shape
    total = local * len(blocks)
    return pl.pallas_call(
        gram_kernel,
        out_shape=jax.ShapeDtypeStruct(packed_shape(total), F32),
        scratch_shapes=[pltpu.VMEM((count, total, d), BF16)],
        compiler_params=pltpu.CompilerParams(vmem_limit_bytes=VMEM_LIMIT),
        cost_estimate=pl.CostEstimate(
            flops=2 * total * total * count * d,
            bytes_accessed=2 * total * count * d,
            transcendentals=0,
        ),
        name="gram_partial",
    )(*in_turn(blocks), energies)


def tree_sum(parts):
    while len(parts) > 1:
        odd = parts[len(parts) // 2 * 2 :]
        parts = [a + b for a, b in zip(parts[::2], parts[1::2])] + odd
    return parts[0]


def pivot_rows(rows, entries):
    count = len(rows)
    rows = list(rows)
    p = [[entries[min(i, l)][max(i, l)] for l in range(count)] for i in range(count)]
    uppers = {}
    for j in range(0, count, 2):
        a, b, c = p[j][j], p[j][j + 1], p[j + 1][j + 1]
        inverse = F32(1.0) / (a * c - b * b)

        def scaled(x, y):
            return (c * x - b * y) * inverse, (a * y - b * x) * inverse

        first, second = rows[j], rows[j + 1]
        rows[j], rows[j + 1] = scaled(first, second)
        later = range(j + 2, count)
        for l in later:
            uppers[j, l], uppers[j + 1, l] = scaled(p[j][l], p[j + 1][l])
        for i in later:
            rows[i] = rows[i] - (p[j][i] * rows[j] + p[j + 1][i] * rows[j + 1])
            for l in range(i, count):
                change = p[j][i] * uppers[j, l] + p[j + 1][i] * uppers[j + 1, l]
                p[i][l] = p[l][i] = p[i][l] - change
    for j in range(count - 4, -1, -2):
        for i in (j, j + 1):
            rows[i] = rows[i] - tree_sum([uppers[i, l] * rows[l] for l in range(j + 2, count)])
    return rows


def eliminate(matrix, total):
    width = matrix.shape[1]
    if total <= 64:
        blocks = [matrix[i : i + PIVOTS] for i in range(0, total, PIVOTS)]
        sub = iota((PIVOTS, width), 0)
        for b in range(len(blocks)):
            spread = [
                [
                    jnp.broadcast_to(block[:, b * PIVOTS + j : b * PIVOTS + j + 1], (PIVOTS, width))
                    for block in blocks
                ]
                for j in range(PIVOTS)
            ]

            def line(value, i):
                return jnp.broadcast_to(value[i : i + 1], (PIVOTS, width))

            entries = [
                [line(spread[l][b], i) if l >= i else None for l in range(PIVOTS)]
                for i in range(PIVOTS)
            ]
            rows = pivot_rows([line(blocks[b], i) for i in range(PIVOTS)], entries)
            for i in range(len(blocks)):
                if i != b:
                    terms = [spread[j][i] * rows[j] for j in range(PIVOTS)]
                    blocks[i] = blocks[i] - tree_sum(terms)
            solved = rows[0]
            for j in range(1, PIVOTS):
                solved = jnp.where(sub == j, rows[j], solved)
            blocks[b] = solved
        return jnp.concatenate([block[:, total : total + 1] for block in blocks], axis=0)
    row = iota(matrix.shape, 0)
    lane = iota(matrix.shape, 1)

    def one(k, held):
        column = jnp.sum(jnp.where(lane == k, held, F32(0.0)), axis=1, keepdims=True)
        pivot_row = jnp.sum(jnp.where(row == k, held, F32(0.0)), axis=0, keepdims=True)
        here = lane[:1] == k
        pivot = jnp.sum(jnp.where(here, pivot_row, F32(0.0)), axis=1, keepdims=True)
        scaled = pivot_row * (F32(1.0) / pivot)
        return held - jnp.where(row == k, F32(0.0), column) * scaled

    matrix = lax.fori_loop(0, total, one, matrix)
    diag = jnp.sum(jnp.where(row == lane, matrix, F32(0.0)), axis=1, keepdims=True)
    return matrix[:, total : total + 1] / diag


def partners(value, axis, first, count):
    size = lax.axis_size(axis)
    parts = [value]
    for k in range(1, count):
        perm = [(i, i ^ (k * first)) for i in range(size)]
        parts.append(lax.ppermute(value, axis, perm))
    return parts


def solve_kernel(grams, *refs):
    gram_refs, (*block_refs, weights_ref, update_ref, held) = refs[:grams], refs[grams:]
    block_refs = in_place(block_refs)
    mats, share, d = update_ref.shape
    local = weights_ref.shape[1]
    packed = tree_sum([ref[...] for ref in gram_refs])
    half, packed_width = packed.shape
    total = 2 * half
    width = (total // LANES + 1) * LANES
    turned = jnp.swapaxes(packed[:, half:total], 0, 1)
    energy = [packed[:, 3 * half + i : 3 * half + i + 1] for i in range(2)]
    energy = [jnp.broadcast_to(e, (half, width - total)) for e in energy]
    upper = jnp.concatenate([packed[:, :half], turned, energy[0]], axis=1)
    lower = jnp.concatenate([packed[:, half : 3 * half], energy[1]], axis=1)
    raw = jnp.concatenate([upper, lower], axis=0)
    row = iota((total, width), 0)
    lane = iota((total, width), 1)
    inside = lane < total
    scale = F32(1.0 / total)
    row_mean = jnp.sum(jnp.where(inside, raw, F32(0.0)), axis=1, keepdims=True) * scale
    col_mean = jnp.sum(raw, axis=0, keepdims=True) * scale
    mean = jnp.sum(row_mean, axis=0, keepdims=True) * scale
    gram = (raw - col_mean - row_mean + mean) * scale
    eps = (raw - col_mean) * F32(1.0 / total**0.5)
    on_diag = row == lane
    trace = jnp.sum(
        jnp.sum(jnp.where(on_diag, gram, F32(0.0)), axis=1, keepdims=True), axis=0, keepdims=True
    )
    shift = F32(shift_ratio) * trace * scale
    system = jnp.where(inside, gram + jnp.where(on_diag, shift, F32(0.0)), eps)
    weights = eliminate(system, total)
    me = lax.axis_index("samp")
    own = jnp.where(row - me * local == lane, weights, F32(0.0))
    weights_ref[...] = jnp.sum(own, axis=0, keepdims=True)[:, :local]
    coeffs = weights - jnp.sum(weights, axis=0, keepdims=True) * scale
    held[...] = jnp.broadcast_to(coeffs, (total, d))
    acc = jnp.zeros((mats * share, d), F32)
    for k, block_ref in enumerate(block_refs):
        mine = held[pl.ds(pl.multiple_of((me ^ k) * local, local), local)]
        for s in range(local):
            acc = acc + mine[s : s + 1] * block_ref[s].astype(F32)
    for m in range(mats):
        update_ref[m] = acc[m * share : (m + 1) * share]


def solve_and_project(grams, blocks, mats):
    local, count, d = blocks[0].shape
    total = local * len(blocks)
    return pl.pallas_call(
        functools.partial(solve_kernel, len(grams)),
        out_shape=(
            jax.ShapeDtypeStruct((1, local), F32),
            jax.ShapeDtypeStruct((mats, count // mats, d), F32),
        ),
        scratch_shapes=[pltpu.VMEM((total, d), F32)],
        compiler_params=pltpu.CompilerParams(vmem_limit_bytes=VMEM_LIMIT),
        name="solve_and_project",
    )(*grams, *in_turn(blocks))


def body(spins, activations, cotangents, offdiag):
    local, mats = activations.shape[:2]
    owners = lax.axis_size("samp")
    total = local * owners
    blocks = list(jac_rows(activations, cotangents, owners))
    for k in turns(owners)[:-1]:
        blocks[k] = lax.ppermute(blocks[k], "samp", [(i, i ^ k) for i in range(owners)])
    partial = gram_partial(blocks, packed_energy(spins, offdiag, total))
    grams = partners(partial, "layer", 1, lax.axis_size("layer"))
    first = 1
    while first < owners:
        count = min(4, owners // first)
        grams = partners(tree_sum(grams), "samp", first, count)
        first *= count
    weights, update = solve_and_project(grams, blocks, mats)
    return weights.reshape(local), update


def solution(mesh):
    placed = (
        P("samp", None),
        P("samp", "layer", None, None),
        P("samp", "layer", None, None),
        P("samp"),
    )
    return jax.shard_map(
        body,
        mesh=mesh,
        in_specs=placed,
        out_specs=(P("samp"), P("layer", "samp", None)),
        check_vma=False,
    )
```

```python
import functools

import jax
import jax.numpy as jnp
from jax import lax
from jax.experimental import pallas as pl
from jax.experimental.pallas import tpu as pltpu
from jax.sharding import PartitionSpec as P

SIDE = 16
LANES = 128
CHUNK = 16
PIVOTS = 8
VMEM_LIMIT = 24 * 2**20
JAC_VMEM_LIMIT = 52 * 2**20
shift_ratio = 0.1
F32 = jnp.float32
BF16 = jnp.bfloat16


def iota(shape, dim):
    return lax.broadcasted_iota(jnp.int32, shape, dim)


def turns(owners):
    far, near = list(range(owners // 2, owners)), list(range(owners // 2 - 1, 0, -1))
    order = [far.pop(0)]
    while far or near:
        order += far[:1] + near[:1]
        far, near = far[1:], near[1:]
    return order + [0]


def in_turn(blocks):
    return [blocks[k] for k in turns(len(blocks))]


def in_place(blocks):
    order = turns(len(blocks))
    return [blocks[order.index(k)] for k in range(len(blocks))]


def jac_kernel(act_hbm, cot_hbm, *refs):
    *out_refs, act_buf, cot_buf, held, sems = refs
    samples, mats = act_buf.shape[:2]
    share = out_refs[0].shape[1] // mats
    me = lax.axis_index("samp")
    copies = []
    for s in range(samples):
        copies.append(
            (
                pltpu.make_async_copy(act_hbm.at[s], act_buf.at[s], sems.at[0, s]),
                pltpu.make_async_copy(cot_hbm.at[s], cot_buf.at[s], sems.at[1, s]),
            )
        )
    for pair in copies:
        for copy in pair:
            copy.start()
    group = 2
    for first in range(0, samples, group):
        for s in range(first, first + group):
            for copy in copies[s]:
                copy.wait()
        for s in range(first, first + group):
            for m in range(mats):
                held[s, m] = lax.dot_general(
                    act_buf[s, m],
                    cot_buf[s, m],
                    (((0,), (0,)), ((), ())),
                    preferred_element_type=F32,
                )
    for k, out_ref in enumerate(out_refs):
        owned = pl.ds(pl.multiple_of((me ^ k) * share, share), share)
        for s in range(samples):
            rows = [held[s, m, owned] for m in range(mats)]
            out_ref[s] = jnp.concatenate(rows, axis=0).astype(BF16)


def jac_rows(activations, cotangents, owners):
    samples, mats, sites, d = activations.shape
    rows = mats * d // owners
    hbm = pl.BlockSpec(memory_space=pltpu.HBM)
    return pl.pallas_call(
        jac_kernel,
        in_specs=[hbm, hbm],
        out_shape=[jax.ShapeDtypeStruct((samples, rows, d), BF16)] * owners,
        scratch_shapes=[
            pltpu.VMEM((samples, mats, sites, d), BF16),
            pltpu.VMEM((samples, mats, sites, d), BF16),
            pltpu.VMEM((samples, mats, d, d), F32),
            pltpu.SemaphoreType.DMA((2, samples)),
        ],
        compiler_params=pltpu.CompilerParams(vmem_limit_bytes=JAC_VMEM_LIMIT),
        cost_estimate=pl.CostEstimate(
            flops=2 * samples * mats * sites * d * d,
            bytes_accessed=6 * samples * mats * sites * d,
            transcendentals=0,
        ),
        name="jac_rows",
    )(activations, cotangents)


def packed_shape(total):
    half = total // 2
    return half, -(-(3 * half + 2) // LANES) * LANES


def energy_kernel(total, spins_ref, offdiag_ref, out_ref):
    shape = out_ref.shape
    local = spins_ref.shape[0]
    sites = SIDE * SIDE
    z = (2 * spins_ref[...] - 1).astype(F32)
    column = iota((local, sites), 1) % SIDE
    right = jnp.where(
        column == SIDE - 1, pltpu.roll(z, SIDE - 1, 1), pltpu.roll(z, sites - 1, 1)
    )
    below = pltpu.roll(z, sites - SIDE, 1)
    energy = offdiag_ref[...] + jnp.sum(z * (right + below), axis=1, keepdims=True)
    half = total // 2
    first = lax.axis_index("samp") * local
    lower = first // half
    first = first - lower * half
    spread = jnp.concatenate([energy] * (half // local), axis=0)
    row = iota(shape, 0)
    here = (row >= first) & (row < first + local) & (iota(shape, 1) == 3 * half + lower)
    here = here & (lax.axis_index("layer") == 0)
    out_ref[...] = jnp.where(here, spread, F32(0.0))


def packed_energy(spins, offdiag, total):
    return pl.pallas_call(
        functools.partial(energy_kernel, total),
        out_shape=jax.ShapeDtypeStruct(packed_shape(total), F32),
        compiler_params=pltpu.CompilerParams(vmem_limit_bytes=VMEM_LIMIT),
        name="packed_energy",
    )(spins, offdiag[:, None])


def gram_kernel(*refs):
    *block_refs, energy_ref, out_ref, flat, whole = refs
    block_refs = in_place(block_refs)
    local, count, d = block_refs[0].shape
    total = local * len(block_refs)
    joined = CHUNK // local
    me = lax.axis_index("samp")
    block = CHUNK * CHUNK
    dest = iota((block, block), 0)
    sample = dest % CHUNK
    sample = (sample // local ^ me % joined) * local + sample % local
    source = sample * CHUNK + dest // CHUNK
    swap = (iota((block, block), 1) == source).astype(F32).astype(BF16)
    for row in range(0, count, CHUNK):
        for j in range(len(block_refs) // joined):
            pieces = [ref[:, row : row + CHUNK] for ref in block_refs[j * joined : (j + 1) * joined]]
            piece = jnp.concatenate(pieces, axis=0).reshape(block, d)
            turned = jnp.dot(swap, piece, preferred_element_type=F32).astype(BF16)
            place = pl.ds(pl.multiple_of((me // joined ^ j) * CHUNK, CHUNK), CHUNK)
            for r in range(CHUNK):
                flat[row + r, place] = turned[r * CHUNK : (r + 1) * CHUNK]
    lined = jnp.concatenate([flat[r] for r in range(count)], axis=1)
    whole[:, :total] = lax.dot_general(
        lined, lined, (((1,), (1,)), ((), ())), preferred_element_type=F32
    )
    half, width = out_ref.shape
    lane = iota((half, width), 1)
    lower = pltpu.roll(whole[half:], half, 1)
    packed = jnp.where(lane < 3 * half, lower, energy_ref[...])
    out_ref[...] = jnp.where(lane < half, whole[:half], packed)


def gram_partial(blocks, energies):
    local, count, d = blocks[0].shape
    total = local * len(blocks)
    return pl.pallas_call(
        gram_kernel,
        out_shape=jax.ShapeDtypeStruct(packed_shape(total), F32),
        scratch_shapes=[
            pltpu.VMEM((count, total, d), BF16),
            pltpu.VMEM((total, packed_shape(total)[1]), F32),
        ],
        compiler_params=pltpu.CompilerParams(vmem_limit_bytes=VMEM_LIMIT),
        cost_estimate=pl.CostEstimate(
            flops=2 * total * total * count * d,
            bytes_accessed=2 * total * count * d,
            transcendentals=0,
        ),
        name="gram_partial",
    )(*in_turn(blocks), energies)


def tree_sum(parts):
    while len(parts) > 1:
        odd = parts[len(parts) // 2 * 2 :]
        parts = [a + b for a, b in zip(parts[::2], parts[1::2])] + odd
    return parts[0]


def pivot_rows(rows, entries):
    count = len(rows)
    rows = list(rows)
    p = [[entries[min(i, l)][max(i, l)] for l in range(count)] for i in range(count)]
    uppers = {}
    for j in range(0, count, 2):
        a, b, c = p[j][j], p[j][j + 1], p[j + 1][j + 1]
        inverse = F32(1.0) / (a * c - b * b)

        def scaled(x, y):
            return (c * x - b * y) * inverse, (a * y - b * x) * inverse

        first, second = rows[j], rows[j + 1]
        rows[j], rows[j + 1] = scaled(first, second)
        later = range(j + 2, count)
        for l in later:
            uppers[j, l], uppers[j + 1, l] = scaled(p[j][l], p[j + 1][l])
        for i in later:
            rows[i] = rows[i] - (p[j][i] * rows[j] + p[j + 1][i] * rows[j + 1])
            for l in range(i, count):
                change = p[j][i] * uppers[j, l] + p[j + 1][i] * uppers[j + 1, l]
                p[i][l] = p[l][i] = p[i][l] - change
    for j in range(count - 4, -1, -2):
        for i in (j, j + 1):
            rows[i] = rows[i] - tree_sum([uppers[i, l] * rows[l] for l in range(j + 2, count)])
    return rows


def eliminate(matrix, total):
    width = matrix.shape[1]
    if total <= 64:
        blocks = [matrix[i : i + PIVOTS] for i in range(0, total, PIVOTS)]
        sub = iota((PIVOTS, width), 0)
        for b in range(len(blocks)):
            spread = [
                [
                    jnp.broadcast_to(block[:, b * PIVOTS + j : b * PIVOTS + j + 1], (PIVOTS, width))
                    for block in blocks
                ]
                for j in range(PIVOTS)
            ]

            def line(value, i):
                return jnp.broadcast_to(value[i : i + 1], (PIVOTS, width))

            entries = [
                [line(spread[l][b], i) if l >= i else None for l in range(PIVOTS)]
                for i in range(PIVOTS)
            ]
            rows = pivot_rows([line(blocks[b], i) for i in range(PIVOTS)], entries)
            for i in range(len(blocks)):
                if i != b:
                    terms = [spread[j][i] * rows[j] for j in range(PIVOTS)]
                    blocks[i] = blocks[i] - tree_sum(terms)
            solved = rows[0]
            for j in range(1, PIVOTS):
                solved = jnp.where(sub == j, rows[j], solved)
            blocks[b] = solved
        return jnp.concatenate([block[:, total : total + 1] for block in blocks], axis=0)
    row = iota(matrix.shape, 0)
    lane = iota(matrix.shape, 1)

    def one(k, held):
        column = jnp.sum(jnp.where(lane == k, held, F32(0.0)), axis=1, keepdims=True)
        pivot_row = jnp.sum(jnp.where(row == k, held, F32(0.0)), axis=0, keepdims=True)
        here = lane[:1] == k
        pivot = jnp.sum(jnp.where(here, pivot_row, F32(0.0)), axis=1, keepdims=True)
        scaled = pivot_row * (F32(1.0) / pivot)
        return held - jnp.where(row == k, F32(0.0), column) * scaled

    matrix = lax.fori_loop(0, total, one, matrix)
    diag = jnp.sum(jnp.where(row == lane, matrix, F32(0.0)), axis=1, keepdims=True)
    return matrix[:, total : total + 1] / diag


def sum_kernel(*refs):
    *part_refs, out_ref = refs
    out_ref[...] = tree_sum([ref[...] for ref in part_refs[::-1]])


def partners(value, axis, first, count):
    size = lax.axis_size(axis)
    parts = []
    for k in range(count - 1, 0, -1):
        perm = [(i, i ^ (k * first)) for i in range(size)]
        parts.append(lax.ppermute(value, axis, perm))
    return parts + [value]


def sum_over(value, axis, first, count):
    return pl.pallas_call(
        sum_kernel,
        out_shape=jax.ShapeDtypeStruct(value.shape, F32),
        compiler_params=pltpu.CompilerParams(vmem_limit_bytes=VMEM_LIMIT),
        name="sum_over",
    )(*partners(value, axis, first, count))


def solve_kernel(grams, *refs):
    gram_refs, (*block_refs, weights_ref, update_ref, held) = refs[:grams], refs[grams:]
    block_refs = in_place(block_refs)
    mats, share, d = update_ref.shape
    local = weights_ref.shape[1]
    packed = tree_sum([ref[...] for ref in gram_refs[::-1]])
    half, packed_width = packed.shape
    total = 2 * half
    width = (total // LANES + 1) * LANES
    turned = jnp.swapaxes(packed[:, half:total], 0, 1)
    energy = [packed[:, 3 * half + i : 3 * half + i + 1] for i in range(2)]
    energy = [jnp.broadcast_to(e, (half, width - total)) for e in energy]
    upper = jnp.concatenate([packed[:, :half], turned, energy[0]], axis=1)
    lower = jnp.concatenate([packed[:, half : 3 * half], energy[1]], axis=1)
    raw = jnp.concatenate([upper, lower], axis=0)
    row = iota((total, width), 0)
    lane = iota((total, width), 1)
    inside = lane < total
    scale = F32(1.0 / total)
    row_mean = jnp.sum(jnp.where(inside, raw, F32(0.0)), axis=1, keepdims=True) * scale
    col_mean = jnp.sum(raw, axis=0, keepdims=True) * scale
    mean = jnp.sum(row_mean, axis=0, keepdims=True) * scale
    gram = (raw - col_mean - row_mean + mean) * scale
    eps = (raw - col_mean) * F32(1.0 / total**0.5)
    on_diag = row == lane
    trace = jnp.sum(
        jnp.sum(jnp.where(on_diag, gram, F32(0.0)), axis=1, keepdims=True), axis=0, keepdims=True
    )
    shift = F32(shift_ratio) * trace * scale
    system = jnp.where(inside, gram + jnp.where(on_diag, shift, F32(0.0)), eps)
    weights = eliminate(system, total)
    me = lax.axis_index("samp")
    own = jnp.where(row - me * local == lane, weights, F32(0.0))
    weights_ref[...] = jnp.sum(own, axis=0, keepdims=True)[:, :local]
    coeffs = weights - jnp.sum(weights, axis=0, keepdims=True) * scale
    held[...] = jnp.broadcast_to(coeffs, (total, d))
    acc = jnp.zeros((mats * share, d), F32)
    for k, block_ref in enumerate(block_refs):
        mine = held[pl.ds(pl.multiple_of((me ^ k) * local, local), local)]
        for s in range(local):
            acc = acc + mine[s : s + 1] * block_ref[s].astype(F32)
    for m in range(mats):
        update_ref[m] = acc[m * share : (m + 1) * share]


def solve_and_project(grams, blocks, mats):
    local, count, d = blocks[0].shape
    total = local * len(blocks)
    return pl.pallas_call(
        functools.partial(solve_kernel, len(grams)),
        out_shape=(
            jax.ShapeDtypeStruct((1, local), F32),
            jax.ShapeDtypeStruct((mats, count // mats, d), F32),
        ),
        scratch_shapes=[pltpu.VMEM((total, d), F32)],
        compiler_params=pltpu.CompilerParams(vmem_limit_bytes=VMEM_LIMIT),
        name="solve_and_project",
    )(*grams, *in_turn(blocks))


def body(spins, activations, cotangents, offdiag):
    local, mats = activations.shape[:2]
    owners = lax.axis_size("samp")
    total = local * owners
    blocks = list(jac_rows(activations, cotangents, owners))
    for k in turns(owners)[:-1]:
        blocks[k] = lax.ppermute(blocks[k], "samp", [(i, i ^ k) for i in range(owners)])
    partial = gram_partial(blocks, packed_energy(spins, offdiag, total))
    gram = sum_over(partial, "layer", 1, lax.axis_size("layer"))
    first = 1
    while 4 * first < owners:
        gram = sum_over(gram, "samp", first, 4)
        first *= 4
    grams = partners(gram, "samp", first, owners // first)
    weights, update = solve_and_project(grams, blocks, mats)
    return weights.reshape(local), update


def solution(mesh):
    placed = (
        P("samp", None),
        P("samp", "layer", None, None),
        P("samp", "layer", None, None),
        P("samp"),
    )
    return jax.shard_map(
        body,
        mesh=mesh,
        in_specs=placed,
        out_specs=(P("samp"), P("layer", "samp", None)),
        check_vma=False,
    )
```

```python
import functools

import jax
import jax.numpy as jnp
from jax import lax
from jax.experimental import pallas as pl
from jax.experimental.pallas import tpu as pltpu
from jax.sharding import PartitionSpec as P

SIDE = 16
LANES = 128
CHUNK = 16
PIVOTS = 8
VMEM_LIMIT = 24 * 2**20
JAC_VMEM_LIMIT = 52 * 2**20
shift_ratio = 0.1
F32 = jnp.float32
BF16 = jnp.bfloat16


def iota(shape, dim):
    return lax.broadcasted_iota(jnp.int32, shape, dim)


def turns(owners):
    far, near = list(range(owners // 2, owners)), list(range(owners // 2 - 1, 0, -1))
    order = [far.pop(0)]
    while far or near:
        order += far[:1] + near[:1]
        far, near = far[1:], near[1:]
    return order + [0]


def in_turn(blocks):
    return [blocks[k] for k in turns(len(blocks))]


def in_place(blocks):
    order = turns(len(blocks))
    return [blocks[order.index(k)] for k in range(len(blocks))]


def jac_kernel(act_hbm, cot_hbm, *refs):
    *out_refs, act_buf, cot_buf, held, sems = refs
    samples, mats = act_buf.shape[:2]
    share = out_refs[0].shape[1] // mats
    me = lax.axis_index("samp")
    copies = []
    for s in range(samples):
        copies.append(
            (
                pltpu.make_async_copy(act_hbm.at[s], act_buf.at[s], sems.at[0, s]),
                pltpu.make_async_copy(cot_hbm.at[s], cot_buf.at[s], sems.at[1, s]),
            )
        )
    for pair in copies:
        for copy in pair:
            copy.start()

    def share_out(samples):
        for k, out_ref in enumerate(out_refs):
            owned = pl.ds(pl.multiple_of((me ^ k) * share, share), share)
            for s in samples:
                rows = [held[s, m, owned] for m in range(mats)]
                out_ref[s] = jnp.concatenate(rows, axis=0).astype(BF16)

    group = 2
    for first in range(0, samples, group):
        here = range(first, first + group)
        for s in here:
            for copy in copies[s]:
                copy.wait()
        for s in here:
            for m in range(mats):
                held[s, m] = lax.dot_general(
                    act_buf[s, m],
                    cot_buf[s, m],
                    (((0,), (0,)), ((), ())),
                    preferred_element_type=F32,
                ).astype(held.dtype)
        if first > 0:
            share_out(range(first - group, first))
    share_out(range(samples - group, samples))


def jac_rows(activations, cotangents, owners):
    samples, mats, sites, d = activations.shape
    rows = mats * d // owners
    hbm = pl.BlockSpec(memory_space=pltpu.HBM)
    return pl.pallas_call(
        jac_kernel,
        in_specs=[hbm, hbm],
        out_shape=[jax.ShapeDtypeStruct((samples, rows, d), BF16)] * owners,
        scratch_shapes=[
            pltpu.VMEM((samples, mats, sites, d), BF16),
            pltpu.VMEM((samples, mats, sites, d), BF16),
            pltpu.VMEM((samples, mats, d, d), BF16 if d // owners % CHUNK == 0 else F32),
            pltpu.SemaphoreType.DMA((2, samples)),
        ],
        compiler_params=pltpu.CompilerParams(vmem_limit_bytes=JAC_VMEM_LIMIT),
        cost_estimate=pl.CostEstimate(
            flops=2 * samples * mats * sites * d * d,
            bytes_accessed=6 * samples * mats * sites * d,
            transcendentals=0,
        ),
        name="jac_rows",
    )(activations, cotangents)


def packed_shape(total):
    half = total // 2
    return half, -(-(3 * half + 2) // LANES) * LANES


def energy_kernel(total, spins_ref, offdiag_ref, out_ref):
    shape = out_ref.shape
    local = spins_ref.shape[0]
    sites = SIDE * SIDE
    z = (2 * spins_ref[...] - 1).astype(F32)
    column = iota((local, sites), 1) % SIDE
    right = jnp.where(
        column == SIDE - 1, pltpu.roll(z, SIDE - 1, 1), pltpu.roll(z, sites - 1, 1)
    )
    below = pltpu.roll(z, sites - SIDE, 1)
    energy = offdiag_ref[...] + jnp.sum(z * (right + below), axis=1, keepdims=True)
    half = total // 2
    first = lax.axis_index("samp") * local
    lower = first // half
    first = first - lower * half
    spread = jnp.concatenate([energy] * (half // local), axis=0)
    row = iota(shape, 0)
    here = (row >= first) & (row < first + local) & (iota(shape, 1) == 3 * half + lower)
    here = here & (lax.axis_index("layer") == 0)
    out_ref[...] = jnp.where(here, spread, F32(0.0))


def packed_energy(spins, offdiag, total):
    return pl.pallas_call(
        functools.partial(energy_kernel, total),
        out_shape=jax.ShapeDtypeStruct(packed_shape(total), F32),
        compiler_params=pltpu.CompilerParams(vmem_limit_bytes=VMEM_LIMIT),
        name="packed_energy",
    )(spins, offdiag[:, None])


def gram_kernel(*refs):
    *block_refs, energy_ref, out_ref, flat, whole = refs
    block_refs = in_place(block_refs)
    local, count, d = block_refs[0].shape
    total = local * len(block_refs)
    joined = CHUNK // local
    me = lax.axis_index("samp")
    block = CHUNK * CHUNK
    dest = iota((block, block), 0)
    sample = dest % CHUNK
    sample = (sample // local ^ me % joined) * local + sample % local
    source = sample * CHUNK + dest // CHUNK
    swap = (iota((block, block), 1) == source).astype(F32).astype(BF16)
    for row in range(0, count, CHUNK):
        for j in range(len(block_refs) // joined):
            pieces = [ref[:, row : row + CHUNK] for ref in block_refs[j * joined : (j + 1) * joined]]
            piece = jnp.concatenate(pieces, axis=0).reshape(block, d)
            turned = jnp.dot(swap, piece, preferred_element_type=F32).astype(BF16)
            place = pl.ds(pl.multiple_of((me // joined ^ j) * CHUNK, CHUNK), CHUNK)
            for r in range(CHUNK):
                flat[row + r, place] = turned[r * CHUNK : (r + 1) * CHUNK]
    lined = jnp.concatenate([flat[r] for r in range(count)], axis=1)
    gram = lax.dot_general(lined, lined, (((1,), (1,)), ((), ())), preferred_element_type=F32)
    whole[...] = jnp.zeros_like(whole)
    whole[:, :total] += gram
    half, width = out_ref.shape
    lane = iota((half, width), 1)
    lower = pltpu.roll(whole[half:], half, 1)
    packed = jnp.where(lane < 3 * half, lower, energy_ref[...])
    out_ref[...] = jnp.where(lane < half, whole[:half], packed)


def gram_partial(blocks, energies):
    local, count, d = blocks[0].shape
    total = local * len(blocks)
    return pl.pallas_call(
        gram_kernel,
        out_shape=jax.ShapeDtypeStruct(packed_shape(total), F32),
        scratch_shapes=[
            pltpu.VMEM((count, total, d), BF16),
            pltpu.VMEM((total, packed_shape(total)[1]), F32),
        ],
        compiler_params=pltpu.CompilerParams(vmem_limit_bytes=VMEM_LIMIT),
        cost_estimate=pl.CostEstimate(
            flops=2 * total * total * count * d,
            bytes_accessed=2 * total * count * d,
            transcendentals=0,
        ),
        name="gram_partial",
    )(*in_turn(blocks), energies)


def tree_sum(parts):
    while len(parts) > 1:
        odd = parts[len(parts) // 2 * 2 :]
        parts = [a + b for a, b in zip(parts[::2], parts[1::2])] + odd
    return parts[0]


def pivot_rows(rows, entries):
    count = len(rows)
    rows = list(rows)
    p = [[entries[min(i, l)][max(i, l)] for l in range(count)] for i in range(count)]
    uppers = {}
    for j in range(0, count, 2):
        a, b, c = p[j][j], p[j][j + 1], p[j + 1][j + 1]
        inverse = F32(1.0) / (a * c - b * b)

        def scaled(x, y):
            return (c * x - b * y) * inverse, (a * y - b * x) * inverse

        first, second = rows[j], rows[j + 1]
        rows[j], rows[j + 1] = scaled(first, second)
        later = range(j + 2, count)
        for l in later:
            uppers[j, l], uppers[j + 1, l] = scaled(p[j][l], p[j + 1][l])
        for i in later:
            rows[i] = rows[i] - (p[j][i] * rows[j] + p[j + 1][i] * rows[j + 1])
            for l in range(i, count):
                change = p[j][i] * uppers[j, l] + p[j + 1][i] * uppers[j + 1, l]
                p[i][l] = p[l][i] = p[i][l] - change
    for j in range(count - 4, -1, -2):
        for i in (j, j + 1):
            rows[i] = rows[i] - tree_sum([uppers[i, l] * rows[l] for l in range(j + 2, count)])
    return rows


def eliminate(matrix, total):
    width = matrix.shape[1]
    if total <= 64:
        blocks = [matrix[i : i + PIVOTS] for i in range(0, total, PIVOTS)]
        sub = iota((PIVOTS, width), 0)
        for b in range(len(blocks)):
            spread = [
                [
                    jnp.broadcast_to(block[:, b * PIVOTS + j : b * PIVOTS + j + 1], (PIVOTS, width))
                    for block in blocks
                ]
                for j in range(PIVOTS)
            ]

            def line(value, i):
                return jnp.broadcast_to(value[i : i + 1], (PIVOTS, width))

            entries = [
                [line(spread[l][b], i) if l >= i else None for l in range(PIVOTS)]
                for i in range(PIVOTS)
            ]
            rows = pivot_rows([line(blocks[b], i) for i in range(PIVOTS)], entries)
            for i in range(len(blocks)):
                if i != b:
                    terms = [spread[j][i] * rows[j] for j in range(PIVOTS)]
                    blocks[i] = blocks[i] - tree_sum(terms)
            solved = rows[0]
            for j in range(1, PIVOTS):
                solved = jnp.where(sub == j, rows[j], solved)
            blocks[b] = solved
        return jnp.concatenate([block[:, total : total + 1] for block in blocks], axis=0)
    row = iota(matrix.shape, 0)
    lane = iota(matrix.shape, 1)

    def one(k, held):
        column = jnp.sum(jnp.where(lane == k, held, F32(0.0)), axis=1, keepdims=True)
        pivot_row = jnp.sum(jnp.where(row == k, held, F32(0.0)), axis=0, keepdims=True)
        here = lane[:1] == k
        pivot = jnp.sum(jnp.where(here, pivot_row, F32(0.0)), axis=1, keepdims=True)
        scaled = pivot_row * (F32(1.0) / pivot)
        return held - jnp.where(row == k, F32(0.0), column) * scaled

    matrix = lax.fori_loop(0, total, one, matrix)
    diag = jnp.sum(jnp.where(row == lane, matrix, F32(0.0)), axis=1, keepdims=True)
    return matrix[:, total : total + 1] / diag


def sum_kernel(*refs):
    *part_refs, out_ref = refs
    out_ref[...] = tree_sum([ref[...] for ref in part_refs[::-1]])


def partners(value, axis, first, count):
    size = lax.axis_size(axis)
    parts = []
    for k in range(count - 1, 0, -1):
        perm = [(i, i ^ (k * first)) for i in range(size)]
        parts.append(lax.ppermute(value, axis, perm))
    return parts + [value]


def sum_over(value, axis, first, count):
    return pl.pallas_call(
        sum_kernel,
        out_shape=jax.ShapeDtypeStruct(value.shape, F32),
        compiler_params=pltpu.CompilerParams(vmem_limit_bytes=VMEM_LIMIT),
        name="sum_over",
    )(*partners(value, axis, first, count))


def solve_kernel(grams, *refs):
    gram_refs, (*block_refs, weights_ref, update_ref, held) = refs[:grams], refs[grams:]
    block_refs = in_place(block_refs)
    mats, share, d = update_ref.shape
    local = weights_ref.shape[1]
    packed = tree_sum([ref[...] for ref in gram_refs[::-1]])
    half, packed_width = packed.shape
    total = 2 * half
    width = (total // LANES + 1) * LANES
    turned = jnp.swapaxes(packed[:, half:total], 0, 1)
    energy = [packed[:, 3 * half + i : 3 * half + i + 1] for i in range(2)]
    energy = [jnp.broadcast_to(e, (half, width - total)) for e in energy]
    upper = jnp.concatenate([packed[:, :half], turned, energy[0]], axis=1)
    lower = jnp.concatenate([packed[:, half : 3 * half], energy[1]], axis=1)
    raw = jnp.concatenate([upper, lower], axis=0)
    row = iota((total, width), 0)
    lane = iota((total, width), 1)
    inside = lane < total
    scale = F32(1.0 / total)
    row_mean = jnp.sum(jnp.where(inside, raw, F32(0.0)), axis=1, keepdims=True) * scale
    col_mean = jnp.sum(raw, axis=0, keepdims=True) * scale
    mean = jnp.sum(row_mean, axis=0, keepdims=True) * scale
    gram = (raw - col_mean - row_mean + mean) * scale
    eps = (raw - col_mean) * F32(1.0 / total**0.5)
    on_diag = row == lane
    trace = jnp.sum(
        jnp.sum(jnp.where(on_diag, gram, F32(0.0)), axis=1, keepdims=True), axis=0, keepdims=True
    )
    shift = F32(shift_ratio) * trace * scale
    system = jnp.where(inside, gram + jnp.where(on_diag, shift, F32(0.0)), eps)
    weights = eliminate(system, total)
    me = lax.axis_index("samp")
    own = jnp.where(row - me * local == lane, weights, F32(0.0))
    weights_ref[...] = jnp.sum(own, axis=0, keepdims=True)[:, :local]
    coeffs = weights - jnp.sum(weights, axis=0, keepdims=True) * scale
    held[...] = jnp.broadcast_to(coeffs, (total, d))
    acc = jnp.zeros((mats * share, d), F32)
    for k, block_ref in enumerate(block_refs):
        mine = held[pl.ds(pl.multiple_of((me ^ k) * local, local), local)]
        for s in range(local):
            acc = acc + mine[s : s + 1] * block_ref[s].astype(F32)
    for m in range(mats):
        update_ref[m] = acc[m * share : (m + 1) * share]


def solve_and_project(grams, blocks, mats):
    local, count, d = blocks[0].shape
    total = local * len(blocks)
    return pl.pallas_call(
        functools.partial(solve_kernel, len(grams)),
        out_shape=(
            jax.ShapeDtypeStruct((1, local), F32),
            jax.ShapeDtypeStruct((mats, count // mats, d), F32),
        ),
        scratch_shapes=[pltpu.VMEM((total, d), F32)],
        compiler_params=pltpu.CompilerParams(vmem_limit_bytes=VMEM_LIMIT),
        name="solve_and_project",
    )(*grams, *in_turn(blocks))


def body(spins, activations, cotangents, offdiag):
    local, mats = activations.shape[:2]
    owners = lax.axis_size("samp")
    total = local * owners
    blocks = list(jac_rows(activations, cotangents, owners))
    for k in turns(owners)[:-1]:
        blocks[k] = lax.ppermute(blocks[k], "samp", [(i, i ^ k) for i in range(owners)])
    partial = gram_partial(blocks, packed_energy(spins, offdiag, total))
    gram = sum_over(partial, "layer", 1, lax.axis_size("layer"))
    first = 1
    while 4 * first < owners:
        gram = sum_over(gram, "samp", first, 4)
        first *= 4
    grams = partners(gram, "samp", first, owners // first)
    weights, update = solve_and_project(grams, blocks, mats)
    return weights.reshape(local), update


def solution(mesh):
    placed = (
        P("samp", None),
        P("samp", "layer", None, None),
        P("samp", "layer", None, None),
        P("samp"),
    )
    return jax.shard_map(
        body,
        mesh=mesh,
        in_specs=placed,
        out_specs=(P("samp"), P("layer", "samp", None)),
        check_vma=False,
    )
```

```python
import functools

import jax
import jax.numpy as jnp
from jax import lax
from jax.experimental import pallas as pl
from jax.experimental.pallas import tpu as pltpu
from jax.sharding import PartitionSpec as P

SIDE = 16
LANES = 128
CHUNK = 16
PIVOTS = 8
VMEM_LIMIT = 24 * 2**20
JAC_VMEM_LIMIT = 52 * 2**20
shift_ratio = 0.1
F32 = jnp.float32
BF16 = jnp.bfloat16


def iota(shape, dim):
    return lax.broadcasted_iota(jnp.int32, shape, dim)


def turns(owners):
    far, near = list(range(owners // 2, owners)), list(range(owners // 2 - 1, 0, -1))
    order = [far.pop(0)]
    while far or near:
        order += far[:1] + near[:1]
        far, near = far[1:], near[1:]
    return order + [0]


def in_turn(blocks):
    return [blocks[k] for k in turns(len(blocks))]


def in_place(blocks):
    order = turns(len(blocks))
    return [blocks[order.index(k)] for k in range(len(blocks))]


def jac_kernel(act_hbm, cot_hbm, *refs):
    *out_refs, act_buf, cot_buf, held, sems = refs
    samples, mats = act_buf.shape[:2]
    share = out_refs[0].shape[1] // mats
    me = lax.axis_index("samp")
    copies = []
    for s in range(samples):
        copies.append(
            (
                pltpu.make_async_copy(act_hbm.at[s], act_buf.at[s], sems.at[0, s]),
                pltpu.make_async_copy(cot_hbm.at[s], cot_buf.at[s], sems.at[1, s]),
            )
        )
    for pair in copies:
        for copy in pair:
            copy.start()

    def share_out(samples):
        for k, out_ref in enumerate(out_refs):
            owned = pl.ds(pl.multiple_of((me ^ k) * share, share), share)
            for s in samples:
                rows = [held[s, m, owned] for m in range(mats)]
                out_ref[s] = jnp.concatenate(rows, axis=0).astype(BF16)

    group = 2
    for first in range(0, samples, group):
        here = range(first, first + group)
        for s in here:
            for copy in copies[s]:
                copy.wait()
        for s in here:
            for m in range(mats):
                held[s, m] = lax.dot_general(
                    act_buf[s, m],
                    cot_buf[s, m],
                    (((0,), (0,)), ((), ())),
                    preferred_element_type=F32,
                ).astype(held.dtype)
        if first > 0:
            share_out(range(first - group, first))
    share_out(range(samples - group, samples))


def jac_rows(activations, cotangents, owners):
    samples, mats, sites, d = activations.shape
    rows = mats * d // owners
    hbm = pl.BlockSpec(memory_space=pltpu.HBM)
    return pl.pallas_call(
        jac_kernel,
        in_specs=[hbm, hbm],
        out_shape=[jax.ShapeDtypeStruct((samples, rows, d), BF16)] * owners,
        scratch_shapes=[
            pltpu.VMEM((samples, mats, sites, d), BF16),
            pltpu.VMEM((samples, mats, sites, d), BF16),
            pltpu.VMEM((samples, mats, d, d), BF16 if d // owners % CHUNK == 0 else F32),
            pltpu.SemaphoreType.DMA((2, samples)),
        ],
        compiler_params=pltpu.CompilerParams(vmem_limit_bytes=JAC_VMEM_LIMIT),
        cost_estimate=pl.CostEstimate(
            flops=2 * samples * mats * sites * d * d,
            bytes_accessed=6 * samples * mats * sites * d,
            transcendentals=0,
        ),
        name="jac_rows",
    )(activations, cotangents)


def packed_shape(total):
    half = total // 2
    return half, -(-(3 * half + 2) // LANES) * LANES


def energy_kernel(total, spins_ref, offdiag_ref, out_ref):
    shape = out_ref.shape
    local = spins_ref.shape[0]
    sites = SIDE * SIDE
    z = (2 * spins_ref[...] - 1).astype(F32)
    column = iota((local, sites), 1) % SIDE
    right = jnp.where(
        column == SIDE - 1, pltpu.roll(z, SIDE - 1, 1), pltpu.roll(z, sites - 1, 1)
    )
    below = pltpu.roll(z, sites - SIDE, 1)
    energy = offdiag_ref[...] + jnp.sum(z * (right + below), axis=1, keepdims=True)
    half = total // 2
    first = lax.axis_index("samp") * local
    lower = first // half
    first = first - lower * half
    spread = jnp.concatenate([energy] * (half // local), axis=0)
    row = iota(shape, 0)
    here = (row >= first) & (row < first + local) & (iota(shape, 1) == 3 * half + lower)
    here = here & (lax.axis_index("layer") == 0)
    out_ref[...] = jnp.where(here, spread, F32(0.0))


def packed_energy(spins, offdiag, total):
    return pl.pallas_call(
        functools.partial(energy_kernel, total),
        out_shape=jax.ShapeDtypeStruct(packed_shape(total), F32),
        compiler_params=pltpu.CompilerParams(vmem_limit_bytes=VMEM_LIMIT),
        name="packed_energy",
    )(spins, offdiag[:, None])


def gram_kernel(*refs):
    *block_refs, energy_ref, out_ref, flat, whole = refs
    block_refs = in_place(block_refs)
    local, count, d = block_refs[0].shape
    total = local * len(block_refs)
    joined = CHUNK // local
    me = lax.axis_index("samp")
    block = CHUNK * CHUNK
    dest = iota((block, block), 0)
    sample = dest % CHUNK
    sample = (sample // local ^ me % joined) * local + sample % local
    source = sample * CHUNK + dest // CHUNK
    swap = (iota((block, block), 1) == source).astype(F32).astype(BF16)
    for row in range(0, count, CHUNK):
        for j in range(len(block_refs) // joined):
            pieces = [ref[:, row : row + CHUNK] for ref in block_refs[j * joined : (j + 1) * joined]]
            piece = jnp.concatenate(pieces, axis=0).reshape(block, d)
            turned = jnp.dot(swap, piece, preferred_element_type=F32).astype(BF16)
            place = pl.ds(pl.multiple_of((me // joined ^ j) * CHUNK, CHUNK), CHUNK)
            for r in range(CHUNK):
                flat[row + r, place] = turned[r * CHUNK : (r + 1) * CHUNK]
    lined = jnp.concatenate([flat[r] for r in range(count)], axis=1)
    gram = lax.dot_general(lined, lined, (((1,), (1,)), ((), ())), preferred_element_type=F32)
    whole[...] = jnp.zeros_like(whole)
    whole[:, :total] += gram
    half, width = out_ref.shape
    lane = iota((half, width), 1)
    lower = pltpu.roll(whole[half:], half, 1)
    packed = jnp.where(lane < 3 * half, lower, energy_ref[...])
    out_ref[...] = jnp.where(lane < half, whole[:half], packed)


def gram_partial(blocks, energies):
    local, count, d = blocks[0].shape
    total = local * len(blocks)
    return pl.pallas_call(
        gram_kernel,
        out_shape=jax.ShapeDtypeStruct(packed_shape(total), F32),
        scratch_shapes=[
            pltpu.VMEM((count, total, d), BF16),
            pltpu.VMEM((total, packed_shape(total)[1]), F32),
        ],
        compiler_params=pltpu.CompilerParams(vmem_limit_bytes=VMEM_LIMIT),
        cost_estimate=pl.CostEstimate(
            flops=2 * total * total * count * d,
            bytes_accessed=2 * total * count * d,
            transcendentals=0,
        ),
        name="gram_partial",
    )(*in_turn(blocks), energies)


def tree_sum(parts):
    while len(parts) > 1:
        odd = parts[len(parts) // 2 * 2 :]
        parts = [a + b for a, b in zip(parts[::2], parts[1::2])] + odd
    return parts[0]


def pivot_rows(rows, entries):
    count = len(rows)
    rows = list(rows)
    p = [[entries[min(i, l)][max(i, l)] for l in range(count)] for i in range(count)]
    uppers = {}
    for j in range(0, count, 2):
        a, b, c = p[j][j], p[j][j + 1], p[j + 1][j + 1]
        inverse = F32(1.0) / (a * c - b * b)

        def scaled(x, y):
            return (c * x - b * y) * inverse, (a * y - b * x) * inverse

        first, second = rows[j], rows[j + 1]
        rows[j], rows[j + 1] = scaled(first, second)
        later = range(j + 2, count)
        for l in later:
            uppers[j, l], uppers[j + 1, l] = scaled(p[j][l], p[j + 1][l])
        for i in later:
            rows[i] = rows[i] - (p[j][i] * rows[j] + p[j + 1][i] * rows[j + 1])
            for l in range(i, count):
                change = p[j][i] * uppers[j, l] + p[j + 1][i] * uppers[j + 1, l]
                p[i][l] = p[l][i] = p[i][l] - change
    for j in range(count - 4, -1, -2):
        for i in (j, j + 1):
            rows[i] = rows[i] - tree_sum([uppers[i, l] * rows[l] for l in range(j + 2, count)])
    return rows


def eliminate(matrix, total):
    width = matrix.shape[1]
    if total <= 64:
        blocks = [matrix[i : i + PIVOTS] for i in range(0, total, PIVOTS)]
        sub = iota((PIVOTS, width), 0)
        for b in range(len(blocks)):
            spread = [
                [
                    jnp.broadcast_to(block[:, b * PIVOTS + j : b * PIVOTS + j + 1], (PIVOTS, width))
                    for block in blocks
                ]
                for j in range(PIVOTS)
            ]

            def line(value, i):
                return jnp.broadcast_to(value[i : i + 1], (PIVOTS, width))

            entries = [
                [line(spread[l][b], i) if l >= i else None for l in range(PIVOTS)]
                for i in range(PIVOTS)
            ]
            rows = pivot_rows([line(blocks[b], i) for i in range(PIVOTS)], entries)
            for i in range(len(blocks)):
                if i != b:
                    terms = [spread[j][i] * rows[j] for j in range(PIVOTS)]
                    blocks[i] = blocks[i] - tree_sum(terms)
            solved = rows[0]
            for j in range(1, PIVOTS):
                solved = jnp.where(sub == j, rows[j], solved)
            blocks[b] = solved
        return jnp.concatenate([block[:, total : total + 1] for block in blocks], axis=0)
    row = iota(matrix.shape, 0)
    lane = iota(matrix.shape, 1)

    def one(k, held):
        column = jnp.sum(jnp.where(lane == k, held, F32(0.0)), axis=1, keepdims=True)
        pivot_row = jnp.sum(jnp.where(row == k, held, F32(0.0)), axis=0, keepdims=True)
        here = lane[:1] == k
        pivot = jnp.sum(jnp.where(here, pivot_row, F32(0.0)), axis=1, keepdims=True)
        scaled = pivot_row * (F32(1.0) / pivot)
        return held - jnp.where(row == k, F32(0.0), column) * scaled

    matrix = lax.fori_loop(0, total, one, matrix)
    diag = jnp.sum(jnp.where(row == lane, matrix, F32(0.0)), axis=1, keepdims=True)
    return matrix[:, total : total + 1] / diag


def sum_kernel(*refs):
    *part_refs, out_ref = refs
    out_ref[...] = tree_sum([ref[...] for ref in part_refs[::-1]])


def partners(value, axis, masks):
    size = lax.axis_size(axis)
    parts = []
    for mask in masks[::-1]:
        parts.append(lax.ppermute(value, axis, [(i, i ^ mask) for i in range(size)]))
    return parts + [value]


def sum_over(value, axis, masks):
    return pl.pallas_call(
        sum_kernel,
        out_shape=jax.ShapeDtypeStruct(value.shape, F32),
        compiler_params=pltpu.CompilerParams(vmem_limit_bytes=VMEM_LIMIT),
        name="sum_over",
    )(*partners(value, axis, masks))


def rounds(size):
    masks = [1, size - 2] + [1 << bit for bit in range(1, size.bit_length() - 2)]
    return [
        [a, b, a ^ b] if b else [a] for a, b in zip(masks[::2], masks[1::2] + [0] * (len(masks) % 2))
    ]


def solve_kernel(grams, *refs):
    gram_refs, (*block_refs, weights_ref, update_ref, held) = refs[:grams], refs[grams:]
    block_refs = in_place(block_refs)
    mats, share, d = update_ref.shape
    local = weights_ref.shape[1]
    packed = tree_sum([ref[...] for ref in gram_refs[::-1]])
    half, packed_width = packed.shape
    total = 2 * half
    width = (total // LANES + 1) * LANES
    turned = jnp.swapaxes(packed[:, half:total], 0, 1)
    energy = [packed[:, 3 * half + i : 3 * half + i + 1] for i in range(2)]
    energy = [jnp.broadcast_to(e, (half, width - total)) for e in energy]
    upper = jnp.concatenate([packed[:, :half], turned, energy[0]], axis=1)
    lower = jnp.concatenate([packed[:, half : 3 * half], energy[1]], axis=1)
    raw = jnp.concatenate([upper, lower], axis=0)
    row = iota((total, width), 0)
    lane = iota((total, width), 1)
    inside = lane < total
    scale = F32(1.0 / total)
    row_mean = jnp.sum(jnp.where(inside, raw, F32(0.0)), axis=1, keepdims=True) * scale
    col_mean = jnp.sum(raw, axis=0, keepdims=True) * scale
    mean = jnp.sum(row_mean, axis=0, keepdims=True) * scale
    gram = (raw - col_mean - row_mean + mean) * scale
    eps = (raw - col_mean) * F32(1.0 / total**0.5)
    on_diag = row == lane
    trace = jnp.sum(
        jnp.sum(jnp.where(on_diag, gram, F32(0.0)), axis=1, keepdims=True), axis=0, keepdims=True
    )
    shift = F32(shift_ratio) * trace * scale
    system = jnp.where(inside, gram + jnp.where(on_diag, shift, F32(0.0)), eps)
    weights = eliminate(system, total)
    me = lax.axis_index("samp")
    own = jnp.where(row - me * local == lane, weights, F32(0.0))
    weights_ref[...] = jnp.sum(own, axis=0, keepdims=True)[:, :local]
    coeffs = weights - jnp.sum(weights, axis=0, keepdims=True) * scale
    held[...] = jnp.broadcast_to(coeffs, (total, d))
    acc = jnp.zeros((mats * share, d), F32)
    for k, block_ref in enumerate(block_refs):
        mine = held[pl.ds(pl.multiple_of((me ^ k) * local, local), local)]
        for s in range(local):
            acc = acc + mine[s : s + 1] * block_ref[s].astype(F32)
    for m in range(mats):
        update_ref[m] = acc[m * share : (m + 1) * share]


def solve_and_project(grams, blocks, mats):
    local, count, d = blocks[0].shape
    total = local * len(blocks)
    return pl.pallas_call(
        functools.partial(solve_kernel, len(grams)),
        out_shape=(
            jax.ShapeDtypeStruct((1, local), F32),
            jax.ShapeDtypeStruct((mats, count // mats, d), F32),
        ),
        scratch_shapes=[pltpu.VMEM((total, d), F32)],
        compiler_params=pltpu.CompilerParams(vmem_limit_bytes=VMEM_LIMIT),
        name="solve_and_project",
    )(*grams, *in_turn(blocks))


def body(spins, activations, cotangents, offdiag):
    local, mats = activations.shape[:2]
    owners = lax.axis_size("samp")
    total = local * owners
    blocks = list(jac_rows(activations, cotangents, owners))
    for k in turns(owners)[:-1]:
        blocks[k] = lax.ppermute(blocks[k], "samp", [(i, i ^ k) for i in range(owners)])
    partial = gram_partial(blocks, packed_energy(spins, offdiag, total))
    gram = sum_over(partial, "layer", list(range(1, lax.axis_size("layer"))))
    *early, last = rounds(owners)
    for masks in early:
        gram = sum_over(gram, "samp", masks)
    grams = partners(gram, "samp", last)
    weights, update = solve_and_project(grams, blocks, mats)
    return weights.reshape(local), update


def solution(mesh):
    placed = (
        P("samp", None),
        P("samp", "layer", None, None),
        P("samp", "layer", None, None),
        P("samp"),
    )
    return jax.shard_map(
        body,
        mesh=mesh,
        in_specs=placed,
        out_specs=(P("samp"), P("layer", "samp", None)),
        check_vma=False,
    )
```

```python
import functools

import jax
import jax.numpy as jnp
from jax import lax
from jax.experimental import pallas as pl
from jax.experimental.pallas import tpu as pltpu
from jax.sharding import PartitionSpec as P

SIDE = 16
LANES = 128
CHUNK = 16
PIVOTS = 8
VMEM_LIMIT = 24 * 2**20
JAC_VMEM_LIMIT = 52 * 2**20
shift_ratio = 0.1
F32 = jnp.float32
BF16 = jnp.bfloat16


def iota(shape, dim):
    return lax.broadcasted_iota(jnp.int32, shape, dim)


def turns(owners):
    far, near = list(range(owners // 2, owners)), list(range(owners // 2 - 1, 0, -1))
    order = [far.pop(0)]
    while far or near:
        order += far[:1] + near[:1]
        far, near = far[1:], near[1:]
    return order + [0]


def in_turn(blocks):
    return [blocks[k] for k in turns(len(blocks))]


def in_place(blocks):
    order = turns(len(blocks))
    return [blocks[order.index(k)] for k in range(len(blocks))]


def jac_kernel(act_hbm, cot_hbm, *refs):
    *out_refs, act_buf, cot_buf, held, sems = refs
    samples, mats = act_buf.shape[:2]
    share = out_refs[0].shape[1] // mats
    me = lax.axis_index("samp")
    copies = []
    for s in range(samples):
        copies.append(
            (
                pltpu.make_async_copy(act_hbm.at[s], act_buf.at[s], sems.at[0, s]),
                pltpu.make_async_copy(cot_hbm.at[s], cot_buf.at[s], sems.at[1, s]),
            )
        )
    for pair in copies:
        for copy in pair:
            copy.start()

    def share_out(samples):
        for k, out_ref in enumerate(out_refs):
            owned = pl.ds(pl.multiple_of((me ^ k) * share, share), share)
            for s in samples:
                rows = [held[s, m, owned] for m in range(mats)]
                out_ref[s] = jnp.concatenate(rows, axis=0).astype(BF16)

    group = 2
    for first in range(0, samples, group):
        here = range(first, first + group)
        for s in here:
            for copy in copies[s]:
                copy.wait()
        for s in here:
            for m in range(mats):
                held[s, m] = lax.dot_general(
                    act_buf[s, m],
                    cot_buf[s, m],
                    (((0,), (0,)), ((), ())),
                    preferred_element_type=F32,
                ).astype(held.dtype)
        if first > 0:
            share_out(range(first - group, first))
    share_out(range(samples - group, samples))


def jac_rows(activations, cotangents, owners):
    samples, mats, sites, d = activations.shape
    rows = mats * d // owners
    hbm = pl.BlockSpec(memory_space=pltpu.HBM)
    return pl.pallas_call(
        jac_kernel,
        in_specs=[hbm, hbm],
        out_shape=[jax.ShapeDtypeStruct((samples, rows, d), BF16)] * owners,
        scratch_shapes=[
            pltpu.VMEM((samples, mats, sites, d), BF16),
            pltpu.VMEM((samples, mats, sites, d), BF16),
            pltpu.VMEM((samples, mats, d, d), BF16 if d // owners % CHUNK == 0 else F32),
            pltpu.SemaphoreType.DMA((2, samples)),
        ],
        compiler_params=pltpu.CompilerParams(vmem_limit_bytes=JAC_VMEM_LIMIT),
        cost_estimate=pl.CostEstimate(
            flops=2 * samples * mats * sites * d * d,
            bytes_accessed=6 * samples * mats * sites * d,
            transcendentals=0,
        ),
        name="jac_rows",
    )(activations, cotangents)


def packed_shape(total):
    half = total // 2
    return half, -(-(3 * half + 2) // LANES) * LANES


def energy_kernel(total, spins_ref, offdiag_ref, out_ref):
    shape = out_ref.shape
    local = spins_ref.shape[0]
    sites = SIDE * SIDE
    z = (2 * spins_ref[...] - 1).astype(F32)
    column = iota((local, sites), 1) % SIDE
    right = jnp.where(
        column == SIDE - 1, pltpu.roll(z, SIDE - 1, 1), pltpu.roll(z, sites - 1, 1)
    )
    below = pltpu.roll(z, sites - SIDE, 1)
    energy = offdiag_ref[...] + jnp.sum(z * (right + below), axis=1, keepdims=True)
    half = total // 2
    first = lax.axis_index("samp") * local
    lower = first // half
    first = first - lower * half
    spread = jnp.concatenate([energy] * (half // local), axis=0)
    row = iota(shape, 0)
    here = (row >= first) & (row < first + local) & (iota(shape, 1) == 3 * half + lower)
    here = here & (lax.axis_index("layer") == 0)
    out_ref[...] = jnp.where(here, spread, F32(0.0))


def packed_energy(spins, offdiag, total):
    return pl.pallas_call(
        functools.partial(energy_kernel, total),
        out_shape=jax.ShapeDtypeStruct(packed_shape(total), F32),
        compiler_params=pltpu.CompilerParams(vmem_limit_bytes=VMEM_LIMIT),
        name="packed_energy",
    )(spins, offdiag[:, None])


def gram_kernel(*refs):
    *block_refs, energy_ref, out_ref, flat, whole = refs
    block_refs = in_place(block_refs)
    local, count, d = block_refs[0].shape
    total = local * len(block_refs)
    joined = CHUNK // local
    me = lax.axis_index("samp")
    block = CHUNK * CHUNK
    dest = iota((block, block), 0)
    sample = dest % CHUNK
    sample = (sample // local ^ me % joined) * local + sample % local
    source = sample * CHUNK + dest // CHUNK
    swap = (iota((block, block), 1) == source).astype(F32).astype(BF16)
    for row in range(0, count, CHUNK):
        for j in range(len(block_refs) // joined):
            pieces = [ref[:, row : row + CHUNK] for ref in block_refs[j * joined : (j + 1) * joined]]
            piece = jnp.concatenate(pieces, axis=0).reshape(block, d)
            turned = jnp.dot(swap, piece, preferred_element_type=F32).astype(BF16)
            place = pl.ds(pl.multiple_of((me // joined ^ j) * CHUNK, CHUNK), CHUNK)
            for r in range(CHUNK):
                flat[row + r, place] = turned[r * CHUNK : (r + 1) * CHUNK]
    lined = jnp.concatenate([flat[r] for r in range(count)], axis=1)
    gram = lax.dot_general(lined, lined, (((1,), (1,)), ((), ())), preferred_element_type=F32)
    whole[...] = jnp.zeros_like(whole)
    whole[:, :total] += gram
    half, width = out_ref.shape
    lane = iota((half, width), 1)
    lower = pltpu.roll(whole[half:], half, 1)
    packed = jnp.where(lane < 3 * half, lower, energy_ref[...])
    out_ref[...] = jnp.where(lane < half, whole[:half], packed)


def gram_partial(blocks, energies):
    local, count, d = blocks[0].shape
    total = local * len(blocks)
    return pl.pallas_call(
        gram_kernel,
        out_shape=jax.ShapeDtypeStruct(packed_shape(total), F32),
        scratch_shapes=[
            pltpu.VMEM((count, total, d), BF16),
            pltpu.VMEM((total, packed_shape(total)[1]), F32),
        ],
        compiler_params=pltpu.CompilerParams(vmem_limit_bytes=VMEM_LIMIT),
        cost_estimate=pl.CostEstimate(
            flops=2 * total * total * count * d,
            bytes_accessed=2 * total * count * d,
            transcendentals=0,
        ),
        name="gram_partial",
    )(*in_turn(blocks), energies)


def tree_sum(parts):
    while len(parts) > 1:
        odd = parts[len(parts) // 2 * 2 :]
        parts = [a + b for a, b in zip(parts[::2], parts[1::2])] + odd
    return parts[0]


def pivot_rows(rows, entries):
    count = len(rows)
    rows = list(rows)
    p = [[entries[min(i, l)][max(i, l)] for l in range(count)] for i in range(count)]
    uppers = {}
    for j in range(0, count, 2):
        a, b, c = p[j][j], p[j][j + 1], p[j + 1][j + 1]
        inverse = F32(1.0) / (a * c - b * b)

        def scaled(x, y):
            return (c * x - b * y) * inverse, (a * y - b * x) * inverse

        first, second = rows[j], rows[j + 1]
        rows[j], rows[j + 1] = scaled(first, second)
        later = range(j + 2, count)
        for l in later:
            uppers[j, l], uppers[j + 1, l] = scaled(p[j][l], p[j + 1][l])
        for i in later:
            rows[i] = rows[i] - (p[j][i] * rows[j] + p[j + 1][i] * rows[j + 1])
            for l in range(i, count):
                change = p[j][i] * uppers[j, l] + p[j + 1][i] * uppers[j + 1, l]
                p[i][l] = p[l][i] = p[i][l] - change
    for j in range(count - 4, -1, -2):
        for i in (j, j + 1):
            rows[i] = rows[i] - tree_sum([uppers[i, l] * rows[l] for l in range(j + 2, count)])
    return rows


def eliminate(matrix, total):
    width = matrix.shape[1]
    if total <= 64:
        blocks = [matrix[i : i + PIVOTS] for i in range(0, total, PIVOTS)]
        sub = iota((PIVOTS, width), 0)
        for b in range(len(blocks)):
            spread = [
                [
                    jnp.broadcast_to(block[:, b * PIVOTS + j : b * PIVOTS + j + 1], (PIVOTS, width))
                    for block in blocks
                ]
                for j in range(PIVOTS)
            ]

            def line(value, i):
                return jnp.broadcast_to(value[i : i + 1], (PIVOTS, width))

            entries = [
                [line(spread[l][b], i) if l >= i else None for l in range(PIVOTS)]
                for i in range(PIVOTS)
            ]
            rows = pivot_rows([line(blocks[b], i) for i in range(PIVOTS)], entries)
            for i in range(len(blocks)):
                if i != b:
                    terms = [spread[j][i] * rows[j] for j in range(PIVOTS)]
                    blocks[i] = blocks[i] - tree_sum(terms)
            solved = rows[0]
            for j in range(1, PIVOTS):
                solved = jnp.where(sub == j, rows[j], solved)
            blocks[b] = solved
        return jnp.concatenate([block[:, total : total + 1] for block in blocks], axis=0)
    row = iota(matrix.shape, 0)
    lane = iota(matrix.shape, 1)

    def one(k, held):
        column = jnp.sum(jnp.where(lane == k, held, F32(0.0)), axis=1, keepdims=True)
        pivot_row = jnp.sum(jnp.where(row == k, held, F32(0.0)), axis=0, keepdims=True)
        here = lane[:1] == k
        pivot = jnp.sum(jnp.where(here, pivot_row, F32(0.0)), axis=1, keepdims=True)
        scaled = pivot_row * (F32(1.0) / pivot)
        return held - jnp.where(row == k, F32(0.0), column) * scaled

    matrix = lax.fori_loop(0, total, one, matrix)
    diag = jnp.sum(jnp.where(row == lane, matrix, F32(0.0)), axis=1, keepdims=True)
    return matrix[:, total : total + 1] / diag


def sum_kernel(*refs):
    *part_refs, out_ref = refs
    out_ref[...] = tree_sum([ref[...] for ref in part_refs[::-1]])


def partners(value, axis, masks):
    size = lax.axis_size(axis)
    parts = []
    for mask in masks[::-1]:
        parts.append(lax.ppermute(value, axis, [(i, i ^ mask) for i in range(size)]))
    return parts + [value]


def sum_over(value, axis, masks):
    return pl.pallas_call(
        sum_kernel,
        out_shape=jax.ShapeDtypeStruct(value.shape, F32),
        compiler_params=pltpu.CompilerParams(vmem_limit_bytes=VMEM_LIMIT),
        name="sum_over",
    )(*partners(value, axis, masks))


def rounds(size):
    masks = [1, size - 2] + [1 << bit for bit in range(1, size.bit_length() - 2)]
    return [
        [a, b, a ^ b] if b else [a] for a, b in zip(masks[::2], masks[1::2] + [0] * (len(masks) % 2))
    ]


def solve_kernel(grams, *refs):
    gram_refs, (*block_refs, weights_ref, update_ref, held) = refs[:grams], refs[grams:]
    block_refs = in_place(block_refs)
    mats, share, d = update_ref.shape
    local = weights_ref.shape[1]
    packed = tree_sum([gram_refs[0][i] for i in range(gram_refs[0].shape[0])])
    half, packed_width = packed.shape
    total = 2 * half
    width = (total // LANES + 1) * LANES
    turned = jnp.swapaxes(packed[:, half:total], 0, 1)
    energy = [packed[:, 3 * half + i : 3 * half + i + 1] for i in range(2)]
    energy = [jnp.broadcast_to(e, (half, width - total)) for e in energy]
    upper = jnp.concatenate([packed[:, :half], turned, energy[0]], axis=1)
    lower = jnp.concatenate([packed[:, half : 3 * half], energy[1]], axis=1)
    raw = jnp.concatenate([upper, lower], axis=0)
    row = iota((total, width), 0)
    lane = iota((total, width), 1)
    inside = lane < total
    scale = F32(1.0 / total)
    row_mean = jnp.sum(jnp.where(inside, raw, F32(0.0)), axis=1, keepdims=True) * scale
    col_mean = jnp.sum(raw, axis=0, keepdims=True) * scale
    mean = jnp.sum(row_mean, axis=0, keepdims=True) * scale
    gram = (raw - col_mean - row_mean + mean) * scale
    eps = (raw - col_mean) * F32(1.0 / total**0.5)
    on_diag = row == lane
    trace = jnp.sum(
        jnp.sum(jnp.where(on_diag, gram, F32(0.0)), axis=1, keepdims=True), axis=0, keepdims=True
    )
    shift = F32(shift_ratio) * trace * scale
    system = jnp.where(inside, gram + jnp.where(on_diag, shift, F32(0.0)), eps)
    weights = eliminate(system, total)
    me = lax.axis_index("samp")
    own = jnp.where(row - me * local == lane, weights, F32(0.0))
    weights_ref[...] = jnp.sum(own, axis=0, keepdims=True)[:, :local]
    coeffs = weights - jnp.sum(weights, axis=0, keepdims=True) * scale
    held[...] = jnp.broadcast_to(coeffs, (total, d))
    acc = jnp.zeros((mats * share, d), F32)
    for k, block_ref in enumerate(block_refs):
        mine = held[pl.ds(pl.multiple_of((me ^ k) * local, local), local)]
        for s in range(local):
            acc = acc + mine[s : s + 1] * block_ref[s].astype(F32)
    for m in range(mats):
        update_ref[m] = acc[m * share : (m + 1) * share]


def solve_and_project(grams, blocks, mats):
    local, count, d = blocks[0].shape
    total = local * len(blocks)
    return pl.pallas_call(
        functools.partial(solve_kernel, len(grams)),
        out_shape=(
            jax.ShapeDtypeStruct((1, local), F32),
            jax.ShapeDtypeStruct((mats, count // mats, d), F32),
        ),
        scratch_shapes=[pltpu.VMEM((total, d), F32)],
        compiler_params=pltpu.CompilerParams(vmem_limit_bytes=VMEM_LIMIT),
        name="solve_and_project",
    )(*grams, *in_turn(blocks))


def body(spins, activations, cotangents, offdiag):
    local, mats = activations.shape[:2]
    owners = lax.axis_size("samp")
    total = local * owners
    blocks = list(jac_rows(activations, cotangents, owners))
    for k in turns(owners)[:-1]:
        blocks[k] = lax.ppermute(blocks[k], "samp", [(i, i ^ k) for i in range(owners)])
    partial = gram_partial(blocks, packed_energy(spins, offdiag, total))
    gram = sum_over(partial, "layer", list(range(1, lax.axis_size("layer"))))
    gathered = lax.all_gather(gram, "samp", axis=0)
    grams = [gathered]
    weights, update = solve_and_project(grams, blocks, mats)
    return weights.reshape(local), update


def solution(mesh):
    placed = (
        P("samp", None),
        P("samp", "layer", None, None),
        P("samp", "layer", None, None),
        P("samp"),
    )
    return jax.shard_map(
        body,
        mesh=mesh,
        in_specs=placed,
        out_specs=(P("samp"), P("layer", "samp", None)),
        check_vma=False,
    )
```

```python
import functools

import jax
import jax.numpy as jnp
from jax import lax
from jax.experimental import pallas as pl
from jax.experimental.pallas import tpu as pltpu
from jax.sharding import PartitionSpec as P

SIDE = 16
LANES = 128
CHUNK = 16
PIVOTS = 8
VMEM_LIMIT = 24 * 2**20
JAC_VMEM_LIMIT = 52 * 2**20
shift_ratio = 0.1
F32 = jnp.float32
BF16 = jnp.bfloat16


def iota(shape, dim):
    return lax.broadcasted_iota(jnp.int32, shape, dim)


def turns(owners, split):
    far, near = list(range(owners // 2, owners)), list(range(owners // 2 - 1, 0, -1))
    cut = split_partners(owners, split)
    order = [(k, part) for part in range(split) for k in cut]
    far = [k for k in far if k not in cut]
    while far or near:
        order += [(k, 0) for k in near[:1] + far[:1]]
        far, near = far[1:], near[1:]
    return order + [(0, 0)]


def split_partners(owners, split):
    return [owners // 2, owners // 2 + 1] if split > 1 else []


def in_turn(blocks, split):
    return [blocks[k][part] for k, part in turns(len(blocks), split)]


def in_place(refs, owners):
    split = 1 + (len(refs) > owners)
    blocks = [[] for _ in range(owners)]
    for (k, _), ref in zip(turns(owners, split), refs):
        blocks[k].append(ref)
    return blocks


def jac_kernel(first_mat, joined, act_hbm, cot_hbm, *refs):
    before, refs = refs[: len(joined)], refs[len(joined) :]
    *out_refs, act_buf, cot_buf, held, sems = refs
    samples, mats, _, d = held.shape
    share = d // len(out_refs)
    me = lax.axis_index("samp")
    copies = []
    for s in range(samples):
        here = (s, pl.ds(first_mat, mats))
        copies.append(
            (
                pltpu.make_async_copy(act_hbm.at[here], act_buf.at[s], sems.at[0, s]),
                pltpu.make_async_copy(cot_hbm.at[here], cot_buf.at[s], sems.at[1, s]),
            )
        )
    for pair in copies:
        for copy in pair:
            copy.start()
    for k, ref in zip(joined, before):
        out_refs[k][:, : ref.shape[1]] = ref[...]

    def share_out(samples):
        for k, out_ref in enumerate(out_refs):
            owned = pl.ds(pl.multiple_of((me ^ k) * share, share), share)
            for s in samples:
                rows = [held[s, m, owned] for m in range(mats)]
                rows = jnp.concatenate(rows, axis=0).astype(BF16)
                out_ref[s, out_ref.shape[1] - mats * share :] = rows

    group = 2
    for first in range(0, samples, group):
        here = range(first, first + group)
        for s in here:
            for copy in copies[s]:
                copy.wait()
        for s in here:
            for m in range(mats):
                held[s, m] = lax.dot_general(
                    act_buf[s, m],
                    cot_buf[s, m],
                    (((0,), (0,)), ((), ())),
                    preferred_element_type=F32,
                ).astype(held.dtype)
        if first > 0:
            share_out(range(first - group, first))
    share_out(range(samples - group, samples))


def jac_rows(activations, cotangents, owners, part, split, before=()):
    samples, mats, sites, d = activations.shape
    mats //= split
    rows = mats * d // owners
    joined = [k for k, block in enumerate(before) if block is not None]
    out_rows = [rows + (before[k].shape[1] if k in joined else 0) for k in range(owners)]
    hbm = pl.BlockSpec(memory_space=pltpu.HBM)
    vmem = pl.BlockSpec(memory_space=pltpu.VMEM)
    return pl.pallas_call(
        functools.partial(jac_kernel, part * mats, joined),
        in_specs=[hbm, hbm] + [vmem] * len(joined),
        out_shape=[jax.ShapeDtypeStruct((samples, count, d), BF16) for count in out_rows],
        scratch_shapes=[
            pltpu.VMEM((samples, mats, sites, d), BF16),
            pltpu.VMEM((samples, mats, sites, d), BF16),
            pltpu.VMEM((samples, mats, d, d), BF16 if d // owners % CHUNK == 0 else F32),
            pltpu.SemaphoreType.DMA((2, samples)),
        ],
        compiler_params=pltpu.CompilerParams(vmem_limit_bytes=JAC_VMEM_LIMIT),
        cost_estimate=pl.CostEstimate(
            flops=2 * samples * mats * sites * d * d,
            bytes_accessed=6 * samples * mats * sites * d,
            transcendentals=0,
        ),
        name="jac_rows",
    )(activations, cotangents, *[before[k] for k in joined])


def jac_blocks(activations, cotangents, owners):
    mats, d = activations.shape[1], activations.shape[3]
    split = mats if mats == 2 and d // owners % CHUNK == 0 else 1
    blocks = [[block] for block in jac_rows(activations, cotangents, owners, 0, split)]
    if split > 1:
        cut = split_partners(owners, split)
        before = [None if k in cut else block[0] for k, block in enumerate(blocks)]
        later = jac_rows(activations, cotangents, owners, 1, split, before)
        blocks = [b + [new] if k in cut else [new] for k, (b, new) in enumerate(zip(blocks, later))]
    return blocks, split


def packed_shape(total):
    half = total // 2
    return half, -(-(3 * half + 2) // LANES) * LANES


def energy_kernel(total, spins_ref, offdiag_ref, out_ref):
    shape = out_ref.shape
    local = spins_ref.shape[0]
    sites = SIDE * SIDE
    z = (2 * spins_ref[...] - 1).astype(F32)
    column = iota((local, sites), 1) % SIDE
    right = jnp.where(
        column == SIDE - 1, pltpu.roll(z, SIDE - 1, 1), pltpu.roll(z, sites - 1, 1)
    )
    below = pltpu.roll(z, sites - SIDE, 1)
    energy = offdiag_ref[...] + jnp.sum(z * (right + below), axis=1, keepdims=True)
    half = total // 2
    first = lax.axis_index("samp") * local
    lower = first // half
    first = first - lower * half
    spread = jnp.concatenate([energy] * (half // local), axis=0)
    row = iota(shape, 0)
    here = (row >= first) & (row < first + local) & (iota(shape, 1) == 3 * half + lower)
    here = here & (lax.axis_index("layer") == 0)
    out_ref[...] = jnp.where(here, spread, F32(0.0))


def packed_energy(spins, offdiag, total):
    return pl.pallas_call(
        functools.partial(energy_kernel, total),
        out_shape=jax.ShapeDtypeStruct(packed_shape(total), F32),
        compiler_params=pltpu.CompilerParams(vmem_limit_bytes=VMEM_LIMIT),
        name="packed_energy",
    )(spins, offdiag[:, None])


def rows_of(parts, row, rows):
    for ref in parts:
        if row < ref.shape[1]:
            return ref[:, row : row + rows]
        row -= ref.shape[1]


def gram_kernel(owners, *refs):
    *block_refs, energy_ref, out_ref, flat, whole = refs
    blocks = in_place(block_refs, owners)
    local, count, d = blocks[0][0].shape
    total = local * owners
    joined = CHUNK // local
    me = lax.axis_index("samp")
    block = CHUNK * CHUNK
    dest = iota((block, block), 0)
    sample = dest % CHUNK
    sample = (sample // local ^ me % joined) * local + sample % local
    source = sample * CHUNK + dest // CHUNK
    swap = (iota((block, block), 1) == source).astype(F32).astype(BF16)
    for row in range(0, count, CHUNK):
        for j in range(owners // joined):
            pieces = [rows_of(p, row, CHUNK) for p in blocks[j * joined : (j + 1) * joined]]
            piece = jnp.concatenate(pieces, axis=0).reshape(block, d)
            turned = jnp.dot(swap, piece, preferred_element_type=F32).astype(BF16)
            place = pl.ds(pl.multiple_of((me // joined ^ j) * CHUNK, CHUNK), CHUNK)
            for r in range(CHUNK):
                flat[row + r, place] = turned[r * CHUNK : (r + 1) * CHUNK]
    lined = jnp.concatenate([flat[r] for r in range(count)], axis=1)
    gram = lax.dot_general(lined, lined, (((1,), (1,)), ((), ())), preferred_element_type=F32)
    whole[...] = jnp.zeros_like(whole)
    whole[:, :total] += gram
    half, width = out_ref.shape
    lane = iota((half, width), 1)
    lower = pltpu.roll(whole[half:], half, 1)
    packed = jnp.where(lane < 3 * half, lower, energy_ref[...])
    out_ref[...] = jnp.where(lane < half, whole[:half], packed)


def gram_partial(blocks, split, energies):
    local, count, d = blocks[0][0].shape
    total = local * len(blocks)
    return pl.pallas_call(
        functools.partial(gram_kernel, len(blocks)),
        out_shape=jax.ShapeDtypeStruct(packed_shape(total), F32),
        scratch_shapes=[
            pltpu.VMEM((count, total, d), BF16),
            pltpu.VMEM((total, packed_shape(total)[1]), F32),
        ],
        compiler_params=pltpu.CompilerParams(vmem_limit_bytes=VMEM_LIMIT),
        cost_estimate=pl.CostEstimate(
            flops=2 * total * total * count * d,
            bytes_accessed=2 * total * count * d,
            transcendentals=0,
        ),
        name="gram_partial",
    )(*in_turn(blocks, split), energies)


def tree_sum(parts):
    while len(parts) > 1:
        odd = parts[len(parts) // 2 * 2 :]
        parts = [a + b for a, b in zip(parts[::2], parts[1::2])] + odd
    return parts[0]


def pivot_rows(rows, entries):
    count = len(rows)
    rows = list(rows)
    p = [[entries[min(i, l)][max(i, l)] for l in range(count)] for i in range(count)]
    uppers = {}
    for j in range(0, count, 2):
        a, b, c = p[j][j], p[j][j + 1], p[j + 1][j + 1]
        inverse = F32(1.0) / (a * c - b * b)

        def scaled(x, y):
            return (c * x - b * y) * inverse, (a * y - b * x) * inverse

        first, second = rows[j], rows[j + 1]
        rows[j], rows[j + 1] = scaled(first, second)
        later = range(j + 2, count)
        for l in later:
            uppers[j, l], uppers[j + 1, l] = scaled(p[j][l], p[j + 1][l])
        for i in later:
            rows[i] = rows[i] - (p[j][i] * rows[j] + p[j + 1][i] * rows[j + 1])
            for l in range(i, count):
                change = p[j][i] * uppers[j, l] + p[j + 1][i] * uppers[j + 1, l]
                p[i][l] = p[l][i] = p[i][l] - change
    for j in range(count - 4, -1, -2):
        for i in (j, j + 1):
            rows[i] = rows[i] - tree_sum([uppers[i, l] * rows[l] for l in range(j + 2, count)])
    return rows


def eliminate(matrix, total):
    width = matrix.shape[1]
    if total <= 64:
        blocks = [matrix[i : i + PIVOTS] for i in range(0, total, PIVOTS)]
        sub = iota((PIVOTS, width), 0)
        for b in range(len(blocks)):
            spread = [
                [
                    jnp.broadcast_to(block[:, b * PIVOTS + j : b * PIVOTS + j + 1], (PIVOTS, width))
                    for block in blocks
                ]
                for j in range(PIVOTS)
            ]

            def line(value, i):
                return jnp.broadcast_to(value[i : i + 1], (PIVOTS, width))

            entries = [
                [line(spread[l][b], i) if l >= i else None for l in range(PIVOTS)]
                for i in range(PIVOTS)
            ]
            rows = pivot_rows([line(blocks[b], i) for i in range(PIVOTS)], entries)
            for i in range(len(blocks)):
                if i != b:
                    terms = [spread[j][i] * rows[j] for j in range(PIVOTS)]
                    blocks[i] = blocks[i] - tree_sum(terms)
            solved = rows[0]
            for j in range(1, PIVOTS):
                solved = jnp.where(sub == j, rows[j], solved)
            blocks[b] = solved
        return jnp.concatenate([block[:, total : total + 1] for block in blocks], axis=0)
    row = iota(matrix.shape, 0)
    lane = iota(matrix.shape, 1)

    def one(k, held):
        column = jnp.sum(jnp.where(lane == k, held, F32(0.0)), axis=1, keepdims=True)
        pivot_row = jnp.sum(jnp.where(row == k, held, F32(0.0)), axis=0, keepdims=True)
        here = lane[:1] == k
        pivot = jnp.sum(jnp.where(here, pivot_row, F32(0.0)), axis=1, keepdims=True)
        scaled = pivot_row * (F32(1.0) / pivot)
        return held - jnp.where(row == k, F32(0.0), column) * scaled

    matrix = lax.fori_loop(0, total, one, matrix)
    diag = jnp.sum(jnp.where(row == lane, matrix, F32(0.0)), axis=1, keepdims=True)
    return matrix[:, total : total + 1] / diag


def sum_kernel(*refs):
    *part_refs, out_ref = refs
    out_ref[...] = tree_sum([ref[...] for ref in part_refs[::-1]])


def partners(value, axis, masks):
    size = lax.axis_size(axis)
    parts = []
    for mask in masks[::-1]:
        parts.append(lax.ppermute(value, axis, [(i, i ^ mask) for i in range(size)]))
    return parts + [value]


def sum_over(value, axis, masks):
    return pl.pallas_call(
        sum_kernel,
        out_shape=jax.ShapeDtypeStruct(value.shape, F32),
        compiler_params=pltpu.CompilerParams(vmem_limit_bytes=VMEM_LIMIT),
        name="sum_over",
    )(*partners(value, axis, masks))


def rounds(size):
    masks = [1, size - 2] + [1 << bit for bit in range(1, size.bit_length() - 2)]
    return [
        [a, b, a ^ b] if b else [a] for a, b in zip(masks[::2], masks[1::2] + [0] * (len(masks) % 2))
    ]


def solve_kernel(grams, owners, *refs):
    gram_refs, (*block_refs, weights_ref, update_ref, held) = refs[:grams], refs[grams:]
    blocks = in_place(block_refs, owners)
    mats, share, d = update_ref.shape
    local = weights_ref.shape[1]
    packed = tree_sum([ref[...] for ref in gram_refs[::-1]])
    half, packed_width = packed.shape
    total = 2 * half
    width = (total // LANES + 1) * LANES
    turned = jnp.swapaxes(packed[:, half:total], 0, 1)
    energy = [packed[:, 3 * half + i : 3 * half + i + 1] for i in range(2)]
    energy = [jnp.broadcast_to(e, (half, width - total)) for e in energy]
    upper = jnp.concatenate([packed[:, :half], turned, energy[0]], axis=1)
    lower = jnp.concatenate([packed[:, half : 3 * half], energy[1]], axis=1)
    raw = jnp.concatenate([upper, lower], axis=0)
    row = iota((total, width), 0)
    lane = iota((total, width), 1)
    inside = lane < total
    scale = F32(1.0 / total)
    row_mean = jnp.sum(jnp.where(inside, raw, F32(0.0)), axis=1, keepdims=True) * scale
    col_mean = jnp.sum(raw, axis=0, keepdims=True) * scale
    mean = jnp.sum(row_mean, axis=0, keepdims=True) * scale
    gram = (raw - col_mean - row_mean + mean) * scale
    eps = (raw - col_mean) * F32(1.0 / total**0.5)
    on_diag = row == lane
    trace = jnp.sum(
        jnp.sum(jnp.where(on_diag, gram, F32(0.0)), axis=1, keepdims=True), axis=0, keepdims=True
    )
    shift = F32(shift_ratio) * trace * scale
    system = jnp.where(inside, gram + jnp.where(on_diag, shift, F32(0.0)), eps)
    weights = eliminate(system, total)
    me = lax.axis_index("samp")
    own = jnp.where(row - me * local == lane, weights, F32(0.0))
    weights_ref[...] = jnp.sum(own, axis=0, keepdims=True)[:, :local]
    coeffs = weights - jnp.sum(weights, axis=0, keepdims=True) * scale
    held[...] = jnp.broadcast_to(coeffs, (total, d))
    acc = jnp.zeros((mats * share, d), F32)
    for k, parts in enumerate(blocks):
        mine = held[pl.ds(pl.multiple_of((me ^ k) * local, local), local)]
        for s in range(local):
            rows = jnp.concatenate([ref[s].astype(F32) for ref in parts], axis=0)
            acc = acc + mine[s : s + 1] * rows
    for m in range(mats):
        update_ref[m] = acc[m * share : (m + 1) * share]


def solve_and_project(grams, blocks, split, mats):
    local, count, d = blocks[0][0].shape
    total = local * len(blocks)
    return pl.pallas_call(
        functools.partial(solve_kernel, len(grams), len(blocks)),
        out_shape=(
            jax.ShapeDtypeStruct((1, local), F32),
            jax.ShapeDtypeStruct((mats, count // mats, d), F32),
        ),
        scratch_shapes=[pltpu.VMEM((total, d), F32)],
        compiler_params=pltpu.CompilerParams(vmem_limit_bytes=VMEM_LIMIT),
        name="solve_and_project",
    )(*grams, *in_turn(blocks, split))


def body(spins, activations, cotangents, offdiag):
    local, mats = activations.shape[:2]
    owners = lax.axis_size("samp")
    total = local * owners
    blocks, split = jac_blocks(activations, cotangents, owners)
    for k, part in turns(owners, split)[:-1]:
        perm = [(i, i ^ k) for i in range(owners)]
        blocks[k][part] = lax.ppermute(blocks[k][part], "samp", perm)
    partial = gram_partial(blocks, split, packed_energy(spins, offdiag, total))
    gram = sum_over(partial, "layer", list(range(1, lax.axis_size("layer"))))
    *early, last = rounds(owners)
    for masks in early:
        gram = sum_over(gram, "samp", masks)
    grams = partners(gram, "samp", last)
    weights, update = solve_and_project(grams, blocks, split, mats)
    return weights.reshape(local), update


def solution(mesh):
    placed = (
        P("samp", None),
        P("samp", "layer", None, None),
        P("samp", "layer", None, None),
        P("samp"),
    )
    return jax.shard_map(
        body,
        mesh=mesh,
        in_specs=placed,
        out_specs=(P("samp"), P("layer", "samp", None)),
        check_vma=False,
    )
```

```python
import functools

import jax
import jax.numpy as jnp
from jax import lax
from jax.experimental import pallas as pl
from jax.experimental.pallas import tpu as pltpu
from jax.sharding import PartitionSpec as P

SIDE = 16
LANES = 128
CHUNK = 16
PIVOTS = 8
VMEM_LIMIT = 24 * 2**20
JAC_VMEM_LIMIT = 52 * 2**20
shift_ratio = 0.1
F32 = jnp.float32
BF16 = jnp.bfloat16


def iota(shape, dim):
    return lax.broadcasted_iota(jnp.int32, shape, dim)


def turns(owners, split):
    far, near = list(range(owners // 2, owners)), list(range(owners // 2 - 1, 0, -1))
    cut = split_partners(owners, split)
    order = [(k, part) for part in range(split) for k in cut]
    far = [k for k in far if k not in cut]
    while far or near:
        order += [(k, 0) for k in near[:1] + far[:1]]
        far, near = far[1:], near[1:]
    return order + [(0, 0)]


def split_partners(owners, split):
    return [owners // 2, owners // 2 + 1] if split > 1 else []


def in_turn(blocks, split):
    return [blocks[k][part] for k, part in turns(len(blocks), split)]


def in_place(refs, owners):
    split = 1 + (len(refs) > owners)
    blocks = [[] for _ in range(owners)]
    for (k, _), ref in zip(turns(owners, split), refs):
        blocks[k].append(ref)
    return blocks


def jac_kernel(first_mat, joined, act_hbm, cot_hbm, *refs):
    before, refs = refs[: len(joined)], refs[len(joined) :]
    *out_refs, act_buf, cot_buf, held, sems = refs
    samples, mats, _, d = held.shape
    share = d // len(out_refs)
    me = lax.axis_index("samp")
    copies = []
    for s in range(samples):
        here = (s, pl.ds(first_mat, mats))
        copies.append(
            (
                pltpu.make_async_copy(act_hbm.at[here], act_buf.at[s], sems.at[0, s]),
                pltpu.make_async_copy(cot_hbm.at[here], cot_buf.at[s], sems.at[1, s]),
            )
        )
    for pair in copies:
        for copy in pair:
            copy.start()
    for k, ref in zip(joined, before):
        out_refs[k][:, : ref.shape[1]] = ref[...]

    def share_out(samples):
        for k, out_ref in enumerate(out_refs):
            owned = pl.ds(pl.multiple_of((me ^ k) * share, share), share)
            for s in samples:
                rows = [held[s, m, owned] for m in range(mats)]
                rows = jnp.concatenate(rows, axis=0).astype(BF16)
                out_ref[s, out_ref.shape[1] - mats * share :] = rows

    group = 2
    for first in range(0, samples, group):
        here = range(first, first + group)
        for s in here:
            for copy in copies[s]:
                copy.wait()
        for s in here:
            for m in range(mats):
                held[s, m] = lax.dot_general(
                    act_buf[s, m],
                    cot_buf[s, m],
                    (((0,), (0,)), ((), ())),
                    preferred_element_type=F32,
                ).astype(held.dtype)
        if first > 0:
            share_out(range(first - group, first))
    share_out(range(samples - group, samples))


def jac_rows(activations, cotangents, owners, part, split, before=()):
    samples, mats, sites, d = activations.shape
    mats //= split
    rows = mats * d // owners
    joined = [k for k, block in enumerate(before) if block is not None]
    out_rows = [rows + (before[k].shape[1] if k in joined else 0) for k in range(owners)]
    hbm = pl.BlockSpec(memory_space=pltpu.HBM)
    vmem = pl.BlockSpec(memory_space=pltpu.VMEM)
    return pl.pallas_call(
        functools.partial(jac_kernel, part * mats, joined),
        in_specs=[hbm, hbm] + [vmem] * len(joined),
        out_shape=[jax.ShapeDtypeStruct((samples, count, d), BF16) for count in out_rows],
        scratch_shapes=[
            pltpu.VMEM((samples, mats, sites, d), BF16),
            pltpu.VMEM((samples, mats, sites, d), BF16),
            pltpu.VMEM((samples, mats, d, d), BF16 if d // owners % CHUNK == 0 else F32),
            pltpu.SemaphoreType.DMA((2, samples)),
        ],
        compiler_params=pltpu.CompilerParams(vmem_limit_bytes=JAC_VMEM_LIMIT),
        cost_estimate=pl.CostEstimate(
            flops=2 * samples * mats * sites * d * d,
            bytes_accessed=6 * samples * mats * sites * d,
            transcendentals=0,
        ),
        name="jac_rows",
    )(activations, cotangents, *[before[k] for k in joined])


def jac_blocks(activations, cotangents, owners):
    mats, d = activations.shape[1], activations.shape[3]
    split = mats if mats == 2 and d // owners % CHUNK == 0 else 1
    blocks = [[block] for block in jac_rows(activations, cotangents, owners, 0, split)]
    if split > 1:
        cut = split_partners(owners, split)
        before = [None if k in cut else block[0] for k, block in enumerate(blocks)]
        later = jac_rows(activations, cotangents, owners, 1, split, before)
        blocks = [b + [new] if k in cut else [new] for k, (b, new) in enumerate(zip(blocks, later))]
    return blocks, split


def packed_shape(total):
    half = total // 2
    return half, -(-(3 * half + 2) // LANES) * LANES


def energy_kernel(total, spins_ref, offdiag_ref, out_ref):
    shape = out_ref.shape
    local = spins_ref.shape[0]
    sites = SIDE * SIDE
    z = (2 * spins_ref[...] - 1).astype(F32)
    column = iota((local, sites), 1) % SIDE
    right = jnp.where(
        column == SIDE - 1, pltpu.roll(z, SIDE - 1, 1), pltpu.roll(z, sites - 1, 1)
    )
    below = pltpu.roll(z, sites - SIDE, 1)
    energy = offdiag_ref[...] + jnp.sum(z * (right + below), axis=1, keepdims=True)
    half = total // 2
    first = lax.axis_index("samp") * local
    lower = first // half
    first = first - lower * half
    spread = jnp.concatenate([energy] * (half // local), axis=0)
    row = iota(shape, 0)
    here = (row >= first) & (row < first + local) & (iota(shape, 1) == 3 * half + lower)
    here = here & (lax.axis_index("layer") == 0)
    out_ref[...] = jnp.where(here, spread, F32(0.0))


def packed_energy(spins, offdiag, total):
    return pl.pallas_call(
        functools.partial(energy_kernel, total),
        out_shape=jax.ShapeDtypeStruct(packed_shape(total), F32),
        compiler_params=pltpu.CompilerParams(vmem_limit_bytes=VMEM_LIMIT),
        name="packed_energy",
    )(spins, offdiag[:, None])


def rows_of(parts, row, rows):
    for ref in parts:
        if row < ref.shape[1]:
            return ref[:, row : row + rows]
        row -= ref.shape[1]


def gram_kernel(owners, *refs):
    *block_refs, energy_ref, out_ref, flat, whole = refs
    blocks = in_place(block_refs, owners)
    local, count, d = blocks[0][0].shape
    total = local * owners
    joined = CHUNK // local
    me = lax.axis_index("samp")
    block = CHUNK * CHUNK
    dest = iota((block, block), 0)
    sample = dest % CHUNK
    sample = (sample // local ^ me % joined) * local + sample % local
    source = sample * CHUNK + dest // CHUNK
    swap = (iota((block, block), 1) == source).astype(F32).astype(BF16)
    for row in range(0, count, CHUNK):
        for j in range(owners // joined):
            pieces = [rows_of(p, row, CHUNK) for p in blocks[j * joined : (j + 1) * joined]]
            piece = jnp.concatenate(pieces, axis=0).reshape(block, d)
            turned = jnp.dot(swap, piece, preferred_element_type=F32).astype(BF16)
            place = pl.ds(pl.multiple_of((me // joined ^ j) * CHUNK, CHUNK), CHUNK)
            for r in range(CHUNK):
                flat[row + r, place] = turned[r * CHUNK : (r + 1) * CHUNK]
    lined = jnp.concatenate([flat[r] for r in range(count)], axis=1)
    gram = lax.dot_general(lined, lined, (((1,), (1,)), ((), ())), preferred_element_type=F32)
    whole[...] = jnp.zeros_like(whole)
    whole[:, :total] += gram
    half, width = out_ref.shape
    lane = iota((half, width), 1)
    lower = pltpu.roll(whole[half:], half, 1)
    packed = jnp.where(lane < 3 * half, lower, energy_ref[...])
    out_ref[...] = jnp.where(lane < half, whole[:half], packed)


def gram_partial(blocks, split, energies):
    local, count, d = blocks[0][0].shape
    total = local * len(blocks)
    return pl.pallas_call(
        functools.partial(gram_kernel, len(blocks)),
        out_shape=jax.ShapeDtypeStruct(packed_shape(total), F32),
        scratch_shapes=[
            pltpu.VMEM((count, total, d), BF16),
            pltpu.VMEM((total, packed_shape(total)[1]), F32),
        ],
        compiler_params=pltpu.CompilerParams(vmem_limit_bytes=VMEM_LIMIT),
        cost_estimate=pl.CostEstimate(
            flops=2 * total * total * count * d,
            bytes_accessed=2 * total * count * d,
            transcendentals=0,
        ),
        name="gram_partial",
    )(*in_turn(blocks, split), energies)


def tree_sum(parts):
    while len(parts) > 1:
        odd = parts[len(parts) // 2 * 2 :]
        parts = [a + b for a, b in zip(parts[::2], parts[1::2])] + odd
    return parts[0]


def pivot_rows(rows, entries):
    count = len(rows)
    rows = list(rows)
    p = [[entries[min(i, l)][max(i, l)] for l in range(count)] for i in range(count)]
    uppers = {}
    for j in range(0, count, 2):
        a, b, c = p[j][j], p[j][j + 1], p[j + 1][j + 1]
        inverse = F32(1.0) / (a * c - b * b)

        def scaled(x, y):
            return (c * x - b * y) * inverse, (a * y - b * x) * inverse

        first, second = rows[j], rows[j + 1]
        rows[j], rows[j + 1] = scaled(first, second)
        later = range(j + 2, count)
        for l in later:
            uppers[j, l], uppers[j + 1, l] = scaled(p[j][l], p[j + 1][l])
        for i in later:
            rows[i] = rows[i] - (p[j][i] * rows[j] + p[j + 1][i] * rows[j + 1])
            for l in range(i, count):
                change = p[j][i] * uppers[j, l] + p[j + 1][i] * uppers[j + 1, l]
                p[i][l] = p[l][i] = p[i][l] - change
    for j in range(count - 4, -1, -2):
        for i in (j, j + 1):
            rows[i] = rows[i] - tree_sum([uppers[i, l] * rows[l] for l in range(j + 2, count)])
    return rows


def eliminate(matrix, total):
    width = matrix.shape[1]
    if total <= 64:
        blocks = [matrix[i : i + PIVOTS] for i in range(0, total, PIVOTS)]
        sub = iota((PIVOTS, width), 0)
        for b in range(len(blocks)):
            spread = [
                [
                    jnp.broadcast_to(block[:, b * PIVOTS + j : b * PIVOTS + j + 1], (PIVOTS, width))
                    for block in blocks
                ]
                for j in range(PIVOTS)
            ]

            def line(value, i):
                return jnp.broadcast_to(value[i : i + 1], (PIVOTS, width))

            entries = [
                [line(spread[l][b], i) if l >= i else None for l in range(PIVOTS)]
                for i in range(PIVOTS)
            ]
            rows = pivot_rows([line(blocks[b], i) for i in range(PIVOTS)], entries)
            for i in range(len(blocks)):
                if i != b:
                    terms = [spread[j][i] * rows[j] for j in range(PIVOTS)]
                    blocks[i] = blocks[i] - tree_sum(terms)
            solved = rows[0]
            for j in range(1, PIVOTS):
                solved = jnp.where(sub == j, rows[j], solved)
            blocks[b] = solved
        return jnp.concatenate([block[:, total : total + 1] for block in blocks], axis=0)
    row = iota(matrix.shape, 0)
    lane = iota(matrix.shape, 1)

    def one(k, held):
        column = jnp.sum(jnp.where(lane == k, held, F32(0.0)), axis=1, keepdims=True)
        pivot_row = jnp.sum(jnp.where(row == k, held, F32(0.0)), axis=0, keepdims=True)
        here = lane[:1] == k
        pivot = jnp.sum(jnp.where(here, pivot_row, F32(0.0)), axis=1, keepdims=True)
        scaled = pivot_row * (F32(1.0) / pivot)
        return held - jnp.where(row == k, F32(0.0), column) * scaled

    matrix = lax.fori_loop(0, total, one, matrix)
    diag = jnp.sum(jnp.where(row == lane, matrix, F32(0.0)), axis=1, keepdims=True)
    return matrix[:, total : total + 1] / diag


def sum_kernel(*refs):
    *part_refs, out_ref = refs
    out_ref[...] = tree_sum([ref[...] for ref in part_refs[::-1]])


def partners(value, masks):
    axes = ("samp", "layer")
    places = lax.axis_size("samp") * lax.axis_size("layer")
    parts = []
    for mask in masks[::-1]:
        perm = [(i, i ^ mask) for i in range(places) if i % 2 == 1]
        parts.append(lax.ppermute(value, axes, perm))
    return parts + [value]


def sum_over(parts):
    return pl.pallas_call(
        sum_kernel,
        out_shape=jax.ShapeDtypeStruct(parts[0].shape, F32),
        compiler_params=pltpu.CompilerParams(vmem_limit_bytes=VMEM_LIMIT),
        name="sum_over",
    )(*parts)


def rounds(samp, layer):
    masks = [1 << bit for bit in range(1, layer.bit_length() - 1)]
    masks += [layer, layer * (samp - 2)]
    masks += [layer << bit for bit in range(1, samp.bit_length() - 2)]
    return [
        [a, b, a ^ b] if b else [a] for a, b in zip(masks[::2], masks[1::2] + [0] * (len(masks) % 2))
    ]


def total_sum(value):
    layer = lax.axis_size("layer")
    lower = lax.ppermute(value, "layer", [(i, i + 1) for i in range(0, layer, 2)])
    value = sum_over([lower, value])
    for masks in rounds(lax.axis_size("samp"), layer):
        value = sum_over(partners(value, masks))
    return value, lax.ppermute(value, "layer", [(i + 1, i) for i in range(0, layer, 2)])


def solve_kernel(owners, odd_ref, even_ref, *refs):
    *block_refs, weights_ref, update_ref, held = refs
    blocks = in_place(block_refs, owners)
    mats, share, d = update_ref.shape
    local = weights_ref.shape[1]
    odd = lax.axis_index("layer") % 2 == 1
    packed = jnp.where(odd, odd_ref[...], even_ref[...])
    half, packed_width = packed.shape
    total = 2 * half
    width = (total // LANES + 1) * LANES
    turned = jnp.swapaxes(packed[:, half:total], 0, 1)
    energy = [packed[:, 3 * half + i : 3 * half + i + 1] for i in range(2)]
    energy = [jnp.broadcast_to(e, (half, width - total)) for e in energy]
    upper = jnp.concatenate([packed[:, :half], turned, energy[0]], axis=1)
    lower = jnp.concatenate([packed[:, half : 3 * half], energy[1]], axis=1)
    raw = jnp.concatenate([upper, lower], axis=0)
    row = iota((total, width), 0)
    lane = iota((total, width), 1)
    inside = lane < total
    scale = F32(1.0 / total)
    row_mean = jnp.sum(jnp.where(inside, raw, F32(0.0)), axis=1, keepdims=True) * scale
    col_mean = jnp.sum(raw, axis=0, keepdims=True) * scale
    mean = jnp.sum(row_mean, axis=0, keepdims=True) * scale
    gram = (raw - col_mean - row_mean + mean) * scale
    eps = (raw - col_mean) * F32(1.0 / total**0.5)
    on_diag = row == lane
    trace = jnp.sum(
        jnp.sum(jnp.where(on_diag, gram, F32(0.0)), axis=1, keepdims=True), axis=0, keepdims=True
    )
    shift = F32(shift_ratio) * trace * scale
    system = jnp.where(inside, gram + jnp.where(on_diag, shift, F32(0.0)), eps)
    weights = eliminate(system, total)
    me = lax.axis_index("samp")
    own = jnp.where(row - me * local == lane, weights, F32(0.0))
    weights_ref[...] = jnp.sum(own, axis=0, keepdims=True)[:, :local]
    coeffs = weights - jnp.sum(weights, axis=0, keepdims=True) * scale
    held[...] = jnp.broadcast_to(coeffs, (total, d))
    acc = jnp.zeros((mats * share, d), F32)
    for k, parts in enumerate(blocks):
        mine = held[pl.ds(pl.multiple_of((me ^ k) * local, local), local)]
        for s in range(local):
            rows = jnp.concatenate([ref[s].astype(F32) for ref in parts], axis=0)
            acc = acc + mine[s : s + 1] * rows
    for m in range(mats):
        update_ref[m] = acc[m * share : (m + 1) * share]


def solve_and_project(sums, blocks, split, mats):
    local, count, d = blocks[0][0].shape
    total = local * len(blocks)
    return pl.pallas_call(
        functools.partial(solve_kernel, len(blocks)),
        out_shape=(
            jax.ShapeDtypeStruct((1, local), F32),
            jax.ShapeDtypeStruct((mats, count // mats, d), F32),
        ),
        scratch_shapes=[pltpu.VMEM((total, d), F32)],
        compiler_params=pltpu.CompilerParams(vmem_limit_bytes=VMEM_LIMIT),
        name="solve_and_project",
    )(*sums, *in_turn(blocks, split))


def body(spins, activations, cotangents, offdiag):
    local, mats = activations.shape[:2]
    owners = lax.axis_size("samp")
    total = local * owners
    blocks, split = jac_blocks(activations, cotangents, owners)
    for k, part in turns(owners, split)[:-1]:
        perm = [(i, i ^ k) for i in range(owners)]
        blocks[k][part] = lax.ppermute(blocks[k][part], "samp", perm)
    partial = gram_partial(blocks, split, packed_energy(spins, offdiag, total))
    weights, update = solve_and_project(total_sum(partial), blocks, split, mats)
    return weights.reshape(local), update


def solution(mesh):
    placed = (
        P("samp", None),
        P("samp", "layer", None, None),
        P("samp", "layer", None, None),
        P("samp"),
    )
    return jax.shard_map(
        body,
        mesh=mesh,
        in_specs=placed,
        out_specs=(P("samp"), P("layer", "samp", None)),
        check_vma=False,
    )
```

```python
import functools

import jax
import jax.numpy as jnp
from jax import lax
from jax.experimental import pallas as pl
from jax.experimental.pallas import tpu as pltpu
from jax.sharding import PartitionSpec as P

SIDE = 16
LANES = 128
CHUNK = 16
PIVOTS = 8
VMEM_LIMIT = 24 * 2**20
JAC_VMEM_LIMIT = 52 * 2**20
shift_ratio = 0.1
F32 = jnp.float32
BF16 = jnp.bfloat16


def iota(shape, dim):
    return lax.broadcasted_iota(jnp.int32, shape, dim)


def turns(owners, split):
    far, near = list(range(owners // 2, owners)), list(range(owners // 2 - 1, 0, -1))
    cut = split_partners(owners, split)
    order = [(k, part) for part in range(split) for k in cut]
    far = [k for k in far if k not in cut]
    while far or near:
        order += [(k, 0) for k in near[:1] + far[:1]]
        far, near = far[1:], near[1:]
    return order + [(0, 0)]


def split_partners(owners, split):
    return [owners // 2, owners // 2 + 1] if split > 1 else []


def in_turn(blocks, split):
    return [blocks[k][part] for k, part in turns(len(blocks), split)]


def in_place(refs, owners):
    split = 1 + (len(refs) > owners)
    blocks = [[] for _ in range(owners)]
    for (k, _), ref in zip(turns(owners, split), refs):
        blocks[k].append(ref)
    return blocks


def jac_kernel(first_mat, joined, act_hbm, cot_hbm, *refs):
    before, refs = refs[: len(joined)], refs[len(joined) :]
    *out_refs, act_buf, cot_buf, held, sems = refs
    samples, mats, _, d = held.shape
    share = d // len(out_refs)
    me = lax.axis_index("samp")
    copies = []
    for s in range(samples):
        here = (s, pl.ds(first_mat, mats))
        copies.append(
            (
                pltpu.make_async_copy(act_hbm.at[here], act_buf.at[s], sems.at[0, s]),
                pltpu.make_async_copy(cot_hbm.at[here], cot_buf.at[s], sems.at[1, s]),
            )
        )
    for pair in copies:
        for copy in pair:
            copy.start()
    for k, ref in zip(joined, before):
        out_refs[k][:, : ref.shape[1]] = ref[...]

    def share_out(samples):
        for k, out_ref in enumerate(out_refs):
            owned = pl.ds(pl.multiple_of((me ^ k) * share, share), share)
            for s in samples:
                rows = [held[s, m, owned] for m in range(mats)]
                rows = jnp.concatenate(rows, axis=0).astype(BF16)
                out_ref[s, out_ref.shape[1] - mats * share :] = rows

    group = 2
    for first in range(0, samples, group):
        here = range(first, first + group)
        for s in here:
            for copy in copies[s]:
                copy.wait()
        for s in here:
            for m in range(mats):
                held[s, m] = lax.dot_general(
                    act_buf[s, m],
                    cot_buf[s, m],
                    (((0,), (0,)), ((), ())),
                    preferred_element_type=F32,
                ).astype(held.dtype)
        if first > 0:
            share_out(range(first - group, first))
    share_out(range(samples - group, samples))


def jac_rows(activations, cotangents, owners, part, split, before=()):
    samples, mats, sites, d = activations.shape
    mats //= split
    rows = mats * d // owners
    joined = [k for k, block in enumerate(before) if block is not None]
    out_rows = [rows + (before[k].shape[1] if k in joined else 0) for k in range(owners)]
    hbm = pl.BlockSpec(memory_space=pltpu.HBM)
    vmem = pl.BlockSpec(memory_space=pltpu.VMEM)
    return pl.pallas_call(
        functools.partial(jac_kernel, part * mats, joined),
        in_specs=[hbm, hbm] + [vmem] * len(joined),
        out_shape=[jax.ShapeDtypeStruct((samples, count, d), BF16) for count in out_rows],
        scratch_shapes=[
            pltpu.VMEM((samples, mats, sites, d), BF16),
            pltpu.VMEM((samples, mats, sites, d), BF16),
            pltpu.VMEM((samples, mats, d, d), BF16 if d // owners % CHUNK == 0 else F32),
            pltpu.SemaphoreType.DMA((2, samples)),
        ],
        compiler_params=pltpu.CompilerParams(vmem_limit_bytes=JAC_VMEM_LIMIT),
        cost_estimate=pl.CostEstimate(
            flops=2 * samples * mats * sites * d * d,
            bytes_accessed=6 * samples * mats * sites * d,
            transcendentals=0,
        ),
        name="jac_rows",
    )(activations, cotangents, *[before[k] for k in joined])


def jac_blocks(activations, cotangents, owners):
    mats, d = activations.shape[1], activations.shape[3]
    split = mats if mats == 2 and d // owners % CHUNK == 0 else 1
    blocks = [[block] for block in jac_rows(activations, cotangents, owners, 0, split)]
    if split > 1:
        cut = split_partners(owners, split)
        before = [None if k in cut else block[0] for k, block in enumerate(blocks)]
        later = jac_rows(activations, cotangents, owners, 1, split, before)
        blocks = [b + [new] if k in cut else [new] for k, (b, new) in enumerate(zip(blocks, later))]
    return blocks, split


def packed_shape(total):
    half = total // 2
    return half, -(-(3 * half + 2) // LANES) * LANES


def energy_kernel(total, spins_ref, offdiag_ref, out_ref):
    shape = out_ref.shape
    local = spins_ref.shape[0]
    sites = SIDE * SIDE
    z = (2 * spins_ref[...] - 1).astype(F32)
    column = iota((local, sites), 1) % SIDE
    right = jnp.where(
        column == SIDE - 1, pltpu.roll(z, SIDE - 1, 1), pltpu.roll(z, sites - 1, 1)
    )
    below = pltpu.roll(z, sites - SIDE, 1)
    energy = offdiag_ref[...] + jnp.sum(z * (right + below), axis=1, keepdims=True)
    half = total // 2
    first = lax.axis_index("samp") * local
    lower = first // half
    first = first - lower * half
    spread = jnp.concatenate([energy] * (half // local), axis=0)
    row = iota(shape, 0)
    here = (row >= first) & (row < first + local) & (iota(shape, 1) == 3 * half + lower)
    here = here & (lax.axis_index("layer") == 0)
    out_ref[...] = jnp.where(here, spread, F32(0.0))


def packed_energy(spins, offdiag, total):
    return pl.pallas_call(
        functools.partial(energy_kernel, total),
        out_shape=jax.ShapeDtypeStruct(packed_shape(total), F32),
        compiler_params=pltpu.CompilerParams(vmem_limit_bytes=VMEM_LIMIT),
        name="packed_energy",
    )(spins, offdiag[:, None])


def rows_of(parts, row, rows):
    for ref in parts:
        if row < ref.shape[1]:
            return ref[:, row : row + rows]
        row -= ref.shape[1]


def gram_kernel(owners, *refs):
    *block_refs, energy_ref, out_ref, flat, whole = refs
    blocks = in_place(block_refs, owners)
    local, count, d = blocks[0][0].shape
    total = local * owners
    joined = CHUNK // local
    me = lax.axis_index("samp")
    block = CHUNK * CHUNK
    dest = iota((block, block), 0)
    sample = dest % CHUNK
    sample = (sample // local ^ me % joined) * local + sample % local
    source = sample * CHUNK + dest // CHUNK
    swap = (iota((block, block), 1) == source).astype(F32).astype(BF16)
    for row in range(0, count, CHUNK):
        for j in range(owners // joined):
            pieces = [rows_of(p, row, CHUNK) for p in blocks[j * joined : (j + 1) * joined]]
            piece = jnp.concatenate(pieces, axis=0).reshape(block, d)
            turned = jnp.dot(swap, piece, preferred_element_type=F32).astype(BF16)
            place = pl.ds(pl.multiple_of((me // joined ^ j) * CHUNK, CHUNK), CHUNK)
            for r in range(CHUNK):
                flat[row + r, place] = turned[r * CHUNK : (r + 1) * CHUNK]
    lined = jnp.concatenate([flat[r] for r in range(count)], axis=1)
    gram = lax.dot_general(lined, lined, (((1,), (1,)), ((), ())), preferred_element_type=F32)
    whole[...] = jnp.zeros_like(whole)
    whole[:, :total] += gram
    half, width = out_ref.shape
    lane = iota((half, width), 1)
    lower = pltpu.roll(whole[half:], half, 1)
    packed = jnp.where(lane < 3 * half, lower, energy_ref[...])
    out_ref[...] = jnp.where(lane < half, whole[:half], packed)


def gram_partial(blocks, split, energies):
    local, count, d = blocks[0][0].shape
    total = local * len(blocks)
    return pl.pallas_call(
        functools.partial(gram_kernel, len(blocks)),
        out_shape=jax.ShapeDtypeStruct(packed_shape(total), F32),
        scratch_shapes=[
            pltpu.VMEM((count, total, d), BF16),
            pltpu.VMEM((total, packed_shape(total)[1]), F32),
        ],
        compiler_params=pltpu.CompilerParams(vmem_limit_bytes=VMEM_LIMIT),
        cost_estimate=pl.CostEstimate(
            flops=2 * total * total * count * d,
            bytes_accessed=2 * total * count * d,
            transcendentals=0,
        ),
        name="gram_partial",
    )(*in_turn(blocks, split), energies)


def tree_sum(parts):
    while len(parts) > 1:
        odd = parts[len(parts) // 2 * 2 :]
        parts = [a + b for a, b in zip(parts[::2], parts[1::2])] + odd
    return parts[0]


def pivot_rows(rows, entries):
    count = len(rows)
    rows = list(rows)
    p = [[entries[min(i, l)][max(i, l)] for l in range(count)] for i in range(count)]
    uppers = {}
    for j in range(0, count, 2):
        a, b, c = p[j][j], p[j][j + 1], p[j + 1][j + 1]
        inverse = F32(1.0) / (a * c - b * b)

        def scaled(x, y):
            return (c * x - b * y) * inverse, (a * y - b * x) * inverse

        first, second = rows[j], rows[j + 1]
        rows[j], rows[j + 1] = scaled(first, second)
        later = range(j + 2, count)
        for l in later:
            uppers[j, l], uppers[j + 1, l] = scaled(p[j][l], p[j + 1][l])
        for i in later:
            rows[i] = rows[i] - (p[j][i] * rows[j] + p[j + 1][i] * rows[j + 1])
            for l in range(i, count):
                change = p[j][i] * uppers[j, l] + p[j + 1][i] * uppers[j + 1, l]
                p[i][l] = p[l][i] = p[i][l] - change
    for j in range(count - 4, -1, -2):
        for i in (j, j + 1):
            rows[i] = rows[i] - tree_sum([uppers[i, l] * rows[l] for l in range(j + 2, count)])
    return rows


def eliminate(matrix, total):
    width = matrix.shape[1]
    if total <= 64:
        blocks = [matrix[i : i + PIVOTS] for i in range(0, total, PIVOTS)]
        sub = iota((PIVOTS, width), 0)
        for b in range(len(blocks)):
            spread = [
                [
                    jnp.broadcast_to(block[:, b * PIVOTS + j : b * PIVOTS + j + 1], (PIVOTS, width))
                    for block in blocks
                ]
                for j in range(PIVOTS)
            ]

            def line(value, i):
                return jnp.broadcast_to(value[i : i + 1], (PIVOTS, width))

            entries = [
                [line(spread[l][b], i) if l >= i else None for l in range(PIVOTS)]
                for i in range(PIVOTS)
            ]
            rows = pivot_rows([line(blocks[b], i) for i in range(PIVOTS)], entries)
            for i in range(len(blocks)):
                if i != b:
                    terms = [spread[j][i] * rows[j] for j in range(PIVOTS)]
                    blocks[i] = blocks[i] - tree_sum(terms)
            solved = rows[0]
            for j in range(1, PIVOTS):
                solved = jnp.where(sub == j, rows[j], solved)
            blocks[b] = solved
        return jnp.concatenate([block[:, total : total + 1] for block in blocks], axis=0)
    row = iota(matrix.shape, 0)
    lane = iota(matrix.shape, 1)

    def one(k, held):
        column = jnp.sum(jnp.where(lane == k, held, F32(0.0)), axis=1, keepdims=True)
        pivot_row = jnp.sum(jnp.where(row == k, held, F32(0.0)), axis=0, keepdims=True)
        here = lane[:1] == k
        pivot = jnp.sum(jnp.where(here, pivot_row, F32(0.0)), axis=1, keepdims=True)
        scaled = pivot_row * (F32(1.0) / pivot)
        return held - jnp.where(row == k, F32(0.0), column) * scaled

    matrix = lax.fori_loop(0, total, one, matrix)
    diag = jnp.sum(jnp.where(row == lane, matrix, F32(0.0)), axis=1, keepdims=True)
    return matrix[:, total : total + 1] / diag


def sum_kernel(*refs):
    *part_refs, out_ref = refs
    out_ref[...] = tree_sum([ref[...] for ref in part_refs[::-1]])


def partners(value, masks):
    axes = ("samp", "layer")
    places = lax.axis_size("samp") * lax.axis_size("layer")
    parts = []
    for mask in masks[::-1]:
        perm = [(i, i ^ mask if i % 2 == 1 else i) for i in range(places)]
        parts.append(lax.ppermute(value, axes, perm))
    return parts + [value]


def sum_over(parts):
    return pl.pallas_call(
        sum_kernel,
        out_shape=jax.ShapeDtypeStruct(parts[0].shape, F32),
        compiler_params=pltpu.CompilerParams(vmem_limit_bytes=VMEM_LIMIT),
        name="sum_over",
    )(*parts)


def rounds(samp, layer):
    masks = [1 << bit for bit in range(1, layer.bit_length() - 1)]
    masks += [layer, layer * (samp - 2)]
    masks += [layer << bit for bit in range(1, samp.bit_length() - 2)]
    return [
        [a, b, a ^ b] if b else [a] for a, b in zip(masks[::2], masks[1::2] + [0] * (len(masks) % 2))
    ]


def total_sum(value):
    layer = lax.axis_size("layer")
    pairs = [(i, i ^ 1) for i in range(layer)]
    value = sum_over([lax.ppermute(value, "layer", pairs), value])
    for masks in rounds(lax.axis_size("samp"), layer):
        value = sum_over(partners(value, masks))
    return value, lax.ppermute(value, "layer", pairs)


def solve_kernel(owners, odd_ref, even_ref, *refs):
    *block_refs, weights_ref, update_ref, held = refs
    blocks = in_place(block_refs, owners)
    mats, share, d = update_ref.shape
    local = weights_ref.shape[1]
    odd = lax.axis_index("layer") % 2 == 1
    packed = jnp.where(odd, odd_ref[...], even_ref[...])
    half, packed_width = packed.shape
    total = 2 * half
    width = (total // LANES + 1) * LANES
    turned = jnp.swapaxes(packed[:, half:total], 0, 1)
    energy = [packed[:, 3 * half + i : 3 * half + i + 1] for i in range(2)]
    energy = [jnp.broadcast_to(e, (half, width - total)) for e in energy]
    upper = jnp.concatenate([packed[:, :half], turned, energy[0]], axis=1)
    lower = jnp.concatenate([packed[:, half : 3 * half], energy[1]], axis=1)
    raw = jnp.concatenate([upper, lower], axis=0)
    row = iota((total, width), 0)
    lane = iota((total, width), 1)
    inside = lane < total
    scale = F32(1.0 / total)
    row_mean = jnp.sum(jnp.where(inside, raw, F32(0.0)), axis=1, keepdims=True) * scale
    col_mean = jnp.sum(raw, axis=0, keepdims=True) * scale
    mean = jnp.sum(row_mean, axis=0, keepdims=True) * scale
    gram = (raw - col_mean - row_mean + mean) * scale
    eps = (raw - col_mean) * F32(1.0 / total**0.5)
    on_diag = row == lane
    trace = jnp.sum(
        jnp.sum(jnp.where(on_diag, gram, F32(0.0)), axis=1, keepdims=True), axis=0, keepdims=True
    )
    shift = F32(shift_ratio) * trace * scale
    system = jnp.where(inside, gram + jnp.where(on_diag, shift, F32(0.0)), eps)
    weights = eliminate(system, total)
    me = lax.axis_index("samp")
    own = jnp.where(row - me * local == lane, weights, F32(0.0))
    weights_ref[...] = jnp.sum(own, axis=0, keepdims=True)[:, :local]
    coeffs = weights - jnp.sum(weights, axis=0, keepdims=True) * scale
    held[...] = jnp.broadcast_to(coeffs, (total, d))
    acc = jnp.zeros((mats * share, d), F32)
    for k, parts in enumerate(blocks):
        mine = held[pl.ds(pl.multiple_of((me ^ k) * local, local), local)]
        for s in range(local):
            rows = jnp.concatenate([ref[s].astype(F32) for ref in parts], axis=0)
            acc = acc + mine[s : s + 1] * rows
    for m in range(mats):
        update_ref[m] = acc[m * share : (m + 1) * share]


def solve_and_project(sums, blocks, split, mats):
    local, count, d = blocks[0][0].shape
    total = local * len(blocks)
    return pl.pallas_call(
        functools.partial(solve_kernel, len(blocks)),
        out_shape=(
            jax.ShapeDtypeStruct((1, local), F32),
            jax.ShapeDtypeStruct((mats, count // mats, d), F32),
        ),
        scratch_shapes=[pltpu.VMEM((total, d), F32)],
        compiler_params=pltpu.CompilerParams(vmem_limit_bytes=VMEM_LIMIT),
        name="solve_and_project",
    )(*sums, *in_turn(blocks, split))


def body(spins, activations, cotangents, offdiag):
    local, mats = activations.shape[:2]
    owners = lax.axis_size("samp")
    total = local * owners
    blocks, split = jac_blocks(activations, cotangents, owners)
    for k, part in turns(owners, split)[:-1]:
        perm = [(i, i ^ k) for i in range(owners)]
        blocks[k][part] = lax.ppermute(blocks[k][part], "samp", perm)
    partial = gram_partial(blocks, split, packed_energy(spins, offdiag, total))
    weights, update = solve_and_project(total_sum(partial), blocks, split, mats)
    return weights.reshape(local), update


def solution(mesh):
    placed = (
        P("samp", None),
        P("samp", "layer", None, None),
        P("samp", "layer", None, None),
        P("samp"),
    )
    return jax.shard_map(
        body,
        mesh=mesh,
        in_specs=placed,
        out_specs=(P("samp"), P("layer", "samp", None)),
        check_vma=False,
    )
```

```python
import functools

import jax
import jax.numpy as jnp
from jax import lax
from jax.experimental import pallas as pl
from jax.experimental.pallas import tpu as pltpu
from jax.sharding import PartitionSpec as P

SIDE = 16
LANES = 128
CHUNK = 16
PIVOTS = 8
VMEM_LIMIT = 24 * 2**20
JAC_VMEM_LIMIT = 52 * 2**20
shift_ratio = 0.1
F32 = jnp.float32
BF16 = jnp.bfloat16


def iota(shape, dim):
    return lax.broadcasted_iota(jnp.int32, shape, dim)


def turns(owners, split):
    far, near = list(range(owners // 2, owners)), list(range(owners // 2 - 1, 0, -1))
    cut = split_partners(owners, split)
    order = [(k, part) for part in range(split) for k in cut]
    far = [k for k in far if k not in cut]
    while far or near:
        order += [(k, 0) for k in near[:1] + far[:1]]
        far, near = far[1:], near[1:]
    return order + [(0, 0)]


def split_partners(owners, split):
    return [owners // 2, owners // 2 + 1] if split > 1 else []


def in_turn(blocks, split):
    return [blocks[k][part] for k, part in turns(len(blocks), split)]


def in_place(refs, owners):
    split = 1 + (len(refs) > owners)
    blocks = [[] for _ in range(owners)]
    for (k, _), ref in zip(turns(owners, split), refs):
        blocks[k].append(ref)
    return blocks


def jac_kernel(first_mat, joined, act_hbm, cot_hbm, *refs):
    before, refs = refs[: len(joined)], refs[len(joined) :]
    *out_refs, act_buf, cot_buf, held, sems = refs
    samples, mats, _, d = held.shape
    share = d // len(out_refs)
    me = lax.axis_index("samp")
    copies = []
    for s in range(samples):
        here = (s, pl.ds(first_mat, mats))
        copies.append(
            (
                pltpu.make_async_copy(act_hbm.at[here], act_buf.at[s], sems.at[0, s]),
                pltpu.make_async_copy(cot_hbm.at[here], cot_buf.at[s], sems.at[1, s]),
            )
        )
    for pair in copies:
        for copy in pair:
            copy.start()
    for k, ref in zip(joined, before):
        out_refs[k][:, : ref.shape[1]] = ref[...]

    def share_out(samples):
        for k, out_ref in enumerate(out_refs):
            owned = pl.ds(pl.multiple_of((me ^ k) * share, share), share)
            for s in samples:
                rows = [held[s, m, owned] for m in range(mats)]
                rows = jnp.concatenate(rows, axis=0).astype(BF16)
                out_ref[s, out_ref.shape[1] - mats * share :] = rows

    group = 2
    for first in range(0, samples, group):
        here = range(first, first + group)
        for s in here:
            for copy in copies[s]:
                copy.wait()
        for s in here:
            for m in range(mats):
                held[s, m] = lax.dot_general(
                    act_buf[s, m],
                    cot_buf[s, m],
                    (((0,), (0,)), ((), ())),
                    preferred_element_type=F32,
                ).astype(held.dtype)
        if first > 0:
            share_out(range(first - group, first))
    share_out(range(samples - group, samples))


def jac_rows(activations, cotangents, owners, part, split, before=()):
    samples, mats, sites, d = activations.shape
    mats //= split
    rows = mats * d // owners
    joined = [k for k, block in enumerate(before) if block is not None]
    out_rows = [rows + (before[k].shape[1] if k in joined else 0) for k in range(owners)]
    hbm = pl.BlockSpec(memory_space=pltpu.HBM)
    vmem = pl.BlockSpec(memory_space=pltpu.VMEM)
    return pl.pallas_call(
        functools.partial(jac_kernel, part * mats, joined),
        in_specs=[hbm, hbm] + [vmem] * len(joined),
        out_shape=[jax.ShapeDtypeStruct((samples, count, d), BF16) for count in out_rows],
        scratch_shapes=[
            pltpu.VMEM((samples, mats, sites, d), BF16),
            pltpu.VMEM((samples, mats, sites, d), BF16),
            pltpu.VMEM((samples, mats, d, d), BF16 if d // owners % CHUNK == 0 else F32),
            pltpu.SemaphoreType.DMA((2, samples)),
        ],
        compiler_params=pltpu.CompilerParams(vmem_limit_bytes=JAC_VMEM_LIMIT),
        cost_estimate=pl.CostEstimate(
            flops=2 * samples * mats * sites * d * d,
            bytes_accessed=6 * samples * mats * sites * d,
            transcendentals=0,
        ),
        name="jac_rows",
    )(activations, cotangents, *[before[k] for k in joined])


def jac_blocks(activations, cotangents, owners):
    mats, d = activations.shape[1], activations.shape[3]
    split = mats if mats == 2 and d // owners % CHUNK == 0 else 1
    blocks = [[block] for block in jac_rows(activations, cotangents, owners, 0, split)]
    if split > 1:
        cut = split_partners(owners, split)
        before = [None if k in cut else block[0] for k, block in enumerate(blocks)]
        later = jac_rows(activations, cotangents, owners, 1, split, before)
        blocks = [b + [new] if k in cut else [new] for k, (b, new) in enumerate(zip(blocks, later))]
    return blocks, split


def packed_shape(total):
    half = total // 2
    return half, -(-(3 * half + 2) // LANES) * LANES


def energy_kernel(total, spins_ref, offdiag_ref, out_ref):
    shape = out_ref.shape
    local = spins_ref.shape[0]
    sites = SIDE * SIDE
    z = (2 * spins_ref[...] - 1).astype(F32)
    column = iota((local, sites), 1) % SIDE
    right = jnp.where(
        column == SIDE - 1, pltpu.roll(z, SIDE - 1, 1), pltpu.roll(z, sites - 1, 1)
    )
    below = pltpu.roll(z, sites - SIDE, 1)
    energy = offdiag_ref[...] + jnp.sum(z * (right + below), axis=1, keepdims=True)
    half = total // 2
    first = lax.axis_index("samp") * local
    lower = first // half
    first = first - lower * half
    spread = jnp.concatenate([energy] * (half // local), axis=0)
    row = iota(shape, 0)
    here = (row >= first) & (row < first + local) & (iota(shape, 1) == 3 * half + lower)
    here = here & (lax.axis_index("layer") == 0)
    out_ref[...] = jnp.where(here, spread, F32(0.0))


def packed_energy(spins, offdiag, total):
    return pl.pallas_call(
        functools.partial(energy_kernel, total),
        out_shape=jax.ShapeDtypeStruct(packed_shape(total), F32),
        compiler_params=pltpu.CompilerParams(vmem_limit_bytes=VMEM_LIMIT),
        name="packed_energy",
    )(spins, offdiag[:, None])


def rows_of(parts, row, rows):
    for ref in parts:
        if row < ref.shape[1]:
            return ref[:, row : row + rows]
        row -= ref.shape[1]


def gram_kernel(owners, *refs):
    *block_refs, energy_ref, out_ref, flat, whole = refs
    blocks = in_place(block_refs, owners)
    local, count, d = blocks[0][0].shape
    total = local * owners
    joined = CHUNK // local
    me = lax.axis_index("samp")
    block = CHUNK * CHUNK
    dest = iota((block, block), 0)
    sample = dest % CHUNK
    sample = (sample // local ^ me % joined) * local + sample % local
    source = sample * CHUNK + dest // CHUNK
    swap = (iota((block, block), 1) == source).astype(F32).astype(BF16)
    for row in range(0, count, CHUNK):
        for j in range(owners // joined):
            pieces = [rows_of(p, row, CHUNK) for p in blocks[j * joined : (j + 1) * joined]]
            piece = jnp.concatenate(pieces, axis=0).reshape(block, d)
            turned = jnp.dot(swap, piece, preferred_element_type=F32).astype(BF16)
            place = pl.ds(pl.multiple_of((me // joined ^ j) * CHUNK, CHUNK), CHUNK)
            for r in range(CHUNK):
                flat[row + r, place] = turned[r * CHUNK : (r + 1) * CHUNK]
    lined = jnp.concatenate([flat[r] for r in range(count)], axis=1)
    gram = lax.dot_general(lined, lined, (((1,), (1,)), ((), ())), preferred_element_type=F32)
    whole[...] = jnp.zeros_like(whole)
    whole[:, :total] += gram
    half, width = out_ref.shape
    lane = iota((half, width), 1)
    lower = pltpu.roll(whole[half:], half, 1)
    packed = jnp.where(lane < 3 * half, lower, energy_ref[...])
    out_ref[...] = jnp.where(lane < half, whole[:half], packed)


def gram_partial(blocks, split, energies):
    local, count, d = blocks[0][0].shape
    total = local * len(blocks)
    return pl.pallas_call(
        functools.partial(gram_kernel, len(blocks)),
        out_shape=jax.ShapeDtypeStruct(packed_shape(total), F32),
        scratch_shapes=[
            pltpu.VMEM((count, total, d), BF16),
            pltpu.VMEM((total, packed_shape(total)[1]), F32),
        ],
        compiler_params=pltpu.CompilerParams(vmem_limit_bytes=VMEM_LIMIT),
        cost_estimate=pl.CostEstimate(
            flops=2 * total * total * count * d,
            bytes_accessed=2 * total * count * d,
            transcendentals=0,
        ),
        name="gram_partial",
    )(*in_turn(blocks, split), energies)


def tree_sum(parts):
    while len(parts) > 1:
        odd = parts[len(parts) // 2 * 2 :]
        parts = [a + b for a, b in zip(parts[::2], parts[1::2])] + odd
    return parts[0]


def pivot_rows(rows, entries):
    count = len(rows)
    rows = list(rows)
    p = [[entries[min(i, l)][max(i, l)] for l in range(count)] for i in range(count)]
    uppers = {}
    for j in range(0, count, 2):
        a, b, c = p[j][j], p[j][j + 1], p[j + 1][j + 1]
        inverse = F32(1.0) / (a * c - b * b)

        def scaled(x, y):
            return (c * x - b * y) * inverse, (a * y - b * x) * inverse

        first, second = rows[j], rows[j + 1]
        rows[j], rows[j + 1] = scaled(first, second)
        later = range(j + 2, count)
        for l in later:
            uppers[j, l], uppers[j + 1, l] = scaled(p[j][l], p[j + 1][l])
        for i in later:
            rows[i] = rows[i] - (p[j][i] * rows[j] + p[j + 1][i] * rows[j + 1])
            for l in range(i, count):
                change = p[j][i] * uppers[j, l] + p[j + 1][i] * uppers[j + 1, l]
                p[i][l] = p[l][i] = p[i][l] - change
    for j in range(count - 4, -1, -2):
        for i in (j, j + 1):
            rows[i] = rows[i] - tree_sum([uppers[i, l] * rows[l] for l in range(j + 2, count)])
    return rows


def eliminate(matrix, total):
    width = matrix.shape[1]
    if total <= 64:
        blocks = [matrix[i : i + PIVOTS] for i in range(0, total, PIVOTS)]
        sub = iota((PIVOTS, width), 0)
        for b in range(len(blocks)):
            spread = [
                [
                    jnp.broadcast_to(block[:, b * PIVOTS + j : b * PIVOTS + j + 1], (PIVOTS, width))
                    for block in blocks
                ]
                for j in range(PIVOTS)
            ]

            def line(value, i):
                return jnp.broadcast_to(value[i : i + 1], (PIVOTS, width))

            entries = [
                [line(spread[l][b], i) if l >= i else None for l in range(PIVOTS)]
                for i in range(PIVOTS)
            ]
            rows = pivot_rows([line(blocks[b], i) for i in range(PIVOTS)], entries)
            for i in range(len(blocks)):
                if i != b:
                    terms = [spread[j][i] * rows[j] for j in range(PIVOTS)]
                    blocks[i] = blocks[i] - tree_sum(terms)
            solved = rows[0]
            for j in range(1, PIVOTS):
                solved = jnp.where(sub == j, rows[j], solved)
            blocks[b] = solved
        return jnp.concatenate([block[:, total : total + 1] for block in blocks], axis=0)
    row = iota(matrix.shape, 0)
    lane = iota(matrix.shape, 1)

    def one(k, held):
        column = jnp.sum(jnp.where(lane == k, held, F32(0.0)), axis=1, keepdims=True)
        pivot_row = jnp.sum(jnp.where(row == k, held, F32(0.0)), axis=0, keepdims=True)
        here = lane[:1] == k
        pivot = jnp.sum(jnp.where(here, pivot_row, F32(0.0)), axis=1, keepdims=True)
        scaled = pivot_row * (F32(1.0) / pivot)
        return held - jnp.where(row == k, F32(0.0), column) * scaled

    matrix = lax.fori_loop(0, total, one, matrix)
    diag = jnp.sum(jnp.where(row == lane, matrix, F32(0.0)), axis=1, keepdims=True)
    return matrix[:, total : total + 1] / diag


def sum_kernel(*refs):
    *part_refs, out_ref = refs
    out_ref[...] = tree_sum([ref[...] for ref in part_refs[::-1]])


def partners(value, masks):
    axes = ("samp", "layer")
    places = lax.axis_size("samp") * lax.axis_size("layer")
    perms = [[(i, i ^ mask) for i in range(places)] for mask in masks[::-1]]
    return [lax.ppermute(value, axes, perm) for perm in perms] + [value]


def sum_over(parts):
    return pl.pallas_call(
        sum_kernel,
        out_shape=jax.ShapeDtypeStruct(parts[0].shape, F32),
        compiler_params=pltpu.CompilerParams(vmem_limit_bytes=VMEM_LIMIT),
        name="sum_over",
    )(*parts)


def rounds(samp, layer):
    masks = [1 << bit for bit in range(1, layer.bit_length() - 1)]
    masks += [layer, layer * (samp - 2)]
    masks += [layer << bit for bit in range(1, samp.bit_length() - 2)]
    later = zip(masks[::2], masks[1::2] + [0] * (len(masks) % 2))
    return [[1]] + [[a, b, a ^ b] if b else [a] for a, b in later]


def solve_kernel(sums, owners, *refs):
    sum_refs, (*block_refs, weights_ref, update_ref, held) = refs[:sums], refs[sums:]
    blocks = in_place(block_refs, owners)
    mats, share, d = update_ref.shape
    local = weights_ref.shape[1]
    packed = tree_sum([ref[...] for ref in sum_refs[::-1]])
    half, packed_width = packed.shape
    total = 2 * half
    width = (total // LANES + 1) * LANES
    turned = jnp.swapaxes(packed[:, half:total], 0, 1)
    energy = [packed[:, 3 * half + i : 3 * half + i + 1] for i in range(2)]
    energy = [jnp.broadcast_to(e, (half, width - total)) for e in energy]
    upper = jnp.concatenate([packed[:, :half], turned, energy[0]], axis=1)
    lower = jnp.concatenate([packed[:, half : 3 * half], energy[1]], axis=1)
    raw = jnp.concatenate([upper, lower], axis=0)
    row = iota((total, width), 0)
    lane = iota((total, width), 1)
    inside = lane < total
    scale = F32(1.0 / total)
    row_mean = jnp.sum(jnp.where(inside, raw, F32(0.0)), axis=1, keepdims=True) * scale
    col_mean = jnp.sum(raw, axis=0, keepdims=True) * scale
    mean = jnp.sum(row_mean, axis=0, keepdims=True) * scale
    gram = (raw - col_mean - row_mean + mean) * scale
    eps = (raw - col_mean) * F32(1.0 / total**0.5)
    on_diag = row == lane
    trace = jnp.sum(
        jnp.sum(jnp.where(on_diag, gram, F32(0.0)), axis=1, keepdims=True), axis=0, keepdims=True
    )
    shift = F32(shift_ratio) * trace * scale
    system = jnp.where(inside, gram + jnp.where(on_diag, shift, F32(0.0)), eps)
    weights = eliminate(system, total)
    me = lax.axis_index("samp")
    own = jnp.where(row - me * local == lane, weights, F32(0.0))
    weights_ref[...] = jnp.sum(own, axis=0, keepdims=True)[:, :local]
    coeffs = weights - jnp.sum(weights, axis=0, keepdims=True) * scale
    held[...] = jnp.broadcast_to(coeffs, (total, d))
    acc = jnp.zeros((mats * share, d), F32)
    for k, parts in enumerate(blocks):
        mine = held[pl.ds(pl.multiple_of((me ^ k) * local, local), local)]
        for s in range(local):
            rows = jnp.concatenate([ref[s].astype(F32) for ref in parts], axis=0)
            acc = acc + mine[s : s + 1] * rows
    for m in range(mats):
        update_ref[m] = acc[m * share : (m + 1) * share]


def solve_and_project(sums, blocks, split, mats):
    local, count, d = blocks[0][0].shape
    total = local * len(blocks)
    return pl.pallas_call(
        functools.partial(solve_kernel, len(sums), len(blocks)),
        out_shape=(
            jax.ShapeDtypeStruct((1, local), F32),
            jax.ShapeDtypeStruct((mats, count // mats, d), F32),
        ),
        scratch_shapes=[pltpu.VMEM((total, d), F32)],
        compiler_params=pltpu.CompilerParams(vmem_limit_bytes=VMEM_LIMIT),
        name="solve_and_project",
    )(*sums, *in_turn(blocks, split))


def body(spins, activations, cotangents, offdiag):
    local, mats = activations.shape[:2]
    owners = lax.axis_size("samp")
    total = local * owners
    blocks, split = jac_blocks(activations, cotangents, owners)
    for k, part in turns(owners, split)[:-1]:
        perm = [(i, i ^ k) for i in range(owners)]
        blocks[k][part] = lax.ppermute(blocks[k][part], "samp", perm)
    partial = gram_partial(blocks, split, packed_energy(spins, offdiag, total))
    *early, last = rounds(owners, lax.axis_size("layer"))
    for masks in early:
        partial = sum_over(partners(partial, masks))
    weights, update = solve_and_project(partners(partial, last), blocks, split, mats)
    return weights.reshape(local), update


def solution(mesh):
    placed = (
        P("samp", None),
        P("samp", "layer", None, None),
        P("samp", "layer", None, None),
        P("samp"),
    )
    return jax.shard_map(
        body,
        mesh=mesh,
        in_specs=placed,
        out_specs=(P("samp"), P("layer", "samp", None)),
        check_vma=False,
    )
```

```python
import functools

import jax
import jax.numpy as jnp
from jax import lax
from jax.experimental import pallas as pl
from jax.experimental.pallas import tpu as pltpu
from jax.sharding import PartitionSpec as P

SIDE = 16
LANES = 128
CHUNK = 16
PIVOTS = 8
VMEM_LIMIT = 24 * 2**20
JAC_VMEM_LIMIT = 52 * 2**20
shift_ratio = 0.1
F32 = jnp.float32
BF16 = jnp.bfloat16


def iota(shape, dim):
    return lax.broadcasted_iota(jnp.int32, shape, dim)


def turns(owners, split):
    far, near = list(range(owners // 2, owners)), list(range(owners // 2 - 1, 0, -1))
    cut = split_partners(owners, split)
    order = [(k, part) for part in range(split) for k in cut]
    far = [k for k in far if k not in cut]
    while far or near:
        order += [(k, 0) for k in near[:1] + far[:1]]
        far, near = far[1:], near[1:]
    return order + [(0, 0)]


def split_partners(owners, split):
    return [owners // 2, owners // 2 + 1] if split > 1 else []


def in_turn(blocks, split):
    return [blocks[k][part] for k, part in turns(len(blocks), split)]


def in_place(refs, owners):
    split = 1 + (len(refs) > owners)
    blocks = [[] for _ in range(owners)]
    for (k, _), ref in zip(turns(owners, split), refs):
        blocks[k].append(ref)
    return blocks


def jac_kernel(first_mat, joined, act_hbm, cot_hbm, *refs):
    before, refs = refs[: len(joined)], refs[len(joined) :]
    *out_refs, act_buf, cot_buf, held, sems = refs
    samples, mats, _, d = held.shape
    share = d // len(out_refs)
    me = lax.axis_index("samp")
    copies = []
    for s in range(samples):
        here = (s, pl.ds(first_mat, mats))
        copies.append(
            (
                pltpu.make_async_copy(act_hbm.at[here], act_buf.at[s], sems.at[0, s]),
                pltpu.make_async_copy(cot_hbm.at[here], cot_buf.at[s], sems.at[1, s]),
            )
        )
    for pair in copies:
        for copy in pair:
            copy.start()
    for k, ref in zip(joined, before):
        out_refs[k][:, : ref.shape[1]] = ref[...]

    def share_out(samples):
        for k, out_ref in enumerate(out_refs):
            owned = pl.ds(pl.multiple_of((me ^ k) * share, share), share)
            for s in samples:
                rows = [held[s, m, owned] for m in range(mats)]
                rows = jnp.concatenate(rows, axis=0).astype(BF16)
                out_ref[s, out_ref.shape[1] - mats * share :] = rows

    group = 2
    for first in range(0, samples, group):
        here = range(first, first + group)
        for s in here:
            for copy in copies[s]:
                copy.wait()
        for s in here:
            for m in range(mats):
                held[s, m] = lax.dot_general(
                    act_buf[s, m],
                    cot_buf[s, m],
                    (((0,), (0,)), ((), ())),
                    preferred_element_type=F32,
                ).astype(held.dtype)
        if first > 0:
            share_out(range(first - group, first))
    share_out(range(samples - group, samples))


def jac_rows(activations, cotangents, owners, part, split, before=()):
    samples, mats, sites, d = activations.shape
    mats //= split
    rows = mats * d // owners
    joined = [k for k, block in enumerate(before) if block is not None]
    out_rows = [rows + (before[k].shape[1] if k in joined else 0) for k in range(owners)]
    hbm = pl.BlockSpec(memory_space=pltpu.HBM)
    vmem = pl.BlockSpec(memory_space=pltpu.VMEM)
    return pl.pallas_call(
        functools.partial(jac_kernel, part * mats, joined),
        in_specs=[hbm, hbm] + [vmem] * len(joined),
        out_shape=[jax.ShapeDtypeStruct((samples, count, d), BF16) for count in out_rows],
        scratch_shapes=[
            pltpu.VMEM((samples, mats, sites, d), BF16),
            pltpu.VMEM((samples, mats, sites, d), BF16),
            pltpu.VMEM((samples, mats, d, d), BF16 if d // owners % CHUNK == 0 else F32),
            pltpu.SemaphoreType.DMA((2, samples)),
        ],
        compiler_params=pltpu.CompilerParams(vmem_limit_bytes=JAC_VMEM_LIMIT),
        cost_estimate=pl.CostEstimate(
            flops=2 * samples * mats * sites * d * d,
            bytes_accessed=6 * samples * mats * sites * d,
            transcendentals=0,
        ),
        name="jac_rows",
    )(activations, cotangents, *[before[k] for k in joined])


def jac_blocks(activations, cotangents, owners):
    mats, d = activations.shape[1], activations.shape[3]
    split = mats if mats == 2 and d // owners % CHUNK == 0 else 1
    blocks = [[block] for block in jac_rows(activations, cotangents, owners, 0, split)]
    if split > 1:
        cut = split_partners(owners, split)
        before = [None if k in cut else block[0] for k, block in enumerate(blocks)]
        later = jac_rows(activations, cotangents, owners, 1, split, before)
        blocks = [b + [new] if k in cut else [new] for k, (b, new) in enumerate(zip(blocks, later))]
    return blocks, split


def packed_shape(total):
    half = total // 2
    return half, -(-(3 * half + 2) // LANES) * LANES


def energy_kernel(total, spins_ref, offdiag_ref, out_ref):
    shape = out_ref.shape
    local = spins_ref.shape[0]
    sites = SIDE * SIDE
    z = (2 * spins_ref[...] - 1).astype(F32)
    column = iota((local, sites), 1) % SIDE
    right = jnp.where(
        column == SIDE - 1, pltpu.roll(z, SIDE - 1, 1), pltpu.roll(z, sites - 1, 1)
    )
    below = pltpu.roll(z, sites - SIDE, 1)
    energy = offdiag_ref[...] + jnp.sum(z * (right + below), axis=1, keepdims=True)
    half = total // 2
    first = lax.axis_index("samp") * local
    lower = first // half
    first = first - lower * half
    spread = jnp.concatenate([energy] * (half // local), axis=0)
    row = iota(shape, 0)
    here = (row >= first) & (row < first + local) & (iota(shape, 1) == 3 * half + lower)
    here = here & (lax.axis_index("layer") == 0)
    out_ref[...] = jnp.where(here, spread, F32(0.0))


def packed_energy(spins, offdiag, total):
    return pl.pallas_call(
        functools.partial(energy_kernel, total),
        out_shape=jax.ShapeDtypeStruct(packed_shape(total), F32),
        compiler_params=pltpu.CompilerParams(vmem_limit_bytes=VMEM_LIMIT),
        name="packed_energy",
    )(spins, offdiag[:, None])


def rows_of(parts, row, rows):
    for ref in parts:
        if row < ref.shape[1]:
            return ref[:, row : row + rows]
        row -= ref.shape[1]


def gram_kernel(owners, *refs):
    *block_refs, energy_ref, out_ref, flat, whole = refs
    blocks = in_place(block_refs, owners)
    local, count, d = blocks[0][0].shape
    total = local * owners
    joined = CHUNK // local
    me = lax.axis_index("samp")
    block = CHUNK * CHUNK
    dest = iota((block, block), 0)
    sample = dest % CHUNK
    sample = (sample // local ^ me % joined) * local + sample % local
    source = sample * CHUNK + dest // CHUNK
    swap = (iota((block, block), 1) == source).astype(F32).astype(BF16)
    for row in range(0, count, CHUNK):
        for j in range(owners // joined):
            pieces = [rows_of(p, row, CHUNK) for p in blocks[j * joined : (j + 1) * joined]]
            piece = jnp.concatenate(pieces, axis=0).reshape(block, d)
            turned = jnp.dot(swap, piece, preferred_element_type=F32).astype(BF16)
            place = pl.ds(pl.multiple_of((me // joined ^ j) * CHUNK, CHUNK), CHUNK)
            for r in range(CHUNK):
                flat[row + r, place] = turned[r * CHUNK : (r + 1) * CHUNK]
    lined = jnp.concatenate([flat[r] for r in range(count)], axis=1)
    gram = lax.dot_general(lined, lined, (((1,), (1,)), ((), ())), preferred_element_type=F32)
    whole[...] = jnp.zeros_like(whole)
    whole[:, :total] += gram
    half, width = out_ref.shape
    lane = iota((half, width), 1)
    lower = pltpu.roll(whole[half:], half, 1)
    packed = jnp.where(lane < 3 * half, lower, energy_ref[...])
    out_ref[...] = jnp.where(lane < half, whole[:half], packed)


def gram_partial(blocks, split, energies):
    local, count, d = blocks[0][0].shape
    total = local * len(blocks)
    return pl.pallas_call(
        functools.partial(gram_kernel, len(blocks)),
        out_shape=jax.ShapeDtypeStruct(packed_shape(total), F32),
        scratch_shapes=[
            pltpu.VMEM((count, total, d), BF16),
            pltpu.VMEM((total, packed_shape(total)[1]), F32),
        ],
        compiler_params=pltpu.CompilerParams(vmem_limit_bytes=VMEM_LIMIT),
        cost_estimate=pl.CostEstimate(
            flops=2 * total * total * count * d,
            bytes_accessed=2 * total * count * d,
            transcendentals=0,
        ),
        name="gram_partial",
    )(*in_turn(blocks, split), energies)


def tree_sum(parts):
    while len(parts) > 1:
        odd = parts[len(parts) // 2 * 2 :]
        parts = [a + b for a, b in zip(parts[::2], parts[1::2])] + odd
    return parts[0]


def pivot_rows(rows, entries):
    count = len(rows)
    rows = list(rows)
    p = [[entries[min(i, l)][max(i, l)] for l in range(count)] for i in range(count)]
    uppers = {}
    for j in range(0, count, 2):
        a, b, c = p[j][j], p[j][j + 1], p[j + 1][j + 1]
        inverse = F32(1.0) / (a * c - b * b)

        def scaled(x, y):
            return (c * x - b * y) * inverse, (a * y - b * x) * inverse

        first, second = rows[j], rows[j + 1]
        rows[j], rows[j + 1] = scaled(first, second)
        later = range(j + 2, count)
        for l in later:
            uppers[j, l], uppers[j + 1, l] = scaled(p[j][l], p[j + 1][l])
        for i in later:
            rows[i] = rows[i] - (p[j][i] * rows[j] + p[j + 1][i] * rows[j + 1])
            for l in range(i, count):
                change = p[j][i] * uppers[j, l] + p[j + 1][i] * uppers[j + 1, l]
                p[i][l] = p[l][i] = p[i][l] - change
    for j in range(count - 4, -1, -2):
        for i in (j, j + 1):
            rows[i] = rows[i] - tree_sum([uppers[i, l] * rows[l] for l in range(j + 2, count)])
    return rows


def eliminate(matrix, total):
    width = matrix.shape[1]
    if total <= 64:
        blocks = [matrix[i : i + PIVOTS] for i in range(0, total, PIVOTS)]
        sub = iota((PIVOTS, width), 0)
        for b in range(len(blocks)):
            spread = [
                [
                    jnp.broadcast_to(block[:, b * PIVOTS + j : b * PIVOTS + j + 1], (PIVOTS, width))
                    for block in blocks
                ]
                for j in range(PIVOTS)
            ]

            def line(value, i):
                return jnp.broadcast_to(value[i : i + 1], (PIVOTS, width))

            entries = [
                [line(spread[l][b], i) if l >= i else None for l in range(PIVOTS)]
                for i in range(PIVOTS)
            ]
            rows = pivot_rows([line(blocks[b], i) for i in range(PIVOTS)], entries)
            for i in range(len(blocks)):
                if i != b:
                    terms = [spread[j][i] * rows[j] for j in range(PIVOTS)]
                    blocks[i] = blocks[i] - tree_sum(terms)
            solved = rows[0]
            for j in range(1, PIVOTS):
                solved = jnp.where(sub == j, rows[j], solved)
            blocks[b] = solved
        return jnp.concatenate([block[:, total : total + 1] for block in blocks], axis=0)
    row = iota(matrix.shape, 0)
    lane = iota(matrix.shape, 1)

    def one(k, held):
        column = jnp.sum(jnp.where(lane == k, held, F32(0.0)), axis=1, keepdims=True)
        pivot_row = jnp.sum(jnp.where(row == k, held, F32(0.0)), axis=0, keepdims=True)
        here = lane[:1] == k
        pivot = jnp.sum(jnp.where(here, pivot_row, F32(0.0)), axis=1, keepdims=True)
        scaled = pivot_row * (F32(1.0) / pivot)
        return held - jnp.where(row == k, F32(0.0), column) * scaled

    matrix = lax.fori_loop(0, total, one, matrix)
    diag = jnp.sum(jnp.where(row == lane, matrix, F32(0.0)), axis=1, keepdims=True)
    return matrix[:, total : total + 1] / diag


def sum_kernel(*refs):
    *part_refs, out_ref = refs
    out_ref[...] = tree_sum([ref[...] for ref in part_refs[::-1]])


def partners(value, masks):
    axes = ("samp", "layer")
    places = lax.axis_size("samp") * lax.axis_size("layer")
    perms = [[(i, i ^ mask) for i in range(places)] for mask in masks[::-1]]
    return [lax.ppermute(value, axes, perm) for perm in perms] + [value]


def sum_over(parts):
    return pl.pallas_call(
        sum_kernel,
        out_shape=jax.ShapeDtypeStruct(parts[0].shape, F32),
        compiler_params=pltpu.CompilerParams(vmem_limit_bytes=VMEM_LIMIT),
        name="sum_over",
    )(*parts)


def rounds(samp, layer):
    masks = [1 << bit for bit in range(1, layer.bit_length() - 1)]
    masks += [layer * (samp - 2), layer]
    masks += [layer << bit for bit in range(1, samp.bit_length() - 2)]
    later = zip(masks[::2], masks[1::2] + [0] * (len(masks) % 2))
    return [[1]] + [[a, b, a ^ b] if b else [a] for a, b in later]


def solve_kernel(sums, owners, *refs):
    sum_refs, (*block_refs, weights_ref, update_ref, held) = refs[:sums], refs[sums:]
    blocks = in_place(block_refs, owners)
    mats, share, d = update_ref.shape
    local = weights_ref.shape[1]
    packed = tree_sum([ref[...] for ref in sum_refs[::-1]])
    half, packed_width = packed.shape
    total = 2 * half
    width = (total // LANES + 1) * LANES
    turned = jnp.swapaxes(packed[:, half:total], 0, 1)
    energy = [packed[:, 3 * half + i : 3 * half + i + 1] for i in range(2)]
    energy = [jnp.broadcast_to(e, (half, width - total)) for e in energy]
    upper = jnp.concatenate([packed[:, :half], turned, energy[0]], axis=1)
    lower = jnp.concatenate([packed[:, half : 3 * half], energy[1]], axis=1)
    raw = jnp.concatenate([upper, lower], axis=0)
    row = iota((total, width), 0)
    lane = iota((total, width), 1)
    inside = lane < total
    scale = F32(1.0 / total)
    row_mean = jnp.sum(jnp.where(inside, raw, F32(0.0)), axis=1, keepdims=True) * scale
    col_mean = jnp.sum(raw, axis=0, keepdims=True) * scale
    mean = jnp.sum(row_mean, axis=0, keepdims=True) * scale
    gram = (raw - col_mean - row_mean + mean) * scale
    eps = (raw - col_mean) * F32(1.0 / total**0.5)
    on_diag = row == lane
    trace = jnp.sum(
        jnp.sum(jnp.where(on_diag, gram, F32(0.0)), axis=1, keepdims=True), axis=0, keepdims=True
    )
    shift = F32(shift_ratio) * trace * scale
    system = jnp.where(inside, gram + jnp.where(on_diag, shift, F32(0.0)), eps)
    weights = eliminate(system, total)
    me = lax.axis_index("samp")
    own = jnp.where(row - me * local == lane, weights, F32(0.0))
    weights_ref[...] = jnp.sum(own, axis=0, keepdims=True)[:, :local]
    coeffs = weights - jnp.sum(weights, axis=0, keepdims=True) * scale
    held[...] = jnp.broadcast_to(coeffs, (total, d))
    acc = jnp.zeros((mats * share, d), F32)
    for k, parts in enumerate(blocks):
        mine = held[pl.ds(pl.multiple_of((me ^ k) * local, local), local)]
        for s in range(local):
            rows = jnp.concatenate([ref[s].astype(F32) for ref in parts], axis=0)
            acc = acc + mine[s : s + 1] * rows
    for m in range(mats):
        update_ref[m] = acc[m * share : (m + 1) * share]


def solve_and_project(sums, blocks, split, mats):
    local, count, d = blocks[0][0].shape
    total = local * len(blocks)
    return pl.pallas_call(
        functools.partial(solve_kernel, len(sums), len(blocks)),
        out_shape=(
            jax.ShapeDtypeStruct((1, local), F32),
            jax.ShapeDtypeStruct((mats, count // mats, d), F32),
        ),
        scratch_shapes=[pltpu.VMEM((total, d), F32)],
        compiler_params=pltpu.CompilerParams(vmem_limit_bytes=VMEM_LIMIT),
        name="solve_and_project",
    )(*sums, *in_turn(blocks, split))


def body(spins, activations, cotangents, offdiag):
    local, mats = activations.shape[:2]
    owners = lax.axis_size("samp")
    total = local * owners
    blocks, split = jac_blocks(activations, cotangents, owners)
    for k, part in turns(owners, split)[:-1]:
        perm = [(i, i ^ k) for i in range(owners)]
        blocks[k][part] = lax.ppermute(blocks[k][part], "samp", perm)
    partial = gram_partial(blocks, split, packed_energy(spins, offdiag, total))
    *early, last = rounds(owners, lax.axis_size("layer"))
    for masks in early:
        partial = sum_over(partners(partial, masks))
    weights, update = solve_and_project(partners(partial, last), blocks, split, mats)
    return weights.reshape(local), update


def solution(mesh):
    placed = (
        P("samp", None),
        P("samp", "layer", None, None),
        P("samp", "layer", None, None),
        P("samp"),
    )
    return jax.shard_map(
        body,
        mesh=mesh,
        in_specs=placed,
        out_specs=(P("samp"), P("layer", "samp", None)),
        check_vma=False,
    )
```

```python
import functools

import jax
import jax.numpy as jnp
from jax import lax
from jax.experimental import pallas as pl
from jax.experimental.pallas import tpu as pltpu
from jax.sharding import PartitionSpec as P

SIDE = 16
LANES = 128
CHUNK = 16
PIVOTS = 8
VMEM_LIMIT = 24 * 2**20
JAC_VMEM_LIMIT = 52 * 2**20
shift_ratio = 0.1
F32 = jnp.float32
BF16 = jnp.bfloat16


def iota(shape, dim):
    return lax.broadcasted_iota(jnp.int32, shape, dim)


def turns(owners, split):
    far, near = list(range(owners // 2, owners)), list(range(owners // 2 - 1, 0, -1))
    cut = split_partners(owners, split)
    order = [(k, part) for part in range(split) for k in cut]
    far = [k for k in far if k not in cut]
    while far or near:
        order += [(k, 0) for k in near[:1] + far[:1]]
        far, near = far[1:], near[1:]
    return order + [(0, 0)]


def split_partners(owners, split):
    return [owners // 2, owners // 2 + 1] if split > 1 else []


def in_turn(blocks, split):
    return [blocks[k][part] for k, part in turns(len(blocks), split)]


def in_place(refs, owners):
    split = 1 + (len(refs) > owners)
    blocks = [[] for _ in range(owners)]
    for (k, _), ref in zip(turns(owners, split), refs):
        blocks[k].append(ref)
    return blocks


def jac_kernel(first_mat, joined, act_hbm, cot_hbm, *refs):
    before, refs = refs[: len(joined)], refs[len(joined) :]
    *out_refs, act_buf, cot_buf, held, sems = refs
    samples, mats, _, d = held.shape
    share = d // len(out_refs)
    me = lax.axis_index("samp")
    group = 2
    copies = []
    for first in range(0, samples, group):
        here = pl.ds(first, group)
        mine = (here, pl.ds(first_mat, mats))
        sem = first // group
        copies.append(pltpu.make_async_copy(act_hbm.at[mine], act_buf.at[here], sems.at[0, sem]))
        copies.append(pltpu.make_async_copy(cot_hbm.at[mine], cot_buf.at[here], sems.at[1, sem]))
    for copy in copies:
        copy.start()
    for k, ref in zip(joined, before):
        out_refs[k][:, : ref.shape[1]] = ref[...]

    def share_out(samples):
        for k, out_ref in enumerate(out_refs):
            owned = pl.ds(pl.multiple_of((me ^ k) * share, share), share)
            for s in samples:
                rows = [held[s, m, owned] for m in range(mats)]
                rows = jnp.concatenate(rows, axis=0).astype(BF16)
                out_ref[s, out_ref.shape[1] - mats * share :] = rows

    for first in range(0, samples, group):
        here = range(first, first + group)
        copies[first].wait()
        copies[first + 1].wait()
        for s in here:
            for m in range(mats):
                held[s, m] = lax.dot_general(
                    act_buf[s, m],
                    cot_buf[s, m],
                    (((0,), (0,)), ((), ())),
                    preferred_element_type=F32,
                ).astype(held.dtype)
        if first > 0:
            share_out(range(first - group, first))
    share_out(range(samples - group, samples))


def jac_rows(activations, cotangents, owners, part, split, before=()):
    samples, mats, sites, d = activations.shape
    mats //= split
    rows = mats * d // owners
    joined = [k for k, block in enumerate(before) if block is not None]
    out_rows = [rows + (before[k].shape[1] if k in joined else 0) for k in range(owners)]
    hbm = pl.BlockSpec(memory_space=pltpu.HBM)
    vmem = pl.BlockSpec(memory_space=pltpu.VMEM)
    return pl.pallas_call(
        functools.partial(jac_kernel, part * mats, joined),
        in_specs=[hbm, hbm] + [vmem] * len(joined),
        out_shape=[jax.ShapeDtypeStruct((samples, count, d), BF16) for count in out_rows],
        scratch_shapes=[
            pltpu.VMEM((samples, mats, sites, d), BF16),
            pltpu.VMEM((samples, mats, sites, d), BF16),
            pltpu.VMEM((samples, mats, d, d), BF16 if d // owners % CHUNK == 0 else F32),
            pltpu.SemaphoreType.DMA((2, samples)),
        ],
        compiler_params=pltpu.CompilerParams(vmem_limit_bytes=JAC_VMEM_LIMIT),
        cost_estimate=pl.CostEstimate(
            flops=2 * samples * mats * sites * d * d,
            bytes_accessed=6 * samples * mats * sites * d,
            transcendentals=0,
        ),
        name="jac_rows",
    )(activations, cotangents, *[before[k] for k in joined])


def jac_blocks(activations, cotangents, owners):
    mats, d = activations.shape[1], activations.shape[3]
    split = mats if mats == 2 and d // owners % CHUNK == 0 else 1
    blocks = [[block] for block in jac_rows(activations, cotangents, owners, 0, split)]
    if split > 1:
        cut = split_partners(owners, split)
        before = [None if k in cut else block[0] for k, block in enumerate(blocks)]
        later = jac_rows(activations, cotangents, owners, 1, split, before)
        blocks = [b + [new] if k in cut else [new] for k, (b, new) in enumerate(zip(blocks, later))]
    return blocks, split


def packed_shape(total):
    half = total // 2
    return half, -(-(3 * half + 2) // LANES) * LANES


def energy_kernel(total, spins_ref, offdiag_ref, out_ref):
    shape = out_ref.shape
    local = spins_ref.shape[0]
    sites = SIDE * SIDE
    z = (2 * spins_ref[...] - 1).astype(F32)
    column = iota((local, sites), 1) % SIDE
    right = jnp.where(
        column == SIDE - 1, pltpu.roll(z, SIDE - 1, 1), pltpu.roll(z, sites - 1, 1)
    )
    below = pltpu.roll(z, sites - SIDE, 1)
    energy = offdiag_ref[...] + jnp.sum(z * (right + below), axis=1, keepdims=True)
    half = total // 2
    first = lax.axis_index("samp") * local
    lower = first // half
    first = first - lower * half
    spread = jnp.concatenate([energy] * (half // local), axis=0)
    row = iota(shape, 0)
    here = (row >= first) & (row < first + local) & (iota(shape, 1) == 3 * half + lower)
    here = here & (lax.axis_index("layer") == 0)
    out_ref[...] = jnp.where(here, spread, F32(0.0))


def packed_energy(spins, offdiag, total):
    return pl.pallas_call(
        functools.partial(energy_kernel, total),
        out_shape=jax.ShapeDtypeStruct(packed_shape(total), F32),
        compiler_params=pltpu.CompilerParams(vmem_limit_bytes=VMEM_LIMIT),
        name="packed_energy",
    )(spins, offdiag[:, None])


def rows_of(parts, row, rows):
    for ref in parts:
        if row < ref.shape[1]:
            return ref[:, row : row + rows]
        row -= ref.shape[1]


def gram_kernel(owners, *refs):
    *block_refs, energy_ref, out_ref, flat, whole = refs
    blocks = in_place(block_refs, owners)
    local, count, d = blocks[0][0].shape
    total = local * owners
    joined = CHUNK // local
    me = lax.axis_index("samp")
    block = CHUNK * CHUNK
    dest = iota((block, block), 0)
    sample = dest % CHUNK
    sample = (sample // local ^ me % joined) * local + sample % local
    source = sample * CHUNK + dest // CHUNK
    swap = (iota((block, block), 1) == source).astype(F32).astype(BF16)
    for row in range(0, count, CHUNK):
        for j in range(owners // joined):
            pieces = [rows_of(p, row, CHUNK) for p in blocks[j * joined : (j + 1) * joined]]
            piece = jnp.concatenate(pieces, axis=0).reshape(block, d)
            turned = jnp.dot(swap, piece, preferred_element_type=F32).astype(BF16)
            place = pl.ds(pl.multiple_of((me // joined ^ j) * CHUNK, CHUNK), CHUNK)
            for r in range(CHUNK):
                flat[row + r, place] = turned[r * CHUNK : (r + 1) * CHUNK]
    lined = jnp.concatenate([flat[r] for r in range(count)], axis=1)
    gram = lax.dot_general(lined, lined, (((1,), (1,)), ((), ())), preferred_element_type=F32)
    whole[...] = jnp.zeros_like(whole)
    whole[:, :total] += gram
    half, width = out_ref.shape
    lane = iota((half, width), 1)
    lower = pltpu.roll(whole[half:], half, 1)
    packed = jnp.where(lane < 3 * half, lower, energy_ref[...])
    out_ref[...] = jnp.where(lane < half, whole[:half], packed)


def gram_partial(blocks, split, energies):
    local, count, d = blocks[0][0].shape
    total = local * len(blocks)
    return pl.pallas_call(
        functools.partial(gram_kernel, len(blocks)),
        out_shape=jax.ShapeDtypeStruct(packed_shape(total), F32),
        scratch_shapes=[
            pltpu.VMEM((count, total, d), BF16),
            pltpu.VMEM((total, packed_shape(total)[1]), F32),
        ],
        compiler_params=pltpu.CompilerParams(vmem_limit_bytes=VMEM_LIMIT),
        cost_estimate=pl.CostEstimate(
            flops=2 * total * total * count * d,
            bytes_accessed=2 * total * count * d,
            transcendentals=0,
        ),
        name="gram_partial",
    )(*in_turn(blocks, split), energies)


def tree_sum(parts):
    while len(parts) > 1:
        odd = parts[len(parts) // 2 * 2 :]
        parts = [a + b for a, b in zip(parts[::2], parts[1::2])] + odd
    return parts[0]


def pivot_rows(rows, entries):
    count = len(rows)
    rows = list(rows)
    p = [[entries[min(i, l)][max(i, l)] for l in range(count)] for i in range(count)]
    uppers = {}
    for j in range(0, count, 2):
        a, b, c = p[j][j], p[j][j + 1], p[j + 1][j + 1]
        inverse = F32(1.0) / (a * c - b * b)

        def scaled(x, y):
            return (c * x - b * y) * inverse, (a * y - b * x) * inverse

        first, second = rows[j], rows[j + 1]
        rows[j], rows[j + 1] = scaled(first, second)
        later = range(j + 2, count)
        for l in later:
            uppers[j, l], uppers[j + 1, l] = scaled(p[j][l], p[j + 1][l])
        for i in later:
            rows[i] = rows[i] - (p[j][i] * rows[j] + p[j + 1][i] * rows[j + 1])
            for l in range(i, count):
                change = p[j][i] * uppers[j, l] + p[j + 1][i] * uppers[j + 1, l]
                p[i][l] = p[l][i] = p[i][l] - change
    for j in range(count - 4, -1, -2):
        for i in (j, j + 1):
            rows[i] = rows[i] - tree_sum([uppers[i, l] * rows[l] for l in range(j + 2, count)])
    return rows


def eliminate(matrix, total):
    width = matrix.shape[1]
    if total <= 64:
        blocks = [matrix[i : i + PIVOTS] for i in range(0, total, PIVOTS)]
        sub = iota((PIVOTS, width), 0)
        for b in range(len(blocks)):
            spread = [
                [
                    jnp.broadcast_to(block[:, b * PIVOTS + j : b * PIVOTS + j + 1], (PIVOTS, width))
                    for block in blocks
                ]
                for j in range(PIVOTS)
            ]

            def line(value, i):
                return jnp.broadcast_to(value[i : i + 1], (PIVOTS, width))

            entries = [
                [line(spread[l][b], i) if l >= i else None for l in range(PIVOTS)]
                for i in range(PIVOTS)
            ]
            rows = pivot_rows([line(blocks[b], i) for i in range(PIVOTS)], entries)
            for i in range(len(blocks)):
                if i != b:
                    terms = [spread[j][i] * rows[j] for j in range(PIVOTS)]
                    blocks[i] = blocks[i] - tree_sum(terms)
            solved = rows[0]
            for j in range(1, PIVOTS):
                solved = jnp.where(sub == j, rows[j], solved)
            blocks[b] = solved
        return jnp.concatenate([block[:, total : total + 1] for block in blocks], axis=0)
    row = iota(matrix.shape, 0)
    lane = iota(matrix.shape, 1)

    def one(k, held):
        column = jnp.sum(jnp.where(lane == k, held, F32(0.0)), axis=1, keepdims=True)
        pivot_row = jnp.sum(jnp.where(row == k, held, F32(0.0)), axis=0, keepdims=True)
        here = lane[:1] == k
        pivot = jnp.sum(jnp.where(here, pivot_row, F32(0.0)), axis=1, keepdims=True)
        scaled = pivot_row * (F32(1.0) / pivot)
        return held - jnp.where(row == k, F32(0.0), column) * scaled

    matrix = lax.fori_loop(0, total, one, matrix)
    diag = jnp.sum(jnp.where(row == lane, matrix, F32(0.0)), axis=1, keepdims=True)
    return matrix[:, total : total + 1] / diag


def sum_kernel(*refs):
    *part_refs, out_ref = refs
    out_ref[...] = tree_sum([ref[...] for ref in part_refs[::-1]])


def partners(value, masks):
    axes = ("samp", "layer")
    places = lax.axis_size("samp") * lax.axis_size("layer")
    perms = [[(i, i ^ mask) for i in range(places)] for mask in masks[::-1]]
    return [lax.ppermute(value, axes, perm) for perm in perms] + [value]


def sum_over(parts):
    return pl.pallas_call(
        sum_kernel,
        out_shape=jax.ShapeDtypeStruct(parts[0].shape, F32),
        compiler_params=pltpu.CompilerParams(vmem_limit_bytes=VMEM_LIMIT),
        name="sum_over",
    )(*parts)


def rounds(samp, layer):
    masks = [1 << bit for bit in range(1, layer.bit_length() - 1)]
    masks += [layer * (samp - 2), layer]
    masks += [layer << bit for bit in range(1, samp.bit_length() - 2)]
    later = zip(masks[::2], masks[1::2] + [0] * (len(masks) % 2))
    return [[1]] + [[a, b, a ^ b] if b else [a] for a, b in later]


def solve_kernel(sums, owners, *refs):
    sum_refs, (*block_refs, weights_ref, update_ref, held) = refs[:sums], refs[sums:]
    blocks = in_place(block_refs, owners)
    mats, share, d = update_ref.shape
    local = weights_ref.shape[1]
    packed = tree_sum([ref[...] for ref in sum_refs[::-1]])
    half, packed_width = packed.shape
    total = 2 * half
    width = (total // LANES + 1) * LANES
    turned = jnp.swapaxes(packed[:, half:total], 0, 1)
    energy = [packed[:, 3 * half + i : 3 * half + i + 1] for i in range(2)]
    energy = [jnp.broadcast_to(e, (half, width - total)) for e in energy]
    upper = jnp.concatenate([packed[:, :half], turned, energy[0]], axis=1)
    lower = jnp.concatenate([packed[:, half : 3 * half], energy[1]], axis=1)
    raw = jnp.concatenate([upper, lower], axis=0)
    row = iota((total, width), 0)
    lane = iota((total, width), 1)
    inside = lane < total
    scale = F32(1.0 / total)
    row_mean = jnp.sum(jnp.where(inside, raw, F32(0.0)), axis=1, keepdims=True) * scale
    col_mean = jnp.sum(raw, axis=0, keepdims=True) * scale
    mean = jnp.sum(row_mean, axis=0, keepdims=True) * scale
    gram = (raw - col_mean - row_mean + mean) * scale
    eps = (raw - col_mean) * F32(1.0 / total**0.5)
    on_diag = row == lane
    diag = jnp.where(on_diag, raw, F32(0.0))
    trace = jnp.sum(jnp.sum(diag, axis=0, keepdims=True), axis=1, keepdims=True) * scale - mean
    shift = F32(shift_ratio) * trace * scale
    system = jnp.where(inside, gram + jnp.where(on_diag, shift, F32(0.0)), eps)
    weights = eliminate(system, total)
    me = lax.axis_index("samp")
    own = jnp.where(row - me * local == lane, weights, F32(0.0))
    weights_ref[...] = jnp.sum(own, axis=0, keepdims=True)[:, :local]
    coeffs = weights - jnp.sum(weights, axis=0, keepdims=True) * scale
    held[...] = jnp.broadcast_to(coeffs, (total, d))
    acc = jnp.zeros((mats * share, d), F32)
    for k, parts in enumerate(blocks):
        mine = held[pl.ds(pl.multiple_of((me ^ k) * local, local), local)]
        for s in range(local):
            rows = jnp.concatenate([ref[s].astype(F32) for ref in parts], axis=0)
            acc = acc + mine[s : s + 1] * rows
    for m in range(mats):
        update_ref[m] = acc[m * share : (m + 1) * share]


def solve_and_project(sums, blocks, split, mats):
    local, count, d = blocks[0][0].shape
    total = local * len(blocks)
    return pl.pallas_call(
        functools.partial(solve_kernel, len(sums), len(blocks)),
        out_shape=(
            jax.ShapeDtypeStruct((1, local), F32),
            jax.ShapeDtypeStruct((mats, count // mats, d), F32),
        ),
        scratch_shapes=[pltpu.VMEM((total, d), F32)],
        compiler_params=pltpu.CompilerParams(vmem_limit_bytes=VMEM_LIMIT),
        name="solve_and_project",
    )(*sums, *in_turn(blocks, split))


def body(spins, activations, cotangents, offdiag):
    local, mats = activations.shape[:2]
    owners = lax.axis_size("samp")
    total = local * owners
    blocks, split = jac_blocks(activations, cotangents, owners)
    for k, part in turns(owners, split)[:-1]:
        perm = [(i, i ^ k) for i in range(owners)]
        blocks[k][part] = lax.ppermute(blocks[k][part], "samp", perm)
    partial = gram_partial(blocks, split, packed_energy(spins, offdiag, total))
    *early, last = rounds(owners, lax.axis_size("layer"))
    for masks in early:
        partial = sum_over(partners(partial, masks))
    weights, update = solve_and_project(partners(partial, last), blocks, split, mats)
    return weights.reshape(local), update


def solution(mesh):
    placed = (
        P("samp", None),
        P("samp", "layer", None, None),
        P("samp", "layer", None, None),
        P("samp"),
    )
    return jax.shard_map(
        body,
        mesh=mesh,
        in_specs=placed,
        out_specs=(P("samp"), P("layer", "samp", None)),
        check_vma=False,
    )
```

```python
import functools

import jax
import jax.numpy as jnp
from jax import lax
from jax.experimental import pallas as pl
from jax.experimental.pallas import tpu as pltpu
from jax.sharding import PartitionSpec as P

SIDE = 16
LANES = 128
CHUNK = 16
PIVOTS = 8
VMEM_LIMIT = 24 * 2**20
JAC_VMEM_LIMIT = 52 * 2**20
shift_ratio = 0.1
F32 = jnp.float32
BF16 = jnp.bfloat16


def iota(shape, dim):
    return lax.broadcasted_iota(jnp.int32, shape, dim)


def turns(owners, split):
    far, near = list(range(owners // 2, owners)), list(range(owners // 2 - 1, 0, -1))
    cut = split_partners(owners, split)
    order = [(k, part) for part in range(split) for k in cut]
    far = [k for k in far if k not in cut]
    last = far.pop()
    while far or near:
        order += [(k, 0) for k in near[:1] + far[:1]]
        far, near = far[1:], near[1:]
    return order + [(last, 0), (0, 0)]


def split_partners(owners, split):
    return [owners // 2, owners // 2 + 1] if split > 1 else []


def in_turn(blocks, split):
    return [blocks[k][part] for k, part in turns(len(blocks), split)]


def in_place(refs, owners):
    split = 1 + (len(refs) > owners)
    blocks = [[] for _ in range(owners)]
    for (k, _), ref in zip(turns(owners, split), refs):
        blocks[k].append(ref)
    return blocks


def jac_kernel(first_mat, joined, act_hbm, cot_hbm, *refs):
    before, refs = refs[: len(joined)], refs[len(joined) :]
    *out_refs, act_buf, cot_buf, held, sems = refs
    samples, mats, _, d = held.shape
    share = d // len(out_refs)
    me = lax.axis_index("samp")
    group = 2
    copies = []
    for first in range(0, samples, group):
        here = pl.ds(first, group)
        mine = (here, pl.ds(first_mat, mats))
        sem = first // group
        copies.append(pltpu.make_async_copy(act_hbm.at[mine], act_buf.at[here], sems.at[0, sem]))
        copies.append(pltpu.make_async_copy(cot_hbm.at[mine], cot_buf.at[here], sems.at[1, sem]))
    for copy in copies:
        copy.start()
    for k, ref in zip(joined, before):
        out_refs[k][:, : ref.shape[1]] = ref[...]

    def share_out(samples):
        for k, out_ref in enumerate(out_refs):
            owned = pl.ds(pl.multiple_of((me ^ k) * share, share), share)
            for s in samples:
                rows = [held[s, m, owned] for m in range(mats)]
                rows = jnp.concatenate(rows, axis=0).astype(BF16)
                out_ref[s, out_ref.shape[1] - mats * share :] = rows

    for first in range(0, samples, group):
        here = range(first, first + group)
        copies[first].wait()
        copies[first + 1].wait()
        for s in here:
            for m in range(mats):
                held[s, m] = lax.dot_general(
                    act_buf[s, m],
                    cot_buf[s, m],
                    (((0,), (0,)), ((), ())),
                    preferred_element_type=F32,
                ).astype(held.dtype)
        if first > 0:
            share_out(range(first - group, first))
    share_out(range(samples - group, samples))


def jac_rows(activations, cotangents, owners, part, split, before=()):
    samples, mats, sites, d = activations.shape
    mats //= split
    rows = mats * d // owners
    joined = [k for k, block in enumerate(before) if block is not None]
    out_rows = [rows + (before[k].shape[1] if k in joined else 0) for k in range(owners)]
    hbm = pl.BlockSpec(memory_space=pltpu.HBM)
    vmem = pl.BlockSpec(memory_space=pltpu.VMEM)
    return pl.pallas_call(
        functools.partial(jac_kernel, part * mats, joined),
        in_specs=[hbm, hbm] + [vmem] * len(joined),
        out_shape=[jax.ShapeDtypeStruct((samples, count, d), BF16) for count in out_rows],
        scratch_shapes=[
            pltpu.VMEM((samples, mats, sites, d), BF16),
            pltpu.VMEM((samples, mats, sites, d), BF16),
            pltpu.VMEM((samples, mats, d, d), BF16 if d // owners % CHUNK == 0 else F32),
            pltpu.SemaphoreType.DMA((2, samples)),
        ],
        compiler_params=pltpu.CompilerParams(vmem_limit_bytes=JAC_VMEM_LIMIT),
        cost_estimate=pl.CostEstimate(
            flops=2 * samples * mats * sites * d * d,
            bytes_accessed=6 * samples * mats * sites * d,
            transcendentals=0,
        ),
        name="jac_rows",
    )(activations, cotangents, *[before[k] for k in joined])


def jac_blocks(activations, cotangents, owners):
    mats, d = activations.shape[1], activations.shape[3]
    split = mats if mats == 2 and d // owners % CHUNK == 0 else 1
    blocks = [[block] for block in jac_rows(activations, cotangents, owners, 0, split)]
    if split > 1:
        cut = split_partners(owners, split)
        before = [None if k in cut else block[0] for k, block in enumerate(blocks)]
        later = jac_rows(activations, cotangents, owners, 1, split, before)
        blocks = [b + [new] if k in cut else [new] for k, (b, new) in enumerate(zip(blocks, later))]
    return blocks, split


def packed_shape(total):
    half = total // 2
    return half, -(-(3 * half + 2) // LANES) * LANES


def energy_kernel(total, spins_ref, offdiag_ref, out_ref):
    shape = out_ref.shape
    local = spins_ref.shape[0]
    sites = SIDE * SIDE
    z = (2 * spins_ref[...] - 1).astype(F32)
    column = iota((local, sites), 1) % SIDE
    right = jnp.where(
        column == SIDE - 1, pltpu.roll(z, SIDE - 1, 1), pltpu.roll(z, sites - 1, 1)
    )
    below = pltpu.roll(z, sites - SIDE, 1)
    energy = offdiag_ref[...] + jnp.sum(z * (right + below), axis=1, keepdims=True)
    half = total // 2
    first = lax.axis_index("samp") * local
    lower = first // half
    first = first - lower * half
    spread = jnp.concatenate([energy] * (half // local), axis=0)
    row = iota(shape, 0)
    here = (row >= first) & (row < first + local) & (iota(shape, 1) == 3 * half + lower)
    here = here & (lax.axis_index("layer") == 0)
    out_ref[...] = jnp.where(here, spread, F32(0.0))


def packed_energy(spins, offdiag, total):
    return pl.pallas_call(
        functools.partial(energy_kernel, total),
        out_shape=jax.ShapeDtypeStruct(packed_shape(total), F32),
        compiler_params=pltpu.CompilerParams(vmem_limit_bytes=VMEM_LIMIT),
        name="packed_energy",
    )(spins, offdiag[:, None])


def rows_of(parts, row, rows):
    for ref in parts:
        if row < ref.shape[1]:
            return ref[:, row : row + rows]
        row -= ref.shape[1]


def swap_matrix(local, me):
    joined = CHUNK // local
    block = CHUNK * CHUNK
    dest = iota((block, block), 0)
    sample = dest % CHUNK
    sample = (sample // local ^ me % joined) * local + sample % local
    source = sample * CHUNK + dest // CHUNK
    return (iota((block, block), 1) == source).astype(F32).astype(BF16)


def turned(swap, group, row, d):
    pieces = [rows_of(parts, row, CHUNK) for parts in group]
    piece = jnp.concatenate(pieces, axis=0).reshape(CHUNK * CHUNK, d)
    return jnp.dot(swap, piece, preferred_element_type=F32).astype(BF16)


def products(left, right):
    return lax.dot_general(left, right, (((1,), (1,)), ((), ())), preferred_element_type=F32)


def early_kernel(order, joined, *refs):
    *block_refs, flat, gram_ref = refs
    blocks = {k: [] for k, _ in order}
    for (k, _), ref in zip(order, block_refs):
        blocks[k].append(ref)
    count, total, d = flat.shape
    owners = len(blocks) + joined
    me = lax.axis_index("samp")
    swap = swap_matrix(CHUNK // joined, me)
    for j in range(owners // joined):
        place = pl.ds(pl.multiple_of((me // joined ^ j) * CHUNK, CHUNK), CHUNK)
        group = [blocks.get(k) for k in range(j * joined, (j + 1) * joined)]
        for row in range(0, count, CHUNK):
            if group[0] is None:
                flat[row : row + CHUNK, place] = jnp.zeros((CHUNK, CHUNK, d), BF16)
                continue
            rows = turned(swap, group, row, d)
            for r in range(CHUNK):
                flat[row + r, place] = rows[r * CHUNK : (r + 1) * CHUNK]
    lined = jnp.concatenate([flat[r] for r in range(count)], axis=1)
    gram = products(lined, lined)
    gram_ref[...] = jnp.zeros_like(gram_ref)
    gram_ref[:, :total] += gram


def late_kernel(owners, *refs):
    *block_refs, flat, gram_ref, energy_ref, out_ref, whole, edge = refs
    count, total, d = flat.shape
    joined = len(block_refs)
    me = lax.axis_index("samp")
    swap = swap_matrix(CHUNK // joined, me)
    group = [[ref] for ref in block_refs]
    late = []
    for row in range(0, count, CHUNK):
        rows = turned(swap, group, row, d)
        late += [rows[r * CHUNK : (r + 1) * CHUNK] for r in range(CHUNK)]
    late = jnp.concatenate(late, axis=1)
    lined = jnp.concatenate([flat[r] for r in range(count)], axis=1)
    edge[...] = jnp.zeros_like(edge)
    edge[:total, :CHUNK] += products(lined, late)
    edge[total:, :CHUNK] += products(late, late)
    first = (me // joined ^ (owners // joined - 1)) * CHUNK
    moved = pltpu.roll(edge[...], first, 1)
    columns = moved[:total]
    whole[...] = gram_ref[...] + columns
    whole[:, :total] += jnp.swapaxes(columns[:, :total], 0, 1)
    whole[pl.ds(pl.multiple_of(first, CHUNK), CHUNK)] += moved[total:]
    half, width = out_ref.shape
    lane = iota((half, width), 1)
    lower = pltpu.roll(whole[half:], half, 1)
    packed = jnp.where(lane < 3 * half, lower, energy_ref[...])
    out_ref[...] = jnp.where(lane < half, whole[:half], packed)


def gram_partial(blocks, split, energies):
    owners = len(blocks)
    local, count, d = blocks[0][0].shape
    total = local * owners
    joined = CHUNK // local
    order = [(k, part) for k, part in turns(owners, split) if k < owners - joined]
    width = packed_shape(total)[1]
    params = pltpu.CompilerParams(vmem_limit_bytes=VMEM_LIMIT)
    flat, gram = pl.pallas_call(
        functools.partial(early_kernel, order, joined),
        out_shape=(
            jax.ShapeDtypeStruct((count, total, d), BF16),
            jax.ShapeDtypeStruct((total, width), F32),
        ),
        compiler_params=params,
        cost_estimate=pl.CostEstimate(
            flops=2 * total * total * count * d,
            bytes_accessed=2 * total * count * d,
            transcendentals=0,
        ),
        name="gram_early",
    )(*[blocks[k][part] for k, part in order])
    return pl.pallas_call(
        functools.partial(late_kernel, owners),
        out_shape=jax.ShapeDtypeStruct(packed_shape(total), F32),
        scratch_shapes=[
            pltpu.VMEM((total, width), F32),
            pltpu.VMEM((total + CHUNK, width), F32),
        ],
        compiler_params=params,
        cost_estimate=pl.CostEstimate(
            flops=2 * total * CHUNK * count * d,
            bytes_accessed=2 * total * count * d,
            transcendentals=0,
        ),
        name="gram_late",
    )(*[blocks[k][0] for k in range(owners - joined, owners)], flat, gram, energies)


def tree_sum(parts):
    while len(parts) > 1:
        odd = parts[len(parts) // 2 * 2 :]
        parts = [a + b for a, b in zip(parts[::2], parts[1::2])] + odd
    return parts[0]


def pivot_rows(rows, entries):
    count = len(rows)
    rows = list(rows)
    p = [[entries[min(i, l)][max(i, l)] for l in range(count)] for i in range(count)]
    uppers = {}
    for j in range(0, count, 2):
        a, b, c = p[j][j], p[j][j + 1], p[j + 1][j + 1]
        inverse = F32(1.0) / (a * c - b * b)

        def scaled(x, y):
            return (c * x - b * y) * inverse, (a * y - b * x) * inverse

        first, second = rows[j], rows[j + 1]
        rows[j], rows[j + 1] = scaled(first, second)
        later = range(j + 2, count)
        for l in later:
            uppers[j, l], uppers[j + 1, l] = scaled(p[j][l], p[j + 1][l])
        for i in later:
            rows[i] = rows[i] - (p[j][i] * rows[j] + p[j + 1][i] * rows[j + 1])
            for l in range(i, count):
                change = p[j][i] * uppers[j, l] + p[j + 1][i] * uppers[j + 1, l]
                p[i][l] = p[l][i] = p[i][l] - change
    for j in range(count - 4, -1, -2):
        for i in (j, j + 1):
            rows[i] = rows[i] - tree_sum([uppers[i, l] * rows[l] for l in range(j + 2, count)])
    return rows


def eliminate(matrix, total):
    width = matrix.shape[1]
    if total <= 64:
        blocks = [matrix[i : i + PIVOTS] for i in range(0, total, PIVOTS)]
        sub = iota((PIVOTS, width), 0)
        for b in range(len(blocks)):
            spread = [
                [
                    jnp.broadcast_to(block[:, b * PIVOTS + j : b * PIVOTS + j + 1], (PIVOTS, width))
                    for block in blocks
                ]
                for j in range(PIVOTS)
            ]

            def line(value, i):
                return jnp.broadcast_to(value[i : i + 1], (PIVOTS, width))

            entries = [
                [line(spread[l][b], i) if l >= i else None for l in range(PIVOTS)]
                for i in range(PIVOTS)
            ]
            rows = pivot_rows([line(blocks[b], i) for i in range(PIVOTS)], entries)
            for i in range(len(blocks)):
                if i != b:
                    terms = [spread[j][i] * rows[j] for j in range(PIVOTS)]
                    blocks[i] = blocks[i] - tree_sum(terms)
            solved = rows[0]
            for j in range(1, PIVOTS):
                solved = jnp.where(sub == j, rows[j], solved)
            blocks[b] = solved
        return jnp.concatenate([block[:, total : total + 1] for block in blocks], axis=0)
    row = iota(matrix.shape, 0)
    lane = iota(matrix.shape, 1)

    def one(k, held):
        column = jnp.sum(jnp.where(lane == k, held, F32(0.0)), axis=1, keepdims=True)
        pivot_row = jnp.sum(jnp.where(row == k, held, F32(0.0)), axis=0, keepdims=True)
        here = lane[:1] == k
        pivot = jnp.sum(jnp.where(here, pivot_row, F32(0.0)), axis=1, keepdims=True)
        scaled = pivot_row * (F32(1.0) / pivot)
        return held - jnp.where(row == k, F32(0.0), column) * scaled

    matrix = lax.fori_loop(0, total, one, matrix)
    diag = jnp.sum(jnp.where(row == lane, matrix, F32(0.0)), axis=1, keepdims=True)
    return matrix[:, total : total + 1] / diag


def sum_kernel(*refs):
    *part_refs, out_ref = refs
    out_ref[...] = tree_sum([ref[...] for ref in part_refs[::-1]])


def partners(value, masks):
    axes = ("samp", "layer")
    places = lax.axis_size("samp") * lax.axis_size("layer")
    perms = [[(i, i ^ mask) for i in range(places)] for mask in masks[::-1]]
    return [lax.ppermute(value, axes, perm) for perm in perms] + [value]


def sum_over(parts):
    return pl.pallas_call(
        sum_kernel,
        out_shape=jax.ShapeDtypeStruct(parts[0].shape, F32),
        compiler_params=pltpu.CompilerParams(vmem_limit_bytes=VMEM_LIMIT),
        name="sum_over",
    )(*parts)


def rounds(samp, layer):
    masks = [1 << bit for bit in range(1, layer.bit_length() - 1)]
    masks += [layer * (samp - 2), layer]
    masks += [layer << bit for bit in range(1, samp.bit_length() - 2)]
    later = zip(masks[::2], masks[1::2] + [0] * (len(masks) % 2))
    return [[1]] + [[a, b, a ^ b] if b else [a] for a, b in later]


def solve_kernel(sums, owners, *refs):
    sum_refs, (*block_refs, weights_ref, update_ref, held) = refs[:sums], refs[sums:]
    blocks = in_place(block_refs, owners)
    mats, share, d = update_ref.shape
    local = weights_ref.shape[1]
    packed = tree_sum([ref[...] for ref in sum_refs[::-1]])
    half, packed_width = packed.shape
    total = 2 * half
    width = (total // LANES + 1) * LANES
    turned = jnp.swapaxes(packed[:, half:total], 0, 1)
    energy = [packed[:, 3 * half + i : 3 * half + i + 1] for i in range(2)]
    energy = [jnp.broadcast_to(e, (half, width - total)) for e in energy]
    upper = jnp.concatenate([packed[:, :half], turned, energy[0]], axis=1)
    lower = jnp.concatenate([packed[:, half : 3 * half], energy[1]], axis=1)
    raw = jnp.concatenate([upper, lower], axis=0)
    row = iota((total, width), 0)
    lane = iota((total, width), 1)
    inside = lane < total
    scale = F32(1.0 / total)
    row_mean = jnp.sum(jnp.where(inside, raw, F32(0.0)), axis=1, keepdims=True) * scale
    col_mean = jnp.sum(raw, axis=0, keepdims=True) * scale
    mean = jnp.sum(row_mean, axis=0, keepdims=True) * scale
    gram = (raw - col_mean - row_mean + mean) * scale
    eps = (raw - col_mean) * F32(1.0 / total**0.5)
    on_diag = row == lane
    diag = jnp.where(on_diag, raw, F32(0.0))
    trace = jnp.sum(jnp.sum(diag, axis=0, keepdims=True), axis=1, keepdims=True) * scale - mean
    shift = F32(shift_ratio) * trace * scale
    system = jnp.where(inside, gram + jnp.where(on_diag, shift, F32(0.0)), eps)
    weights = eliminate(system, total)
    me = lax.axis_index("samp")
    own = jnp.where(row - me * local == lane, weights, F32(0.0))
    weights_ref[...] = jnp.sum(own, axis=0, keepdims=True)[:, :local]
    coeffs = weights - jnp.sum(weights, axis=0, keepdims=True) * scale
    held[...] = jnp.broadcast_to(coeffs, (total, d))
    acc = jnp.zeros((mats * share, d), F32)
    for k, parts in enumerate(blocks):
        mine = held[pl.ds(pl.multiple_of((me ^ k) * local, local), local)]
        for s in range(local):
            rows = jnp.concatenate([ref[s].astype(F32) for ref in parts], axis=0)
            acc = acc + mine[s : s + 1] * rows
    for m in range(mats):
        update_ref[m] = acc[m * share : (m + 1) * share]


def solve_and_project(sums, blocks, split, mats):
    local, count, d = blocks[0][0].shape
    total = local * len(blocks)
    return pl.pallas_call(
        functools.partial(solve_kernel, len(sums), len(blocks)),
        out_shape=(
            jax.ShapeDtypeStruct((1, local), F32),
            jax.ShapeDtypeStruct((mats, count // mats, d), F32),
        ),
        scratch_shapes=[pltpu.VMEM((total, d), F32)],
        compiler_params=pltpu.CompilerParams(vmem_limit_bytes=VMEM_LIMIT),
        name="solve_and_project",
    )(*sums, *in_turn(blocks, split))


def body(spins, activations, cotangents, offdiag):
    local, mats = activations.shape[:2]
    owners = lax.axis_size("samp")
    total = local * owners
    blocks, split = jac_blocks(activations, cotangents, owners)
    for k, part in turns(owners, split)[:-1]:
        perm = [(i, i ^ k) for i in range(owners)]
        blocks[k][part] = lax.ppermute(blocks[k][part], "samp", perm)
    partial = gram_partial(blocks, split, packed_energy(spins, offdiag, total))
    *early, last = rounds(owners, lax.axis_size("layer"))
    for masks in early:
        partial = sum_over(partners(partial, masks))
    weights, update = solve_and_project(partners(partial, last), blocks, split, mats)
    return weights.reshape(local), update


def solution(mesh):
    placed = (
        P("samp", None),
        P("samp", "layer", None, None),
        P("samp", "layer", None, None),
        P("samp"),
    )
    return jax.shard_map(
        body,
        mesh=mesh,
        in_specs=placed,
        out_specs=(P("samp"), P("layer", "samp", None)),
        check_vma=False,
    )
```

```python
import functools

import jax
import jax.numpy as jnp
from jax import lax
from jax.experimental import pallas as pl
from jax.experimental.pallas import tpu as pltpu
from jax.sharding import PartitionSpec as P

SIDE = 16
LANES = 128
CHUNK = 16
PIVOTS = 8
VMEM_LIMIT = 24 * 2**20
JAC_VMEM_LIMIT = 52 * 2**20
shift_ratio = 0.1
F32 = jnp.float32
BF16 = jnp.bfloat16


def iota(shape, dim):
    return lax.broadcasted_iota(jnp.int32, shape, dim)


def turns(owners, split):
    far, near = list(range(owners // 2, owners)), list(range(owners // 2 - 1, 0, -1))
    cut = split_partners(owners, split)
    order = [(k, part) for part in range(split) for k in cut]
    far = [k for k in far if k not in cut]
    while far or near:
        order += [(k, 0) for k in near[:1] + far[:1]]
        far, near = far[1:], near[1:]
    return order + [(0, 0)]


def split_partners(owners, split):
    return [owners // 2, owners // 2 + 1] if split > 1 else []


def in_turn(blocks, split):
    return [blocks[k][part] for k, part in turns(len(blocks), split)]


def in_place(refs, owners):
    split = 1 + (len(refs) > owners)
    blocks = [[] for _ in range(owners)]
    for (k, _), ref in zip(turns(owners, split), refs):
        blocks[k].append(ref)
    return blocks


def jac_kernel(first_mat, joined, act_hbm, cot_hbm, *refs):
    before, refs = refs[: len(joined)], refs[len(joined) :]
    *out_refs, act_buf, cot_buf, held, sems = refs
    samples, mats, _, d = held.shape
    share = d // len(out_refs)
    me = lax.axis_index("samp")
    group = 2
    copies = []
    for first in range(0, samples, group):
        here = pl.ds(first, group)
        mine = (here, pl.ds(first_mat, mats))
        sem = first // group
        copies.append(pltpu.make_async_copy(act_hbm.at[mine], act_buf.at[here], sems.at[0, sem]))
        copies.append(pltpu.make_async_copy(cot_hbm.at[mine], cot_buf.at[here], sems.at[1, sem]))
    for copy in copies:
        copy.start()
    for k, ref in zip(joined, before):
        out_refs[k][:, : ref.shape[1]] = ref[...]

    def share_out(samples):
        for k, out_ref in enumerate(out_refs):
            owned = pl.ds(pl.multiple_of((me ^ k) * share, share), share)
            for s in samples:
                rows = [held[s, m, owned] for m in range(mats)]
                rows = jnp.concatenate(rows, axis=0).astype(BF16)
                out_ref[s, out_ref.shape[1] - mats * share :] = rows

    for first in range(0, samples, group):
        here = range(first, first + group)
        copies[first].wait()
        copies[first + 1].wait()
        for s in here:
            for m in range(mats):
                held[s, m] = lax.dot_general(
                    act_buf[s, m],
                    cot_buf[s, m],
                    (((0,), (0,)), ((), ())),
                    preferred_element_type=F32,
                ).astype(held.dtype)
        if first > 0:
            share_out(range(first - group, first))
    share_out(range(samples - group, samples))


def jac_rows(activations, cotangents, owners, part, split, before=()):
    samples, mats, sites, d = activations.shape
    mats //= split
    rows = mats * d // owners
    joined = [k for k, block in enumerate(before) if block is not None]
    out_rows = [rows + (before[k].shape[1] if k in joined else 0) for k in range(owners)]
    hbm = pl.BlockSpec(memory_space=pltpu.HBM)
    vmem = pl.BlockSpec(memory_space=pltpu.VMEM)
    return pl.pallas_call(
        functools.partial(jac_kernel, part * mats, joined),
        in_specs=[hbm, hbm] + [vmem] * len(joined),
        out_shape=[jax.ShapeDtypeStruct((samples, count, d), BF16) for count in out_rows],
        scratch_shapes=[
            pltpu.VMEM((samples, mats, sites, d), BF16),
            pltpu.VMEM((samples, mats, sites, d), BF16),
            pltpu.VMEM((samples, mats, d, d), BF16 if d // owners % CHUNK == 0 else F32),
            pltpu.SemaphoreType.DMA((2, samples)),
        ],
        compiler_params=pltpu.CompilerParams(vmem_limit_bytes=JAC_VMEM_LIMIT),
        cost_estimate=pl.CostEstimate(
            flops=2 * samples * mats * sites * d * d,
            bytes_accessed=6 * samples * mats * sites * d,
            transcendentals=0,
        ),
        name="jac_rows",
    )(activations, cotangents, *[before[k] for k in joined])


def jac_blocks(activations, cotangents, owners):
    mats, d = activations.shape[1], activations.shape[3]
    split = mats if mats == 2 and d // owners % CHUNK == 0 else 1
    blocks = [[block] for block in jac_rows(activations, cotangents, owners, 0, split)]
    if split > 1:
        cut = split_partners(owners, split)
        before = [None if k in cut else block[0] for k, block in enumerate(blocks)]
        later = jac_rows(activations, cotangents, owners, 1, split, before)
        blocks = [b + [new] if k in cut else [new] for k, (b, new) in enumerate(zip(blocks, later))]
    return blocks, split


def packed_shape(total):
    half = total // 2
    return half, -(-(3 * half + 2) // LANES) * LANES


def energy_kernel(total, spins_ref, offdiag_ref, out_ref):
    shape = out_ref.shape
    local = spins_ref.shape[0]
    sites = SIDE * SIDE
    z = (2 * spins_ref[...] - 1).astype(F32)
    column = iota((local, sites), 1) % SIDE
    right = jnp.where(
        column == SIDE - 1, pltpu.roll(z, SIDE - 1, 1), pltpu.roll(z, sites - 1, 1)
    )
    below = pltpu.roll(z, sites - SIDE, 1)
    energy = offdiag_ref[...] + jnp.sum(z * (right + below), axis=1, keepdims=True)
    half = total // 2
    first = lax.axis_index("samp") * local
    lower = first // half
    first = first - lower * half
    spread = jnp.concatenate([energy] * (half // local), axis=0)
    row = iota(shape, 0)
    here = (row >= first) & (row < first + local) & (iota(shape, 1) == 3 * half + lower)
    here = here & (lax.axis_index("layer") == 0)
    out_ref[...] = jnp.where(here, spread, F32(0.0))


def packed_energy(spins, offdiag, total):
    return pl.pallas_call(
        functools.partial(energy_kernel, total),
        out_shape=jax.ShapeDtypeStruct(packed_shape(total), F32),
        compiler_params=pltpu.CompilerParams(vmem_limit_bytes=VMEM_LIMIT),
        name="packed_energy",
    )(spins, offdiag[:, None])


def rows_of(parts, row, rows):
    for ref in parts:
        if row < ref.shape[1]:
            return ref[:, row : row + rows]
        row -= ref.shape[1]


def gram_kernel(owners, *refs):
    *block_refs, energy_ref, out_ref, flat, whole = refs
    blocks = in_place(block_refs, owners)
    local, count, d = blocks[0][0].shape
    total = local * owners
    joined = CHUNK // local
    me = lax.axis_index("samp")
    block = CHUNK * CHUNK
    dest = iota((block, block), 0)
    sample = dest % CHUNK
    sample = (sample // local ^ me % joined) * local + sample % local
    source = sample * CHUNK + dest // CHUNK
    swap = (iota((block, block), 1) == source).astype(F32).astype(BF16)
    for row in range(0, count, CHUNK):
        for j in range(owners // joined):
            pieces = [rows_of(p, row, CHUNK) for p in blocks[j * joined : (j + 1) * joined]]
            piece = jnp.concatenate(pieces, axis=0).reshape(block, d)
            turned = jnp.dot(swap, piece, preferred_element_type=F32).astype(BF16)
            place = pl.ds(pl.multiple_of((me // joined ^ j) * CHUNK, CHUNK), CHUNK)
            for r in range(CHUNK):
                flat[row + r, place] = turned[r * CHUNK : (r + 1) * CHUNK]
    lined = jnp.concatenate([flat[r] for r in range(count)], axis=1)
    gram = lax.dot_general(lined, lined, (((1,), (1,)), ((), ())), preferred_element_type=F32)
    whole[...] = jnp.zeros_like(whole)
    whole[:, :total] += gram
    half, width = out_ref.shape
    lane = iota((half, width), 1)
    lower = pltpu.roll(whole[half:], half, 1)
    packed = jnp.where(lane < 3 * half, lower, energy_ref[...])
    out_ref[...] = jnp.where(lane < half, whole[:half], packed)


def gram_partial(blocks, split, energies):
    local, count, d = blocks[0][0].shape
    total = local * len(blocks)
    return pl.pallas_call(
        functools.partial(gram_kernel, len(blocks)),
        out_shape=jax.ShapeDtypeStruct(packed_shape(total), F32),
        scratch_shapes=[
            pltpu.VMEM((count, total, d), BF16),
            pltpu.VMEM((total, packed_shape(total)[1]), F32),
        ],
        compiler_params=pltpu.CompilerParams(vmem_limit_bytes=VMEM_LIMIT),
        cost_estimate=pl.CostEstimate(
            flops=2 * total * total * count * d,
            bytes_accessed=2 * total * count * d,
            transcendentals=0,
        ),
        name="gram_partial",
    )(*in_turn(blocks, split), energies)


def tree_sum(parts):
    while len(parts) > 1:
        odd = parts[len(parts) // 2 * 2 :]
        parts = [a + b for a, b in zip(parts[::2], parts[1::2])] + odd
    return parts[0]


def pivot_rows(rows, entries):
    count = len(rows)
    rows = list(rows)
    p = [[entries[min(i, l)][max(i, l)] for l in range(count)] for i in range(count)]
    uppers = {}
    for j in range(0, count, 2):
        a, b, c = p[j][j], p[j][j + 1], p[j + 1][j + 1]
        inverse = F32(1.0) / (a * c - b * b)

        def scaled(x, y):
            return (c * x - b * y) * inverse, (a * y - b * x) * inverse

        first, second = rows[j], rows[j + 1]
        rows[j], rows[j + 1] = scaled(first, second)
        later = range(j + 2, count)
        for l in later:
            uppers[j, l], uppers[j + 1, l] = scaled(p[j][l], p[j + 1][l])
        for i in later:
            rows[i] = rows[i] - (p[j][i] * rows[j] + p[j + 1][i] * rows[j + 1])
            for l in range(i, count):
                change = p[j][i] * uppers[j, l] + p[j + 1][i] * uppers[j + 1, l]
                p[i][l] = p[l][i] = p[i][l] - change
    for j in range(count - 4, -1, -2):
        for i in (j, j + 1):
            rows[i] = rows[i] - tree_sum([uppers[i, l] * rows[l] for l in range(j + 2, count)])
    return rows


def eliminate(matrix, total):
    width = matrix.shape[1]
    if total <= 64:
        blocks = [matrix[i : i + PIVOTS] for i in range(0, total, PIVOTS)]
        sub = iota((PIVOTS, width), 0)
        for b in range(len(blocks)):
            spread = [
                [
                    jnp.broadcast_to(block[:, b * PIVOTS + j : b * PIVOTS + j + 1], (PIVOTS, width))
                    for block in blocks
                ]
                for j in range(PIVOTS)
            ]

            def line(value, i):
                return jnp.broadcast_to(value[i : i + 1], (PIVOTS, width))

            entries = [
                [line(spread[l][b], i) if l >= i else None for l in range(PIVOTS)]
                for i in range(PIVOTS)
            ]
            rows = pivot_rows([line(blocks[b], i) for i in range(PIVOTS)], entries)
            for i in range(len(blocks)):
                if i != b:
                    terms = [spread[j][i] * rows[j] for j in range(PIVOTS)]
                    blocks[i] = blocks[i] - tree_sum(terms)
            solved = rows[0]
            for j in range(1, PIVOTS):
                solved = jnp.where(sub == j, rows[j], solved)
            blocks[b] = solved
        return jnp.concatenate([block[:, total : total + 1] for block in blocks], axis=0)
    row = iota(matrix.shape, 0)
    lane = iota(matrix.shape, 1)

    def one(k, held):
        column = jnp.sum(jnp.where(lane == k, held, F32(0.0)), axis=1, keepdims=True)
        pivot_row = jnp.sum(jnp.where(row == k, held, F32(0.0)), axis=0, keepdims=True)
        here = lane[:1] == k
        pivot = jnp.sum(jnp.where(here, pivot_row, F32(0.0)), axis=1, keepdims=True)
        scaled = pivot_row * (F32(1.0) / pivot)
        return held - jnp.where(row == k, F32(0.0), column) * scaled

    matrix = lax.fori_loop(0, total, one, matrix)
    diag = jnp.sum(jnp.where(row == lane, matrix, F32(0.0)), axis=1, keepdims=True)
    return matrix[:, total : total + 1] / diag


def sum_kernel(*refs):
    *part_refs, out_ref = refs
    out_ref[...] = tree_sum([ref[...] for ref in part_refs[::-1]])


def partners(value, masks):
    axes = ("samp", "layer")
    places = lax.axis_size("samp") * lax.axis_size("layer")
    perms = [[(i, i ^ mask) for i in range(places)] for mask in masks[::-1]]
    return [lax.ppermute(value, axes, perm) for perm in perms] + [value]


def sum_over(parts):
    return pl.pallas_call(
        sum_kernel,
        out_shape=jax.ShapeDtypeStruct(parts[0].shape, F32),
        compiler_params=pltpu.CompilerParams(vmem_limit_bytes=VMEM_LIMIT),
        name="sum_over",
    )(*parts)


def rounds(samp, layer):
    masks = [1 << bit for bit in range(1, layer.bit_length() - 1)]
    masks += [layer * (samp - 2), layer]
    masks += [layer << bit for bit in range(1, samp.bit_length() - 2)]
    later = zip(masks[::2], masks[1::2] + [0] * (len(masks) % 2))
    later = [[a, b, a ^ b] if b else [a] for a, b in later]
    return [[1]] + [[mask ^ 1 for mask in masks] for masks in later]


def solve_kernel(sums, owners, *refs):
    sum_refs, (*block_refs, weights_ref, update_ref, held) = refs[:sums], refs[sums:]
    blocks = in_place(block_refs, owners)
    mats, share, d = update_ref.shape
    local = weights_ref.shape[1]
    packed = tree_sum([ref[...] for ref in sum_refs[::-1]])
    half, packed_width = packed.shape
    total = 2 * half
    width = (total // LANES + 1) * LANES
    turned = jnp.swapaxes(packed[:, half:total], 0, 1)
    energy = [packed[:, 3 * half + i : 3 * half + i + 1] for i in range(2)]
    energy = [jnp.broadcast_to(e, (half, width - total)) for e in energy]
    upper = jnp.concatenate([packed[:, :half], turned, energy[0]], axis=1)
    lower = jnp.concatenate([packed[:, half : 3 * half], energy[1]], axis=1)
    raw = jnp.concatenate([upper, lower], axis=0)
    row = iota((total, width), 0)
    lane = iota((total, width), 1)
    inside = lane < total
    scale = F32(1.0 / total)
    row_mean = jnp.sum(jnp.where(inside, raw, F32(0.0)), axis=1, keepdims=True) * scale
    col_mean = jnp.sum(raw, axis=0, keepdims=True) * scale
    mean = jnp.sum(row_mean, axis=0, keepdims=True) * scale
    gram = (raw - col_mean - row_mean + mean) * scale
    eps = (raw - col_mean) * F32(1.0 / total**0.5)
    on_diag = row == lane
    diag = jnp.where(on_diag, raw, F32(0.0))
    trace = jnp.sum(jnp.sum(diag, axis=0, keepdims=True), axis=1, keepdims=True) * scale - mean
    shift = F32(shift_ratio) * trace * scale
    system = jnp.where(inside, gram + jnp.where(on_diag, shift, F32(0.0)), eps)
    weights = eliminate(system, total)
    me = lax.axis_index("samp")
    own = jnp.where(row - me * local == lane, weights, F32(0.0))
    weights_ref[...] = jnp.sum(own, axis=0, keepdims=True)[:, :local]
    coeffs = weights - jnp.sum(weights, axis=0, keepdims=True) * scale
    held[...] = jnp.broadcast_to(coeffs, (total, d))
    acc = jnp.zeros((mats * share, d), F32)
    for k, parts in enumerate(blocks):
        mine = held[pl.ds(pl.multiple_of((me ^ k) * local, local), local)]
        for s in range(local):
            rows = jnp.concatenate([ref[s].astype(F32) for ref in parts], axis=0)
            acc = acc + mine[s : s + 1] * rows
    for m in range(mats):
        update_ref[m] = acc[m * share : (m + 1) * share]


def solve_and_project(sums, blocks, split, mats):
    local, count, d = blocks[0][0].shape
    total = local * len(blocks)
    return pl.pallas_call(
        functools.partial(solve_kernel, len(sums), len(blocks)),
        out_shape=(
            jax.ShapeDtypeStruct((1, local), F32),
            jax.ShapeDtypeStruct((mats, count // mats, d), F32),
        ),
        scratch_shapes=[pltpu.VMEM((total, d), F32)],
        compiler_params=pltpu.CompilerParams(vmem_limit_bytes=VMEM_LIMIT),
        name="solve_and_project",
    )(*sums, *in_turn(blocks, split))


def body(spins, activations, cotangents, offdiag):
    local, mats = activations.shape[:2]
    owners = lax.axis_size("samp")
    total = local * owners
    blocks, split = jac_blocks(activations, cotangents, owners)
    for k, part in turns(owners, split)[:-1]:
        perm = [(i, i ^ k) for i in range(owners)]
        blocks[k][part] = lax.ppermute(blocks[k][part], "samp", perm)
    partial = gram_partial(blocks, split, packed_energy(spins, offdiag, total))
    *early, last = rounds(owners, lax.axis_size("layer"))
    for masks in early:
        partial = sum_over(partners(partial, masks))
    weights, update = solve_and_project(partners(partial, last), blocks, split, mats)
    return weights.reshape(local), update


def solution(mesh):
    placed = (
        P("samp", None),
        P("samp", "layer", None, None),
        P("samp", "layer", None, None),
        P("samp"),
    )
    return jax.shard_map(
        body,
        mesh=mesh,
        in_specs=placed,
        out_specs=(P("samp"), P("layer", "samp", None)),
        check_vma=False,
    )
```

```python
import functools

import jax
import jax.numpy as jnp
from jax import lax
from jax.experimental import pallas as pl
from jax.experimental.pallas import tpu as pltpu
from jax.sharding import PartitionSpec as P

SIDE = 16
LANES = 128
CHUNK = 16
PIVOTS = 8
VMEM_LIMIT = 24 * 2**20
JAC_VMEM_LIMIT = 52 * 2**20
shift_ratio = 0.1
F32 = jnp.float32
BF16 = jnp.bfloat16


def iota(shape, dim):
    return lax.broadcasted_iota(jnp.int32, shape, dim)


def turns(owners, split):
    far, near = list(range(owners // 2, owners)), list(range(owners // 2 - 1, 0, -1))
    cut = split_partners(owners, split)
    order = [(k, part) for part in range(split) for k in cut]
    far = [k for k in far if k not in cut]
    while far or near:
        order += [(k, 0) for k in near[:1] + far[:1]]
        far, near = far[1:], near[1:]
    return order + [(0, 0)]


def split_partners(owners, split):
    return [owners - 2, owners // 2] if split > 1 else []


def in_turn(blocks, split):
    return [blocks[k][part] for k, part in turns(len(blocks), split)]


def in_place(refs, owners):
    split = 1 + (len(refs) > owners)
    blocks = [[] for _ in range(owners)]
    for (k, _), ref in zip(turns(owners, split), refs):
        blocks[k].append(ref)
    return blocks


def jac_kernel(first_mat, joined, act_hbm, cot_hbm, *refs):
    before, refs = refs[: len(joined)], refs[len(joined) :]
    *out_refs, act_buf, cot_buf, held, sems = refs
    samples, mats, _, d = held.shape
    share = d // len(out_refs)
    me = lax.axis_index("samp")
    group = 2
    copies = []
    for first in range(0, samples, group):
        here = pl.ds(first, group)
        mine = (here, pl.ds(first_mat, mats))
        sem = first // group
        copies.append(pltpu.make_async_copy(act_hbm.at[mine], act_buf.at[here], sems.at[0, sem]))
        copies.append(pltpu.make_async_copy(cot_hbm.at[mine], cot_buf.at[here], sems.at[1, sem]))
    for copy in copies:
        copy.start()
    for k, ref in zip(joined, before):
        out_refs[k][:, : ref.shape[1]] = ref[...]

    def share_out(samples):
        for k, out_ref in enumerate(out_refs):
            owned = pl.ds(pl.multiple_of((me ^ k) * share, share), share)
            for s in samples:
                rows = [held[s, m, owned] for m in range(mats)]
                rows = jnp.concatenate(rows, axis=0).astype(BF16)
                out_ref[s, out_ref.shape[1] - mats * share :] = rows

    for first in range(0, samples, group):
        here = range(first, first + group)
        copies[first].wait()
        copies[first + 1].wait()
        for s in here:
            for m in range(mats):
                held[s, m] = lax.dot_general(
                    act_buf[s, m],
                    cot_buf[s, m],
                    (((0,), (0,)), ((), ())),
                    preferred_element_type=F32,
                ).astype(held.dtype)
        if first > 0:
            share_out(range(first - group, first))
    share_out(range(samples - group, samples))


def jac_rows(activations, cotangents, owners, part, split, before=()):
    samples, mats, sites, d = activations.shape
    mats //= split
    rows = mats * d // owners
    joined = [k for k, block in enumerate(before) if block is not None]
    out_rows = [rows + (before[k].shape[1] if k in joined else 0) for k in range(owners)]
    hbm = pl.BlockSpec(memory_space=pltpu.HBM)
    vmem = pl.BlockSpec(memory_space=pltpu.VMEM)
    return pl.pallas_call(
        functools.partial(jac_kernel, part * mats, joined),
        in_specs=[hbm, hbm] + [vmem] * len(joined),
        out_shape=[jax.ShapeDtypeStruct((samples, count, d), BF16) for count in out_rows],
        scratch_shapes=[
            pltpu.VMEM((samples, mats, sites, d), BF16),
            pltpu.VMEM((samples, mats, sites, d), BF16),
            pltpu.VMEM((samples, mats, d, d), BF16 if d // owners % CHUNK == 0 else F32),
            pltpu.SemaphoreType.DMA((2, samples)),
        ],
        compiler_params=pltpu.CompilerParams(vmem_limit_bytes=JAC_VMEM_LIMIT),
        cost_estimate=pl.CostEstimate(
            flops=2 * samples * mats * sites * d * d,
            bytes_accessed=6 * samples * mats * sites * d,
            transcendentals=0,
        ),
        name="jac_rows",
    )(activations, cotangents, *[before[k] for k in joined])


def jac_blocks(activations, cotangents, owners):
    mats, d = activations.shape[1], activations.shape[3]
    split = mats if mats == 2 and d // owners % CHUNK == 0 else 1
    blocks = [[block] for block in jac_rows(activations, cotangents, owners, 0, split)]
    if split > 1:
        cut = split_partners(owners, split)
        before = [None if k in cut else block[0] for k, block in enumerate(blocks)]
        later = jac_rows(activations, cotangents, owners, 1, split, before)
        blocks = [b + [new] if k in cut else [new] for k, (b, new) in enumerate(zip(blocks, later))]
    return blocks, split


def packed_shape(total):
    half = total // 2
    return half, -(-(3 * half + 2) // LANES) * LANES


def energy_kernel(total, spins_ref, offdiag_ref, out_ref):
    shape = out_ref.shape
    local = spins_ref.shape[0]
    sites = SIDE * SIDE
    z = (2 * spins_ref[...] - 1).astype(F32)
    column = iota((local, sites), 1) % SIDE
    right = jnp.where(
        column == SIDE - 1, pltpu.roll(z, SIDE - 1, 1), pltpu.roll(z, sites - 1, 1)
    )
    below = pltpu.roll(z, sites - SIDE, 1)
    energy = offdiag_ref[...] + jnp.sum(z * (right + below), axis=1, keepdims=True)
    half = total // 2
    first = lax.axis_index("samp") * local
    lower = first // half
    first = first - lower * half
    spread = jnp.concatenate([energy] * (half // local), axis=0)
    row = iota(shape, 0)
    here = (row >= first) & (row < first + local) & (iota(shape, 1) == 3 * half + lower)
    here = here & (lax.axis_index("layer") == 0)
    out_ref[...] = jnp.where(here, spread, F32(0.0))


def packed_energy(spins, offdiag, total):
    return pl.pallas_call(
        functools.partial(energy_kernel, total),
        out_shape=jax.ShapeDtypeStruct(packed_shape(total), F32),
        compiler_params=pltpu.CompilerParams(vmem_limit_bytes=VMEM_LIMIT),
        name="packed_energy",
    )(spins, offdiag[:, None])


def rows_of(parts, row, rows):
    for ref in parts:
        if row < ref.shape[1]:
            return ref[:, row : row + rows]
        row -= ref.shape[1]


def gram_kernel(owners, *refs):
    *block_refs, energy_ref, out_ref, flat, whole = refs
    blocks = in_place(block_refs, owners)
    local, count, d = blocks[0][0].shape
    total = local * owners
    joined = CHUNK // local
    me = lax.axis_index("samp")
    block = CHUNK * CHUNK
    dest = iota((block, block), 0)
    sample = dest % CHUNK
    sample = (sample // local ^ me % joined) * local + sample % local
    source = sample * CHUNK + dest // CHUNK
    swap = (iota((block, block), 1) == source).astype(F32).astype(BF16)
    for row in range(0, count, CHUNK):
        for j in range(owners // joined):
            pieces = [rows_of(p, row, CHUNK) for p in blocks[j * joined : (j + 1) * joined]]
            piece = jnp.concatenate(pieces, axis=0).reshape(block, d)
            turned = jnp.dot(swap, piece, preferred_element_type=F32).astype(BF16)
            place = pl.ds(pl.multiple_of((me // joined ^ j) * CHUNK, CHUNK), CHUNK)
            for r in range(CHUNK):
                flat[row + r, place] = turned[r * CHUNK : (r + 1) * CHUNK]
    lined = jnp.concatenate([flat[r] for r in range(count)], axis=1)
    gram = lax.dot_general(lined, lined, (((1,), (1,)), ((), ())), preferred_element_type=F32)
    whole[...] = jnp.zeros_like(whole)
    whole[:, :total] += gram
    half, width = out_ref.shape
    lane = iota((half, width), 1)
    lower = pltpu.roll(whole[half:], half, 1)
    packed = jnp.where(lane < 3 * half, lower, energy_ref[...])
    out_ref[...] = jnp.where(lane < half, whole[:half], packed)


def gram_partial(blocks, split, energies):
    local, count, d = blocks[0][0].shape
    total = local * len(blocks)
    return pl.pallas_call(
        functools.partial(gram_kernel, len(blocks)),
        out_shape=jax.ShapeDtypeStruct(packed_shape(total), F32),
        scratch_shapes=[
            pltpu.VMEM((count, total, d), BF16),
            pltpu.VMEM((total, packed_shape(total)[1]), F32),
        ],
        compiler_params=pltpu.CompilerParams(vmem_limit_bytes=VMEM_LIMIT),
        cost_estimate=pl.CostEstimate(
            flops=2 * total * total * count * d,
            bytes_accessed=2 * total * count * d,
            transcendentals=0,
        ),
        name="gram_partial",
    )(*in_turn(blocks, split), energies)


def tree_sum(parts):
    while len(parts) > 1:
        odd = parts[len(parts) // 2 * 2 :]
        parts = [a + b for a, b in zip(parts[::2], parts[1::2])] + odd
    return parts[0]


def pivot_rows(rows, entries):
    count = len(rows)
    rows = list(rows)
    p = [[entries[min(i, l)][max(i, l)] for l in range(count)] for i in range(count)]
    uppers = {}
    for j in range(0, count, 2):
        a, b, c = p[j][j], p[j][j + 1], p[j + 1][j + 1]
        inverse = F32(1.0) / (a * c - b * b)

        def scaled(x, y):
            return (c * x - b * y) * inverse, (a * y - b * x) * inverse

        first, second = rows[j], rows[j + 1]
        rows[j], rows[j + 1] = scaled(first, second)
        later = range(j + 2, count)
        for l in later:
            uppers[j, l], uppers[j + 1, l] = scaled(p[j][l], p[j + 1][l])
        for i in later:
            rows[i] = rows[i] - (p[j][i] * rows[j] + p[j + 1][i] * rows[j + 1])
            for l in range(i, count):
                change = p[j][i] * uppers[j, l] + p[j + 1][i] * uppers[j + 1, l]
                p[i][l] = p[l][i] = p[i][l] - change
    for j in range(count - 4, -1, -2):
        for i in (j, j + 1):
            rows[i] = rows[i] - tree_sum([uppers[i, l] * rows[l] for l in range(j + 2, count)])
    return rows


def eliminate(matrix, total):
    width = matrix.shape[1]
    if total <= 64:
        blocks = [matrix[i : i + PIVOTS] for i in range(0, total, PIVOTS)]
        sub = iota((PIVOTS, width), 0)
        for b in range(len(blocks)):
            spread = [
                [
                    jnp.broadcast_to(block[:, b * PIVOTS + j : b * PIVOTS + j + 1], (PIVOTS, width))
                    for block in blocks
                ]
                for j in range(PIVOTS)
            ]

            def line(value, i):
                return jnp.broadcast_to(value[i : i + 1], (PIVOTS, width))

            entries = [
                [line(spread[l][b], i) if l >= i else None for l in range(PIVOTS)]
                for i in range(PIVOTS)
            ]
            rows = pivot_rows([line(blocks[b], i) for i in range(PIVOTS)], entries)
            for i in range(len(blocks)):
                if i != b:
                    terms = [spread[j][i] * rows[j] for j in range(PIVOTS)]
                    blocks[i] = blocks[i] - tree_sum(terms)
            solved = rows[0]
            for j in range(1, PIVOTS):
                solved = jnp.where(sub == j, rows[j], solved)
            blocks[b] = solved
        return jnp.concatenate([block[:, total : total + 1] for block in blocks], axis=0)
    row = iota(matrix.shape, 0)
    lane = iota(matrix.shape, 1)

    def one(k, held):
        column = jnp.sum(jnp.where(lane == k, held, F32(0.0)), axis=1, keepdims=True)
        pivot_row = jnp.sum(jnp.where(row == k, held, F32(0.0)), axis=0, keepdims=True)
        here = lane[:1] == k
        pivot = jnp.sum(jnp.where(here, pivot_row, F32(0.0)), axis=1, keepdims=True)
        scaled = pivot_row * (F32(1.0) / pivot)
        return held - jnp.where(row == k, F32(0.0), column) * scaled

    matrix = lax.fori_loop(0, total, one, matrix)
    diag = jnp.sum(jnp.where(row == lane, matrix, F32(0.0)), axis=1, keepdims=True)
    return matrix[:, total : total + 1] / diag


def sum_kernel(*refs):
    *part_refs, out_ref = refs
    out_ref[...] = tree_sum([ref[...] for ref in part_refs[::-1]])


def partners(value, masks):
    axes = ("samp", "layer")
    places = lax.axis_size("samp") * lax.axis_size("layer")
    perms = [[(i, i ^ mask) for i in range(places)] for mask in masks[::-1]]
    return [lax.ppermute(value, axes, perm) for perm in perms] + [value]


def sum_over(parts):
    return pl.pallas_call(
        sum_kernel,
        out_shape=jax.ShapeDtypeStruct(parts[0].shape, F32),
        compiler_params=pltpu.CompilerParams(vmem_limit_bytes=VMEM_LIMIT),
        name="sum_over",
    )(*parts)


def rounds(samp, layer):
    masks = [1 << bit for bit in range(1, layer.bit_length() - 1)]
    masks += [layer * (samp - 2), layer]
    masks += [layer << bit for bit in range(1, samp.bit_length() - 2)]
    later = zip(masks[::2], masks[1::2] + [0] * (len(masks) % 2))
    later = [[a, b, a ^ b] if b else [a] for a, b in later]
    return [[1]] + [[mask ^ 1 for mask in masks] for masks in later]


def solve_kernel(sums, owners, *refs):
    sum_refs, (*block_refs, weights_ref, update_ref, held) = refs[:sums], refs[sums:]
    blocks = in_place(block_refs, owners)
    mats, share, d = update_ref.shape
    local = weights_ref.shape[1]
    packed = tree_sum([ref[...] for ref in sum_refs[::-1]])
    half, packed_width = packed.shape
    total = 2 * half
    width = (total // LANES + 1) * LANES
    turned = jnp.swapaxes(packed[:, half:total], 0, 1)
    energy = [packed[:, 3 * half + i : 3 * half + i + 1] for i in range(2)]
    energy = [jnp.broadcast_to(e, (half, width - total)) for e in energy]
    upper = jnp.concatenate([packed[:, :half], turned, energy[0]], axis=1)
    lower = jnp.concatenate([packed[:, half : 3 * half], energy[1]], axis=1)
    raw = jnp.concatenate([upper, lower], axis=0)
    row = iota((total, width), 0)
    lane = iota((total, width), 1)
    inside = lane < total
    scale = F32(1.0 / total)
    row_mean = jnp.sum(jnp.where(inside, raw, F32(0.0)), axis=1, keepdims=True) * scale
    col_mean = jnp.sum(raw, axis=0, keepdims=True) * scale
    mean = jnp.sum(row_mean, axis=0, keepdims=True) * scale
    gram = (raw - col_mean - row_mean + mean) * scale
    eps = (raw - col_mean) * F32(1.0 / total**0.5)
    on_diag = row == lane
    diag = jnp.where(on_diag, raw, F32(0.0))
    trace = jnp.sum(jnp.sum(diag, axis=0, keepdims=True), axis=1, keepdims=True) * scale - mean
    shift = F32(shift_ratio) * trace * scale
    system = jnp.where(inside, gram + jnp.where(on_diag, shift, F32(0.0)), eps)
    weights = eliminate(system, total)
    me = lax.axis_index("samp")
    own = jnp.where(row - me * local == lane, weights, F32(0.0))
    weights_ref[...] = jnp.sum(own, axis=0, keepdims=True)[:, :local]
    coeffs = weights - jnp.sum(weights, axis=0, keepdims=True) * scale
    held[...] = jnp.broadcast_to(coeffs, (total, d))
    acc = jnp.zeros((mats * share, d), F32)
    for k, parts in enumerate(blocks):
        mine = held[pl.ds(pl.multiple_of((me ^ k) * local, local), local)]
        for s in range(local):
            rows = jnp.concatenate([ref[s].astype(F32) for ref in parts], axis=0)
            acc = acc + mine[s : s + 1] * rows
    for m in range(mats):
        update_ref[m] = acc[m * share : (m + 1) * share]


def solve_and_project(sums, blocks, split, mats):
    local, count, d = blocks[0][0].shape
    total = local * len(blocks)
    return pl.pallas_call(
        functools.partial(solve_kernel, len(sums), len(blocks)),
        out_shape=(
            jax.ShapeDtypeStruct((1, local), F32),
            jax.ShapeDtypeStruct((mats, count // mats, d), F32),
        ),
        scratch_shapes=[pltpu.VMEM((total, d), F32)],
        compiler_params=pltpu.CompilerParams(vmem_limit_bytes=VMEM_LIMIT),
        name="solve_and_project",
    )(*sums, *in_turn(blocks, split))


def body(spins, activations, cotangents, offdiag):
    local, mats = activations.shape[:2]
    owners = lax.axis_size("samp")
    total = local * owners
    blocks, split = jac_blocks(activations, cotangents, owners)
    for k, part in turns(owners, split)[:-1]:
        perm = [(i, i ^ k) for i in range(owners)]
        blocks[k][part] = lax.ppermute(blocks[k][part], "samp", perm)
    partial = gram_partial(blocks, split, packed_energy(spins, offdiag, total))
    *early, last = rounds(owners, lax.axis_size("layer"))
    for masks in early:
        partial = sum_over(partners(partial, masks))
    weights, update = solve_and_project(partners(partial, last), blocks, split, mats)
    return weights.reshape(local), update


def solution(mesh):
    placed = (
        P("samp", None),
        P("samp", "layer", None, None),
        P("samp", "layer", None, None),
        P("samp"),
    )
    return jax.shard_map(
        body,
        mesh=mesh,
        in_specs=placed,
        out_specs=(P("samp"), P("layer", "samp", None)),
        check_vma=False,
    )
```

```python
import functools

import jax
import jax.numpy as jnp
from jax import lax
from jax.experimental import pallas as pl
from jax.experimental.pallas import tpu as pltpu
from jax.sharding import PartitionSpec as P

SIDE = 16
LANES = 128
CHUNK = 16
PIVOTS = 8
VMEM_LIMIT = 24 * 2**20
JAC_VMEM_LIMIT = 52 * 2**20
shift_ratio = 0.1
F32 = jnp.float32
BF16 = jnp.bfloat16


def iota(shape, dim):
    return lax.broadcasted_iota(jnp.int32, shape, dim)


def turns(owners, split):
    far, near = list(range(owners // 2, owners)), list(range(owners // 2 - 1, 0, -1))
    cut = split_partners(owners, split)
    order = [(k, part) for part in range(split) for k in cut]
    far = [k for k in far if k not in cut]
    while far or near:
        order += [(k, 0) for k in near[:1] + far[:1]]
        far, near = far[1:], near[1:]
    return order + [(0, 0)]


def split_partners(owners, split):
    return [owners // 2, owners // 2 + 1] if split > 1 else []


def in_turn(blocks, split):
    return [blocks[k][part] for k, part in turns(len(blocks), split)]


def in_place(refs, owners):
    split = 1 + (len(refs) > owners)
    blocks = [[] for _ in range(owners)]
    for (k, _), ref in zip(turns(owners, split), refs):
        blocks[k].append(ref)
    return blocks


def jac_kernel(first_mat, joined, act_hbm, cot_hbm, *refs):
    before, refs = refs[: len(joined)], refs[len(joined) :]
    *out_refs, act_buf, cot_buf, held, sems = refs
    samples, mats, _, d = held.shape
    share = d // len(out_refs)
    me = lax.axis_index("samp")
    group = 2
    copies = []
    for first in range(0, samples, group):
        here = pl.ds(first, group)
        mine = (here, pl.ds(first_mat, mats))
        sem = first // group
        copies.append(pltpu.make_async_copy(act_hbm.at[mine], act_buf.at[here], sems.at[0, sem]))
        copies.append(pltpu.make_async_copy(cot_hbm.at[mine], cot_buf.at[here], sems.at[1, sem]))
    for copy in copies:
        copy.start()
    for k, ref in zip(joined, before):
        out_refs[k][:, : ref.shape[1]] = ref[...]

    def share_out(samples):
        for k, out_ref in enumerate(out_refs):
            owned = pl.ds(pl.multiple_of((me ^ k) * share, share), share)
            for s in samples:
                rows = [held[s, m, owned] for m in range(mats)]
                rows = jnp.concatenate(rows, axis=0).astype(BF16)
                out_ref[s, out_ref.shape[1] - mats * share :] = rows

    for first in range(0, samples, group):
        here = range(first, first + group)
        copies[first].wait()
        copies[first + 1].wait()
        for s in here:
            for m in range(mats):
                held[s, m] = lax.dot_general(
                    act_buf[s, m],
                    cot_buf[s, m],
                    (((0,), (0,)), ((), ())),
                    preferred_element_type=F32,
                ).astype(held.dtype)
        if first > 0:
            share_out(range(first - group, first))
    share_out(range(samples - group, samples))


def jac_rows(activations, cotangents, owners, part, split, before=()):
    samples, mats, sites, d = activations.shape
    mats //= split
    rows = mats * d // owners
    joined = [k for k, block in enumerate(before) if block is not None]
    out_rows = [rows + (before[k].shape[1] if k in joined else 0) for k in range(owners)]
    hbm = pl.BlockSpec(memory_space=pltpu.HBM)
    vmem = pl.BlockSpec(memory_space=pltpu.VMEM)
    return pl.pallas_call(
        functools.partial(jac_kernel, part * mats, joined),
        in_specs=[hbm, hbm] + [vmem] * len(joined),
        out_shape=[jax.ShapeDtypeStruct((samples, count, d), BF16) for count in out_rows],
        scratch_shapes=[
            pltpu.VMEM((samples, mats, sites, d), BF16),
            pltpu.VMEM((samples, mats, sites, d), BF16),
            pltpu.VMEM((samples, mats, d, d), BF16 if d // owners % CHUNK == 0 else F32),
            pltpu.SemaphoreType.DMA((2, samples)),
        ],
        compiler_params=pltpu.CompilerParams(vmem_limit_bytes=JAC_VMEM_LIMIT),
        cost_estimate=pl.CostEstimate(
            flops=2 * samples * mats * sites * d * d,
            bytes_accessed=6 * samples * mats * sites * d,
            transcendentals=0,
        ),
        name="jac_rows",
    )(activations, cotangents, *[before[k] for k in joined])


def jac_blocks(activations, cotangents, owners):
    mats, d = activations.shape[1], activations.shape[3]
    split = mats if mats == 2 and d // owners % CHUNK == 0 else 1
    blocks = [[block] for block in jac_rows(activations, cotangents, owners, 0, split)]
    if split > 1:
        cut = split_partners(owners, split)
        before = [None if k in cut else block[0] for k, block in enumerate(blocks)]
        later = jac_rows(activations, cotangents, owners, 1, split, before)
        blocks = [b + [new] if k in cut else [new] for k, (b, new) in enumerate(zip(blocks, later))]
    return blocks, split


def packed_shape(total):
    half = total // 2
    return half, -(-(3 * half + 2) // LANES) * LANES


def energy_kernel(total, spins_ref, offdiag_ref, out_ref):
    shape = out_ref.shape
    local = spins_ref.shape[0]
    sites = SIDE * SIDE
    z = (2 * spins_ref[...] - 1).astype(F32)
    column = iota((local, sites), 1) % SIDE
    right = jnp.where(
        column == SIDE - 1, pltpu.roll(z, SIDE - 1, 1), pltpu.roll(z, sites - 1, 1)
    )
    below = pltpu.roll(z, sites - SIDE, 1)
    energy = offdiag_ref[...] + jnp.sum(z * (right + below), axis=1, keepdims=True)
    half = total // 2
    first = lax.axis_index("samp") * local
    lower = first // half
    first = first - lower * half
    spread = jnp.concatenate([energy] * (half // local), axis=0)
    row = iota(shape, 0)
    here = (row >= first) & (row < first + local) & (iota(shape, 1) == 3 * half + lower)
    here = here & (lax.axis_index("layer") == 0)
    out_ref[...] = jnp.where(here, spread, F32(0.0))


def packed_energy(spins, offdiag, total):
    return pl.pallas_call(
        functools.partial(energy_kernel, total),
        out_shape=jax.ShapeDtypeStruct(packed_shape(total), F32),
        compiler_params=pltpu.CompilerParams(vmem_limit_bytes=VMEM_LIMIT),
        name="packed_energy",
    )(spins, offdiag[:, None])


def rows_of(parts, row, rows):
    for ref in parts:
        if row < ref.shape[1]:
            return ref[:, row : row + rows]
        row -= ref.shape[1]


def gram_kernel(owners, *refs):
    *block_refs, energy_ref, out_ref, flat, whole = refs
    blocks = in_place(block_refs, owners)
    local, count, d = blocks[0][0].shape
    total = local * owners
    joined = CHUNK // local
    me = lax.axis_index("samp")
    block = CHUNK * CHUNK
    dest = iota((block, block), 0)
    sample = dest % CHUNK
    sample = (sample // local ^ me % joined) * local + sample % local
    source = sample * CHUNK + dest // CHUNK
    swap = (iota((block, block), 1) == source).astype(F32).astype(BF16)
    for row in range(0, count, CHUNK):
        for j in range(owners // joined):
            pieces = [rows_of(p, row, CHUNK) for p in blocks[j * joined : (j + 1) * joined]]
            piece = jnp.concatenate(pieces, axis=0).reshape(block, d)
            turned = jnp.dot(swap, piece, preferred_element_type=F32).astype(BF16)
            place = pl.ds(pl.multiple_of((me // joined ^ j) * CHUNK, CHUNK), CHUNK)
            for r in range(CHUNK):
                flat[row + r, place] = turned[r * CHUNK : (r + 1) * CHUNK]
    lined = jnp.concatenate([flat[r] for r in range(count)], axis=1)
    gram = lax.dot_general(lined, lined, (((1,), (1,)), ((), ())), preferred_element_type=F32)
    whole[...] = jnp.zeros_like(whole)
    whole[:, :total] += gram
    half, width = out_ref.shape
    lane = iota((half, width), 1)
    lower = pltpu.roll(whole[half:], half, 1)
    packed = jnp.where(lane < 3 * half, lower, energy_ref[...])
    out_ref[...] = jnp.where(lane < half, whole[:half], packed)


def gram_partial(blocks, split, energies):
    local, count, d = blocks[0][0].shape
    total = local * len(blocks)
    return pl.pallas_call(
        functools.partial(gram_kernel, len(blocks)),
        out_shape=jax.ShapeDtypeStruct(packed_shape(total), F32),
        scratch_shapes=[
            pltpu.VMEM((count, total, d), BF16),
            pltpu.VMEM((total, packed_shape(total)[1]), F32),
        ],
        compiler_params=pltpu.CompilerParams(vmem_limit_bytes=VMEM_LIMIT),
        cost_estimate=pl.CostEstimate(
            flops=2 * total * total * count * d,
            bytes_accessed=2 * total * count * d,
            transcendentals=0,
        ),
        name="gram_partial",
    )(*in_turn(blocks, split), energies)


def tree_sum(parts):
    while len(parts) > 1:
        odd = parts[len(parts) // 2 * 2 :]
        parts = [a + b for a, b in zip(parts[::2], parts[1::2])] + odd
    return parts[0]


def pivot_rows(rows, entries):
    count = len(rows)
    rows = list(rows)
    p = [[entries[min(i, l)][max(i, l)] for l in range(count)] for i in range(count)]
    uppers = {}
    for j in range(0, count, 2):
        a, b, c = p[j][j], p[j][j + 1], p[j + 1][j + 1]
        inverse = F32(1.0) / (a * c - b * b)

        def scaled(x, y):
            return (c * x - b * y) * inverse, (a * y - b * x) * inverse

        first, second = rows[j], rows[j + 1]
        rows[j], rows[j + 1] = scaled(first, second)
        later = range(j + 2, count)
        for l in later:
            uppers[j, l], uppers[j + 1, l] = scaled(p[j][l], p[j + 1][l])
        for i in later:
            rows[i] = rows[i] - (p[j][i] * rows[j] + p[j + 1][i] * rows[j + 1])
            for l in range(i, count):
                change = p[j][i] * uppers[j, l] + p[j + 1][i] * uppers[j + 1, l]
                p[i][l] = p[l][i] = p[i][l] - change
    for j in range(count - 4, -1, -2):
        for i in (j, j + 1):
            rows[i] = rows[i] - tree_sum([uppers[i, l] * rows[l] for l in range(j + 2, count)])
    return rows


def eliminate(matrix, total):
    width = matrix.shape[1]
    if total <= 64:
        blocks = [matrix[i : i + PIVOTS] for i in range(0, total, PIVOTS)]
        sub = iota((PIVOTS, width), 0)
        for b in range(len(blocks)):
            spread = [
                [
                    jnp.broadcast_to(block[:, b * PIVOTS + j : b * PIVOTS + j + 1], (PIVOTS, width))
                    for block in blocks
                ]
                for j in range(PIVOTS)
            ]

            def line(value, i):
                return jnp.broadcast_to(value[i : i + 1], (PIVOTS, width))

            entries = [
                [line(spread[l][b], i) if l >= i else None for l in range(PIVOTS)]
                for i in range(PIVOTS)
            ]
            rows = pivot_rows([line(blocks[b], i) for i in range(PIVOTS)], entries)
            for i in range(len(blocks)):
                if i != b:
                    terms = [spread[j][i] * rows[j] for j in range(PIVOTS)]
                    blocks[i] = blocks[i] - tree_sum(terms)
            solved = rows[0]
            for j in range(1, PIVOTS):
                solved = jnp.where(sub == j, rows[j], solved)
            blocks[b] = solved
        return jnp.concatenate([block[:, total : total + 1] for block in blocks], axis=0)
    row = iota(matrix.shape, 0)
    lane = iota(matrix.shape, 1)

    def one(k, held):
        column = jnp.sum(jnp.where(lane == k, held, F32(0.0)), axis=1, keepdims=True)
        pivot_row = jnp.sum(jnp.where(row == k, held, F32(0.0)), axis=0, keepdims=True)
        here = lane[:1] == k
        pivot = jnp.sum(jnp.where(here, pivot_row, F32(0.0)), axis=1, keepdims=True)
        scaled = pivot_row * (F32(1.0) / pivot)
        return held - jnp.where(row == k, F32(0.0), column) * scaled

    matrix = lax.fori_loop(0, total, one, matrix)
    diag = jnp.sum(jnp.where(row == lane, matrix, F32(0.0)), axis=1, keepdims=True)
    return matrix[:, total : total + 1] / diag


def sum_kernel(*refs):
    *part_refs, out_ref = refs
    out_ref[...] = tree_sum([ref[...] for ref in part_refs[::-1]])


def partners(value, masks):
    axes = ("samp", "layer")
    places = lax.axis_size("samp") * lax.axis_size("layer")
    perms = [[(i, i ^ mask) for i in range(places)] for mask in masks[::-1]]
    return [lax.ppermute(value, axes, perm) for perm in perms] + [value]


def sum_over(parts):
    return pl.pallas_call(
        sum_kernel,
        out_shape=jax.ShapeDtypeStruct(parts[0].shape, F32),
        compiler_params=pltpu.CompilerParams(vmem_limit_bytes=VMEM_LIMIT),
        name="sum_over",
    )(*parts)


def rounds(samp, layer):
    masks = [1 << bit for bit in range(1, layer.bit_length() - 1)]
    masks += [layer * (samp - 2), layer]
    masks += [layer << bit for bit in range(1, samp.bit_length() - 2)]
    later = zip(masks[::2], masks[1::2] + [0] * (len(masks) % 2))
    later = [[a, b, a ^ b] if b else [a] for a, b in later]
    return [[1]] + [[mask ^ 1 for mask in masks] for masks in later]


def solve_kernel(sums, owners, *refs):
    sum_refs, (*block_refs, weights_ref, update_ref, held) = refs[:sums], refs[sums:]
    blocks = in_place(block_refs, owners)
    mats, share, d = update_ref.shape
    local = weights_ref.shape[1]
    packed = tree_sum([ref[...] for ref in sum_refs[::-1]])
    half, packed_width = packed.shape
    total = 2 * half
    width = (total // LANES + 1) * LANES
    turned = jnp.swapaxes(packed[:, half:total], 0, 1)
    energy = [packed[:, 3 * half + i : 3 * half + i + 1] for i in range(2)]
    energy = [jnp.broadcast_to(e, (half, width - total)) for e in energy]
    upper = jnp.concatenate([packed[:, :half], turned, energy[0]], axis=1)
    lower = jnp.concatenate([packed[:, half : 3 * half], energy[1]], axis=1)
    raw = jnp.concatenate([upper, lower], axis=0)
    row = iota((total, width), 0)
    lane = iota((total, width), 1)
    inside = lane < total
    scale = F32(1.0 / total)
    row_mean = jnp.sum(jnp.where(inside, raw, F32(0.0)), axis=1, keepdims=True) * scale
    col_mean = jnp.sum(raw, axis=0, keepdims=True) * scale
    mean = jnp.sum(row_mean, axis=0, keepdims=True) * scale
    centered = raw - col_mean - row_mean + mean
    eps = (raw - col_mean) * F32(1.0 / total**0.5)
    on_diag = row == lane
    diag = jnp.where(on_diag, raw, F32(0.0))
    trace = jnp.sum(jnp.sum(diag, axis=0, keepdims=True), axis=1, keepdims=True) * scale - mean
    inverse = F32(1.0) / (trace * scale)
    shift = jnp.where(on_diag, F32(shift_ratio), F32(0.0))
    system = jnp.where(inside, centered * (scale * inverse) + shift, eps)
    weights = eliminate(system, total) * inverse
    me = lax.axis_index("samp")
    own = jnp.where(row - me * local == lane, weights, F32(0.0))
    weights_ref[...] = jnp.sum(own, axis=0, keepdims=True)[:, :local]
    coeffs = weights - jnp.sum(weights, axis=0, keepdims=True) * scale
    held[...] = jnp.broadcast_to(coeffs, (total, d))
    acc = jnp.zeros((mats * share, d), F32)
    for k, parts in enumerate(blocks):
        mine = held[pl.ds(pl.multiple_of((me ^ k) * local, local), local)]
        for s in range(local):
            rows = jnp.concatenate([ref[s].astype(F32) for ref in parts], axis=0)
            acc = acc + mine[s : s + 1] * rows
    for m in range(mats):
        update_ref[m] = acc[m * share : (m + 1) * share]


def solve_and_project(sums, blocks, split, mats):
    local, count, d = blocks[0][0].shape
    total = local * len(blocks)
    return pl.pallas_call(
        functools.partial(solve_kernel, len(sums), len(blocks)),
        out_shape=(
            jax.ShapeDtypeStruct((1, local), F32),
            jax.ShapeDtypeStruct((mats, count // mats, d), F32),
        ),
        scratch_shapes=[pltpu.VMEM((total, d), F32)],
        compiler_params=pltpu.CompilerParams(vmem_limit_bytes=VMEM_LIMIT),
        name="solve_and_project",
    )(*sums, *in_turn(blocks, split))


def body(spins, activations, cotangents, offdiag):
    local, mats = activations.shape[:2]
    owners = lax.axis_size("samp")
    total = local * owners
    blocks, split = jac_blocks(activations, cotangents, owners)
    for k, part in turns(owners, split)[:-1]:
        perm = [(i, i ^ k) for i in range(owners)]
        blocks[k][part] = lax.ppermute(blocks[k][part], "samp", perm)
    partial = gram_partial(blocks, split, packed_energy(spins, offdiag, total))
    *early, last = rounds(owners, lax.axis_size("layer"))
    for masks in early:
        partial = sum_over(partners(partial, masks))
    weights, update = solve_and_project(partners(partial, last), blocks, split, mats)
    return weights.reshape(local), update


def solution(mesh):
    placed = (
        P("samp", None),
        P("samp", "layer", None, None),
        P("samp", "layer", None, None),
        P("samp"),
    )
    return jax.shard_map(
        body,
        mesh=mesh,
        in_specs=placed,
        out_specs=(P("samp"), P("layer", "samp", None)),
        check_vma=False,
    )
```

```python
import functools

import jax
import jax.numpy as jnp
from jax import lax
from jax.experimental import pallas as pl
from jax.experimental.pallas import tpu as pltpu
from jax.sharding import PartitionSpec as P

SIDE = 16
LANES = 128
CHUNK = 16
PIVOTS = 8
VMEM_LIMIT = 24 * 2**20
JAC_VMEM_LIMIT = 52 * 2**20
shift_ratio = 0.1
F32 = jnp.float32
BF16 = jnp.bfloat16


def iota(shape, dim):
    return lax.broadcasted_iota(jnp.int32, shape, dim)


def turns(owners, split):
    far, near = list(range(owners // 2, owners)), list(range(owners // 2 - 1, 0, -1))
    cut = split_partners(owners, split)
    order = [(k, part) for part in range(split) for k in cut]
    far = [k for k in far if k not in cut]
    order += [(k, 0) for k in near[:1] + far + near[1:]]
    return order + [(0, 0)]


def split_partners(owners, split):
    return [owners // 2, owners // 2 + 1] if split > 1 else []


def in_turn(blocks, split):
    return [blocks[k][part] for k, part in turns(len(blocks), split)]


def in_place(refs, owners):
    split = 1 + (len(refs) > owners)
    blocks = [[] for _ in range(owners)]
    for (k, _), ref in zip(turns(owners, split), refs):
        blocks[k].append(ref)
    return blocks


def jac_kernel(first_mat, joined, act_hbm, cot_hbm, *refs):
    before, refs = refs[: len(joined)], refs[len(joined) :]
    *out_refs, act_buf, cot_buf, held, sems = refs
    samples, mats, _, d = held.shape
    share = d // len(out_refs)
    me = lax.axis_index("samp")
    group = 2
    copies = []
    for first in range(0, samples, group):
        here = pl.ds(first, group)
        mine = (here, pl.ds(first_mat, mats))
        sem = first // group
        copies.append(pltpu.make_async_copy(act_hbm.at[mine], act_buf.at[here], sems.at[0, sem]))
        copies.append(pltpu.make_async_copy(cot_hbm.at[mine], cot_buf.at[here], sems.at[1, sem]))
    for copy in copies:
        copy.start()
    for k, ref in zip(joined, before):
        out_refs[k][:, : ref.shape[1]] = ref[...]

    def share_out(samples):
        for k, out_ref in enumerate(out_refs):
            owned = pl.ds(pl.multiple_of((me ^ k) * share, share), share)
            for s in samples:
                rows = [held[s, m, owned] for m in range(mats)]
                rows = jnp.concatenate(rows, axis=0).astype(BF16)
                out_ref[s, out_ref.shape[1] - mats * share :] = rows

    for first in range(0, samples, group):
        here = range(first, first + group)
        copies[first].wait()
        copies[first + 1].wait()
        for s in here:
            for m in range(mats):
                held[s, m] = lax.dot_general(
                    act_buf[s, m],
                    cot_buf[s, m],
                    (((0,), (0,)), ((), ())),
                    preferred_element_type=F32,
                ).astype(held.dtype)
        if first > 0:
            share_out(range(first - group, first))
    share_out(range(samples - group, samples))


def jac_rows(activations, cotangents, owners, part, split, before=()):
    samples, mats, sites, d = activations.shape
    mats //= split
    rows = mats * d // owners
    joined = [k for k, block in enumerate(before) if block is not None]
    out_rows = [rows + (before[k].shape[1] if k in joined else 0) for k in range(owners)]
    hbm = pl.BlockSpec(memory_space=pltpu.HBM)
    vmem = pl.BlockSpec(memory_space=pltpu.VMEM)
    return pl.pallas_call(
        functools.partial(jac_kernel, part * mats, joined),
        in_specs=[hbm, hbm] + [vmem] * len(joined),
        out_shape=[jax.ShapeDtypeStruct((samples, count, d), BF16) for count in out_rows],
        scratch_shapes=[
            pltpu.VMEM((samples, mats, sites, d), BF16),
            pltpu.VMEM((samples, mats, sites, d), BF16),
            pltpu.VMEM((samples, mats, d, d), BF16 if d // owners % CHUNK == 0 else F32),
            pltpu.SemaphoreType.DMA((2, samples)),
        ],
        compiler_params=pltpu.CompilerParams(vmem_limit_bytes=JAC_VMEM_LIMIT),
        cost_estimate=pl.CostEstimate(
            flops=2 * samples * mats * sites * d * d,
            bytes_accessed=6 * samples * mats * sites * d,
            transcendentals=0,
        ),
        name="jac_rows",
    )(activations, cotangents, *[before[k] for k in joined])


def jac_blocks(activations, cotangents, owners):
    mats, d = activations.shape[1], activations.shape[3]
    split = mats if mats == 2 and d // owners % CHUNK == 0 else 1
    blocks = [[block] for block in jac_rows(activations, cotangents, owners, 0, split)]
    if split > 1:
        cut = split_partners(owners, split)
        before = [None if k in cut else block[0] for k, block in enumerate(blocks)]
        later = jac_rows(activations, cotangents, owners, 1, split, before)
        blocks = [b + [new] if k in cut else [new] for k, (b, new) in enumerate(zip(blocks, later))]
    return blocks, split


def packed_shape(total):
    half = total // 2
    return half, -(-(3 * half + 2) // LANES) * LANES


def energy_kernel(total, spins_ref, offdiag_ref, out_ref):
    shape = out_ref.shape
    local = spins_ref.shape[0]
    sites = SIDE * SIDE
    z = (2 * spins_ref[...] - 1).astype(F32)
    column = iota((local, sites), 1) % SIDE
    right = jnp.where(
        column == SIDE - 1, pltpu.roll(z, SIDE - 1, 1), pltpu.roll(z, sites - 1, 1)
    )
    below = pltpu.roll(z, sites - SIDE, 1)
    energy = offdiag_ref[...] + jnp.sum(z * (right + below), axis=1, keepdims=True)
    half = total // 2
    first = lax.axis_index("samp") * local
    lower = first // half
    first = first - lower * half
    spread = jnp.concatenate([energy] * (half // local), axis=0)
    row = iota(shape, 0)
    here = (row >= first) & (row < first + local) & (iota(shape, 1) == 3 * half + lower)
    here = here & (lax.axis_index("layer") == 0)
    out_ref[...] = jnp.where(here, spread, F32(0.0))


def packed_energy(spins, offdiag, total):
    return pl.pallas_call(
        functools.partial(energy_kernel, total),
        out_shape=jax.ShapeDtypeStruct(packed_shape(total), F32),
        compiler_params=pltpu.CompilerParams(vmem_limit_bytes=VMEM_LIMIT),
        name="packed_energy",
    )(spins, offdiag[:, None])


def rows_of(parts, row, rows):
    for ref in parts:
        if row < ref.shape[1]:
            return ref[:, row : row + rows]
        row -= ref.shape[1]


def gram_kernel(owners, *refs):
    *block_refs, energy_ref, out_ref, flat, whole = refs
    blocks = in_place(block_refs, owners)
    local, count, d = blocks[0][0].shape
    total = local * owners
    joined = CHUNK // local
    me = lax.axis_index("samp")
    block = CHUNK * CHUNK
    dest = iota((block, block), 0)
    sample = dest % CHUNK
    sample = (sample // local ^ me % joined) * local + sample % local
    source = sample * CHUNK + dest // CHUNK
    swap = (iota((block, block), 1) == source).astype(F32).astype(BF16)
    for row in range(0, count, CHUNK):
        for j in range(owners // joined):
            pieces = [rows_of(p, row, CHUNK) for p in blocks[j * joined : (j + 1) * joined]]
            piece = jnp.concatenate(pieces, axis=0).reshape(block, d)
            turned = jnp.dot(swap, piece, preferred_element_type=F32).astype(BF16)
            place = pl.ds(pl.multiple_of((me // joined ^ j) * CHUNK, CHUNK), CHUNK)
            for r in range(CHUNK):
                flat[row + r, place] = turned[r * CHUNK : (r + 1) * CHUNK]
    lined = jnp.concatenate([flat[r] for r in range(count)], axis=1)
    gram = lax.dot_general(lined, lined, (((1,), (1,)), ((), ())), preferred_element_type=F32)
    whole[...] = jnp.zeros_like(whole)
    whole[:, :total] += gram
    half, width = out_ref.shape
    lane = iota((half, width), 1)
    lower = pltpu.roll(whole[half:], half, 1)
    packed = jnp.where(lane < 3 * half, lower, energy_ref[...])
    out_ref[...] = jnp.where(lane < half, whole[:half], packed)


def gram_partial(blocks, split, energies):
    local, count, d = blocks[0][0].shape
    total = local * len(blocks)
    return pl.pallas_call(
        functools.partial(gram_kernel, len(blocks)),
        out_shape=jax.ShapeDtypeStruct(packed_shape(total), F32),
        scratch_shapes=[
            pltpu.VMEM((count, total, d), BF16),
            pltpu.VMEM((total, packed_shape(total)[1]), F32),
        ],
        compiler_params=pltpu.CompilerParams(vmem_limit_bytes=VMEM_LIMIT),
        cost_estimate=pl.CostEstimate(
            flops=2 * total * total * count * d,
            bytes_accessed=2 * total * count * d,
            transcendentals=0,
        ),
        name="gram_partial",
    )(*in_turn(blocks, split), energies)


def tree_sum(parts):
    while len(parts) > 1:
        odd = parts[len(parts) // 2 * 2 :]
        parts = [a + b for a, b in zip(parts[::2], parts[1::2])] + odd
    return parts[0]


def pivot_rows(rows, entries):
    count = len(rows)
    rows = list(rows)
    p = [[entries[min(i, l)][max(i, l)] for l in range(count)] for i in range(count)]
    uppers = {}
    for j in range(0, count, 2):
        a, b, c = p[j][j], p[j][j + 1], p[j + 1][j + 1]
        inverse = F32(1.0) / (a * c - b * b)

        def scaled(x, y):
            return (c * x - b * y) * inverse, (a * y - b * x) * inverse

        first, second = rows[j], rows[j + 1]
        rows[j], rows[j + 1] = scaled(first, second)
        later = range(j + 2, count)
        for l in later:
            uppers[j, l], uppers[j + 1, l] = scaled(p[j][l], p[j + 1][l])
        for i in later:
            rows[i] = rows[i] - (p[j][i] * rows[j] + p[j + 1][i] * rows[j + 1])
            for l in range(i, count):
                change = p[j][i] * uppers[j, l] + p[j + 1][i] * uppers[j + 1, l]
                p[i][l] = p[l][i] = p[i][l] - change
    for j in range(count - 4, -1, -2):
        for i in (j, j + 1):
            rows[i] = rows[i] - tree_sum([uppers[i, l] * rows[l] for l in range(j + 2, count)])
    return rows


def eliminate(matrix, total):
    width = matrix.shape[1]
    if total <= 64:
        blocks = [matrix[i : i + PIVOTS] for i in range(0, total, PIVOTS)]
        sub = iota((PIVOTS, width), 0)
        for b in range(len(blocks)):
            spread = [
                [
                    jnp.broadcast_to(block[:, b * PIVOTS + j : b * PIVOTS + j + 1], (PIVOTS, width))
                    for block in blocks
                ]
                for j in range(PIVOTS)
            ]

            def line(value, i):
                return jnp.broadcast_to(value[i : i + 1], (PIVOTS, width))

            entries = [
                [line(spread[l][b], i) if l >= i else None for l in range(PIVOTS)]
                for i in range(PIVOTS)
            ]
            rows = pivot_rows([line(blocks[b], i) for i in range(PIVOTS)], entries)
            for i in range(len(blocks)):
                if i != b:
                    terms = [spread[j][i] * rows[j] for j in range(PIVOTS)]
                    blocks[i] = blocks[i] - tree_sum(terms)
            solved = rows[0]
            for j in range(1, PIVOTS):
                solved = jnp.where(sub == j, rows[j], solved)
            blocks[b] = solved
        return jnp.concatenate([block[:, total : total + 1] for block in blocks], axis=0)
    row = iota(matrix.shape, 0)
    lane = iota(matrix.shape, 1)

    def one(k, held):
        column = jnp.sum(jnp.where(lane == k, held, F32(0.0)), axis=1, keepdims=True)
        pivot_row = jnp.sum(jnp.where(row == k, held, F32(0.0)), axis=0, keepdims=True)
        here = lane[:1] == k
        pivot = jnp.sum(jnp.where(here, pivot_row, F32(0.0)), axis=1, keepdims=True)
        scaled = pivot_row * (F32(1.0) / pivot)
        return held - jnp.where(row == k, F32(0.0), column) * scaled

    matrix = lax.fori_loop(0, total, one, matrix)
    diag = jnp.sum(jnp.where(row == lane, matrix, F32(0.0)), axis=1, keepdims=True)
    return matrix[:, total : total + 1] / diag


def sum_kernel(*refs):
    *part_refs, out_ref = refs
    out_ref[...] = tree_sum([ref[...] for ref in part_refs[::-1]])


def partners(value, masks):
    axes = ("samp", "layer")
    places = lax.axis_size("samp") * lax.axis_size("layer")
    perms = [[(i, i ^ mask) for i in range(places)] for mask in masks[::-1]]
    return [lax.ppermute(value, axes, perm) for perm in perms] + [value]


def sum_over(parts):
    return pl.pallas_call(
        sum_kernel,
        out_shape=jax.ShapeDtypeStruct(parts[0].shape, F32),
        compiler_params=pltpu.CompilerParams(vmem_limit_bytes=VMEM_LIMIT),
        name="sum_over",
    )(*parts)


def rounds(samp, layer):
    masks = [1 << bit for bit in range(1, layer.bit_length() - 1)]
    masks += [layer * (samp - 2), layer]
    masks += [layer << bit for bit in range(1, samp.bit_length() - 2)]
    later = zip(masks[::2], masks[1::2] + [0] * (len(masks) % 2))
    later = [[a, b, a ^ b] if b else [a] for a, b in later]
    return [[1]] + [[mask ^ 1 for mask in masks] for masks in later]


def solve_kernel(sums, owners, *refs):
    sum_refs, (*block_refs, weights_ref, update_ref, held) = refs[:sums], refs[sums:]
    blocks = in_place(block_refs, owners)
    mats, share, d = update_ref.shape
    local = weights_ref.shape[1]
    packed = tree_sum([ref[...] for ref in sum_refs[::-1]])
    half, packed_width = packed.shape
    total = 2 * half
    width = (total // LANES + 1) * LANES
    turned = jnp.swapaxes(packed[:, half:total], 0, 1)
    energy = [packed[:, 3 * half + i : 3 * half + i + 1] for i in range(2)]
    energy = [jnp.broadcast_to(e, (half, width - total)) for e in energy]
    upper = jnp.concatenate([packed[:, :half], turned, energy[0]], axis=1)
    lower = jnp.concatenate([packed[:, half : 3 * half], energy[1]], axis=1)
    raw = jnp.concatenate([upper, lower], axis=0)
    row = iota((total, width), 0)
    lane = iota((total, width), 1)
    inside = lane < total
    scale = F32(1.0 / total)
    row_mean = jnp.sum(jnp.where(inside, raw, F32(0.0)), axis=1, keepdims=True) * scale
    col_mean = jnp.sum(raw, axis=0, keepdims=True) * scale
    mean = jnp.sum(row_mean, axis=0, keepdims=True) * scale
    centered = raw - col_mean - row_mean + mean
    eps = (raw - col_mean) * F32(1.0 / total**0.5)
    on_diag = row == lane
    diag = jnp.where(on_diag, raw, F32(0.0))
    trace = jnp.sum(jnp.sum(diag, axis=0, keepdims=True), axis=1, keepdims=True) * scale - mean
    inverse = F32(1.0) / (trace * scale)
    shift = jnp.where(on_diag, F32(shift_ratio), F32(0.0))
    system = jnp.where(inside, centered * (scale * inverse) + shift, eps)
    weights = eliminate(system, total) * inverse
    me = lax.axis_index("samp")
    own = jnp.where(row - me * local == lane, weights, F32(0.0))
    weights_ref[...] = jnp.sum(own, axis=0, keepdims=True)[:, :local]
    coeffs = weights - jnp.sum(weights, axis=0, keepdims=True) * scale
    held[...] = jnp.broadcast_to(coeffs, (total, d))
    acc = jnp.zeros((mats * share, d), F32)
    for k, parts in enumerate(blocks):
        mine = held[pl.ds(pl.multiple_of((me ^ k) * local, local), local)]
        for s in range(local):
            rows = jnp.concatenate([ref[s].astype(F32) for ref in parts], axis=0)
            acc = acc + mine[s : s + 1] * rows
    for m in range(mats):
        update_ref[m] = acc[m * share : (m + 1) * share]


def solve_and_project(sums, blocks, split, mats):
    local, count, d = blocks[0][0].shape
    total = local * len(blocks)
    return pl.pallas_call(
        functools.partial(solve_kernel, len(sums), len(blocks)),
        out_shape=(
            jax.ShapeDtypeStruct((1, local), F32),
            jax.ShapeDtypeStruct((mats, count // mats, d), F32),
        ),
        scratch_shapes=[pltpu.VMEM((total, d), F32)],
        compiler_params=pltpu.CompilerParams(vmem_limit_bytes=VMEM_LIMIT),
        name="solve_and_project",
    )(*sums, *in_turn(blocks, split))


def body(spins, activations, cotangents, offdiag):
    local, mats = activations.shape[:2]
    owners = lax.axis_size("samp")
    total = local * owners
    blocks, split = jac_blocks(activations, cotangents, owners)
    for k, part in turns(owners, split)[:-1]:
        perm = [(i, i ^ k) for i in range(owners)]
        blocks[k][part] = lax.ppermute(blocks[k][part], "samp", perm)
    partial = gram_partial(blocks, split, packed_energy(spins, offdiag, total))
    *early, last = rounds(owners, lax.axis_size("layer"))
    for masks in early:
        partial = sum_over(partners(partial, masks))
    weights, update = solve_and_project(partners(partial, last), blocks, split, mats)
    return weights.reshape(local), update


def solution(mesh):
    placed = (
        P("samp", None),
        P("samp", "layer", None, None),
        P("samp", "layer", None, None),
        P("samp"),
    )
    return jax.shard_map(
        body,
        mesh=mesh,
        in_specs=placed,
        out_specs=(P("samp"), P("layer", "samp", None)),
        check_vma=False,
    )
```

```python
import functools

import jax
import jax.numpy as jnp
from jax import lax
from jax.experimental import pallas as pl
from jax.experimental.pallas import tpu as pltpu
from jax.sharding import PartitionSpec as P

SIDE = 16
LANES = 128
CHUNK = 16
PIVOTS = 8
VMEM_LIMIT = 24 * 2**20
JAC_VMEM_LIMIT = 52 * 2**20
shift_ratio = 0.1
F32 = jnp.float32
BF16 = jnp.bfloat16


def iota(shape, dim):
    return lax.broadcasted_iota(jnp.int32, shape, dim)


def turns(owners, split):
    far, near = list(range(owners // 2, owners)), list(range(owners // 2 - 1, 0, -1))
    cut = split_partners(owners, split)
    order = [(k, part) for part in range(split) for k in cut]
    far = [k for k in far if k not in cut]
    while far or near:
        order += [(k, 0) for k in near[:1] + far[:1]]
        far, near = far[1:], near[1:]
    return order + [(0, 0)]


def split_partners(owners, split):
    return [owners // 2, owners // 2 + 1] if split > 1 else []


def in_turn(blocks, split):
    return [blocks[k][part] for k, part in turns(len(blocks), split)]


def in_place(refs, owners):
    split = 1 + (len(refs) > owners)
    blocks = [[] for _ in range(owners)]
    for (k, _), ref in zip(turns(owners, split), refs):
        blocks[k].append(ref)
    return blocks


def jac_kernel(first_mat, joined, act_hbm, cot_hbm, *refs):
    before, refs = refs[: len(joined)], refs[len(joined) :]
    *out_refs, act_buf, cot_buf, held, sems = refs
    samples, mats, _, d = held.shape
    share = d // len(out_refs)
    me = lax.axis_index("samp")
    group = 2
    copies = []
    for first in range(0, samples, group):
        here = pl.ds(first, group)
        mine = (here, pl.ds(first_mat, mats))
        sem = first // group
        copies.append(pltpu.make_async_copy(act_hbm.at[mine], act_buf.at[here], sems.at[0, sem]))
        copies.append(pltpu.make_async_copy(cot_hbm.at[mine], cot_buf.at[here], sems.at[1, sem]))
    for copy in copies:
        copy.start()
    for k, ref in zip(joined, before):
        out_refs[k][:, : ref.shape[1]] = ref[...]

    def share_out(samples):
        for k, out_ref in enumerate(out_refs):
            owned = pl.ds(pl.multiple_of((me ^ k) * share, share), share)
            for s in samples:
                rows = [held[s, m, owned] for m in range(mats)]
                rows = jnp.concatenate(rows, axis=0).astype(BF16)
                out_ref[s, out_ref.shape[1] - mats * share :] = rows

    for first in range(0, samples, group):
        here = range(first, first + group)
        copies[first].wait()
        copies[first + 1].wait()
        for s in here:
            for m in range(mats):
                held[s, m] = lax.dot_general(
                    act_buf[s, m],
                    cot_buf[s, m],
                    (((0,), (0,)), ((), ())),
                    preferred_element_type=F32,
                ).astype(held.dtype)
        if first > 0:
            share_out(range(first - group, first))
    share_out(range(samples - group, samples))


def jac_rows(activations, cotangents, owners, part, split, before=()):
    samples, mats, sites, d = activations.shape
    mats //= split
    rows = mats * d // owners
    joined = [k for k, block in enumerate(before) if block is not None]
    out_rows = [rows + (before[k].shape[1] if k in joined else 0) for k in range(owners)]
    hbm = pl.BlockSpec(memory_space=pltpu.HBM)
    vmem = pl.BlockSpec(memory_space=pltpu.VMEM)
    return pl.pallas_call(
        functools.partial(jac_kernel, part * mats, joined),
        in_specs=[hbm, hbm] + [vmem] * len(joined),
        out_shape=[jax.ShapeDtypeStruct((samples, count, d), BF16) for count in out_rows],
        scratch_shapes=[
            pltpu.VMEM((samples, mats, sites, d), BF16),
            pltpu.VMEM((samples, mats, sites, d), BF16),
            pltpu.VMEM((samples, mats, d, d), BF16 if d // owners % CHUNK == 0 else F32),
            pltpu.SemaphoreType.DMA((2, samples)),
        ],
        compiler_params=pltpu.CompilerParams(vmem_limit_bytes=JAC_VMEM_LIMIT),
        cost_estimate=pl.CostEstimate(
            flops=2 * samples * mats * sites * d * d,
            bytes_accessed=6 * samples * mats * sites * d,
            transcendentals=0,
        ),
        name="jac_rows",
    )(activations, cotangents, *[before[k] for k in joined])


def jac_blocks(activations, cotangents, owners):
    mats, d = activations.shape[1], activations.shape[3]
    split = mats if mats == 2 and d // owners % CHUNK == 0 else 1
    blocks = [[block] for block in jac_rows(activations, cotangents, owners, 0, split)]
    if split > 1:
        cut = split_partners(owners, split)
        before = [None if k in cut else block[0] for k, block in enumerate(blocks)]
        later = jac_rows(activations, cotangents, owners, 1, split, before)
        blocks = [b + [new] if k in cut else [new] for k, (b, new) in enumerate(zip(blocks, later))]
    return blocks, split


def packed_shape(total):
    half = total // 2
    return half, -(-(3 * half + 2) // LANES) * LANES


def energy_kernel(total, spins_ref, offdiag_ref, out_ref):
    shape = out_ref.shape
    local = spins_ref.shape[0]
    sites = SIDE * SIDE
    z = (2 * spins_ref[...] - 1).astype(F32)
    column = iota((local, sites), 1) % SIDE
    right = jnp.where(
        column == SIDE - 1, pltpu.roll(z, SIDE - 1, 1), pltpu.roll(z, sites - 1, 1)
    )
    below = pltpu.roll(z, sites - SIDE, 1)
    energy = offdiag_ref[...] + jnp.sum(z * (right + below), axis=1, keepdims=True)
    half = total // 2
    first = lax.axis_index("samp") * local
    lower = first // half
    first = first - lower * half
    spread = jnp.concatenate([energy] * (half // local), axis=0)
    row = iota(shape, 0)
    here = (row >= first) & (row < first + local) & (iota(shape, 1) == 3 * half + lower)
    here = here & (lax.axis_index("layer") == 0)
    out_ref[...] = jnp.where(here, spread, F32(0.0))


def packed_energy(spins, offdiag, total):
    return pl.pallas_call(
        functools.partial(energy_kernel, total),
        out_shape=jax.ShapeDtypeStruct(packed_shape(total), F32),
        compiler_params=pltpu.CompilerParams(vmem_limit_bytes=VMEM_LIMIT),
        name="packed_energy",
    )(spins, offdiag[:, None])


def rows_of(parts, row, rows):
    for ref in parts:
        if row < ref.shape[1]:
            return ref[:, row : row + rows]
        row -= ref.shape[1]


def gram_kernel(owners, *refs):
    *block_refs, energy_ref, out_ref, flat, whole = refs
    blocks = in_place(block_refs, owners)
    local, count, d = blocks[0][0].shape
    total = local * owners
    joined = CHUNK // local
    me = lax.axis_index("samp")
    block = CHUNK * CHUNK
    dest = iota((block, block), 0)
    sample = dest % CHUNK
    sample = (sample // local ^ me % joined) * local + sample % local
    source = sample * CHUNK + dest // CHUNK
    swap = (iota((block, block), 1) == source).astype(F32).astype(BF16)
    for row in range(0, count, CHUNK):
        for j in range(owners // joined):
            pieces = [rows_of(p, row, CHUNK) for p in blocks[j * joined : (j + 1) * joined]]
            piece = jnp.concatenate(pieces, axis=0).reshape(block, d)
            turned = jnp.dot(swap, piece, preferred_element_type=F32).astype(BF16)
            place = pl.ds(pl.multiple_of((me // joined ^ j) * CHUNK, CHUNK), CHUNK)
            for r in range(CHUNK):
                flat[row + r, place] = turned[r * CHUNK : (r + 1) * CHUNK]
    lined = jnp.concatenate([flat[r] for r in range(count)], axis=1)
    gram = lax.dot_general(lined, lined, (((1,), (1,)), ((), ())), preferred_element_type=F32)
    whole[...] = jnp.zeros_like(whole)
    whole[:, :total] += gram
    half, width = out_ref.shape
    lane = iota((half, width), 1)
    lower = pltpu.roll(whole[half:], half, 1)
    packed = jnp.where(lane < 3 * half, lower, energy_ref[...])
    out_ref[...] = jnp.where(lane < half, whole[:half], packed)


def gram_partial(blocks, split, energies):
    local, count, d = blocks[0][0].shape
    total = local * len(blocks)
    return pl.pallas_call(
        functools.partial(gram_kernel, len(blocks)),
        out_shape=jax.ShapeDtypeStruct(packed_shape(total), F32),
        scratch_shapes=[
            pltpu.VMEM((count, total, d), BF16),
            pltpu.VMEM((total, packed_shape(total)[1]), F32),
        ],
        compiler_params=pltpu.CompilerParams(vmem_limit_bytes=VMEM_LIMIT),
        cost_estimate=pl.CostEstimate(
            flops=2 * total * total * count * d,
            bytes_accessed=2 * total * count * d,
            transcendentals=0,
        ),
        name="gram_partial",
    )(*in_turn(blocks, split), energies)


def tree_sum(parts):
    while len(parts) > 1:
        odd = parts[len(parts) // 2 * 2 :]
        parts = [a + b for a, b in zip(parts[::2], parts[1::2])] + odd
    return parts[0]


def pivot_rows(rows, entries):
    count = len(rows)
    rows = list(rows)
    p = [[entries[min(i, l)][max(i, l)] for l in range(count)] for i in range(count)]
    uppers = {}
    for j in range(0, count, 2):
        a, b, c = p[j][j], p[j][j + 1], p[j + 1][j + 1]
        determinant = a * c - b * b
        inverse = pl.reciprocal(determinant, approx=True)
        for _ in range(2):
            inverse = inverse * (F32(2.0) - determinant * inverse)

        def scaled(x, y):
            return (c * x - b * y) * inverse, (a * y - b * x) * inverse

        first, second = rows[j], rows[j + 1]
        rows[j], rows[j + 1] = scaled(first, second)
        later = range(j + 2, count)
        for l in later:
            uppers[j, l], uppers[j + 1, l] = scaled(p[j][l], p[j + 1][l])
        for i in later:
            rows[i] = rows[i] - (p[j][i] * rows[j] + p[j + 1][i] * rows[j + 1])
            for l in range(i, count):
                change = p[j][i] * uppers[j, l] + p[j + 1][i] * uppers[j + 1, l]
                p[i][l] = p[l][i] = p[i][l] - change
    for j in range(count - 4, -1, -2):
        for i in (j, j + 1):
            rows[i] = rows[i] - tree_sum([uppers[i, l] * rows[l] for l in range(j + 2, count)])
    return rows


def eliminate(matrix, total):
    width = matrix.shape[1]
    if total <= 64:
        blocks = [matrix[i : i + PIVOTS] for i in range(0, total, PIVOTS)]
        sub = iota((PIVOTS, width), 0)
        for b in range(len(blocks)):
            spread = [
                [
                    jnp.broadcast_to(block[:, b * PIVOTS + j : b * PIVOTS + j + 1], (PIVOTS, width))
                    for block in blocks
                ]
                for j in range(PIVOTS)
            ]

            def line(value, i):
                return jnp.broadcast_to(value[i : i + 1], (PIVOTS, width))

            entries = [
                [line(spread[l][b], i) if l >= i else None for l in range(PIVOTS)]
                for i in range(PIVOTS)
            ]
            rows = pivot_rows([line(blocks[b], i) for i in range(PIVOTS)], entries)
            for i in range(len(blocks)):
                if i != b:
                    terms = [spread[j][i] * rows[j] for j in range(PIVOTS)]
                    blocks[i] = blocks[i] - tree_sum(terms)
            solved = rows[0]
            for j in range(1, PIVOTS):
                solved = jnp.where(sub == j, rows[j], solved)
            blocks[b] = solved
        return jnp.concatenate([block[:, total : total + 1] for block in blocks], axis=0)
    row = iota(matrix.shape, 0)
    lane = iota(matrix.shape, 1)

    def one(k, held):
        column = jnp.sum(jnp.where(lane == k, held, F32(0.0)), axis=1, keepdims=True)
        pivot_row = jnp.sum(jnp.where(row == k, held, F32(0.0)), axis=0, keepdims=True)
        here = lane[:1] == k
        pivot = jnp.sum(jnp.where(here, pivot_row, F32(0.0)), axis=1, keepdims=True)
        scaled = pivot_row * (F32(1.0) / pivot)
        return held - jnp.where(row == k, F32(0.0), column) * scaled

    matrix = lax.fori_loop(0, total, one, matrix)
    diag = jnp.sum(jnp.where(row == lane, matrix, F32(0.0)), axis=1, keepdims=True)
    return matrix[:, total : total + 1] / diag


def sum_kernel(*refs):
    *part_refs, out_ref = refs
    out_ref[...] = tree_sum([ref[...] for ref in part_refs[::-1]])


def partners(value, masks):
    axes = ("samp", "layer")
    places = lax.axis_size("samp") * lax.axis_size("layer")
    perms = [[(i, i ^ mask) for i in range(places)] for mask in masks[::-1]]
    return [lax.ppermute(value, axes, perm) for perm in perms] + [value]


def sum_over(parts):
    return pl.pallas_call(
        sum_kernel,
        out_shape=jax.ShapeDtypeStruct(parts[0].shape, F32),
        compiler_params=pltpu.CompilerParams(vmem_limit_bytes=VMEM_LIMIT),
        name="sum_over",
    )(*parts)


def rounds(samp, layer):
    masks = [1 << bit for bit in range(1, layer.bit_length() - 1)]
    masks += [layer * (samp - 2), layer]
    masks += [layer << bit for bit in range(1, samp.bit_length() - 2)]
    later = zip(masks[::2], masks[1::2] + [0] * (len(masks) % 2))
    later = [[a, b, a ^ b] if b else [a] for a, b in later]
    return [[1]] + [[mask ^ 1 for mask in masks] for masks in later]


def solve_kernel(sums, owners, *refs):
    sum_refs, (*block_refs, weights_ref, update_ref, held) = refs[:sums], refs[sums:]
    blocks = in_place(block_refs, owners)
    mats, share, d = update_ref.shape
    local = weights_ref.shape[1]
    packed = tree_sum([ref[...] for ref in sum_refs[::-1]])
    half, packed_width = packed.shape
    total = 2 * half
    width = (total // LANES + 1) * LANES
    turned = jnp.swapaxes(packed[:, half:total], 0, 1)
    energy = [packed[:, 3 * half + i : 3 * half + i + 1] for i in range(2)]
    energy = [jnp.broadcast_to(e, (half, width - total)) for e in energy]
    upper = jnp.concatenate([packed[:, :half], turned, energy[0]], axis=1)
    lower = jnp.concatenate([packed[:, half : 3 * half], energy[1]], axis=1)
    raw = jnp.concatenate([upper, lower], axis=0)
    row = iota((total, width), 0)
    lane = iota((total, width), 1)
    inside = lane < total
    scale = F32(1.0 / total)
    row_mean = jnp.sum(jnp.where(inside, raw, F32(0.0)), axis=1, keepdims=True) * scale
    col_mean = jnp.sum(raw, axis=0, keepdims=True) * scale
    mean = jnp.sum(row_mean, axis=0, keepdims=True) * scale
    centered = raw - col_mean - row_mean + mean
    eps = (raw - col_mean) * F32(1.0 / total**0.5)
    on_diag = row == lane
    diag = jnp.where(on_diag, raw, F32(0.0))
    trace = jnp.sum(jnp.sum(diag, axis=0, keepdims=True), axis=1, keepdims=True) * scale - mean
    inverse = F32(1.0) / (trace * scale)
    shift = jnp.where(on_diag, F32(shift_ratio), F32(0.0))
    system = jnp.where(inside, centered * (scale * inverse) + shift, eps)
    weights = eliminate(system, total) * inverse
    me = lax.axis_index("samp")
    own = jnp.where(row - me * local == lane, weights, F32(0.0))
    weights_ref[...] = jnp.sum(own, axis=0, keepdims=True)[:, :local]
    coeffs = weights - jnp.sum(weights, axis=0, keepdims=True) * scale
    held[...] = jnp.broadcast_to(coeffs, (total, d))
    acc = jnp.zeros((mats * share, d), F32)
    for k, parts in enumerate(blocks):
        mine = held[pl.ds(pl.multiple_of((me ^ k) * local, local), local)]
        for s in range(local):
            rows = jnp.concatenate([ref[s].astype(F32) for ref in parts], axis=0)
            acc = acc + mine[s : s + 1] * rows
    for m in range(mats):
        update_ref[m] = acc[m * share : (m + 1) * share]


def solve_and_project(sums, blocks, split, mats):
    local, count, d = blocks[0][0].shape
    total = local * len(blocks)
    return pl.pallas_call(
        functools.partial(solve_kernel, len(sums), len(blocks)),
        out_shape=(
            jax.ShapeDtypeStruct((1, local), F32),
            jax.ShapeDtypeStruct((mats, count // mats, d), F32),
        ),
        scratch_shapes=[pltpu.VMEM((total, d), F32)],
        compiler_params=pltpu.CompilerParams(vmem_limit_bytes=VMEM_LIMIT),
        name="solve_and_project",
    )(*sums, *in_turn(blocks, split))


def body(spins, activations, cotangents, offdiag):
    local, mats = activations.shape[:2]
    owners = lax.axis_size("samp")
    total = local * owners
    blocks, split = jac_blocks(activations, cotangents, owners)
    for k, part in turns(owners, split)[:-1]:
        perm = [(i, i ^ k) for i in range(owners)]
        blocks[k][part] = lax.ppermute(blocks[k][part], "samp", perm)
    partial = gram_partial(blocks, split, packed_energy(spins, offdiag, total))
    *early, last = rounds(owners, lax.axis_size("layer"))
    for masks in early:
        partial = sum_over(partners(partial, masks))
    weights, update = solve_and_project(partners(partial, last), blocks, split, mats)
    return weights.reshape(local), update


def solution(mesh):
    placed = (
        P("samp", None),
        P("samp", "layer", None, None),
        P("samp", "layer", None, None),
        P("samp"),
    )
    return jax.shard_map(
        body,
        mesh=mesh,
        in_specs=placed,
        out_specs=(P("samp"), P("layer", "samp", None)),
        check_vma=False,
    )
```
